32 devices in a mesh: bucket: 8 (over y, x, core), fsdp: 4 (over z).
Axes of the slice: x: 2, y: 2, z: 4, core: 2. Of those that a mesh axis runs over, the one named last changes fastest.
Arguments:
- inputs: bfloat16 [16384, 1152], P(('bucket', 'fsdp')), may hold values from -6 to 6
- condition: bfloat16 [256, 1152], P(('bucket', 'fsdp')), may hold values from -6 to 6
- segment_ids: int32 [16384], P(('bucket', 'fsdp')), may hold values from 0 to 7, as said below
- grid_widths: int32 [256], P(('bucket', 'fsdp')), may hold values from 0 to 32, as said below
- bucket_counts: int32 [8], replicated, may hold values from 512 to 2048
- modulate_weight: bfloat16 [1152, 6912], P('fsdp'), may hold values from -0.1875 to 0.1875
- joint_weight: bfloat16 [1152, 3456], P('fsdp'), may hold values from -0.1875 to 0.1875
- project_weight: bfloat16 [1152, 1152], P('fsdp'), may hold values from -2 to 2
- gate_weight: bfloat16 [1152, 3072], P('fsdp'), may hold values from -0.1875 to 0.1875
- up_weight: bfloat16 [1152, 3072], P('fsdp'), may hold values from -0.1875 to 0.1875
- down_weight: bfloat16 [3072, 1152], P('fsdp'), may hold values from -0.109375 to 0.109375
- cotangent: bfloat16 [16384, 1152], P(('bucket', 'fsdp')), may hold values from -6 to 6
Outputs:
- output: bfloat16 [16384, 1152], P(('bucket', 'fsdp'))
- grad_inputs: float32 [16384, 1152], P(('bucket', 'fsdp'))
- grad_condition: float32 [256, 1152], P(('bucket', 'fsdp'))
- modulate_gradient: float32 [1152, 6912], P('fsdp')
- joint_gradient: float32 [1152, 3456], P('fsdp')
- project_gradient: float32 [1152, 1152], P('fsdp')
- gate_gradient: float32 [1152, 3072], P('fsdp')
- up_gradient: float32 [1152, 3072], P('fsdp')
- down_gradient: float32 [3072, 1152], P('fsdp')
The draws below stay inside these ranges and needn't reach their ends.
Inputs may be any that keep to these rules, and one draw needn't show every extreme that they name: `segment_ids`: each device's 512 tokens are whole images numbered 0, 1, 2, ... in order on that device; an image has 64, 128 or 256 tokens and never crosses a multiple of 256 tokens. `grid_widths`: an image's grid height is its token count divided by its width, from a quarter to four times the width; slots past a device's last image hold 0.
All inputs are finite; a program needn't handle non-finite values.
Results may differ from the reference program's by a relative error of at most 0.02.
The reference program's roundings to bfloat16 on the way count: a program that leaves them out, or rounds other values in their place, can miss the bound.
Values may be sent and summed in bfloat16 or wider, within the bound.
No kernel may reach another device: no remote copies, remote signals or barrier semaphores. Data moves between devices by JAX's collectives and lax.ppermute only.
A program may use at most 384 MiB of HBM per device.

```python
import jax
import jax.numpy as jnp
from jax import lax

D = 1152
HEADS = 16
HEAD_DIM = 72
FF = 3072
BLOCK_SIDE = 16
BLOCKS = 2
BLOCK_TOK = 256
TOK_DEV = 512
IMG_DEV = 8
TOKENS = 16384
SLOTS = 256
N_BUCKET = 8
N_FSDP = 4


def image_layout(key):
    rows = N_BUCKET * N_FSDP
    side = BLOCK_SIDE
    block_tok = side * side
    slots = 4 * BLOCKS
    pick_key, width_key, special_key = jax.random.split(key, 3)
    patterns = jnp.array([[block_tok, 0, 0, 0], [block_tok // 2, block_tok // 2, 0, 0], [block_tok // 4, block_tok // 4, block_tok // 4, block_tok // 4], [block_tok // 4, block_tok // 2, block_tok // 4, 0]], dtype=jnp.int32)
    picks = jax.random.randint(pick_key, (rows, BLOCKS), 0, 4)
    special = jax.random.randint(special_key, (), 0, rows)
    row_ids = jnp.arange(rows, dtype=jnp.int32)
    picks = jnp.where((row_ids == special)[:, None], 2, picks)
    neighbour = (special + 1) % rows
    picks = picks.at[neighbour, 0].set(0)
    lengths = patterns[picks].reshape(rows, slots)
    order_key = (lengths == 0).astype(jnp.int32) * slots + jnp.arange(slots, dtype=jnp.int32)[None, :]
    order = jnp.argsort(order_key, axis=1)
    lengths = jnp.take_along_axis(lengths, order, axis=1)
    choose = jax.random.randint(width_key, (rows, slots), 0, 6)
    choose = choose.at[neighbour, 0].set(2)
    full_table = jnp.array([2, 4, 8], dtype=jnp.int32)
    half_table = jnp.array([2, 4], dtype=jnp.int32)
    quarter_table = jnp.array([1, 2, 4], dtype=jnp.int32)
    quarters = jnp.where(lengths == block_tok, full_table[choose % 3], jnp.where(lengths == block_tok // 2, half_table[choose % 2], quarter_table[choose % 3]))
    widths = jnp.where(lengths > 0, side * quarters // 4, 0)
    starts = jnp.cumsum(lengths, axis=1) - lengths
    positions = jnp.arange(TOK_DEV, dtype=jnp.int32)
    begun = (starts[:, None, :] <= positions[None, :, None]) & (lengths[:, None, :] > 0)
    segments = jnp.sum(begun.astype(jnp.int32), axis=2) - 1
    return (segments.reshape(-1).astype(jnp.int32), widths.reshape(-1).astype(jnp.int32))


def draw_segment_ids(key, part):
    return image_layout(key)[0]


def draw_grid_widths(key, part):
    return image_layout(key)[1]


def with_ends(values, key, low, high):
    spot = [jax.random.randint(jax.random.fold_in(key, axis), (), 0, length) for axis, length in enumerate(values.shape)]
    widest = values.shape.index(max(values.shape))
    beside = spot[:widest] + [(spot[widest] + 1) % values.shape[widest]] + spot[widest + 1:]
    return values.at[tuple(spot)].set(low).at[tuple(beside)].set(high)


def steps_of(key, shape, cuts, smallest, top_value):
    level, own = 1.0, jax.random.fold_in(key, 6)
    for position, parts in cuts:
        draws = jnp.exp(jax.random.uniform(jax.random.fold_in(own, position), (parts,), jnp.float32, smallest / len(cuts), top_value / len(cuts)))
        level = level * jnp.repeat(draws, shape[position] // parts).reshape([-1 if axis == position else 1 for axis in range(len(shape))])
    return level


def noise(rng, dims, deviation, reach, pieces=(), held_as=jnp.bfloat16):
    values = deviation * jax.random.normal(rng, dims, jnp.float32)
    if pieces:
        values = values * steps_of(rng, dims, pieces, -0.22, 0.18)
    return jnp.clip(values, -reach, reach).astype(held_as)


def setup_inputs(seed: int = 0) -> dict:
    key_of = jax.random.split(jax.random.key(seed), 13)
    inputs = noise(key_of[0], (TOKENS, D), 1.0, 6.0, ((0, 32),))
    condition = noise(key_of[1], (SLOTS, D), 1.0, 6.0, ((0, 32),))
    segment_ids = draw_segment_ids(jax.random.fold_in(key_of[12], 71), 0)
    grid_widths = draw_grid_widths(jax.random.fold_in(key_of[12], 71), 0)
    bucket_counts = with_ends(jax.random.randint(key_of[4], (N_BUCKET,), TOK_DEV * N_FSDP // 4, TOK_DEV * N_FSDP + 1), jax.random.fold_in(key_of[4], 1), TOK_DEV * N_FSDP // 4, TOK_DEV * N_FSDP).astype(jnp.int32)
    modulate_weight = noise(key_of[5], (D, 6 * D), D ** -0.5, 0.1875, ((0, 4),))
    joint_weight = noise(key_of[6], (D, 3 * D), D ** -0.5, 0.1875, ((0, 4),))
    project_weight = noise(key_of[7], (D, D), (D * 2 // BLOCK_TOK) ** -0.5, 2.0, ((0, 4),))
    gate_weight = noise(key_of[8], (D, FF), D ** -0.5, 0.1875, ((0, 4),))
    up_weight = noise(key_of[9], (D, FF), D ** -0.5, 0.1875, ((0, 4),))
    down_weight = noise(key_of[10], (FF, D), FF ** -0.5, 0.109375, ((0, 4),))
    cotangent = noise(key_of[11], (TOKENS, D), 1.0, 6.0, ((0, 32),))
    return dict(inputs=inputs, condition=condition, segment_ids=segment_ids, grid_widths=grid_widths, bucket_counts=bucket_counts, modulate_weight=modulate_weight, joint_weight=joint_weight, project_weight=project_weight, gate_weight=gate_weight, up_weight=up_weight, down_weight=down_weight, cotangent=cotangent)


PRECISE = lax.Precision.HIGHEST
epsilon = 1e-06
masked_score = -1e+30

@jax.custom_vjp
def low(v):
    return lax.optimization_barrier(v.astype(jnp.bfloat16)).astype(jnp.float32)

@jax.custom_vjp
def low_back(v):
    return v

def low_keep(v):
    return (low(v), None)

def low_pass(kept, grad):
    return (grad,)

def back_keep(v):
    return (v, None)

def back_low(kept, grad):
    return (low(grad),)
low.defvjp(low_keep, low_pass)
low_back.defvjp(back_keep, back_low)

def product(left, right):
    return jnp.dot(left, right, precision=PRECISE, preferred_element_type=jnp.float32)

def layer_norm(values):
    average = lax.optimization_barrier(jnp.mean(values, axis=-1, keepdims=True))
    centered = values - average
    return centered * lax.rsqrt(lax.optimization_barrier(jnp.mean(centered * centered, axis=-1, keepdims=True)) + epsilon)

def rope_tables(segments, widths, quarter):
    slots = widths.shape[0]
    one_hot = (segments[:, None] == jnp.arange(slots, dtype=jnp.int32)[None, :]).astype(jnp.int32)
    counts = lax.optimization_barrier(jnp.sum(one_hot, axis=0))
    starts = jnp.cumsum(counts) - counts
    start_token = lax.optimization_barrier(jnp.sum(one_hot * starts[None, :], axis=1))
    width_token = jnp.maximum(lax.optimization_barrier(jnp.sum(one_hot * widths[None, :], axis=1)), 1)
    place = jnp.arange(segments.shape[0], dtype=jnp.int32) - start_token
    row_place = (place // width_token).astype(jnp.float32)
    col_place = (place % width_token).astype(jnp.float32)
    freqs = 10000.0 ** (-jnp.arange(quarter, dtype=jnp.float32) / quarter)
    angle_row = row_place[:, None] * freqs[None, :]
    angle_col = col_place[:, None] * freqs[None, :]
    return (jnp.cos(angle_row), jnp.sin(angle_row), jnp.cos(angle_col), jnp.sin(angle_col))

def rotate(values, tables, direction):
    cos_row, sin_row, cos_col, sin_col = tables
    quarter = cos_row.shape[-1]
    first_part = values[..., :quarter]
    second_part = values[..., quarter:2 * quarter]
    third_part = values[..., 2 * quarter:3 * quarter]
    fourth_part = values[..., 3 * quarter:]
    return jnp.concatenate([first_part * cos_row - direction * second_part * sin_row, second_part * cos_row + direction * first_part * sin_row, third_part * cos_col - direction * fourth_part * sin_col, fourth_part * cos_col + direction * third_part * sin_col], axis=-1)

def attend(query, keys, values, segments):
    scores = jnp.einsum('qhd,khd->hqk', query, keys, precision=PRECISE) * HEAD_DIM ** (-0.5)
    scores = low_back(scores)
    allowed = segments[:, None] == segments[None, :]
    scores = jnp.where(allowed[None], scores, masked_score)
    highest = lax.optimization_barrier(jnp.max(scores, axis=-1, keepdims=True))
    exponent = jnp.exp(scores - highest)
    probs = low(exponent / lax.optimization_barrier(jnp.sum(exponent, axis=-1, keepdims=True)))
    return jnp.einsum('hqk,khd->qhd', probs, values, precision=PRECISE)

def forward(inputs, condition, matrices, tables, segments):
    modulate_weight, joint_weight, project_weight, gate_weight, up_weight, down_weight = matrices
    modulation = low_back(product(low(jax.nn.silu(condition)), modulate_weight))
    per_token = jax.vmap(lambda table_rows, picks: table_rows[picks])(modulation, segments)
    shift_one, scale_one, gate_one, shift_two, scale_two, gate_two = jnp.split(per_token, 6, axis=-1)
    first = low(layer_norm(inputs) * (1.0 + scale_one) + shift_one)
    joint = low_back(product(first, joint_weight))
    devices, tokens = (inputs.shape[0], inputs.shape[1])
    joint = joint.reshape(devices, tokens, 3, HEADS, HEAD_DIM)
    query = low(rotate(joint[:, :, 0], tables, 1.0))
    keys = low(rotate(joint[:, :, 1], tables, 1.0))
    values = low(joint[:, :, 2])
    attended = lax.map(jax.checkpoint(lambda item: attend(*item)), (query, keys, values, segments))
    attended = low_back(low(attended.reshape(devices, tokens, HEADS * HEAD_DIM)))
    middle = inputs + gate_one * low_back(product(attended, project_weight))
    second = low(layer_norm(middle) * (1.0 + scale_two) + shift_two)
    gate = low_back(product(second, gate_weight))
    upval = low_back(product(second, up_weight))
    hidden = low(jax.nn.silu(gate) * upval)
    return middle + gate_two * low_back(product(hidden, down_weight))

def reference(inputs, condition, segment_ids, grid_widths, bucket_counts, modulate_weight, joint_weight, project_weight, gate_weight, up_weight, down_weight, cotangent):
    matrices = tuple((matrix.astype(jnp.float32) for matrix in (modulate_weight, joint_weight, project_weight, gate_weight, up_weight, down_weight)))
    counts = bucket_counts.astype(jnp.float32)
    factors = counts * N_BUCKET / jnp.sum(counts)
    bucket_inputs = inputs.astype(jnp.float32).reshape(N_BUCKET, N_FSDP, TOK_DEV, D)
    bucket_conds = condition.astype(jnp.float32).reshape(N_BUCKET, N_FSDP, IMG_DEV, D)
    bucket_segments = segment_ids.reshape(N_BUCKET, N_FSDP, TOK_DEV)
    bucket_widths = grid_widths.reshape(N_BUCKET, N_FSDP, IMG_DEV)
    bucket_cots = cotangent.astype(jnp.float32).reshape(N_BUCKET, N_FSDP, TOK_DEV, D)

    def bucket_step(totals, item):
        here_inputs, here_conds, here_segments, here_widths, here_cots, factor = item
        tables = jax.vmap(lambda segments, widths: rope_tables(segments, widths, HEAD_DIM // 4))(here_segments, here_widths)
        tables = tuple((table[:, :, None, :] for table in tables))

        def apply(values, conds, *weights):
            return forward(values, conds, weights, tables, here_segments)
        result, pull = jax.vjp(apply, here_inputs, here_conds, *matrices)
        grads = pull(here_cots * factor)
        totals = tuple((total + grad for total, grad in zip(totals, grads[2:])))
        return (totals, (result, grads[0], grads[1]))
    start = tuple((jnp.zeros_like(matrix) for matrix in matrices))
    totals, (results, input_grads, cond_grads) = lax.scan(bucket_step, start, (bucket_inputs, bucket_conds, bucket_segments, bucket_widths, bucket_cots, factors))
    output = results.reshape(N_BUCKET * N_FSDP * TOK_DEV, D).astype(jnp.bfloat16)
    grad_inputs = input_grads.reshape(N_BUCKET * N_FSDP * TOK_DEV, D)
    grad_condition = cond_grads.reshape(N_BUCKET * N_FSDP * IMG_DEV, D)
    return (output, grad_inputs, grad_condition, totals[0], totals[1], totals[2], totals[3], totals[4], totals[5])
```

```python
import jax
import jax.numpy as jnp
from jax import lax
from jax.sharding import PartitionSpec as P

HEADS = 16
HEAD_DIM = 72


epsilon = 1e-06
masked_score = -1e30


def rope_tables(segments, widths, quarter):
    slots = widths.shape[0]
    one_hot = (segments[:, None] == jnp.arange(slots, dtype=jnp.int32)[None, :]).astype(jnp.int32)
    counts = jnp.sum(one_hot, axis=0)
    starts = jnp.cumsum(counts) - counts
    start_token = jnp.sum(one_hot * starts[None, :], axis=1)
    width_token = jnp.maximum(jnp.sum(one_hot * widths[None, :], axis=1), 1)
    place = jnp.arange(segments.shape[0], dtype=jnp.int32) - start_token
    row_place = (place // width_token).astype(jnp.float32)
    col_place = (place % width_token).astype(jnp.float32)
    freqs = 10000.0 ** (-jnp.arange(quarter, dtype=jnp.float32) / quarter)
    angle_row = row_place[:, None] * freqs[None, :]
    angle_col = col_place[:, None] * freqs[None, :]
    return (jnp.cos(angle_row), jnp.sin(angle_row), jnp.cos(angle_col), jnp.sin(angle_col))


def rotate(values, tables, direction):
    cos_row, sin_row, cos_col, sin_col = tables
    quarter = cos_row.shape[-1]
    first_part = values[..., :quarter]
    second_part = values[..., quarter : 2 * quarter]
    third_part = values[..., 2 * quarter : 3 * quarter]
    fourth_part = values[..., 3 * quarter :]
    return jnp.concatenate(
        [
            first_part * cos_row - direction * second_part * sin_row,
            second_part * cos_row + direction * first_part * sin_row,
            third_part * cos_col - direction * fourth_part * sin_col,
            fourth_part * cos_col + direction * third_part * sin_col,
        ],
        axis=-1,
    )


def normalize(values):
    average = jnp.mean(values, axis=-1, keepdims=True)
    centered = values - average
    inverse = lax.rsqrt(jnp.mean(centered * centered, axis=-1, keepdims=True) + epsilon)
    return (centered * inverse, inverse)


def normalize_back(normed, inverse, upstream):
    return inverse * (
        upstream
        - jnp.mean(upstream, axis=-1, keepdims=True)
        - normed * jnp.mean(upstream * normed, axis=-1, keepdims=True)
    )


def matmul(left, right):
    return jnp.dot(left, right, preferred_element_type=jnp.float32)


def contract_rows(left, right):
    return lax.dot_general(
        left, right, (((0,), (0,)), ((), ())), preferred_element_type=jnp.float32
    )


def times_transposed(left, right):
    return lax.dot_general(
        left, right, (((1,), (1,)), ((), ())), preferred_element_type=jnp.float32
    )


def silu_slope(values):
    sigmoid = jax.nn.sigmoid(values)
    return sigmoid * (1.0 + values * (1.0 - sigmoid))


BLOCK = 256


def shifts(count, by):
    return [(i, (i + by) % count) for i in range(count)]


def pick(array, index):
    return lax.dynamic_index_in_dim(array, index, 0, keepdims=False)


def gather_pieces(piece, own):
    count = lax.axis_size("fsdp")
    place = lax.axis_index("fsdp")
    foreign = jnp.stack(
        [lax.ppermute(piece, "fsdp", shifts(count, by)) for by in range(1, count)]
    )
    everyone = lax.all_gather(foreign, "bucket", axis=0, tiled=False)
    relative = [own] + [everyone[:, by - 1] for by in range(1, count)]
    relative = jnp.stack(relative)
    return jnp.stack([pick(relative, (place - j) % count) for j in range(count)])


def reduce_pieces(parts):
    count = lax.axis_size("fsdp")
    place = lax.axis_index("fsdp")
    mine = lax.psum_scatter(parts, "bucket", scatter_dimension=0, tiled=False)
    total = pick(mine, place).astype(jnp.float32)
    for by in range(1, count):
        total = total + lax.ppermute(
            pick(mine, (place + by) % count), "fsdp", shifts(count, by)
        ).astype(jnp.float32)
    return lax.all_gather(total.astype(jnp.bfloat16), "bucket", axis=0, tiled=False)


def to_group(rows, count, place):
    relative = jnp.stack(
        [pick(rows, place)]
        + [
            lax.ppermute(pick(rows, (place + by) % count), "fsdp", shifts(count, by))
            for by in range(1, count)
        ]
    )
    return jnp.stack([pick(relative, (place - j) % count) for j in range(count)])


def on_device(
    inputs,
    condition,
    segment_ids,
    grid_widths,
    bucket_counts,
    modulate_weight,
    joint_weight,
    project_weight,
    gate_weight,
    up_weight,
    down_weight,
    cotangent,
):
    fsdp_count = lax.axis_size("fsdp")
    bucket_count = lax.axis_size("bucket")
    place = lax.axis_index("fsdp")
    bucket = lax.axis_index("bucket")
    columns = bucket_count // 2
    height = joint_weight.shape[0]
    width = inputs.shape[1]
    ff = gate_weight.shape[1]
    down_rows = down_weight.shape[0] // bucket_count
    attn_shard = (
        jnp.concatenate([joint_weight, project_weight], axis=1)
        .reshape(2, height // 2, columns, 4 * width // columns)
        .transpose(2, 0, 1, 3)
        .reshape(bucket_count, height // 2, 4 * width // columns)
    )
    ffn_shard = jnp.stack(
        [
            gate_weight.reshape(height, columns, ff // columns).transpose(1, 0, 2),
            up_weight.reshape(height, columns, ff // columns).transpose(1, 0, 2),
        ],
        axis=1,
    ).reshape(bucket_count, height, ff // columns)
    down_shard = down_weight.reshape(bucket_count, down_rows, width)
    attn_full = gather_pieces(pick(attn_shard, bucket), attn_shard)
    attn_full = (
        attn_full.reshape(fsdp_count, columns, 2, height // 2, 4 * width // columns)
        .transpose(0, 2, 3, 1, 4)
        .reshape(width, 4 * width)
    )
    joint_full, project_full = attn_full[:, : 3 * width], attn_full[:, 3 * width :]
    ffn_full = gather_pieces(pick(ffn_shard, bucket), ffn_shard)
    ffn_full = (
        ffn_full.reshape(fsdp_count, columns, 2, height, ff // columns)
        .transpose(2, 0, 3, 1, 4)
        .reshape(2, width, ff)
    )
    gate_full, up_full = ffn_full[0], ffn_full[1]
    down_full = gather_pieces(pick(down_shard, bucket), down_shard).reshape(ff, width)
    tokens, width = inputs.shape
    slots = condition.shape[0]
    heads = HEADS
    head_size = HEAD_DIM
    scaling = head_size ** (-0.5)
    tables = tuple(
        (table[:, None, :] for table in rope_tables(segment_ids, grid_widths, head_size // 4))
    )
    one_hot = (segment_ids[:, None] == jnp.arange(slots, dtype=jnp.int32)[None, :]).astype(
        jnp.float32
    )
    cond_float = condition.astype(jnp.float32)
    lifted = jax.nn.silu(cond_float).astype(jnp.bfloat16)
    lifted_rows = to_group(
        lifted.reshape(slots, fsdp_count, height).transpose(1, 0, 2), fsdp_count, place
    ).reshape(fsdp_count * slots, height)
    modulation = jnp.sum(
        to_group(
            matmul(lifted_rows, modulate_weight).reshape(fsdp_count, slots, 6 * width),
            fsdp_count,
            place,
        ),
        axis=0,
    )
    per_token = jnp.dot(
        one_hot, modulation, precision=lax.Precision.HIGHEST, preferred_element_type=jnp.float32
    )
    shift_one, scale_one, gate_one, shift_two, scale_two, gate_two = jnp.split(per_token, 6, axis=1)
    residual = inputs.astype(jnp.float32)
    normed_one, inverse_one = normalize(residual)
    first = (normed_one * (1.0 + scale_one) + shift_one).astype(jnp.bfloat16)
    joint = matmul(first, joint_full).reshape(tokens, 3, heads, head_size)
    query = rotate(joint[:, 0], tables, 1.0).astype(jnp.bfloat16)
    keys = rotate(joint[:, 1], tables, 1.0).astype(jnp.bfloat16)
    values = joint[:, 2].astype(jnp.bfloat16)
    blocks = tokens // BLOCK
    query, keys, values = (
        part.reshape(blocks, BLOCK, heads, head_size) for part in (query, keys, values)
    )
    block_ids = segment_ids.reshape(blocks, BLOCK)
    allowed = block_ids[:, :, None] == block_ids[:, None, :]
    scores = (
        jnp.einsum("bqhd,bkhd->bhqk", query, keys, preferred_element_type=jnp.float32) * scaling
    )
    scores = jnp.where(allowed[:, None], scores, masked_score)
    exponent = jnp.exp(scores - jnp.max(scores, axis=-1, keepdims=True))
    soft = exponent / jnp.sum(exponent, axis=-1, keepdims=True)
    probs = soft.astype(jnp.bfloat16)
    mixed = jnp.einsum("bhqk,bkhd->bqhd", probs, values, preferred_element_type=jnp.float32)
    attended = mixed.reshape(tokens, width).astype(jnp.bfloat16)
    branch = matmul(attended, project_full)
    middle = residual + gate_one * branch
    normed_two, inverse_two = normalize(middle)
    second = (normed_two * (1.0 + scale_two) + shift_two).astype(jnp.bfloat16)
    gate = matmul(second, gate_full)
    upval = matmul(second, up_full)
    hidden = (jax.nn.silu(gate) * upval).astype(jnp.bfloat16)
    feed = matmul(hidden, down_full)
    output = (middle + gate_two * feed).astype(jnp.bfloat16)
    counts = bucket_counts.astype(jnp.float32)
    mine = jnp.sum(jnp.where(jnp.arange(counts.shape[0], dtype=jnp.int32) == bucket, counts, 0.0))
    upstream = cotangent.astype(jnp.float32) * (mine * counts.shape[0] / jnp.sum(counts))
    feed_back = (upstream * gate_two).astype(jnp.bfloat16)
    down_gradient = contract_rows(hidden, feed_back)
    hidden_back = times_transposed(feed_back, down_full)
    up_back = (hidden_back * jax.nn.silu(gate)).astype(jnp.bfloat16)
    gate_back = (hidden_back * upval * silu_slope(gate)).astype(jnp.bfloat16)
    gate_gradient = contract_rows(second, gate_back)
    up_gradient = contract_rows(second, up_back)
    second_back = times_transposed(gate_back, gate_full) + times_transposed(up_back, up_full)
    middle_back = upstream + normalize_back(
        normed_two, inverse_two, second_back * (1.0 + scale_two)
    )
    branch_back = (middle_back * gate_one).astype(jnp.bfloat16)
    project_gradient = contract_rows(attended, branch_back)
    attended_back = (
        times_transposed(branch_back, project_full)
        .astype(jnp.bfloat16)
        .reshape(blocks, BLOCK, heads, head_size)
    )

    probs_back = jnp.einsum(
        "bqhd,bkhd->bhqk", attended_back, values, preferred_element_type=jnp.float32
    )
    scores_back = (
        soft * (probs_back - jnp.sum(soft * probs_back, axis=-1, keepdims=True))
    ).astype(jnp.bfloat16)
    query_back = (
        jnp.einsum("bhqk,bkhd->bqhd", scores_back, keys, preferred_element_type=jnp.float32) * scaling
    )
    keys_back = (
        jnp.einsum("bhqk,bqhd->bkhd", scores_back, query, preferred_element_type=jnp.float32)
        * scaling
    )
    values_back = jnp.einsum(
        "bhqk,bqhd->bkhd", probs, attended_back, preferred_element_type=jnp.float32
    )
    query_back = query_back.reshape(tokens, heads, head_size)
    keys_back = keys_back.reshape(tokens, heads, head_size)
    values_back = values_back.reshape(tokens, heads, head_size)
    joint_back = (
        jnp.stack(
            [rotate(query_back, tables, -1.0), rotate(keys_back, tables, -1.0), values_back], axis=1
        )
        .reshape(tokens, 3 * width)
        .astype(jnp.bfloat16)
    )
    joint_gradient = contract_rows(first, joint_back)
    first_back = times_transposed(joint_back, joint_full)
    grad_inputs = middle_back + normalize_back(
        normed_one, inverse_one, first_back * (1.0 + scale_one)
    )
    per_token_back = jnp.concatenate(
        [
            first_back,
            first_back * normed_one,
            middle_back * branch,
            second_back,
            second_back * normed_two,
            upstream * feed,
        ],
        axis=1,
    )
    modulation_back = lax.dot_general(
        one_hot,
        per_token_back,
        (((0,), (0,)), ((), ())),
        precision=lax.Precision.HIGHEST,
        preferred_element_type=jnp.float32,
    ).astype(jnp.bfloat16)
    everyone = lax.all_gather(
        jnp.concatenate([modulation_back, lifted], axis=1), ("bucket", "fsdp"), axis=0, tiled=True
    )
    all_back = everyone[:, : 6 * width]
    all_lifted = lax.dynamic_slice_in_dim(everyone, 6 * width + place * height, height, 1)
    modulate_gradient = contract_rows(all_lifted, all_back)
    group_back = lax.dynamic_slice_in_dim(
        all_back, bucket * fsdp_count * slots, fsdp_count * slots, 0
    )
    slope_rows = times_transposed(group_back, modulate_weight)
    condition_slope = (
        to_group(slope_rows.reshape(fsdp_count, slots, height), fsdp_count, place)
        .transpose(1, 0, 2)
        .reshape(slots, width)
    )
    grad_condition = condition_slope * silu_slope(cond_float)
    down_parts = (
        down_gradient.astype(jnp.bfloat16)
        .reshape(fsdp_count, bucket_count, down_rows, width)
        .swapaxes(0, 1)
    )
    down_sum = reduce_pieces(down_parts).reshape(bucket_count * down_rows, width)
    ffn_parts = (
        jnp.stack([gate_gradient.astype(jnp.bfloat16), up_gradient.astype(jnp.bfloat16)])
        .reshape(2, fsdp_count, height, columns, ff // columns)
        .transpose(3, 0, 1, 2, 4)
        .reshape(bucket_count, fsdp_count, height, ff // columns)
    )
    ffn_sum = (
        reduce_pieces(ffn_parts)
        .reshape(columns, 2, height, ff // columns)
        .transpose(1, 2, 0, 3)
        .reshape(2, height, ff)
    )
    attn_parts = (
        jnp.concatenate(
            [joint_gradient.astype(jnp.bfloat16), project_gradient.astype(jnp.bfloat16)], axis=1
        )
        .reshape(fsdp_count, 2, height // 2, columns, 4 * width // columns)
        .transpose(3, 1, 0, 2, 4)
        .reshape(bucket_count, fsdp_count, height // 2, 4 * width // columns)
    )
    attn_sum = (
        reduce_pieces(attn_parts)
        .reshape(columns, 2, height // 2, 4 * width // columns)
        .transpose(1, 2, 0, 3)
        .reshape(height, 4 * width)
    )
    shares = tuple(
        part.astype(jnp.float32)
        for part in (
            attn_sum[:, : 3 * width],
            attn_sum[:, 3 * width :],
            ffn_sum[0],
            ffn_sum[1],
            down_sum,
        )
    )
    return (
        output,
        grad_inputs,
        grad_condition,
        modulate_gradient,
        shares[0],
        shares[1],
        shares[2],
        shares[3],
        shares[4],
    )


def solution(mesh):
    in_specs = (
        P(("bucket", "fsdp"), None),
        P(("bucket", "fsdp"), None),
        P(("bucket", "fsdp")),
        P(("bucket", "fsdp")),
        P(),
        P("fsdp", None),
        P("fsdp", None),
        P("fsdp", None),
        P("fsdp", None),
        P("fsdp", None),
        P("fsdp", None),
        P(("bucket", "fsdp"), None),
    )
    out_specs = (
        P(("bucket", "fsdp"), None),
        P(("bucket", "fsdp"), None),
        P(("bucket", "fsdp"), None),
        P("fsdp", None),
        P("fsdp", None),
        P("fsdp", None),
        P("fsdp", None),
        P("fsdp", None),
        P("fsdp", None),
    )
    return jax.shard_map(
        on_device, mesh=mesh, in_specs=in_specs, out_specs=out_specs, check_vma=False
    )
```

```python
import functools

import jax
import jax.numpy as jnp
from jax import lax
from jax.experimental import pallas as pl
from jax.experimental.pallas import tpu as pltpu
from jax.sharding import PartitionSpec as P

HEADS = 16
HEAD_DIM = 72
WIDTH = HEADS * HEAD_DIM
QUARTER = HEAD_DIM // 4
BLOCK = 256
CHUNK = 64
COLUMNS = 4
HALVES = 2
PIECES = COLUMNS * HALVES
LANES = 128

epsilon = 1e-06
masked_score = -1e30
f32 = jnp.float32
bf16 = jnp.bfloat16
MEGA = 2**20


def normalize(values):
    average = jnp.mean(values, axis=-1, keepdims=True)
    centered = values - average
    inverse = lax.rsqrt(jnp.mean(centered * centered, axis=-1, keepdims=True) + epsilon)
    return (centered * inverse, inverse)


def normalize_back(normed, inverse, upstream):
    return inverse * (
        upstream
        - jnp.mean(upstream, axis=-1, keepdims=True)
        - normed * jnp.mean(upstream * normed, axis=-1, keepdims=True)
    )


def matmul(left, right):
    return jnp.dot(left, right, preferred_element_type=f32)


def contract_rows(left, right):
    return lax.dot_general(left, right, (((0,), (0,)), ((), ())), preferred_element_type=f32)


def times_transposed(left, right):
    return lax.dot_general(left, right, (((1,), (1,)), ((), ())), preferred_element_type=f32)


def silu_slope(values):
    sigmoid = jax.nn.sigmoid(values)
    return sigmoid * (1.0 + values * (1.0 - sigmoid))


def rope_tables(segments, widths):
    slots = widths.shape[0]
    one_hot = (segments[:, None] == jnp.arange(slots, dtype=jnp.int32)[None, :]).astype(jnp.int32)
    counts = jnp.sum(one_hot, axis=0)
    starts = jnp.cumsum(counts) - counts
    start_token = jnp.sum(one_hot * starts[None, :], axis=1)
    width_token = jnp.maximum(jnp.sum(one_hot * widths[None, :], axis=1), 1)
    place = jnp.arange(segments.shape[0], dtype=jnp.int32) - start_token
    row_place = (place // width_token).astype(f32)
    col_place = (place % width_token).astype(f32)
    freqs = 10000.0 ** (-jnp.arange(QUARTER, dtype=f32) / QUARTER)
    angle_row = row_place[:, None] * freqs[None, :]
    angle_col = col_place[:, None] * freqs[None, :]
    cos_row, sin_row, cos_col, sin_col = (
        jnp.cos(angle_row),
        jnp.sin(angle_row),
        jnp.cos(angle_col),
        jnp.sin(angle_col),
    )
    cos = jnp.concatenate([cos_row, cos_row, cos_col, cos_col], axis=1)
    sin = jnp.concatenate([-sin_row, sin_row, -sin_col, sin_col], axis=1)
    return jnp.tile(cos, (1, HEADS)), jnp.tile(sin, (1, HEADS))


def part(index):
    return slice(index * WIDTH, (index + 1) * WIDTH)


def rotate(values, cos, sin):
    lane = lax.broadcasted_iota(jnp.int32, values.shape, 1)
    leading = lane % (2 * QUARTER) < QUARTER
    partner = jnp.where(
        leading,
        pltpu.roll(values, WIDTH - QUARTER, 1),
        pltpu.roll(values, QUARTER, 1),
    )
    return values * cos + partner * sin


def attn_copies(place, column, shard, everyone, target, sems, count):
    rows = shard.shape[0]
    half = rows // HALVES
    copies = [
        pltpu.make_async_copy(
            shard, target.at[pl.ds(pl.multiple_of(place * rows, 16), rows)], sems.at[0]
        )
    ]
    for by in range(1, count):
        start = ((place + (count - by)) % count) * rows
        for h in range(HALVES):
            copies.append(
                pltpu.make_async_copy(
                    everyone.at[column * HALVES + h, by - 1],
                    target.at[pl.ds(pl.multiple_of(start + h * half, 16), half)],
                    sems.at[1 + (by - 1) * HALVES + h],
                )
            )
    return copies


def first_kernel(
    count, place_ref, x_ref, mod_ref, cos_ref, sin_ref, joint_ref, every_ref,
    first_ref, query_ref, keys_ref, values_ref, weight, total, sems,
):
    place = place_ref[0]
    copies = [
        attn_copies(
            place, c, joint_ref.at[:, pl.ds(c * WIDTH, WIDTH)], every_ref, weight.at[c], sems.at[c], count
        )
        for c in range(3)
    ]
    for group in copies:
        for copy in group:
            copy.start()
    tokens = x_ref.shape[0]
    for i in range(tokens // CHUNK):
        rows = slice(i * CHUNK, (i + 1) * CHUNK)
        normed, _ = normalize(x_ref[rows, :].astype(f32))
        first_ref[rows, :] = (
            normed * (1.0 + mod_ref[i : i + 1, part(1)]) + mod_ref[i : i + 1, part(0)]
        ).astype(bf16)
    for c, out in enumerate((query_ref, keys_ref, values_ref)):
        for copy in copies[c]:
            copy.wait()
        if c == 2:
            out[...] = matmul(first_ref[...], weight[c]).astype(bf16)
        else:
            total[...] = matmul(first_ref[...], weight[c])

            @pl.loop(0, tokens // CHUNK)
            def _(i):
                rows = pl.ds(pl.multiple_of(i * CHUNK, CHUNK), CHUNK)
                out[rows, :] = rotate(total[rows, :], cos_ref[rows, :], sin_ref[rows, :]).astype(bf16)


def window(head):
    start = head * HEAD_DIM // LANES * LANES
    stop = -(-(head + 1) * HEAD_DIM // LANES) * LANES
    lane = lax.broadcasted_iota(jnp.int32, (1, stop - start), 1) + start
    inside = (lane >= head * HEAD_DIM) & (lane < (head + 1) * HEAD_DIM)
    return slice(start, stop), inside


def soft_scores(query, keys, allowed):
    scores = times_transposed(query, keys) * HEAD_DIM ** (-0.5)
    scores = jnp.where(allowed, scores, masked_score)
    exponent = jnp.exp(scores - jnp.max(scores, axis=-1, keepdims=True))
    return exponent * (1.0 / jnp.sum(exponent, axis=-1, keepdims=True))


def attend_kernel(
    count, place_ref, query_ref, keys_ref, values_ref, column_ids, row_ids, x_ref, mod_ref,
    project_ref, every_ref, attended_ref, branch_ref, middle_ref, second_ref, weight, mixed, sems,
):
    copies = attn_copies(place_ref[0], 3, project_ref, every_ref, weight, sems, count)

    @pl.when(pl.program_id(0) == 0)
    def _():
        for copy in copies:
            copy.start()

    allowed = column_ids[...] == row_ids[...]
    for head in range(HEADS):
        lanes, inside = window(head)
        query = jnp.where(inside, query_ref[:, lanes], jnp.zeros((), bf16))
        probs = soft_scores(query, keys_ref[:, lanes], allowed).astype(bf16)
        mixed[:, lanes] = jnp.where(inside, matmul(probs, values_ref[:, lanes]), mixed[:, lanes])
    attended_ref[...] = mixed[...].astype(bf16)

    @pl.when(pl.program_id(0) == 0)
    def _():
        for copy in copies:
            copy.wait()

    branch_ref[...] = matmul(attended_ref[...], weight[...])
    for i in range(BLOCK // CHUNK):
        rows = slice(i * CHUNK, (i + 1) * CHUNK)
        mod = mod_ref.at[0]
        middle = x_ref[rows, :].astype(f32) + mod[i : i + 1, part(2)] * branch_ref[rows, :]
        middle_ref[rows, :] = middle
        normed, _ = normalize(middle)
        second_ref[rows, :] = (
            normed * (1.0 + mod[i : i + 1, part(4)]) + mod[i : i + 1, part(3)]
        ).astype(bf16)


def ffn_kernel(
    count, place_ref, factor_ref, second_ref, middle_ref, branch_ref, cot_ref, mod_ref,
    gate_ref, up_ref, down_ref, every_ref, every_down,
    output_ref, hidden_ref, gate_back_ref, up_back_ref, feed_back_ref, middle_back_ref,
    branch_back_ref, sums_ref, gate_w, up_w, down_w, feed, second_back, sems,
):
    step = pl.program_id(0)
    steps = pl.num_programs(0)
    place = place_ref[0]
    rows_in = gate_ref.shape[0]
    tile = hidden_ref.shape[1]
    tokens = second_ref.shape[0]

    def copies(c, slot):
        found = []
        for which, (shard, target) in enumerate(((gate_ref, gate_w), (up_ref, up_w))):
            found.append(
                pltpu.make_async_copy(
                    shard.at[:, pl.ds(pl.multiple_of(c * tile, LANES), tile)],
                    target.at[slot, pl.ds(pl.multiple_of(place * rows_in, 16), rows_in)],
                    sems.at[slot, which * count],
                )
            )
            for by in range(1, count):
                start = ((place + (count - by)) % count) * rows_in
                found.append(
                    pltpu.make_async_copy(
                        every_ref.at[c * HALVES + which, by - 1],
                        target.at[slot, pl.ds(pl.multiple_of(start, 16), rows_in)],
                        sems.at[slot, which * count + by],
                    )
                )
        return found

    def down_copies(c, slot):
        sem = sems.at[slot, 2 * count]
        own = pltpu.make_async_copy(down_ref, down_w.at[slot], sem)
        by = (place + count - c) % count
        other = pltpu.make_async_copy(
            every_down.at[:, jnp.maximum(by, 1) - 1], down_w.at[slot], sem
        )
        return own, other

    def start(c, slot):
        for copy in copies(c, slot):
            copy.start()
        own, other = down_copies(c, slot)

        @pl.when(c == place)
        def _():
            own.start()

        @pl.when(c != place)
        def _():
            other.start()

    slot = step % 2

    @pl.when(step == 0)
    def _():
        start(step, slot)
        for i in range(tokens // CHUNK):
            rows = slice(i * CHUNK, (i + 1) * CHUNK)
            upstream = cot_ref[rows, :].astype(f32) * factor_ref[0]
            feed_back_ref[rows, :] = (upstream * mod_ref[i : i + 1, part(5)]).astype(bf16)

    @pl.when(step + 1 < steps)
    def _():
        start(step + 1, 1 - slot)

    for copy in copies(step, slot):
        copy.wait()
    down_copies(step, slot)[0].wait()

    sub = 256
    for n in range(tile // sub):
        lanes = slice(n * sub, (n + 1) * sub)
        gate = matmul(second_ref[...], gate_w[slot, :, lanes])
        upval = matmul(second_ref[...], up_w[slot, :, lanes])
        down = down_w[slot].reshape(tile, WIDTH)[lanes, :]
        hidden_back = times_transposed(feed_back_ref[...], down)
        sigmoid = jax.nn.sigmoid(gate)
        silu = gate * sigmoid
        hidden_ref[:, lanes] = (silu * upval).astype(bf16)
        up_back_ref[:, lanes] = (hidden_back * silu).astype(bf16)
        gate_back_ref[:, lanes] = (
            hidden_back * upval * (sigmoid * (1.0 + gate * (1.0 - sigmoid)))
        ).astype(bf16)

    feed_part = matmul(hidden_ref[...], down_w[slot].reshape(tile, WIDTH))
    back_part = times_transposed(gate_back_ref[...], gate_w[slot]) + times_transposed(
        up_back_ref[...], up_w[slot]
    )

    @pl.when(step == 0)
    def _():
        feed[...] = feed_part
        second_back[...] = back_part

    @pl.when(step > 0)
    def _():
        feed[...] += feed_part
        second_back[...] += back_part

    @pl.when(step == steps - 1)
    def _():
        for i in range(tokens // CHUNK):
            rows = slice(i * CHUNK, (i + 1) * CHUNK)
            gate_one = mod_ref[i : i + 1, part(2)]
            scale_two = mod_ref[i : i + 1, part(4)]
            gate_two = mod_ref[i : i + 1, part(5)]
            middle = middle_ref[rows, :]
            output_ref[rows, :] = (middle + gate_two * feed[rows, :]).astype(bf16)
            upstream = cot_ref[rows, :].astype(f32) * factor_ref[0]
            normed, inverse = normalize(middle)
            back = second_back[rows, :]
            middle_back = upstream + normalize_back(normed, inverse, back * (1.0 + scale_two))
            middle_back_ref[rows, :] = middle_back
            branch_back_ref[rows, :] = (middle_back * gate_one).astype(bf16)
            for where, values in enumerate(
                (middle_back * branch_ref[rows, :], back, back * normed, upstream * feed[rows, :])
            ):
                sums_ref[i : i + 1, part(where)] = jnp.sum(values, axis=0, keepdims=True)


def ffn_grad_kernel(second_ref, gate_back_ref, up_back_ref, out_ref, turned):
    @pl.when((pl.program_id(0) == 0) & (pl.program_id(1) == 0))
    def _():
        turned[...] = second_ref[...].T

    @pl.when(pl.program_id(1) == 0)
    def _():
        out_ref[0, 0] = matmul(turned[...], gate_back_ref[...]).astype(bf16)

    @pl.when(pl.program_id(1) == 1)
    def _():
        out_ref[0, 0] = matmul(turned[...], up_back_ref[...]).astype(bf16)


def down_grad_kernel(hidden_ref, feed_back_ref, out_ref):
    grad = contract_rows(hidden_ref[...], feed_back_ref[...]).astype(bf16)
    out_ref[...] = grad.reshape(out_ref.shape)


def attn_grad_kernel(first_ref, attended_ref, joint_back_ref, branch_back_ref, out_ref, turned):
    column = pl.program_id(0)
    count, half = out_ref.shape[2], out_ref.shape[3]

    @pl.when(column == 0)
    def _():
        turned[...] = first_ref[...].T

    @pl.when(column == 3)
    def _():
        turned[...] = attended_ref[...].T

    def put(right):
        for z in range(count):
            for h in range(HALVES):
                start = (z * HALVES + h) * half
                out_ref[0, h, z] = matmul(turned[start : start + half, :], right).astype(bf16)

    @pl.when(column < 3)
    def _():
        put(joint_back_ref[...])

    @pl.when(column == 3)
    def _():
        put(branch_back_ref[...])


def attend_back_kernel(
    count, place_ref, query_ref, keys_ref, values_ref, branch_back_ref, column_ids, row_ids, cos_ref,
    sin_ref, project_ref, every_ref, joint_back_ref, weight, mixed_back, query_back, keys_back,
    values_back, sems,
):
    copies = attn_copies(place_ref[0], 3, project_ref, every_ref, weight, sems, count)

    @pl.when(pl.program_id(0) == 0)
    def _():
        for copy in copies:
            copy.start()
        for copy in copies:
            copy.wait()

    mixed_back[...] = times_transposed(branch_back_ref[...], weight[...]).astype(bf16)
    allowed = column_ids[...] == row_ids[...]
    scaling = HEAD_DIM ** (-0.5)
    for head in range(HEADS):
        lanes, inside = window(head)
        zero = jnp.zeros((), bf16)
        query = jnp.where(inside, query_ref[:, lanes], zero)
        back = jnp.where(inside, mixed_back[:, lanes], zero)
        soft = soft_scores(query, keys_ref[:, lanes], allowed)
        probs_back = times_transposed(back, values_ref[:, lanes])
        scores_back = (
            soft * (probs_back - jnp.sum(soft * probs_back, axis=-1, keepdims=True))
        ).astype(bf16)
        query_back[:, lanes] = jnp.where(
            inside, matmul(scores_back, keys_ref[:, lanes]) * scaling, query_back[:, lanes]
        )
        keys_back[:, lanes] = jnp.where(
            inside, contract_rows(scores_back, query) * scaling, keys_back[:, lanes]
        )
        values_back[:, lanes] = jnp.where(
            inside, contract_rows(soft.astype(bf16), back), values_back[:, lanes]
        )

    @pl.loop(0, BLOCK // CHUNK)
    def _(i):
        rows = pl.ds(pl.multiple_of(i * CHUNK, CHUNK), CHUNK)
        cos, sin = cos_ref[rows, :], sin_ref[rows, :]
        joint_back_ref[rows, part(0)] = rotate(query_back[rows, :], cos, -sin).astype(bf16)
        joint_back_ref[rows, part(1)] = rotate(keys_back[rows, :], cos, -sin).astype(bf16)
        joint_back_ref[rows, part(2)] = values_back[rows, :].astype(bf16)


def first_back_kernel(
    count, place_ref, joint_back_ref, x_ref, middle_back_ref, mod_ref, joint_ref, every_ref,
    grad_ref, sums_ref, weight, first_back, sems,
):
    place = place_ref[0]
    copies = [
        attn_copies(
            place, c, joint_ref.at[:, pl.ds(c * WIDTH, WIDTH)], every_ref, weight.at[c], sems.at[c], count
        )
        for c in range(3)
    ]
    for group in copies:
        for copy in group:
            copy.start()
    for c in range(3):
        for copy in copies[c]:
            copy.wait()
        product = times_transposed(joint_back_ref[:, part(c)], weight[c])
        if c == 0:
            first_back[...] = product
        else:
            first_back[...] += product
    for i in range(x_ref.shape[0] // CHUNK):
        rows = slice(i * CHUNK, (i + 1) * CHUNK)
        normed, inverse = normalize(x_ref[rows, :].astype(f32))
        back = first_back[rows, :]
        grad_ref[rows, :] = middle_back_ref[rows, :] + normalize_back(
            normed, inverse, back * (1.0 + mod_ref[i : i + 1, part(1)])
        )
        sums_ref[i : i + 1, part(0)] = jnp.sum(back, axis=0, keepdims=True)
        sums_ref[i : i + 1, part(1)] = jnp.sum(back * normed, axis=0, keepdims=True)


SMEM = pl.BlockSpec(memory_space=pltpu.SMEM)
VMEM = pl.BlockSpec(memory_space=pltpu.VMEM)
ANY = pl.BlockSpec(memory_space=pl.ANY)


def struct(shape, dtype):
    return jax.ShapeDtypeStruct(shape, dtype)


def params(mega=56):
    return pltpu.CompilerParams(vmem_limit_bytes=mega * MEGA)


def cost(flops, *arrays):
    size = sum(a.size * a.dtype.itemsize for a in arrays)
    return pl.CostEstimate(flops=flops, bytes_accessed=size, transcendentals=0)


def by_block(*shape):
    return pl.BlockSpec(shape, lambda b: (b,) + (0,) * (len(shape) - 1))


def whole(*shape):
    return pl.BlockSpec(shape, lambda *_: (0,) * len(shape))


def first_call(place, x, mod, cos, sin, joint, every):
    tokens = x.shape[0]
    count = every.shape[1] + 1
    shape = struct((tokens, WIDTH), bf16)
    return pl.pallas_call(
        functools.partial(first_kernel, count),
        out_shape=(shape,) * 4,
        in_specs=[SMEM, VMEM, VMEM, VMEM, VMEM, ANY, ANY],
        out_specs=(VMEM,) * 4,
        scratch_shapes=[
            pltpu.VMEM((3, WIDTH, WIDTH), bf16),
            pltpu.VMEM((tokens, WIDTH), f32),
            pltpu.SemaphoreType.DMA((3, 1 + HALVES * (count - 1))),
        ],
        compiler_params=params(),
        cost_estimate=cost(6 * tokens * WIDTH * WIDTH, x, every, cos, sin),
    )(place, x, mod, cos, sin, joint, every)


def attend_call(place, query, keys, values, ids, x, mod, project, every):
    tokens = x.shape[0]
    count = every.shape[1] + 1
    return pl.pallas_call(
        functools.partial(attend_kernel, count),
        grid=(tokens // BLOCK,),
        out_shape=(
            struct((tokens, WIDTH), bf16),
            struct((tokens, WIDTH), f32),
            struct((tokens, WIDTH), f32),
            struct((tokens, WIDTH), bf16),
        ),
        in_specs=[SMEM]
        + [by_block(BLOCK, WIDTH)] * 3
        + [by_block(BLOCK, 1), pl.BlockSpec((1, BLOCK), lambda b: (0, b)), by_block(BLOCK, WIDTH)]
        + [by_block(1, BLOCK // CHUNK, 6 * WIDTH), ANY, ANY],
        out_specs=(by_block(BLOCK, WIDTH),) * 4,
        scratch_shapes=[
            pltpu.VMEM((WIDTH, WIDTH), bf16),
            pltpu.VMEM((BLOCK, WIDTH), f32),
            pltpu.SemaphoreType.DMA((1 + HALVES * (count - 1),)),
        ],
        compiler_params=params(),
        cost_estimate=cost(4 * tokens * WIDTH * WIDTH, query, keys, values, x, x, x, x, x),
    )(
        place, query, keys, values, ids[:, None], ids[None, :], x,
        mod.reshape(tokens // BLOCK, BLOCK // CHUNK, 6 * WIDTH), project, every,
    )


def ffn_call(place, factor, second, middle, branch, cot, mod, gate, up, down, every, every_down):
    tokens = second.shape[0]
    count = every.shape[1] + 1
    ff = gate.shape[1]
    tile = ff // COLUMNS
    down = down.reshape(PIECES, -1, WIDTH)
    tiled = pl.BlockSpec((tokens, tile), lambda c: (0, c))
    full = whole(tokens, WIDTH)
    chunks = tokens // CHUNK
    return pl.pallas_call(
        functools.partial(ffn_kernel, count),
        grid=(COLUMNS,),
        out_shape=(struct((tokens, WIDTH), bf16),)
        + (struct((tokens, ff), bf16),) * 3
        + (
            struct((tokens, WIDTH), bf16),
            struct((tokens, WIDTH), f32),
            struct((tokens, WIDTH), bf16),
            struct((chunks, 4 * WIDTH), f32),
        ),
        in_specs=[SMEM, SMEM, full, full, full, full, whole(chunks, 6 * WIDTH)] + [ANY] * 5,
        out_specs=(full, tiled, tiled, tiled, full, full, full, whole(chunks, 4 * WIDTH)),
        scratch_shapes=[
            pltpu.VMEM((2, WIDTH, tile), bf16),
            pltpu.VMEM((2, WIDTH, tile), bf16),
            pltpu.VMEM((2, PIECES, tile // PIECES, WIDTH), bf16),
            pltpu.VMEM((tokens, WIDTH), f32),
            pltpu.VMEM((tokens, WIDTH), f32),
            pltpu.SemaphoreType.DMA((2, 2 * count + 1)),
        ],
        compiler_params=params(),
        cost_estimate=cost(12 * tokens * WIDTH * ff, every, every_down, gate, gate, gate),
    )(place, factor, second, middle, branch, cot, mod, gate, up, down, every, every_down)


def ffn_grad_call(second, gate_back, up_back):
    tokens, ff = gate_back.shape
    tile = ff // COLUMNS
    tiled = pl.BlockSpec((tokens, tile), lambda c, h: (0, c))
    out = struct((COLUMNS, HALVES, WIDTH, tile), bf16)
    return pl.pallas_call(
        ffn_grad_kernel,
        grid=(COLUMNS, HALVES),
        out_shape=out,
        in_specs=[whole(tokens, WIDTH), tiled, tiled],
        out_specs=pl.BlockSpec((1, 1, WIDTH, tile), lambda c, h: (c, h, 0, 0)),
        scratch_shapes=[pltpu.VMEM((WIDTH, tokens), bf16)],
        compiler_params=params(),
        cost_estimate=cost(4 * tokens * WIDTH * ff, second, gate_back, up_back, out),
    )(second, gate_back, up_back)


def down_grad_call(count, hidden, feed_back):
    tokens, ff = hidden.shape
    rows = ff // count
    out = struct((PIECES, count, rows // PIECES, WIDTH), bf16)
    return pl.pallas_call(
        down_grad_kernel,
        grid=(count,),
        out_shape=out,
        in_specs=[pl.BlockSpec((tokens, rows), lambda z: (0, z)), whole(tokens, WIDTH)],
        out_specs=pl.BlockSpec((PIECES, 1, rows // PIECES, WIDTH), lambda z: (0, z, 0, 0)),
        compiler_params=params(),
        cost_estimate=cost(2 * tokens * WIDTH * ff, hidden, feed_back, out),
    )(hidden, feed_back)


def attn_grad_call(count, first, attended, joint_back, branch_back):
    tokens = first.shape[0]
    half = WIDTH // count // HALVES
    full = whole(tokens, WIDTH)
    out = struct((COLUMNS, HALVES, count, half, WIDTH), bf16)
    return pl.pallas_call(
        attn_grad_kernel,
        grid=(COLUMNS,),
        out_shape=out,
        in_specs=[
            full,
            full,
            pl.BlockSpec((tokens, WIDTH), lambda c: (0, jnp.minimum(c, 2))),
            full,
        ],
        out_specs=pl.BlockSpec((1, HALVES, count, half, WIDTH), lambda c: (c, 0, 0, 0, 0)),
        scratch_shapes=[pltpu.VMEM((WIDTH, tokens), bf16)],
        compiler_params=params(),
        cost_estimate=cost(8 * tokens * WIDTH * WIDTH, first, attended, joint_back, branch_back, out),
    )(first, attended, joint_back, branch_back)


def attend_back_call(place, query, keys, values, branch_back, ids, cos, sin, project, every):
    tokens = query.shape[0]
    count = every.shape[1] + 1
    block = by_block(BLOCK, WIDTH)
    return pl.pallas_call(
        functools.partial(attend_back_kernel, count),
        grid=(tokens // BLOCK,),
        out_shape=struct((tokens, 3 * WIDTH), bf16),
        in_specs=[SMEM, block, block, block, block]
        + [by_block(BLOCK, 1), pl.BlockSpec((1, BLOCK), lambda b: (0, b)), block, block, ANY, ANY],
        out_specs=by_block(BLOCK, 3 * WIDTH),
        scratch_shapes=[
            pltpu.VMEM((WIDTH, WIDTH), bf16),
            pltpu.VMEM((BLOCK, WIDTH), bf16),
            pltpu.VMEM((BLOCK, WIDTH), f32),
            pltpu.VMEM((BLOCK, WIDTH), f32),
            pltpu.VMEM((BLOCK, WIDTH), f32),
            pltpu.SemaphoreType.DMA((1 + HALVES * (count - 1),)),
        ],
        compiler_params=params(),
        cost_estimate=cost(8 * tokens * WIDTH * WIDTH, query, keys, values, branch_back, cos, sin),
    )(place, query, keys, values, branch_back, ids[:, None], ids[None, :], cos, sin, project, every)


def first_back_call(place, joint_back, x, middle_back, mod, joint, every):
    tokens = x.shape[0]
    count = every.shape[1] + 1
    return pl.pallas_call(
        functools.partial(first_back_kernel, count),
        out_shape=(struct((tokens, WIDTH), f32), struct((tokens // CHUNK, 2 * WIDTH), f32)),
        in_specs=[SMEM, VMEM, VMEM, VMEM, VMEM, ANY, ANY],
        out_specs=(VMEM, VMEM),
        scratch_shapes=[
            pltpu.VMEM((3, WIDTH, WIDTH), bf16),
            pltpu.VMEM((tokens, WIDTH), f32),
            pltpu.SemaphoreType.DMA((3, 1 + HALVES * (count - 1))),
        ],
        compiler_params=params(),
        cost_estimate=cost(6 * tokens * WIDTH * WIDTH, joint_back, x, middle_back, middle_back, every),
    )(place, joint_back, x, middle_back, mod, joint, every)


def shifts(count, by):
    return [(i, (i + by) % count) for i in range(count)]


def pick(array, index):
    return lax.dynamic_index_in_dim(array, index, 0, keepdims=False)


def gather_pieces(piece):
    count = lax.axis_size("fsdp")
    foreign = jnp.stack(
        [lax.ppermute(piece, "fsdp", shifts(count, by)) for by in range(1, count)]
    )
    return lax.all_gather(foreign, "bucket", axis=0, tiled=False)


def gather_whole(pieces):
    count = lax.axis_size("fsdp")
    place = lax.axis_index("fsdp")
    full = lax.all_gather(pieces, "fsdp", axis=0, tiled=False)
    return jnp.stack([pick(full, (place - by) % count) for by in range(1, count)], axis=1)


def reduce_pieces(parts):
    count = lax.axis_size("fsdp")
    place = lax.axis_index("fsdp")
    split = lax.axis_size("bucket") == PIECES
    if split:
        mine = lax.psum_scatter(parts, "bucket", scatter_dimension=0, tiled=False)
    else:
        mine = lax.psum(parts, "bucket").swapaxes(0, 1)
    total = pick(mine, place).astype(f32)
    for by in range(1, count):
        total = total + lax.ppermute(
            pick(mine, (place + by) % count), "fsdp", shifts(count, by)
        ).astype(f32)
    total = total.astype(bf16)
    return lax.all_gather(total, "bucket", axis=0, tiled=False) if split else total


def to_group(rows, count, place):
    relative = jnp.stack(
        [pick(rows, place)]
        + [
            lax.ppermute(pick(rows, (place + by) % count), "fsdp", shifts(count, by))
            for by in range(1, count)
        ]
    )
    return jnp.stack([pick(relative, (place - j) % count) for j in range(count)])


def on_device(
    inputs,
    condition,
    segment_ids,
    grid_widths,
    bucket_counts,
    modulate_weight,
    joint_weight,
    project_weight,
    gate_weight,
    up_weight,
    down_weight,
    cotangent,
):
    fsdp_count = lax.axis_size("fsdp")
    place = lax.axis_index("fsdp")
    bucket = lax.axis_index("bucket")
    height = joint_weight.shape[0]
    half = height // HALVES
    ff = gate_weight.shape[1]
    tile = ff // COLUMNS
    down_rows = down_weight.shape[0] // PIECES
    slots = condition.shape[0]
    place_array = place.astype(jnp.int32).reshape(1)

    if lax.axis_size("bucket") == PIECES:
        column, side = bucket // HALVES, bucket % HALVES
        attn_piece = jnp.where(
            column == 3,
            lax.dynamic_slice(project_weight, (side * half, 0), (half, WIDTH)),
            lax.dynamic_slice(joint_weight, (side * half, column * WIDTH), (half, WIDTH)),
        )
        ffn_piece = jnp.where(
            side == 0,
            lax.dynamic_slice(gate_weight, (0, column * tile), (height, tile)),
            lax.dynamic_slice(up_weight, (0, column * tile), (height, tile)),
        )
        down_piece = lax.dynamic_slice_in_dim(down_weight, bucket * down_rows, down_rows, 0)
        every_attn = gather_pieces(attn_piece)
        every_ffn = gather_pieces(ffn_piece)
        every_down = gather_pieces(down_piece)
    else:
        every_attn = gather_whole(
            jnp.concatenate([joint_weight, project_weight], axis=1)
            .reshape(HALVES, half, COLUMNS, WIDTH)
            .transpose(2, 0, 1, 3)
            .reshape(PIECES, half, WIDTH)
        )
        every_ffn = gather_whole(
            jnp.stack([gate_weight, up_weight])
            .reshape(HALVES, height, COLUMNS, tile)
            .transpose(2, 0, 1, 3)
            .reshape(PIECES, height, tile)
        )
        every_down = gather_whole(down_weight.reshape(PIECES, down_rows, WIDTH))

    cond_float = condition.astype(f32)
    lifted = jax.nn.silu(cond_float).astype(bf16)
    lifted_rows = to_group(
        lifted.reshape(slots, fsdp_count, height).transpose(1, 0, 2), fsdp_count, place
    ).reshape(fsdp_count * slots, height)
    modulation = jnp.sum(
        to_group(
            matmul(lifted_rows, modulate_weight).reshape(fsdp_count, slots, 6 * WIDTH),
            fsdp_count,
            place,
        ),
        axis=0,
    )
    one_hot = (
        segment_ids[::CHUNK, None] == jnp.arange(slots, dtype=jnp.int32)[None, :]
    ).astype(f32)
    mod = jnp.dot(one_hot, modulation, precision=lax.Precision.HIGHEST, preferred_element_type=f32)
    counts = bucket_counts.astype(f32)
    mine = jnp.sum(jnp.where(jnp.arange(counts.shape[0], dtype=jnp.int32) == bucket, counts, 0.0))
    factor = (mine * counts.shape[0] / jnp.sum(counts)).reshape(1)
    cos, sin = rope_tables(segment_ids, grid_widths)

    first, query, keys, values = first_call(
        place_array, inputs, mod, cos, sin, joint_weight, every_attn
    )
    attended, branch, middle, second = attend_call(
        place_array, query, keys, values, segment_ids, inputs, mod, project_weight, every_attn
    )
    output, hidden, gate_back, up_back, feed_back, middle_back, branch_back, late_sums = ffn_call(
        place_array, factor, second, middle, branch, cotangent, mod,
        gate_weight, up_weight, down_weight, every_ffn, every_down,
    )
    down_sum = reduce_pieces(down_grad_call(fsdp_count, hidden, feed_back)).reshape(-1, WIDTH)
    ffn_parts = ffn_grad_call(second, gate_back, up_back).reshape(
        PIECES, fsdp_count, height, tile
    )
    ffn_sum = (
        reduce_pieces(ffn_parts)
        .reshape(COLUMNS, HALVES, height, tile)
        .transpose(1, 2, 0, 3)
        .reshape(HALVES, height, ff)
    )
    joint_back = attend_back_call(
        place_array, query, keys, values, branch_back, segment_ids, cos, sin, project_weight, every_attn
    )
    attn_parts = attn_grad_call(fsdp_count, first, attended, joint_back, branch_back).reshape(
        PIECES, fsdp_count, half, WIDTH
    )
    attn_sum = (
        reduce_pieces(attn_parts)
        .reshape(COLUMNS, HALVES, half, WIDTH)
        .transpose(1, 2, 0, 3)
        .reshape(height, COLUMNS * WIDTH)
    )
    grad_inputs, early_sums = first_back_call(
        place_array, joint_back, inputs, middle_back, mod, joint_weight, every_attn
    )
    modulation_back = lax.dot_general(
        one_hot,
        jnp.concatenate([early_sums, late_sums], axis=1),
        (((0,), (0,)), ((), ())),
        precision=lax.Precision.HIGHEST,
        preferred_element_type=f32,
    ).astype(bf16)

    everyone = lax.all_gather(
        jnp.concatenate([modulation_back, lifted], axis=1), ("bucket", "fsdp"), axis=0, tiled=True
    )
    all_back = everyone[:, : 6 * WIDTH]
    all_lifted = lax.dynamic_slice_in_dim(everyone, 6 * WIDTH + place * height, height, 1)
    modulate_gradient = contract_rows(all_lifted, all_back)
    group_back = lax.dynamic_slice_in_dim(
        all_back, bucket * fsdp_count * slots, fsdp_count * slots, 0
    )
    slope_rows = times_transposed(group_back, modulate_weight)
    condition_slope = (
        to_group(slope_rows.reshape(fsdp_count, slots, height), fsdp_count, place)
        .transpose(1, 0, 2)
        .reshape(slots, WIDTH)
    )
    grad_condition = condition_slope * silu_slope(cond_float)
    return (
        output,
        grad_inputs,
        grad_condition,
        modulate_gradient,
        attn_sum[:, : 3 * WIDTH].astype(f32),
        attn_sum[:, 3 * WIDTH :].astype(f32),
        ffn_sum[0].astype(f32),
        ffn_sum[1].astype(f32),
        down_sum.astype(f32),
    )


def solution(mesh):
    spread = P(("bucket", "fsdp"), None)
    rows = P("fsdp", None)
    in_specs = (
        spread, spread, P(("bucket", "fsdp")), P(("bucket", "fsdp")), P(),
        rows, rows, rows, rows, rows, rows, spread,
    )
    out_specs = (spread, spread, spread, rows, rows, rows, rows, rows, rows)
    return jax.shard_map(
        on_device, mesh=mesh, in_specs=in_specs, out_specs=out_specs, check_vma=False
    )
```

```python
import functools

import jax
import jax.numpy as jnp
from jax import lax
from jax.experimental import pallas as pl
from jax.experimental.pallas import tpu as pltpu
from jax.sharding import PartitionSpec as P

HEADS = 16
HEAD_DIM = 72
WIDTH = HEADS * HEAD_DIM
QUARTER = HEAD_DIM // 4
BLOCK = 256
CHUNK = 64
COLUMNS = 4
HALVES = 2
PIECES = COLUMNS * HALVES
LANES = 128

epsilon = 1e-06
masked_score = -1e30
f32 = jnp.float32
bf16 = jnp.bfloat16
MEGA = 2**20


def normalize(values):
    average = jnp.mean(values, axis=-1, keepdims=True)
    centered = values - average
    inverse = lax.rsqrt(jnp.mean(centered * centered, axis=-1, keepdims=True) + epsilon)
    return (centered * inverse, inverse)


def normalize_back(normed, inverse, upstream):
    return inverse * (
        upstream
        - jnp.mean(upstream, axis=-1, keepdims=True)
        - normed * jnp.mean(upstream * normed, axis=-1, keepdims=True)
    )


def matmul(left, right):
    return jnp.dot(left, right, preferred_element_type=f32)


def contract_rows(left, right):
    return lax.dot_general(left, right, (((0,), (0,)), ((), ())), preferred_element_type=f32)


def times_transposed(left, right):
    return lax.dot_general(left, right, (((1,), (1,)), ((), ())), preferred_element_type=f32)


def silu_slope(values):
    sigmoid = jax.nn.sigmoid(values)
    return sigmoid * (1.0 + values * (1.0 - sigmoid))


def rope_tables(segments, widths):
    slots = widths.shape[0]
    one_hot = (segments[:, None] == jnp.arange(slots, dtype=jnp.int32)[None, :]).astype(jnp.int32)
    counts = jnp.sum(one_hot, axis=0)
    starts = jnp.cumsum(counts) - counts
    start_token = jnp.sum(one_hot * starts[None, :], axis=1)
    width_token = jnp.maximum(jnp.sum(one_hot * widths[None, :], axis=1), 1)
    place = jnp.arange(segments.shape[0], dtype=jnp.int32) - start_token
    row_place = (place // width_token).astype(f32)
    col_place = (place % width_token).astype(f32)
    freqs = 10000.0 ** (-jnp.arange(QUARTER, dtype=f32) / QUARTER)
    angle_row = row_place[:, None] * freqs[None, :]
    angle_col = col_place[:, None] * freqs[None, :]
    cos_row, sin_row, cos_col, sin_col = (
        jnp.cos(angle_row),
        jnp.sin(angle_row),
        jnp.cos(angle_col),
        jnp.sin(angle_col),
    )
    cos = jnp.concatenate([cos_row, cos_row, cos_col, cos_col], axis=1)
    sin = jnp.concatenate([-sin_row, sin_row, -sin_col, sin_col], axis=1)
    return jnp.tile(cos, (1, HEADS)), jnp.tile(sin, (1, HEADS))


def part(index):
    return slice(index * WIDTH, (index + 1) * WIDTH)


def rotate(values, cos, sin):
    lane = lax.broadcasted_iota(jnp.int32, values.shape, 1)
    leading = lane % (2 * QUARTER) < QUARTER
    partner = jnp.where(
        leading,
        pltpu.roll(values, WIDTH - QUARTER, 1),
        pltpu.roll(values, QUARTER, 1),
    )
    return values * cos + partner * sin


def take(start, size):
    return pl.ds(pl.multiple_of(start, 16), size)


def first_part(rows):
    return -(-rows // 32) * 16


def piece_copies(where, count, sources, target, rows, sem):
    place, column, side = where
    first = first_part(rows)
    copies = []
    for other in range(HALVES):
        here = sources[5 * other : 5 * other + 5]
        for by in range(1, count):
            owner = (place + (count - by)) % count
            for j in range(COLUMNS):
                spans = [(here[j], 0, rows)] if j < 3 else [(here[3], 0, first), (here[4], first, rows - first)]
                for ref, start, size in spans:
                    to = target(column ^ j, side ^ other, owner, start, size)
                    copies.append(pltpu.make_async_copy(ref.at[by - 1], to, sem(column ^ j, side ^ other, owner)))
    return copies


def wait_for(ref, sem):
    pltpu.make_async_copy(ref, ref, sem).wait()


def first_kernel(
    count, where_ref, x_ref, mod_ref, cos_ref, sin_ref, joint_ref, project_ref, *refs
):
    sources = refs[:10]
    first_ref, query_ref, keys_ref, values_ref, weight_ref, weight, total, sems = refs[10:]
    where = where_ref[0], where_ref[1], where_ref[2]
    rows_in = joint_ref.shape[0]
    half = rows_in // HALVES

    def target(column, side, place, start, size):
        return weight.at[column, take(place * rows_in + side * half + start, size)]

    copies = piece_copies(where, count, sources, target, half, lambda c, s, z: sems.at[c])
    for c in range(COLUMNS):
        shard = project_ref if c == 3 else joint_ref.at[:, pl.ds(c * WIDTH, WIDTH)]
        copies.append(pltpu.make_async_copy(shard, weight.at[c, take(where[0] * rows_in, rows_in)], sems.at[c]))
    for copy in copies:
        copy.start()
    tokens = x_ref.shape[0]
    for i in range(tokens // CHUNK):
        rows = slice(i * CHUNK, (i + 1) * CHUNK)
        normed, _ = normalize(x_ref[rows, :].astype(f32))
        first_ref[rows, :] = (
            normed * (1.0 + mod_ref[i : i + 1, part(1)]) + mod_ref[i : i + 1, part(0)]
        ).astype(bf16)
    for c, out in enumerate((query_ref, keys_ref, values_ref)):
        wait_for(weight.at[c], sems.at[c])
        if c == 2:
            out[...] = matmul(first_ref[...], weight[c]).astype(bf16)
        else:
            total[...] = matmul(first_ref[...], weight[c])

            @pl.loop(0, tokens // CHUNK)
            def _(i):
                rows = pl.ds(pl.multiple_of(i * CHUNK, CHUNK), CHUNK)
                out[rows, :] = rotate(total[rows, :], cos_ref[rows, :], sin_ref[rows, :]).astype(bf16)

    wait_for(weight.at[3], sems.at[3])
    write = pltpu.make_async_copy(weight, weight_ref, sems.at[0])
    write.start()
    write.wait()


def window(head):
    start = head * HEAD_DIM // LANES * LANES
    stop = -(-(head + 1) * HEAD_DIM // LANES) * LANES
    lane = lax.broadcasted_iota(jnp.int32, (1, stop - start), 1) + start
    inside = (lane >= head * HEAD_DIM) & (lane < (head + 1) * HEAD_DIM)
    return slice(start, stop), inside


def soft_scores(query, keys, allowed):
    scores = times_transposed(query, keys) * HEAD_DIM ** (-0.5)
    scores = jnp.where(allowed, scores, masked_score)
    exponent = jnp.exp(scores - jnp.max(scores, axis=-1, keepdims=True))
    return exponent * (1.0 / jnp.sum(exponent, axis=-1, keepdims=True))


def attend_kernel(
    query_ref, keys_ref, values_ref, column_ids, row_ids, x_ref, mod_ref,
    weight, attended_ref, branch_ref, middle_ref, second_ref, mixed,
):
    allowed = column_ids[...] == row_ids[...]
    for head in range(HEADS):
        lanes, inside = window(head)
        query = jnp.where(inside, query_ref[:, lanes], jnp.zeros((), bf16))
        probs = soft_scores(query, keys_ref[:, lanes], allowed).astype(bf16)
        mixed[:, lanes] = jnp.where(inside, matmul(probs, values_ref[:, lanes]), mixed[:, lanes])
    attended_ref[...] = mixed[...].astype(bf16)
    branch_ref[...] = matmul(attended_ref[...], weight[0])
    for i in range(BLOCK // CHUNK):
        rows = slice(i * CHUNK, (i + 1) * CHUNK)
        mod = mod_ref.at[0]
        middle = x_ref[rows, :].astype(f32) + mod[i : i + 1, part(2)] * branch_ref[rows, :]
        middle_ref[rows, :] = middle
        normed, _ = normalize(middle)
        second_ref[rows, :] = (
            normed * (1.0 + mod[i : i + 1, part(4)]) + mod[i : i + 1, part(3)]
        ).astype(bf16)


def ffn_kernel(
    count, where_ref, factor_ref, second_ref, middle_ref, branch_ref, cot_ref, mod_ref,
    gate_ref, up_ref, down_ref, *refs
):
    pairs, downs = refs[:10], refs[10:20]
    (
        output_ref, hidden_ref, gate_back_ref, up_back_ref, feed_back_ref, middle_back_ref,
        branch_back_ref, sums_ref, pair_w, down_w, feed, second_back, pair_sems, down_sems,
    ) = refs[20:]
    step = pl.program_id(0)
    steps = pl.num_programs(0)
    rows_in = gate_ref.shape[0]
    tile = hidden_ref.shape[1]
    tokens = second_ref.shape[0]
    down_rows = tile // PIECES

    @pl.when(step == 0)
    def _():
        where = where_ref[0], where_ref[1], where_ref[2]
        own = take(where[0] * rows_in, rows_in)

        def pair_target(column, side, place, start, size):
            return pair_w.at[side, column, take(place * rows_in + start, size)]

        def down_target(column, side, place, start, size):
            return down_w.at[place, take((column * HALVES + side) * down_rows + start, size)]

        copies = piece_copies(
            where, count, pairs, pair_target, rows_in, lambda c, s, z: pair_sems.at[s, c]
        ) + piece_copies(where, count, downs, down_target, down_rows, lambda c, s, z: down_sems.at[z])
        for which, shard in enumerate((gate_ref, up_ref)):
            for c in range(COLUMNS):
                copies.append(
                    pltpu.make_async_copy(
                        shard.at[:, pl.ds(c * tile, tile)], pair_w.at[which, c, own], pair_sems.at[which, c]
                    )
                )
        copies.append(pltpu.make_async_copy(down_ref, down_w.at[where[0]], down_sems.at[where[0]]))
        for copy in copies:
            copy.start()
        for i in range(tokens // CHUNK):
            rows = slice(i * CHUNK, (i + 1) * CHUNK)
            upstream = cot_ref[rows, :].astype(f32) * factor_ref[0]
            feed_back_ref[rows, :] = (upstream * mod_ref[i : i + 1, part(5)]).astype(bf16)

    for which in range(2):
        wait_for(pair_w.at[which, step], pair_sems.at[which, step])
    wait_for(down_w.at[step], down_sems.at[step])
    gate_w, up_w = pair_w.at[0], pair_w.at[1]
    slot = step

    sub = 256
    for n in range(tile // sub):
        lanes = slice(n * sub, (n + 1) * sub)
        gate = matmul(second_ref[...], gate_w[slot, :, lanes])
        upval = matmul(second_ref[...], up_w[slot, :, lanes])
        down = down_w[slot, lanes, :]
        hidden_back = times_transposed(feed_back_ref[...], down)
        sigmoid = jax.nn.sigmoid(gate)
        silu = gate * sigmoid
        hidden_ref[:, lanes] = (silu * upval).astype(bf16)
        up_back_ref[:, lanes] = (hidden_back * silu).astype(bf16)
        gate_back_ref[:, lanes] = (
            hidden_back * upval * (sigmoid * (1.0 + gate * (1.0 - sigmoid)))
        ).astype(bf16)

    feed_part = matmul(hidden_ref[...], down_w[slot])
    back_part = times_transposed(gate_back_ref[...], gate_w[slot]) + times_transposed(
        up_back_ref[...], up_w[slot]
    )

    @pl.when(step == 0)
    def _():
        feed[...] = feed_part
        second_back[...] = back_part

    @pl.when(step > 0)
    def _():
        feed[...] += feed_part
        second_back[...] += back_part

    @pl.when(step == steps - 1)
    def _():
        for i in range(tokens // CHUNK):
            rows = slice(i * CHUNK, (i + 1) * CHUNK)
            gate_one = mod_ref[i : i + 1, part(2)]
            scale_two = mod_ref[i : i + 1, part(4)]
            gate_two = mod_ref[i : i + 1, part(5)]
            middle = middle_ref[rows, :]
            output_ref[rows, :] = (middle + gate_two * feed[rows, :]).astype(bf16)
            upstream = cot_ref[rows, :].astype(f32) * factor_ref[0]
            normed, inverse = normalize(middle)
            back = second_back[rows, :]
            middle_back = upstream + normalize_back(normed, inverse, back * (1.0 + scale_two))
            middle_back_ref[rows, :] = middle_back
            branch_back_ref[rows, :] = (middle_back * gate_one).astype(bf16)
            for where, values in enumerate(
                (middle_back * branch_ref[rows, :], back, back * normed, upstream * feed[rows, :])
            ):
                sums_ref[i : i + 1, part(where)] = jnp.sum(values, axis=0, keepdims=True)


def ffn_grad_kernel(second_ref, gate_back_ref, up_back_ref, out_ref, turned):
    @pl.when((pl.program_id(0) == 0) & (pl.program_id(1) == 0))
    def _():
        turned[...] = second_ref[...].T

    @pl.when(pl.program_id(1) == 0)
    def _():
        out_ref[0, 0] = matmul(turned[...], gate_back_ref[...]).astype(bf16)

    @pl.when(pl.program_id(1) == 1)
    def _():
        out_ref[0, 0] = matmul(turned[...], up_back_ref[...]).astype(bf16)


def down_grad_kernel(hidden_ref, feed_back_ref, out_ref):
    grad = contract_rows(hidden_ref[...], feed_back_ref[...]).astype(bf16)
    out_ref[...] = grad.reshape(out_ref.shape)


def attn_grad_kernel(first_ref, attended_ref, joint_back_ref, branch_back_ref, out_ref, turned):
    column = pl.program_id(0)
    count, half = out_ref.shape[2], out_ref.shape[3]

    @pl.when(column == 0)
    def _():
        turned[...] = first_ref[...].T

    @pl.when(column == 3)
    def _():
        turned[...] = attended_ref[...].T

    def put(right):
        for z in range(count):
            for h in range(HALVES):
                start = (z * HALVES + h) * half
                out_ref[0, h, z] = matmul(turned[start : start + half, :], right).astype(bf16)

    @pl.when(column < 3)
    def _():
        put(joint_back_ref[...])

    @pl.when(column == 3)
    def _():
        put(branch_back_ref[...])


def attend_back_kernel(
    query_ref, keys_ref, values_ref, branch_back_ref, column_ids, row_ids, cos_ref,
    sin_ref, weight, joint_back_ref, mixed_back, query_back, keys_back, values_back,
):
    mixed_back[...] = times_transposed(branch_back_ref[...], weight[0]).astype(bf16)
    allowed = column_ids[...] == row_ids[...]
    scaling = HEAD_DIM ** (-0.5)
    for head in range(HEADS):
        lanes, inside = window(head)
        zero = jnp.zeros((), bf16)
        query = jnp.where(inside, query_ref[:, lanes], zero)
        back = jnp.where(inside, mixed_back[:, lanes], zero)
        soft = soft_scores(query, keys_ref[:, lanes], allowed)
        probs_back = times_transposed(back, values_ref[:, lanes])
        scores_back = (
            soft * (probs_back - jnp.sum(soft * probs_back, axis=-1, keepdims=True))
        ).astype(bf16)
        query_back[:, lanes] = jnp.where(
            inside, matmul(scores_back, keys_ref[:, lanes]) * scaling, query_back[:, lanes]
        )
        keys_back[:, lanes] = jnp.where(
            inside, contract_rows(scores_back, query) * scaling, keys_back[:, lanes]
        )
        values_back[:, lanes] = jnp.where(
            inside, contract_rows(soft.astype(bf16), back), values_back[:, lanes]
        )

    @pl.loop(0, BLOCK // CHUNK)
    def _(i):
        rows = pl.ds(pl.multiple_of(i * CHUNK, CHUNK), CHUNK)
        cos, sin = cos_ref[rows, :], sin_ref[rows, :]
        joint_back_ref[rows, part(0)] = rotate(query_back[rows, :], cos, -sin).astype(bf16)
        joint_back_ref[rows, part(1)] = rotate(keys_back[rows, :], cos, -sin).astype(bf16)
        joint_back_ref[rows, part(2)] = values_back[rows, :].astype(bf16)


def first_back_kernel(
    joint_back_ref, x_ref, middle_back_ref, mod_ref, weight, grad_ref, sums_ref, first_back
):
    step = pl.program_id(0)
    product = times_transposed(joint_back_ref[...], weight[0])

    @pl.when(step == 0)
    def _():
        first_back[...] = product

    @pl.when(step > 0)
    def _():
        first_back[...] += product

    @pl.when(step == pl.num_programs(0) - 1)
    def _():
        finish_first_back(x_ref, middle_back_ref, mod_ref, grad_ref, sums_ref, first_back)


def finish_first_back(x_ref, middle_back_ref, mod_ref, grad_ref, sums_ref, first_back):
    for i in range(x_ref.shape[0] // CHUNK):
        rows = slice(i * CHUNK, (i + 1) * CHUNK)
        normed, inverse = normalize(x_ref[rows, :].astype(f32))
        back = first_back[rows, :]
        grad_ref[rows, :] = middle_back_ref[rows, :] + normalize_back(
            normed, inverse, back * (1.0 + mod_ref[i : i + 1, part(1)])
        )
        sums_ref[i : i + 1, part(0)] = jnp.sum(back, axis=0, keepdims=True)
        sums_ref[i : i + 1, part(1)] = jnp.sum(back * normed, axis=0, keepdims=True)


SMEM = pl.BlockSpec(memory_space=pltpu.SMEM)
VMEM = pl.BlockSpec(memory_space=pltpu.VMEM)
ANY = pl.BlockSpec(memory_space=pl.ANY)


def struct(shape, dtype):
    return jax.ShapeDtypeStruct(shape, dtype)


def params(mega=56):
    return pltpu.CompilerParams(vmem_limit_bytes=mega * MEGA)


def cost(flops, *arrays):
    size = sum(a.size * a.dtype.itemsize for a in arrays)
    return pl.CostEstimate(flops=flops, bytes_accessed=size, transcendentals=0)


def by_block(*shape):
    return pl.BlockSpec(shape, lambda b: (b,) + (0,) * (len(shape) - 1))


def whole(*shape):
    return pl.BlockSpec(shape, lambda *_: (0,) * len(shape))


def first_call(where, x, mod, cos, sin, joint, project, arrived):
    tokens = x.shape[0]
    count = arrived[0].shape[0] + 1
    shape = struct((tokens, WIDTH), bf16)
    return pl.pallas_call(
        functools.partial(first_kernel, count),
        out_shape=(shape,) * 4 + (struct((COLUMNS, WIDTH, WIDTH), bf16),),
        in_specs=[SMEM, VMEM, VMEM, VMEM, VMEM] + [ANY] * (2 + len(arrived)),
        out_specs=(VMEM,) * 4 + (ANY,),
        scratch_shapes=[
            pltpu.VMEM((COLUMNS, WIDTH, WIDTH), bf16),
            pltpu.VMEM((tokens, WIDTH), f32),
            pltpu.SemaphoreType.DMA((COLUMNS,)),
        ],
        compiler_params=params(),
        cost_estimate=cost(18 * tokens * WIDTH * WIDTH, x, x, x, x, cos, sin, joint, *arrived),
    )(where, x, mod, cos, sin, joint, project, *arrived)


def attend_call(query, keys, values, ids, x, mod, weight):
    tokens = x.shape[0]
    return pl.pallas_call(
        attend_kernel,
        grid=(tokens // BLOCK,),
        out_shape=(
            struct((tokens, WIDTH), bf16),
            struct((tokens, WIDTH), f32),
            struct((tokens, WIDTH), f32),
            struct((tokens, WIDTH), bf16),
        ),
        in_specs=[by_block(BLOCK, WIDTH)] * 3
        + [by_block(BLOCK, 1), pl.BlockSpec((1, BLOCK), lambda b: (0, b)), by_block(BLOCK, WIDTH)]
        + [by_block(1, BLOCK // CHUNK, 6 * WIDTH), pl.BlockSpec((1, WIDTH, WIDTH), lambda b: (3, 0, 0))],
        out_specs=(by_block(BLOCK, WIDTH),) * 4,
        scratch_shapes=[pltpu.VMEM((BLOCK, WIDTH), f32)],
        compiler_params=params(),
        cost_estimate=cost(14 * tokens * WIDTH * WIDTH, query, keys, values, x, x, x, x, x),
    )(
        query, keys, values, ids[:, None], ids[None, :], x,
        mod.reshape(tokens // BLOCK, BLOCK // CHUNK, 6 * WIDTH), weight,
    )


def ffn_call(where, factor, second, middle, branch, cot, mod, gate, up, down, pairs, downs):
    tokens = second.shape[0]
    count = pairs[0].shape[0] + 1
    ff = gate.shape[1]
    tile = ff // COLUMNS
    tiled = pl.BlockSpec((tokens, tile), lambda c: (0, c))
    full = whole(tokens, WIDTH)
    chunks = tokens // CHUNK
    return pl.pallas_call(
        functools.partial(ffn_kernel, count),
        grid=(COLUMNS,),
        out_shape=(struct((tokens, WIDTH), bf16),)
        + (struct((tokens, ff), bf16),) * 3
        + (
            struct((tokens, WIDTH), bf16),
            struct((tokens, WIDTH), f32),
            struct((tokens, WIDTH), bf16),
            struct((chunks, 4 * WIDTH), f32),
        ),
        in_specs=[SMEM, SMEM, full, full, full, full, whole(chunks, 6 * WIDTH)] + [ANY] * 23,
        out_specs=(full, tiled, tiled, tiled, full, full, full, whole(chunks, 4 * WIDTH)),
        scratch_shapes=[
            pltpu.VMEM((HALVES, COLUMNS, WIDTH, tile), bf16),
            pltpu.VMEM((count, ff // count, WIDTH), bf16),
            pltpu.VMEM((tokens, WIDTH), f32),
            pltpu.VMEM((tokens, WIDTH), f32),
            pltpu.SemaphoreType.DMA((HALVES, COLUMNS)),
            pltpu.SemaphoreType.DMA((count,)),
        ],
        compiler_params=params(62),
        cost_estimate=cost(24 * tokens * WIDTH * ff, gate, gate, gate),
    )(where, factor, second, middle, branch, cot, mod, gate, up, down, *pairs, *downs)


def ffn_grad_call(second, gate_back, up_back):
    tokens, ff = gate_back.shape
    tile = ff // COLUMNS
    tiled = pl.BlockSpec((tokens, tile), lambda c, h: (0, c))
    out = struct((COLUMNS, HALVES, WIDTH, tile), bf16)
    return pl.pallas_call(
        ffn_grad_kernel,
        grid=(COLUMNS, HALVES),
        out_shape=out,
        in_specs=[whole(tokens, WIDTH), tiled, tiled],
        out_specs=pl.BlockSpec((1, 1, WIDTH, tile), lambda c, h: (c, h, 0, 0)),
        scratch_shapes=[pltpu.VMEM((WIDTH, tokens), bf16)],
        compiler_params=params(),
        cost_estimate=cost(4 * tokens * WIDTH * ff, second, gate_back, up_back, out),
    )(second, gate_back, up_back)


def down_grad_call(count, hidden, feed_back):
    tokens, ff = hidden.shape
    rows = ff // count
    out = struct((PIECES, count, rows // PIECES, WIDTH), bf16)
    return pl.pallas_call(
        down_grad_kernel,
        grid=(count,),
        out_shape=out,
        in_specs=[pl.BlockSpec((tokens, rows), lambda z: (0, z)), whole(tokens, WIDTH)],
        out_specs=pl.BlockSpec((PIECES, 1, rows // PIECES, WIDTH), lambda z: (0, z, 0, 0)),
        compiler_params=params(),
        cost_estimate=cost(2 * tokens * WIDTH * ff, hidden, feed_back, out),
    )(hidden, feed_back)


def attn_grad_call(count, first, attended, joint_back, branch_back):
    tokens = first.shape[0]
    half = WIDTH // count // HALVES
    full = whole(tokens, WIDTH)
    out = struct((COLUMNS, HALVES, count, half, WIDTH), bf16)
    return pl.pallas_call(
        attn_grad_kernel,
        grid=(COLUMNS,),
        out_shape=out,
        in_specs=[
            full,
            full,
            pl.BlockSpec((tokens, WIDTH), lambda c: (0, jnp.minimum(c, 2))),
            full,
        ],
        out_specs=pl.BlockSpec((1, HALVES, count, half, WIDTH), lambda c: (c, 0, 0, 0, 0)),
        scratch_shapes=[pltpu.VMEM((WIDTH, tokens), bf16)],
        compiler_params=params(),
        cost_estimate=cost(8 * tokens * WIDTH * WIDTH, first, attended, joint_back, branch_back, out),
    )(first, attended, joint_back, branch_back)


def attend_back_call(query, keys, values, branch_back, ids, cos, sin, weight):
    tokens = query.shape[0]
    block = by_block(BLOCK, WIDTH)
    return pl.pallas_call(
        attend_back_kernel,
        grid=(tokens // BLOCK,),
        out_shape=struct((tokens, 3 * WIDTH), bf16),
        in_specs=[block, block, block, block]
        + [by_block(BLOCK, 1), pl.BlockSpec((1, BLOCK), lambda b: (0, b)), block, block]
        + [pl.BlockSpec((1, WIDTH, WIDTH), lambda b: (3, 0, 0))],
        out_specs=by_block(BLOCK, 3 * WIDTH),
        scratch_shapes=[
            pltpu.VMEM((BLOCK, WIDTH), bf16),
            pltpu.VMEM((BLOCK, WIDTH), f32),
            pltpu.VMEM((BLOCK, WIDTH), f32),
            pltpu.VMEM((BLOCK, WIDTH), f32),
        ],
        compiler_params=params(),
        cost_estimate=cost(32 * tokens * WIDTH * WIDTH, query, keys, values, branch_back, cos, sin),
    )(query, keys, values, branch_back, ids[:, None], ids[None, :], cos, sin, weight)


def first_back_call(joint_back, x, middle_back, mod, weight):
    tokens = x.shape[0]
    chunks = tokens // CHUNK
    full = whole(tokens, WIDTH)
    return pl.pallas_call(
        first_back_kernel,
        grid=(3,),
        out_shape=(struct((tokens, WIDTH), f32), struct((chunks, 2 * WIDTH), f32)),
        in_specs=[
            pl.BlockSpec((tokens, WIDTH), lambda c: (0, c)),
            full,
            full,
            whole(chunks, 6 * WIDTH),
            pl.BlockSpec((1, WIDTH, WIDTH), lambda c: (c, 0, 0)),
        ],
        out_specs=(full, whole(chunks, 2 * WIDTH)),
        scratch_shapes=[pltpu.VMEM((tokens, WIDTH), f32)],
        compiler_params=params(),
        cost_estimate=cost(14 * tokens * WIDTH * WIDTH, joint_back, x, middle_back, middle_back, weight),
    )(joint_back, x, middle_back, mod, weight)


def shifts(count, by):
    return [(i, (i + by) % count) for i in range(count)]


def pick(array, index):
    return lax.dynamic_index_in_dim(array, index, 0, keepdims=False)


def across(bit):
    return [(i, i ^ bit) for i in range(PIECES)]


def swap(array, bit):
    return lax.ppermute(array, "bucket", across(bit))


def arrived(piece):
    count = lax.axis_size("fsdp")
    first = first_part(piece.shape[0])
    own = jnp.stack(
        [lax.ppermute(piece, "fsdp", shifts(count, by)) for by in range(1, count)]
    )
    by_x, by_y = swap(own, 2), swap(own, 4)
    here = (own, by_x, by_y, swap(by_x[:, :first], 4), swap(by_y[:, first:], 2))
    return here + tuple(swap(array, 1) for array in here)


def arrived_whole(pieces):
    count = lax.axis_size("fsdp")
    place = lax.axis_index("fsdp")
    first = first_part(pieces.shape[1])
    full = lax.all_gather(pieces, "fsdp", axis=0, tiled=False)
    full = jnp.stack([pick(full, (place - by) % count) for by in range(1, count)])

    def of(side):
        own, by_x, by_y, cross = (full[:, c * HALVES + side] for c in range(COLUMNS))
        return own, by_x, by_y, cross[:, :first], cross[:, first:]

    return of(0) + of(1)


def reduce_pieces(parts):
    count = lax.axis_size("fsdp")
    place = lax.axis_index("fsdp")
    split = lax.axis_size("bucket") == PIECES
    if split:
        mine = lax.psum_scatter(parts, "bucket", scatter_dimension=0, tiled=False)
    else:
        mine = lax.psum(parts, "bucket").swapaxes(0, 1)
    total = pick(mine, place).astype(f32)
    for by in range(1, count):
        total = total + lax.ppermute(
            pick(mine, (place + by) % count), "fsdp", shifts(count, by)
        ).astype(f32)
    total = total.astype(bf16)
    return lax.all_gather(total, "bucket", axis=0, tiled=False) if split else total


def to_group(rows, count, place):
    relative = jnp.stack(
        [pick(rows, place)]
        + [
            lax.ppermute(pick(rows, (place + by) % count), "fsdp", shifts(count, by))
            for by in range(1, count)
        ]
    )
    return jnp.stack([pick(relative, (place - j) % count) for j in range(count)])


def on_device(
    inputs,
    condition,
    segment_ids,
    grid_widths,
    bucket_counts,
    modulate_weight,
    joint_weight,
    project_weight,
    gate_weight,
    up_weight,
    down_weight,
    cotangent,
):
    fsdp_count = lax.axis_size("fsdp")
    place = lax.axis_index("fsdp")
    bucket = lax.axis_index("bucket")
    height = joint_weight.shape[0]
    half = height // HALVES
    ff = gate_weight.shape[1]
    tile = ff // COLUMNS
    down_rows = down_weight.shape[0] // PIECES
    slots = condition.shape[0]

    if lax.axis_size("bucket") == PIECES:
        column, side = bucket // HALVES, bucket % HALVES
        where = jnp.stack([place, column, side])
        attn_piece = jnp.where(
            column == 3,
            lax.dynamic_slice(project_weight, (side * half, 0), (half, WIDTH)),
            lax.dynamic_slice(joint_weight, (side * half, column * WIDTH), (half, WIDTH)),
        )
        ffn_piece = jnp.where(
            side == 0,
            lax.dynamic_slice(gate_weight, (0, column * tile), (height, tile)),
            lax.dynamic_slice(up_weight, (0, column * tile), (height, tile)),
        )
        down_piece = lax.dynamic_slice_in_dim(down_weight, bucket * down_rows, down_rows, 0)
        attn_arrived, downs, pairs = arrived(attn_piece), arrived(down_piece), arrived(ffn_piece)
    else:
        where = jnp.stack([place, 0 * place, 0 * place])
        attn_arrived = arrived_whole(
            jnp.concatenate([joint_weight, project_weight], axis=1)
            .reshape(HALVES, half, COLUMNS, WIDTH)
            .transpose(2, 0, 1, 3)
            .reshape(PIECES, half, WIDTH)
        )
        pairs = arrived_whole(
            jnp.stack([gate_weight, up_weight])
            .reshape(HALVES, height, COLUMNS, tile)
            .transpose(2, 0, 1, 3)
            .reshape(PIECES, height, tile)
        )
        downs = arrived_whole(down_weight.reshape(PIECES, down_rows, WIDTH))

    cond_float = condition.astype(f32)
    lifted = jax.nn.silu(cond_float).astype(bf16)
    lifted_rows = to_group(
        lifted.reshape(slots, fsdp_count, height).transpose(1, 0, 2), fsdp_count, place
    ).reshape(fsdp_count * slots, height)
    modulation = jnp.sum(
        to_group(
            matmul(lifted_rows, modulate_weight).reshape(fsdp_count, slots, 6 * WIDTH),
            fsdp_count,
            place,
        ),
        axis=0,
    )
    one_hot = (
        segment_ids[::CHUNK, None] == jnp.arange(slots, dtype=jnp.int32)[None, :]
    ).astype(f32)
    mod = jnp.dot(one_hot, modulation, precision=lax.Precision.HIGHEST, preferred_element_type=f32)
    counts = bucket_counts.astype(f32)
    mine = jnp.sum(jnp.where(jnp.arange(counts.shape[0], dtype=jnp.int32) == bucket, counts, 0.0))
    factor = (mine * counts.shape[0] / jnp.sum(counts)).reshape(1)
    cos, sin = rope_tables(segment_ids, grid_widths)

    first, query, keys, values, weight = first_call(
        where, inputs, mod, cos, sin, joint_weight, project_weight, attn_arrived
    )
    attended, branch, middle, second = attend_call(
        query, keys, values, segment_ids, inputs, mod, weight
    )
    output, hidden, gate_back, up_back, feed_back, middle_back, branch_back, late_sums = ffn_call(
        where, factor, second, middle, branch, cotangent, mod,
        gate_weight, up_weight, down_weight, pairs, downs,
    )
    down_sum = reduce_pieces(down_grad_call(fsdp_count, hidden, feed_back)).reshape(-1, WIDTH)
    ffn_parts = ffn_grad_call(second, gate_back, up_back).reshape(
        PIECES, fsdp_count, height, tile
    )
    ffn_sum = (
        reduce_pieces(ffn_parts)
        .reshape(COLUMNS, HALVES, height, tile)
        .transpose(1, 2, 0, 3)
        .reshape(HALVES, height, ff)
    )
    joint_back = attend_back_call(
        query, keys, values, branch_back, segment_ids, cos, sin, weight
    )
    attn_parts = attn_grad_call(fsdp_count, first, attended, joint_back, branch_back).reshape(
        PIECES, fsdp_count, half, WIDTH
    )
    attn_sum = (
        reduce_pieces(attn_parts)
        .reshape(COLUMNS, HALVES, half, WIDTH)
        .transpose(1, 2, 0, 3)
        .reshape(height, COLUMNS * WIDTH)
    )
    grad_inputs, early_sums = first_back_call(joint_back, inputs, middle_back, mod, weight)
    modulation_back = lax.dot_general(
        one_hot,
        jnp.concatenate([early_sums, late_sums], axis=1),
        (((0,), (0,)), ((), ())),
        precision=lax.Precision.HIGHEST,
        preferred_element_type=f32,
    ).astype(bf16)

    everyone = lax.all_gather(
        jnp.concatenate([modulation_back, lifted], axis=1), ("bucket", "fsdp"), axis=0, tiled=True
    )
    all_back = everyone[:, : 6 * WIDTH]
    all_lifted = lax.dynamic_slice_in_dim(everyone, 6 * WIDTH + place * height, height, 1)
    modulate_gradient = contract_rows(all_lifted, all_back)
    group_back = lax.dynamic_slice_in_dim(
        all_back, bucket * fsdp_count * slots, fsdp_count * slots, 0
    )
    slope_rows = times_transposed(group_back, modulate_weight)
    condition_slope = (
        to_group(slope_rows.reshape(fsdp_count, slots, height), fsdp_count, place)
        .transpose(1, 0, 2)
        .reshape(slots, WIDTH)
    )
    grad_condition = condition_slope * silu_slope(cond_float)
    return (
        output,
        grad_inputs,
        grad_condition,
        modulate_gradient,
        attn_sum[:, : 3 * WIDTH].astype(f32),
        attn_sum[:, 3 * WIDTH :].astype(f32),
        ffn_sum[0].astype(f32),
        ffn_sum[1].astype(f32),
        down_sum.astype(f32),
    )


def solution(mesh):
    spread = P(("bucket", "fsdp"), None)
    rows = P("fsdp", None)
    in_specs = (
        spread, spread, P(("bucket", "fsdp")), P(("bucket", "fsdp")), P(),
        rows, rows, rows, rows, rows, rows, spread,
    )
    out_specs = (spread, spread, spread, rows, rows, rows, rows, rows, rows)
    return jax.shard_map(
        on_device, mesh=mesh, in_specs=in_specs, out_specs=out_specs, check_vma=False
    )
```

```python
import functools

import jax
import jax.numpy as jnp
from jax import lax
from jax.experimental import pallas as pl
from jax.experimental.pallas import tpu as pltpu
from jax.sharding import PartitionSpec as P

HEADS = 16
HEAD_DIM = 72
WIDTH = HEADS * HEAD_DIM
QUARTER = HEAD_DIM // 4
BLOCK = 256
CHUNK = 64
COLUMNS = 4
HALVES = 2
PIECES = COLUMNS * HALVES
LANES = 128

epsilon = 1e-06
masked_score = -1e30
f32 = jnp.float32
bf16 = jnp.bfloat16
MEGA = 2**20


def normalize(values):
    average = jnp.mean(values, axis=-1, keepdims=True)
    centered = values - average
    inverse = lax.rsqrt(jnp.mean(centered * centered, axis=-1, keepdims=True) + epsilon)
    return (centered * inverse, inverse)


def normalize_back(normed, inverse, upstream):
    return inverse * (
        upstream
        - jnp.mean(upstream, axis=-1, keepdims=True)
        - normed * jnp.mean(upstream * normed, axis=-1, keepdims=True)
    )


def matmul(left, right):
    return jnp.dot(left, right, preferred_element_type=f32)


def contract_rows(left, right):
    return lax.dot_general(left, right, (((0,), (0,)), ((), ())), preferred_element_type=f32)


def times_transposed(left, right):
    return lax.dot_general(left, right, (((1,), (1,)), ((), ())), preferred_element_type=f32)


def silu_slope(values):
    sigmoid = jax.nn.sigmoid(values)
    return sigmoid * (1.0 + values * (1.0 - sigmoid))


def rope_tables(segments, widths):
    slots = widths.shape[0]
    one_hot = (segments[:, None] == jnp.arange(slots, dtype=jnp.int32)[None, :]).astype(jnp.int32)
    counts = jnp.sum(one_hot, axis=0)
    starts = jnp.cumsum(counts) - counts
    start_token = jnp.sum(one_hot * starts[None, :], axis=1)
    width_token = jnp.maximum(jnp.sum(one_hot * widths[None, :], axis=1), 1)
    place = jnp.arange(segments.shape[0], dtype=jnp.int32) - start_token
    row_place = (place // width_token).astype(f32)
    col_place = (place % width_token).astype(f32)
    freqs = 10000.0 ** (-jnp.arange(QUARTER, dtype=f32) / QUARTER)
    angle_row = row_place[:, None] * freqs[None, :]
    angle_col = col_place[:, None] * freqs[None, :]
    cos_row, sin_row, cos_col, sin_col = (
        jnp.cos(angle_row),
        jnp.sin(angle_row),
        jnp.cos(angle_col),
        jnp.sin(angle_col),
    )
    cos = jnp.concatenate([cos_row, cos_row, cos_col, cos_col], axis=1)
    sin = jnp.concatenate([-sin_row, sin_row, -sin_col, sin_col], axis=1)
    return jnp.tile(cos, (1, HEADS)), jnp.tile(sin, (1, HEADS))


def part(index):
    return slice(index * WIDTH, (index + 1) * WIDTH)


def rotate(values, cos, sin):
    lane = lax.broadcasted_iota(jnp.int32, values.shape, 1)
    leading = lane % (2 * QUARTER) < QUARTER
    partner = jnp.where(
        leading,
        pltpu.roll(values, WIDTH - QUARTER, 1),
        pltpu.roll(values, QUARTER, 1),
    )
    return values * cos + partner * sin


def take(start, size):
    return pl.ds(pl.multiple_of(start, 128 if size % 128 == 0 else 16), size)


def first_part(rows):
    return -(-rows // 32) * 16


def piece_copies(where, count, sources, target, rows, sem):
    place, column, side = where
    first = first_part(rows)
    copies = []
    for other in range(HALVES):
        here = sources[5 * other : 5 * other + 5]
        for by in range(1, count):
            owner = (place + (count - by)) % count
            for j in range(COLUMNS):
                spans = [(here[j], 0, rows)] if j < 3 else [(here[3], 0, first), (here[4], first, rows - first)]
                for ref, start, size in spans:
                    to = target(column ^ j, side ^ other, owner, start, size)
                    copies.append(pltpu.make_async_copy(ref.at[by - 1], to, sem(column ^ j, side ^ other, owner)))
    return copies


def wait_for(ref, sem):
    pltpu.make_async_copy(ref, ref, sem).wait()


def first_kernel(
    count, where_ref, x_ref, mod_ref, cos_ref, sin_ref, joint_ref, project_ref, *refs
):
    sources = refs[:10]
    turned_ref, query_ref, keys_ref, values_ref, weight_ref, weight, first_ref, total, sems = refs[10:]
    where = where_ref[0], where_ref[1], where_ref[2]
    rows_in = joint_ref.shape[0]
    half = rows_in // HALVES

    def target(column, side, place, start, size):
        return weight.at[column, take(place * rows_in + side * half + start, size)]

    copies = piece_copies(where, count, sources, target, half, lambda c, s, z: sems.at[c])
    for c in range(COLUMNS):
        shard = project_ref if c == 3 else joint_ref.at[:, pl.ds(c * WIDTH, WIDTH)]
        copies.append(pltpu.make_async_copy(shard, weight.at[c, take(where[0] * rows_in, rows_in)], sems.at[c]))
    for copy in copies:
        copy.start()
    tokens = x_ref.shape[0]
    for i in range(tokens // CHUNK):
        rows = slice(i * CHUNK, (i + 1) * CHUNK)
        normed, _ = normalize(x_ref[rows, :].astype(f32))
        first_ref[rows, :] = (
            normed * (1.0 + mod_ref[i : i + 1, part(1)]) + mod_ref[i : i + 1, part(0)]
        ).astype(bf16)
    turned_ref[...] = first_ref[...].T
    for c, out in enumerate((query_ref, keys_ref, values_ref)):
        wait_for(weight.at[c], sems.at[c])
        if c == 2:
            out[...] = matmul(first_ref[...], weight[c]).astype(bf16)
        else:
            total[...] = matmul(first_ref[...], weight[c])

            @pl.loop(0, tokens // CHUNK)
            def _(i):
                rows = pl.ds(pl.multiple_of(i * CHUNK, CHUNK), CHUNK)
                out[rows, :] = rotate(total[rows, :], cos_ref[rows, :], sin_ref[rows, :]).astype(bf16)

    wait_for(weight.at[3], sems.at[3])
    write = pltpu.make_async_copy(weight, weight_ref, sems.at[0])
    write.start()
    write.wait()


def window(head):
    start = head * HEAD_DIM // LANES * LANES
    stop = -(-(head + 1) * HEAD_DIM // LANES) * LANES
    lane = lax.broadcasted_iota(jnp.int32, (1, stop - start), 1) + start
    inside = (lane >= head * HEAD_DIM) & (lane < (head + 1) * HEAD_DIM)
    return slice(start, stop), inside


def soft_scores(query, keys, allowed):
    scores = times_transposed(query, keys) * HEAD_DIM ** (-0.5)
    scores = jnp.where(allowed, scores, masked_score)
    exponent = jnp.exp(scores - jnp.max(scores, axis=-1, keepdims=True))
    return exponent * (1.0 / jnp.sum(exponent, axis=-1, keepdims=True))


def attend_kernel(
    query_ref, keys_ref, values_ref, column_ids, row_ids, x_ref, mod_ref,
    weight, turned_ref, branch_ref, middle_ref, second_ref, mixed,
):
    allowed = column_ids[...] == row_ids[...]
    for head in range(HEADS):
        lanes, inside = window(head)
        query = jnp.where(inside, query_ref[:, lanes], jnp.zeros((), bf16))
        probs = soft_scores(query, keys_ref[:, lanes], allowed).astype(bf16)
        mixed[:, lanes] = jnp.where(inside, matmul(probs, values_ref[:, lanes]), mixed[:, lanes])
    attended = mixed[...].astype(bf16)
    turned_ref[...] = attended.T
    branch_ref[...] = matmul(attended, weight[0])
    for i in range(BLOCK // CHUNK):
        rows = slice(i * CHUNK, (i + 1) * CHUNK)
        mod = mod_ref.at[0]
        middle = x_ref[rows, :].astype(f32) + mod[i : i + 1, part(0)] * branch_ref[rows, :]
        middle_ref[rows, :] = middle
        normed, _ = normalize(middle)
        second_ref[rows, :] = (
            normed * (1.0 + mod[i : i + 1, part(2)]) + mod[i : i + 1, part(1)]
        ).astype(bf16)


def placed(refs, rows):
    first = first_part(rows)
    for other in range(HALVES):
        here = refs[5 * other : 5 * other + 5]
        for j in range(3):
            yield j, other, 0, rows, here[j]
        yield 3, other, 0, first, here[3]
        yield 3, other, first, rows - first, here[4]


def tile_copies(r, where, count, tile, pair, downs):
    place, mine, side = where
    t, j = tile
    column = mine ^ j
    rows, width = r["gate"].shape[0], r["hidden_w"].shape[1]
    sem = r["pair_sems"].at[t]
    copies = [
        pltpu.make_async_copy(
            r[name].at[:, take(column * width, width)], r["pair_w"].at[t, which, take(place * rows, rows)], sem
        )
        for which, name in enumerate(("gate", "up"))
    ]
    first = first_part(rows)
    for other in range(HALVES):
        for by in range(1, count):
            owner = (place + (count - by)) % count
            if j < 3:
                spans = [(pair[other][0].at[by - 1], 0, rows)]
            else:
                spans = [(pair[other][0].at[by - 1], 0, first), (pair[other][1].at[by - 1], first, rows - first)]
            for ref, start, size in spans:
                to = r["pair_w"].at[t, side ^ other, take(owner * rows + start, size)]
                copies.append(pltpu.make_async_copy(ref, to, sem))
    for copy in copies:
        copy.start()

    sem = r["down_sems"].at[t]
    target = r["down_w"].at[t]
    piece = width // PIECES

    @pl.when(column == place)
    def _():
        pltpu.make_async_copy(r["down"], target, sem).start()

    @pl.when(column != place)
    def _():
        by = jnp.maximum((place + count - column) % count, 1)
        for i, other, start, size, ref in placed(downs, piece):
            to = target.at[take(((mine ^ i) * HALVES + (side ^ other)) * piece + start, size)]
            pltpu.make_async_copy(ref.at[by - 1], to, sem).start()


def ffn_kernel(count, js, names, *refs):
    r = dict(zip(names, refs, strict=True))
    r["hidden_w"] = r["hidden"]
    first, last = js[0] == 0, js[-1] == COLUMNS - 1
    step = pl.program_id(0)
    tile = r["hidden"].shape[1]
    tokens = r["second"].shape[0]
    second, feed_back = r["second"], r["feed_back"]
    feed, second_back = r["feed"], r["second_back"]

    @pl.when(step == 0)
    def _():
        where = r["where"][0], r["where"][1], r["where"][2]
        for t, j in enumerate(js):
            pair = [
                [r[f"pair{j}_{other}_{i}"] for i in range(1 if j < 3 else 2)]
                for other in range(HALVES)
            ]
            tile_copies(r, where, count, (t, j), pair, [r[f"down_{i}"] for i in range(10)])
        if first:
            r["turned"][...] = second[...].T
            for i in range(tokens // CHUNK):
                rows = slice(i * CHUNK, (i + 1) * CHUNK)
                upstream = r["cot"][rows, :].astype(f32) * r["factor"][0]
                feed_back[rows, :] = (upstream * r["mod"][i : i + 1, part(3)]).astype(bf16)

    pair_w, down_w = r["pair_w"].at[step], r["down_w"].at[step]
    wait_for(pair_w, r["pair_sems"].at[step])
    wait_for(down_w, r["down_sems"].at[step])
    sub = 256
    for n in range(tile // sub):
        lanes = slice(n * sub, (n + 1) * sub)
        gate = matmul(second[...], pair_w[0, :, lanes])
        upval = matmul(second[...], pair_w[1, :, lanes])
        hidden_back = times_transposed(feed_back[...], down_w[lanes, :])
        sigmoid = jax.nn.sigmoid(gate)
        silu = gate * sigmoid
        r["hidden"][:, lanes] = (silu * upval).astype(bf16)
        r["pair_back"][0, 1, :, lanes] = (hidden_back * silu).astype(bf16)
        r["pair_back"][0, 0, :, lanes] = (
            hidden_back * upval * (sigmoid * (1.0 + gate * (1.0 - sigmoid)))
        ).astype(bf16)

    r["hidden_turned"][0] = r["hidden"][...].T
    feed_part = matmul(r["hidden"][...], down_w[...])
    back_part = times_transposed(r["pair_back"][0, 0], pair_w[0]) + times_transposed(
        r["pair_back"][0, 1], pair_w[1]
    )

    @pl.when(step == 0)
    def _():
        feed[...] = feed_part if first else r["feed_in"][...] + feed_part
        second_back[...] = back_part if first else r["back_in"][...] + back_part

    @pl.when(step > 0)
    def _():
        feed[...] += feed_part
        second_back[...] += back_part

    if not last:
        return

    @pl.when(step == len(js) - 1)
    def _():
        for i in range(tokens // CHUNK):
            rows = slice(i * CHUNK, (i + 1) * CHUNK)
            gate_one = r["mod"][i : i + 1, part(0)]
            scale_two = r["mod"][i : i + 1, part(2)]
            gate_two = r["mod"][i : i + 1, part(3)]
            middle = r["middle"][rows, :]
            r["output"][rows, :] = (middle + gate_two * feed[rows, :]).astype(bf16)
            upstream = r["cot"][rows, :].astype(f32) * r["factor"][0]
            normed, inverse = normalize(middle)
            back = second_back[rows, :]
            middle_back = upstream + normalize_back(normed, inverse, back * (1.0 + scale_two))
            r["middle_back"][rows, :] = middle_back
            r["branch_back"][rows, :] = (middle_back * gate_one).astype(bf16)
            for where, values in enumerate(
                (middle_back * r["branch"][rows, :], back, back * normed, upstream * feed[rows, :])
            ):
                r["sums"][i : i + 1, part(where)] = jnp.sum(values, axis=0, keepdims=True)


ORDER = (1, 3, 2, 0)
SEND_X, KEEP_X, SEND_Y, KEEP_Y = (1, 3), (2, 0), (3, 2), (1, 0)
CUT = (SEND_X, KEEP_X, SEND_Y, KEEP_Y)


def put_grad(grad, other_ref, out_refs):
    step = pl.program_id(0)
    if other_ref is None:
        out_refs[0][0] = grad.astype(bf16)
        return
    total = (grad + other_ref[0].astype(f32)).astype(bf16)
    first = first_part(total.shape[1])
    for at, j in enumerate(ORDER):

        @pl.when(step == at)
        def _():
            for columns, ref in zip(CUT, out_refs, strict=True):
                if j in columns:
                    ref[0] = total[:, :first] if columns in (SEND_X, KEEP_X) else total[:, first:]


def cut_specs(count, rows, breadth):
    first = first_part(rows)
    shapes, specs = [], []
    for columns in CUT:
        size = first if columns in (SEND_X, KEEP_X) else rows - first
        shapes.append(struct((2, count, size, breadth), bf16))
        second = ORDER.index(columns[1])
        specs.append(
            pl.BlockSpec(
                (1, count, size, breadth),
                lambda s, where, second=second: (jnp.where(s >= second, 1, 0), 0, 0, 0),
            )
        )
    return tuple(shapes), tuple(specs)


def split_refs(mine, refs):
    return (refs[0], refs[1:]) if mine else (None, refs)


def pair_grad_kernel(mine, count, where_ref, turned_ref, own_ref, near_ref, far_ref, *refs):
    other_ref, out_refs = split_refs(mine, refs)
    for at, j in enumerate(ORDER):

        @pl.when(pl.program_id(0) == at)
        def _():
            back = {0: own_ref, 3: far_ref}.get(j, near_ref)
            grad = matmul(turned_ref[...], back[0, 0])
            put_grad(grad.reshape(count, grad.shape[0] // count, grad.shape[1]), other_ref, out_refs)


def down_grad_kernel(mine, where_ref, *refs):
    hiddens, feed_back_ref, out_ref = refs[:3], refs[3], refs[-1]
    other_ref = refs[4] if mine else None
    side = where_ref[2] if mine else where_ref[2] ^ 1
    count, _, rows, _ = out_ref.shape
    tiles = [(hidden, t) for hidden in hiddens for t in range(hidden.shape[0])]
    for j, (hidden, t) in enumerate(tiles):
        pieces = [hidden[t, take(((where_ref[1] ^ c) * HALVES + side) * rows, rows), :] for c in ORDER]
        grad = matmul(jnp.concatenate(pieces, axis=0), feed_back_ref[...]).reshape(COLUMNS, rows, WIDTH)
        owner = where_ref[1] ^ j
        if mine:
            grad = grad + other_ref[owner].astype(f32)
        out_ref[owner] = grad.astype(bf16)


def attn_grad_kernel(
    mine, where_ref, first_ref, attended_ref, joint_back_ref, branch_back_ref, *refs
):
    other_ref, out_refs = split_refs(mine, refs)
    column = where_ref[1] ^ where_ref[3 + pl.program_id(0)]
    side = where_ref[2] if mine else where_ref[2] ^ 1
    _, count, _, _ = out_refs[0].shape
    rows = WIDTH // count // HALVES

    def put(turned, right):
        taken = [turned[take((z * HALVES + side) * rows, rows), :] for z in range(count)]
        grad = matmul(jnp.concatenate(taken, axis=0), right[...])
        put_grad(grad.reshape(count, rows, WIDTH), other_ref, out_refs)

    @pl.when(column < 3)
    def _():
        put(first_ref, joint_back_ref)

    @pl.when(column == 3)
    def _():
        put(attended_ref, branch_back_ref)


def place_pair_kernel(where_ref, *refs):
    sources, outs = refs[:10], refs[10:]
    rows, tile = sources[0].shape
    for way in range(HALVES):

        @pl.when(where_ref[2] == way)
        def _():
            for j, other, start, size, ref in placed(sources, rows):
                lanes = take((where_ref[1] ^ j) * tile, tile)
                outs[way ^ other][start : start + size, lanes] = ref[...].astype(f32)


def place_down_kernel(where_ref, *refs):
    sources, out = refs[:10], refs[10]
    rows = sources[0].shape[0]
    for j, other, start, size, ref in placed(sources, rows):
        piece = (where_ref[1] ^ j) * HALVES + (where_ref[2] ^ other)
        out[take(piece * rows + start, size), :] = ref[...].astype(f32)


def place_attn_kernel(where_ref, *refs):
    sources, joint_ref, project_ref = refs[:10], refs[10], refs[11]
    rows = sources[0].shape[0]
    for column in range(COLUMNS):

        @pl.when(where_ref[1] == column)
        def _():
            for j, other, start, size, ref in placed(sources, rows):
                to = take((where_ref[2] ^ other) * rows + start, size)
                if column ^ j == 3:
                    project_ref[to, :] = ref[...].astype(f32)
                else:
                    joint_ref[to, part(column ^ j)] = ref[...].astype(f32)


def attend_back_kernel(
    query_ref, keys_ref, values_ref, branch_back_ref, column_ids, row_ids, cos_ref,
    sin_ref, weight, joint_back_ref, mixed_back, query_back, keys_back, values_back,
):
    mixed_back[...] = times_transposed(branch_back_ref[...], weight[0]).astype(bf16)
    allowed = column_ids[...] == row_ids[...]
    scaling = HEAD_DIM ** (-0.5)
    for head in range(HEADS):
        lanes, inside = window(head)
        zero = jnp.zeros((), bf16)
        query = jnp.where(inside, query_ref[:, lanes], zero)
        back = jnp.where(inside, mixed_back[:, lanes], zero)
        soft = soft_scores(query, keys_ref[:, lanes], allowed)
        probs_back = times_transposed(back, values_ref[:, lanes])
        scores_back = (
            soft * (probs_back - jnp.sum(soft * probs_back, axis=-1, keepdims=True))
        ).astype(bf16)
        query_back[:, lanes] = jnp.where(
            inside, matmul(scores_back, keys_ref[:, lanes]) * scaling, query_back[:, lanes]
        )
        keys_back[:, lanes] = jnp.where(
            inside, contract_rows(scores_back, query) * scaling, keys_back[:, lanes]
        )
        values_back[:, lanes] = jnp.where(
            inside, contract_rows(soft.astype(bf16), back), values_back[:, lanes]
        )

    @pl.loop(0, BLOCK // CHUNK)
    def _(i):
        rows = pl.ds(pl.multiple_of(i * CHUNK, CHUNK), CHUNK)
        cos, sin = cos_ref[rows, :], sin_ref[rows, :]
        joint_back_ref[rows, part(0)] = rotate(query_back[rows, :], cos, -sin).astype(bf16)
        joint_back_ref[rows, part(1)] = rotate(keys_back[rows, :], cos, -sin).astype(bf16)
        joint_back_ref[rows, part(2)] = values_back[rows, :].astype(bf16)


def first_back_kernel(
    joint_back_ref, x_ref, middle_back_ref, mod_ref, weight, grad_ref, sums_ref, first_back
):
    step = pl.program_id(0)
    product = times_transposed(joint_back_ref[...], weight[0])

    @pl.when(step == 0)
    def _():
        first_back[...] = product

    @pl.when(step > 0)
    def _():
        first_back[...] += product

    @pl.when(step == pl.num_programs(0) - 1)
    def _():
        finish_first_back(x_ref, middle_back_ref, mod_ref, grad_ref, sums_ref, first_back)


def finish_first_back(x_ref, middle_back_ref, mod_ref, grad_ref, sums_ref, first_back):
    for i in range(x_ref.shape[0] // CHUNK):
        rows = slice(i * CHUNK, (i + 1) * CHUNK)
        normed, inverse = normalize(x_ref[rows, :].astype(f32))
        back = first_back[rows, :]
        grad_ref[rows, :] = middle_back_ref[rows, :] + normalize_back(
            normed, inverse, back * (1.0 + mod_ref[i : i + 1, part(1)])
        )
        sums_ref[i : i + 1, part(0)] = jnp.sum(back, axis=0, keepdims=True)
        sums_ref[i : i + 1, part(1)] = jnp.sum(back * normed, axis=0, keepdims=True)


SMEM = pl.BlockSpec(memory_space=pltpu.SMEM)
VMEM = pl.BlockSpec(memory_space=pltpu.VMEM)
ANY = pl.BlockSpec(memory_space=pl.ANY)


def struct(shape, dtype):
    return jax.ShapeDtypeStruct(shape, dtype)


def params(mega=56):
    return pltpu.CompilerParams(vmem_limit_bytes=mega * MEGA)


def cost(microseconds):
    return pl.CostEstimate(flops=int(microseconds * 1e9), bytes_accessed=1000, transcendentals=0)


def by_block(*shape):
    return pl.BlockSpec(shape, lambda b: (b,) + (0,) * (len(shape) - 1))


def whole(*shape):
    return pl.BlockSpec(shape, lambda *_: (0,) * len(shape))


def first_call(where, x, mod, cos, sin, joint, project, arrived):
    tokens = x.shape[0]
    count = arrived[0].shape[0] + 1
    shape = struct((tokens, WIDTH), bf16)
    return pl.pallas_call(
        functools.partial(first_kernel, count),
        out_shape=(struct((WIDTH, tokens), bf16),)
        + (shape,) * 3
        + (struct((COLUMNS, WIDTH, WIDTH), bf16),),
        in_specs=[SMEM, VMEM, VMEM, VMEM, VMEM] + [ANY] * (2 + len(arrived)),
        out_specs=(VMEM,) * 4 + (ANY,),
        scratch_shapes=[
            pltpu.VMEM((COLUMNS, WIDTH, WIDTH), bf16),
            pltpu.VMEM((tokens, WIDTH), bf16),
            pltpu.VMEM((tokens, WIDTH), f32),
            pltpu.SemaphoreType.DMA((COLUMNS,)),
        ],
        compiler_params=params(),
        cost_estimate=cost(20),
    )(where, x, mod, cos, sin, joint, project, *arrived)


def attend_call(query, keys, values, ids, x, mod, weight):
    tokens = x.shape[0]
    return pl.pallas_call(
        attend_kernel,
        grid=(tokens // BLOCK,),
        out_shape=(
            struct((WIDTH, tokens), bf16),
            struct((tokens, WIDTH), f32),
            struct((tokens, WIDTH), f32),
            struct((tokens, WIDTH), bf16),
        ),
        in_specs=[by_block(BLOCK, WIDTH)] * 3
        + [by_block(BLOCK, 1), pl.BlockSpec((1, BLOCK), lambda b: (0, b)), by_block(BLOCK, WIDTH)]
        + [by_block(1, BLOCK // CHUNK, 4 * WIDTH), pl.BlockSpec((1, WIDTH, WIDTH), lambda b: (3, 0, 0))],
        out_specs=(pl.BlockSpec((WIDTH, BLOCK), lambda b: (0, b)),) + (by_block(BLOCK, WIDTH),) * 3,
        scratch_shapes=[pltpu.VMEM((BLOCK, WIDTH), f32)],
        compiler_params=params(),
        cost_estimate=cost(12),
    )(
        query, keys, values, ids[:, None], ids[None, :], x,
        mod.reshape(tokens // BLOCK, BLOCK // CHUNK, 4 * WIDTH), weight,
    )


def ffn_call(js, where, given, shards, pairs, downs):
    second = given["second"]
    tokens = second.shape[0]
    ff = shards["gate"].shape[1]
    tile = ff // COLUMNS
    count = ff // shards["down"].shape[0]
    chunks = tokens // CHUNK
    first, last = js[0] == 0, js[-1] == COLUMNS - 1
    full = whole(tokens, WIDTH)
    wide = struct((tokens, WIDTH), f32)
    narrow = struct((tokens, WIDTH), bf16)
    inputs = [("where", where, SMEM), ("second", second, full)]
    if first or last:
        inputs += [
            ("factor", given["factor"], SMEM),
            ("cot", given["cot"], full),
            ("mod", given["mod"], whole(chunks, 4 * WIDTH)),
        ]
    if not first:
        inputs += [
            ("feed_back", given["feed_back"], full),
            ("feed_in", given["feed"], full),
            ("back_in", given["second_back"], full),
        ]
    if last:
        inputs += [("middle", given["middle"], full), ("branch", given["branch"], full)]
    inputs += [(name, shards[name], ANY) for name in ("gate", "up", "down")]
    for j in js:
        for other in range(HALVES):
            inputs += [(f"pair{j}_{other}_{i}", a, ANY) for i, a in enumerate(pairs[other][j])]
    inputs += [(f"down_{i}", a, ANY) for i, a in enumerate(downs)]
    outputs = [
        (
            "hidden_turned",
            struct((len(js), tile, tokens), bf16),
            pl.BlockSpec((1, tile, tokens), lambda t: (t, 0, 0)),
        ),
        (
            "pair_back",
            struct((len(js), HALVES, tokens, tile), bf16),
            pl.BlockSpec((1, HALVES, tokens, tile), lambda t: (t, 0, 0, 0)),
        ),
    ]
    if first:
        outputs += [
            ("turned", struct((WIDTH, tokens), bf16), whole(WIDTH, tokens)),
            ("feed_back", narrow, full),
        ]
    sums = ("feed", "second_back")
    scratch = [
        ("pair_w", pltpu.VMEM((len(js), HALVES, WIDTH, tile), bf16)),
        ("down_w", pltpu.VMEM((len(js), ff // count, WIDTH), bf16)),
        ("hidden", pltpu.VMEM((tokens, tile), bf16)),
        ("pair_sems", pltpu.SemaphoreType.DMA((len(js),))),
        ("down_sems", pltpu.SemaphoreType.DMA((len(js),))),
    ]
    if last:
        outputs += [
            ("output", narrow, full),
            ("middle_back", wide, full),
            ("branch_back", narrow, full),
            ("sums", struct((chunks, 4 * WIDTH), f32), whole(chunks, 4 * WIDTH)),
        ]
        scratch += [(name, pltpu.VMEM((tokens, WIDTH), f32)) for name in sums]
    else:
        outputs += [(name, wide, full) for name in sums]
    names = [each[0] for each in inputs + outputs + scratch]
    found = pl.pallas_call(
        functools.partial(ffn_kernel, count, js, names),
        grid=(len(js),),
        out_shape=tuple(shape for _, shape, _ in outputs),
        in_specs=[spec for _, _, spec in inputs],
        out_specs=tuple(spec for _, _, spec in outputs),
        scratch_shapes=[shape for _, shape in scratch],
        compiler_params=params(),
        cost_estimate=cost(12 * len(js)),
    )(*[array for _, array, _ in inputs])
    return {name: array for (name, _, _), array in zip(outputs, found, strict=True)}


def by_column(call, count, rows, breadth, in_specs, where, arrays, other):
    shapes, specs = cut_specs(count, rows, breadth)
    block = pl.BlockSpec((1, count, rows, breadth), lambda s, where: (s, 0, 0, 0))
    if other is None:
        shapes, specs = (struct((COLUMNS, count, rows, breadth), bf16),), (block,)
    else:
        in_specs, arrays = in_specs + [block], arrays + (other,)
    found = pl.pallas_call(
        call,
        out_shape=shapes,
        grid_spec=pltpu.PrefetchScalarGridSpec(
            num_scalar_prefetch=1, grid=(COLUMNS,), in_specs=in_specs, out_specs=specs
        ),
        compiler_params=params(),
        cost_estimate=cost(10),
    )(where, *arrays)
    return found[0] if other is None else found


def pair_grad_call(count, where, turned, backs, other=None):
    tokens, tile = backs[0].shape[2:]
    mine = other is not None

    def spec(tile_of):
        return pl.BlockSpec(
            (1, 1, tokens, tile),
            lambda s, where: (tile_of(where[3 + s]), where[2] if mine else where[2] ^ 1, 0, 0),
        )

    return by_column(
        functools.partial(pair_grad_kernel, mine, count),
        count, WIDTH // count, tile,
        [whole(WIDTH, tokens), spec(lambda j: 0), spec(lambda j: jnp.clip(j - 1, 0, 1)), spec(lambda j: 0)],
        where, (turned,) + tuple(backs), other,
    )


def attn_grad_call(count, where, first, attended, joint_back, branch_back, other=None):
    tokens = first.shape[1]
    return by_column(
        functools.partial(attn_grad_kernel, other is not None),
        count, WIDTH // count // HALVES, WIDTH,
        [
            whole(WIDTH, tokens),
            whole(WIDTH, tokens),
            pl.BlockSpec((tokens, WIDTH), lambda s, where: (0, jnp.minimum(where[1] ^ where[3 + s], 2))),
            whole(tokens, WIDTH),
        ],
        where, (first, attended, joint_back, branch_back), other,
    )


def down_grad_call(count, where, hiddens, feed_back, other=None):
    ff = sum(h.shape[0] * h.shape[1] for h in hiddens)
    out = struct((count, COLUMNS, ff // count // PIECES, WIDTH), bf16)
    arrays = tuple(hiddens) + (feed_back,) + (() if other is None else (other,))
    return pl.pallas_call(
        functools.partial(down_grad_kernel, other is not None),
        out_shape=out,
        in_specs=[SMEM] + [VMEM] * len(arrays),
        out_specs=VMEM,
        compiler_params=params(),
        cost_estimate=cost(7),
    )(where, *arrays)


def place_call(kernel, where, arrays, outs):
    return pl.pallas_call(
        kernel,
        out_shape=outs,
        in_specs=[SMEM] + [VMEM] * len(arrays),
        out_specs=jax.tree.map(lambda _: VMEM, outs),
        compiler_params=params(),
        cost_estimate=cost(4),
    )(where, *arrays)


def attend_back_call(query, keys, values, branch_back, ids, cos, sin, weight):
    tokens = query.shape[0]
    block = by_block(BLOCK, WIDTH)
    return pl.pallas_call(
        attend_back_kernel,
        grid=(tokens // BLOCK,),
        out_shape=struct((tokens, 3 * WIDTH), bf16),
        in_specs=[block, block, block, block]
        + [by_block(BLOCK, 1), pl.BlockSpec((1, BLOCK), lambda b: (0, b)), block, block]
        + [pl.BlockSpec((1, WIDTH, WIDTH), lambda b: (3, 0, 0))],
        out_specs=by_block(BLOCK, 3 * WIDTH),
        scratch_shapes=[
            pltpu.VMEM((BLOCK, WIDTH), bf16),
            pltpu.VMEM((BLOCK, WIDTH), f32),
            pltpu.VMEM((BLOCK, WIDTH), f32),
            pltpu.VMEM((BLOCK, WIDTH), f32),
        ],
        compiler_params=params(),
        cost_estimate=cost(29),
    )(query, keys, values, branch_back, ids[:, None], ids[None, :], cos, sin, weight)


def first_back_call(joint_back, x, middle_back, mod, weight):
    tokens = x.shape[0]
    chunks = tokens // CHUNK
    full = whole(tokens, WIDTH)
    return pl.pallas_call(
        first_back_kernel,
        grid=(3,),
        out_shape=(struct((tokens, WIDTH), f32), struct((chunks, 2 * WIDTH), f32)),
        in_specs=[
            pl.BlockSpec((tokens, WIDTH), lambda c: (0, c)),
            full,
            full,
            whole(chunks, 2 * WIDTH),
            pl.BlockSpec((1, WIDTH, WIDTH), lambda c: (c, 0, 0)),
        ],
        out_specs=(full, whole(chunks, 2 * WIDTH)),
        scratch_shapes=[pltpu.VMEM((tokens, WIDTH), f32)],
        compiler_params=params(),
        cost_estimate=cost(13),
    )(joint_back, x, middle_back, mod, weight)


def shifts(count, by):
    return [(i, (i + by) % count) for i in range(count)]


def pick(array, index):
    return lax.dynamic_index_in_dim(array, index, 0, keepdims=False)


def across(bit):
    return [(i, i ^ bit) for i in range(PIECES)]


def swap(array, bit):
    return lax.ppermute(array, "bucket", across(bit))


def after(arrays, *others):
    return lax.optimization_barrier((arrays, others))[0]


def add(left, right):
    return (left.astype(f32) + right.astype(f32)).astype(bf16)


def over_z(piece):
    count = lax.axis_size("fsdp")
    return [lax.ppermute(piece, "fsdp", shifts(count, by)) for by in range(1, count)]


def gather_z(piece):
    count = lax.axis_size("fsdp")
    place = lax.axis_index("fsdp")
    full = lax.all_gather(piece, "fsdp", axis=0, tiled=False)
    return jnp.stack([pick(full, (place + count - by) % count) for by in range(1, count)])


def cross(by_x, by_y, first):
    if first is not None:
        by_x, by_y = by_x[..., :first, :], by_y[..., first:, :]
    return swap(by_x, 4), swap(by_y, 2)


def both(here):
    return here + tuple(None if array is None else swap(array, 1) for array in here)


def spread(total):
    by_x, by_y = swap(total, 2), swap(total, 4)
    return both((total, by_x, by_y) + cross(by_x, by_y, first_part(total.shape[0])))


def spread_whole(pieces):
    first = first_part(pieces.shape[1])

    def of(side):
        own, by_x, by_y, far = (pieces[c * HALVES + side] for c in range(COLUMNS))
        return own, by_x, by_y, far[:first], far[first:]

    return of(0) + of(1)


def halve_once(cut):
    send_x, (a2, a0), send_y, (b1, b0) = cut
    from_x, from_y = swap(send_x, 2), swap(send_y, 4)
    return add(a0, from_x[0]), add(a2, from_x[1]), add(b0, from_y[1]), add(b1, from_y[0])


def halve_twice(once):
    a0, a2, b0, b1 = once
    return jnp.concatenate([add(a0, swap(a2, 4)), add(b0, swap(b1, 2))], axis=-2)


def sum_z(parts):
    count = lax.axis_size("fsdp")
    place = lax.axis_index("fsdp")
    total = pick(parts, place).astype(f32)
    for by in range(1, count):
        total = total + lax.ppermute(
            pick(parts, (place + by) % count), "fsdp", shifts(count, by)
        ).astype(f32)
    return total.astype(bf16)


def cut_down(part, first):
    cut = []
    for columns in CUT:
        both_columns = jnp.stack([part[ORDER.index(j)] for j in columns])
        cut.append(both_columns[:, :first] if columns in (SEND_X, KEEP_X) else both_columns[:, first:])
    return cut


def uncut(cut):
    def of(j, pair):
        columns = next(c for c in pair if j in c)
        return cut[CUT.index(columns)][columns.index(j)]

    return jnp.stack(
        [jnp.concatenate([of(j, (SEND_X, KEEP_X)), of(j, (SEND_Y, KEEP_Y))], axis=1) for j in ORDER]
    )


def sum_whole(mine, theirs):
    parts = jnp.stack([mine, theirs], axis=1)
    parts = jnp.stack([parts[ORDER.index(c)] for c in range(COLUMNS)])
    rows, breadth = mine.shape[2:]
    parts = lax.psum(parts, "bucket").transpose(2, 0, 1, 3, 4)
    return spread_whole(sum_z(parts).reshape(PIECES, rows, breadth))


def arrived_whole(pieces):
    count = lax.axis_size("fsdp")
    place = lax.axis_index("fsdp")
    first = first_part(pieces.shape[1])
    full = lax.all_gather(pieces, "fsdp", axis=0, tiled=False)
    full = jnp.stack([pick(full, (place + count - by) % count) for by in range(1, count)])

    def of(side):
        own, by_x, by_y, far = (full[:, c * HALVES + side] for c in range(COLUMNS))
        return own, by_x, by_y, far[:, :first], far[:, first:]

    return of(0) + of(1)


def to_group(rows, count, place):
    relative = jnp.stack(
        [pick(rows, place)]
        + [
            lax.ppermute(pick(rows, (place + by) % count), "fsdp", shifts(count, by))
            for by in range(1, count)
        ]
    )
    return jnp.stack([pick(relative, (place - j) % count) for j in range(count)])


def on_device(
    inputs,
    condition,
    segment_ids,
    grid_widths,
    bucket_counts,
    modulate_weight,
    joint_weight,
    project_weight,
    gate_weight,
    up_weight,
    down_weight,
    cotangent,
):
    fsdp_count = lax.axis_size("fsdp")
    place = lax.axis_index("fsdp")
    bucket = lax.axis_index("bucket")
    height = joint_weight.shape[0]
    half = height // HALVES
    ff = gate_weight.shape[1]
    tile = ff // COLUMNS
    down_rows = down_weight.shape[0] // PIECES
    slots = condition.shape[0]

    fast = lax.axis_size("bucket") == PIECES
    if fast:
        column, side = bucket // HALVES, bucket % HALVES
        where = jnp.stack([place, column, side] + [jnp.int32(j) for j in ORDER])
        attn_piece = jnp.where(
            column == 3,
            lax.dynamic_slice(project_weight, (side * half, 0), (half, WIDTH)),
            lax.dynamic_slice(joint_weight, (side * half, column * WIDTH), (half, WIDTH)),
        )
        ffn_piece = jnp.where(
            side == 0,
            lax.dynamic_slice(gate_weight, (0, column * tile), (height, tile)),
            lax.dynamic_slice(up_weight, (0, column * tile), (height, tile)),
        )
        down_piece = lax.dynamic_slice_in_dim(down_weight, bucket * down_rows, down_rows, 0)
        attn_z = gather_z(attn_piece)
        pair_z = gather_z(after(ffn_piece, attn_z))
        down_k = over_z(after(down_piece, attn_z))
        attn_x, attn_y = swap(attn_z, 2), swap(attn_z, 4)
        attn_arrived = both((attn_z, attn_x, attn_y) + cross(attn_x, attn_y, first_part(half)))
    else:
        where = jnp.stack([place, 0 * place, 0 * place] + [jnp.int32(j) for j in ORDER])
        attn_arrived = arrived_whole(
            jnp.concatenate([joint_weight, project_weight], axis=1)
            .reshape(HALVES, half, COLUMNS, WIDTH)
            .transpose(2, 0, 1, 3)
            .reshape(PIECES, half, WIDTH)
        )
        pairs = arrived_whole(
            jnp.stack([gate_weight, up_weight])
            .reshape(HALVES, height, COLUMNS, tile)
            .transpose(2, 0, 1, 3)
            .reshape(PIECES, height, tile)
        )
        downs = arrived_whole(down_weight.reshape(PIECES, down_rows, WIDTH))

    cond_float = condition.astype(f32)
    lifted = jax.nn.silu(cond_float).astype(bf16)
    lifted_rows = to_group(
        lifted.reshape(slots, fsdp_count, height).transpose(1, 0, 2), fsdp_count, place
    ).reshape(fsdp_count * slots, height)
    one_hot = (
        segment_ids[::CHUNK, None] == jnp.arange(slots, dtype=jnp.int32)[None, :]
    ).astype(f32)

    def modulation_parts(weight, rows):
        parts = matmul(rows, weight).reshape(fsdp_count, slots, weight.shape[1])
        return to_group(parts, fsdp_count, place)

    def modulation(parts):
        return jnp.dot(
            one_hot,
            jnp.sum(parts, axis=0),
            precision=lax.Precision.HIGHEST,
            preferred_element_type=f32,
        )

    mod_one = modulation(modulation_parts(modulate_weight[:, : 2 * WIDTH], lifted_rows))
    if fast:
        lifted_rows = after(lifted_rows, attn_z)
    mod_parts = modulation_parts(modulate_weight[:, 2 * WIDTH :], lifted_rows)
    counts = bucket_counts.astype(f32)
    mine = jnp.sum(jnp.where(jnp.arange(counts.shape[0], dtype=jnp.int32) == bucket, counts, 0.0))
    factor = (mine * counts.shape[0] / jnp.sum(counts)).reshape(1)
    cos, sin = rope_tables(segment_ids, grid_widths)

    first, query, keys, values, weight = first_call(
        where, inputs, mod_one, cos, sin, joint_weight, project_weight, attn_arrived
    )
    if fast:
        mod_parts, down_k = after((mod_parts, down_k), query)
        down_z = jnp.stack(down_k)
        down_x, down_y = swap(down_z, 2), swap(down_z, 4)
    mod = modulation(mod_parts)
    attended, branch, middle, second = attend_call(
        query, keys, values, segment_ids, inputs, mod, weight
    )
    shards = dict(gate=gate_weight, up=up_weight, down=down_weight)
    given = dict(
        second=second, factor=factor, cot=cotangent, mod=mod, middle=middle, branch=branch
    )
    if fast:
        down_x, down_y, pair_z = after((down_x, down_y, pair_z), second)
        down_far = cross(down_x, down_y, first_part(down_rows))
        downs = both((down_z, down_x, down_y) + down_far)
        pair_z = after(pair_z, down_far)
        pair_x, pair_y = swap(pair_z, 2), swap(pair_z, 4)
        pairs = (pair_z, pair_x, pair_y, None, None, swap(pair_z, 1), None, None, None, None)
    pairs = [
        [[group] for group in pairs[5 * k : 5 * k + 3]] + [list(pairs[5 * k + 3 : 5 * k + 5])]
        for k in range(HALVES)
    ]
    found = ffn_call((0,), where, given, shards, pairs, downs)
    turned, feed_back = found["turned"], found["feed_back"]
    steps = [found]
    if fast:
        pair_x, pair_y = after((pair_x, pair_y), feed_back)
        far = cross(pair_x, pair_y, first_part(height))
        pairs[1][1:3] = [swap(pair_x, 1)], [swap(pair_y, 1)]
    for js in ((1, 2), (3,)):
        given.update(feed_back=feed_back, feed=found["feed"], second_back=found["second_back"])
        if fast and js == (3,):
            far = after(far, found["feed"])
            pairs[0][3], pairs[1][3] = list(far), [swap(array, 1) for array in far]
        found = ffn_call(js, where, given, shards, pairs, downs)
        steps.append(found)
    output, middle_back, branch_back = found["output"], found["middle_back"], found["branch_back"]
    late_sums = found["sums"]

    count = fsdp_count
    hiddens = [step["hidden_turned"] for step in steps]
    backs = [step["pair_back"] for step in steps]
    down_theirs = down_grad_call(count, where, hiddens, feed_back)
    if fast:
        turned = after(turned, down_theirs)
    pair_theirs = pair_grad_call(count, where, turned, backs)
    if fast:
        down_other = swap(down_theirs, 1)
        down_other, pair_theirs = after((down_other, pair_theirs))
        pair_other = swap(pair_theirs, 1)
    else:
        down_other, pair_other = jnp.zeros_like(down_theirs), jnp.zeros_like(pair_theirs)
    down_mine = down_grad_call(count, where, hiddens, feed_back, down_other)
    if fast:
        turned = after(turned, down_mine)
    pair_cut = pair_grad_call(count, where, turned, backs, pair_other)
    if fast:
        down_part = lax.psum_scatter(down_mine, "fsdp", scatter_dimension=0, tiled=False)
        branch_back = after(branch_back, pair_cut)
    joint_back = attend_back_call(
        query, keys, values, branch_back, segment_ids, cos, sin, weight
    )
    if fast:
        send_x, keep_x, send_y, keep_y = pair_cut
        keep_x, keep_y = after((keep_x, keep_y), joint_back)
        pair_once = halve_once((send_x, keep_x, send_y, keep_y))
        branch_back = after(branch_back, pair_once)
        branch_back = after(branch_back, pair_once)
    attn_theirs = attn_grad_call(count, where, first, attended, joint_back, branch_back)
    if fast:
        pair_parts, down_part = after((halve_twice(pair_once), down_part), attn_theirs)
        pair_sum = lax.psum_scatter(pair_parts, "fsdp", scatter_dimension=0, tiled=False)
        down_cut = cut_down(down_part, first_part(down_rows))
        middle_back = after(middle_back, attn_theirs, down_cut)
    grad_inputs, early_sums = first_back_call(joint_back, inputs, middle_back, mod_one, weight)
    if fast:
        down_cut = [down_cut[0], after(down_cut[1], grad_inputs), down_cut[2], after(down_cut[3], grad_inputs)]
        down_once = halve_once(down_cut)
        attn_other, down_once = after((swap(attn_theirs, 1), down_once), grad_inputs)
        attn_cut = attn_grad_call(
            count, where, first, attended, joint_back, branch_back, attn_other
        )
        down_total = after(halve_twice(down_once), attn_cut)
        attn_once = halve_once(attn_cut)
        pair_sum, down_total = after((pair_sum, down_total), attn_once)
        attn_parts = halve_twice(attn_once)
        pair_x, pair_y = swap(pair_sum, 2), swap(pair_sum, 4)
        down_x, down_y = swap(down_total, 2), swap(down_total, 4)
        attn_z = [
            lax.ppermute(pick(attn_parts, (place + by) % count), "fsdp", shifts(count, by))
            for by in range(1, count)
        ]
        pair_x, pair_y, down_x, down_y = after((pair_x, pair_y, down_x, down_y), attn_parts)
        down_far = cross(down_x, down_y, first_part(down_rows))
        pair_far = cross(pair_x, pair_y, first_part(height))
        attn_sum = pick(attn_parts, place).astype(f32)
        for array in after(attn_z, pair_far, down_far):
            attn_sum = attn_sum + array.astype(f32)
        attn_sum = attn_sum.astype(bf16)
        down_sums = both((down_total, down_x, down_y) + down_far)
        pair_sums = both((pair_sum, pair_x, pair_y) + pair_far)
        attn_sums = spread(attn_sum)
    else:
        down_sums = sum_whole(down_mine.swapaxes(0, 1), down_theirs.swapaxes(0, 1))
        pair_sums = sum_whole(uncut(pair_cut), pair_theirs)
        attn_cut = attn_grad_call(
            count, where, first, attended, joint_back, branch_back, jnp.zeros_like(attn_theirs)
        )
        attn_sums = sum_whole(uncut(attn_cut), attn_theirs)
    down_grad = place_call(place_down_kernel, where, down_sums, struct(down_weight.shape, f32))
    pair_grad = place_call(
        place_pair_kernel, where, pair_sums, (struct(gate_weight.shape, f32),) * 2
    )
    attn_grad = place_call(
        place_attn_kernel,
        where,
        attn_sums,
        (struct(joint_weight.shape, f32), struct(project_weight.shape, f32)),
    )

    def by_slot(chunk_sums):
        return lax.dot_general(
            one_hot,
            chunk_sums,
            (((0,), (0,)), ((), ())),
            precision=lax.Precision.HIGHEST,
            preferred_element_type=f32,
        ).astype(bf16)

    everyone = lax.all_gather(
        jnp.concatenate([by_slot(early_sums), by_slot(late_sums), lifted], axis=1),
        ("bucket", "fsdp"),
        axis=0,
        tiled=True,
    )
    if fast:
        everyone = after(everyone, attn_sum)
    all_back = everyone[:, : 6 * WIDTH]
    all_lifted = lax.dynamic_slice_in_dim(everyone, 6 * WIDTH + place * height, height, 1)
    modulate_gradient = contract_rows(all_lifted, all_back)
    group_back = lax.dynamic_slice_in_dim(
        all_back, bucket * fsdp_count * slots, fsdp_count * slots, 0
    )
    slope_rows = times_transposed(group_back, modulate_weight)
    condition_slope = (
        to_group(slope_rows.reshape(fsdp_count, slots, height), fsdp_count, place)
        .transpose(1, 0, 2)
        .reshape(slots, WIDTH)
    )
    grad_condition = condition_slope * silu_slope(cond_float)
    return (
        output,
        grad_inputs,
        grad_condition,
        modulate_gradient,
        *attn_grad,
        *pair_grad,
        down_grad,
    )


def solution(mesh):
    spread = P(("bucket", "fsdp"), None)
    rows = P("fsdp", None)
    in_specs = (
        spread, spread, P(("bucket", "fsdp")), P(("bucket", "fsdp")), P(),
        rows, rows, rows, rows, rows, rows, spread,
    )
    out_specs = (spread, spread, spread, rows, rows, rows, rows, rows, rows)
    return jax.shard_map(
        on_device, mesh=mesh, in_specs=in_specs, out_specs=out_specs, check_vma=False
    )
```

```python
import functools

import jax
import jax.numpy as jnp
from jax import lax
from jax.experimental import pallas as pl
from jax.experimental.pallas import tpu as pltpu
from jax.sharding import PartitionSpec as P

HEADS = 16
HEAD_DIM = 72
WIDTH = HEADS * HEAD_DIM
QUARTER = HEAD_DIM // 4
BLOCK = 256
CHUNK = 64
COLUMNS = 4
HALVES = 2
PIECES = COLUMNS * HALVES
LANES = 128

epsilon = 1e-06
masked_score = -1e30
f32 = jnp.float32
bf16 = jnp.bfloat16
MEGA = 2**20


def normalize(values):
    average = jnp.mean(values, axis=-1, keepdims=True)
    centered = values - average
    inverse = lax.rsqrt(jnp.mean(centered * centered, axis=-1, keepdims=True) + epsilon)
    return (centered * inverse, inverse)


def normalize_back(normed, inverse, upstream):
    return inverse * (
        upstream
        - jnp.mean(upstream, axis=-1, keepdims=True)
        - normed * jnp.mean(upstream * normed, axis=-1, keepdims=True)
    )


def matmul(left, right):
    return jnp.dot(left, right, preferred_element_type=f32)


def contract_rows(left, right):
    return lax.dot_general(left, right, (((0,), (0,)), ((), ())), preferred_element_type=f32)


def times_transposed(left, right):
    return lax.dot_general(left, right, (((1,), (1,)), ((), ())), preferred_element_type=f32)


def silu_slope(values):
    sigmoid = jax.nn.sigmoid(values)
    return sigmoid * (1.0 + values * (1.0 - sigmoid))


def rope_tables(segments, widths):
    slots = widths.shape[0]
    one_hot = (segments[:, None] == jnp.arange(slots, dtype=jnp.int32)[None, :]).astype(jnp.int32)
    counts = jnp.sum(one_hot, axis=0)
    starts = jnp.cumsum(counts) - counts
    start_token = jnp.sum(one_hot * starts[None, :], axis=1)
    width_token = jnp.maximum(jnp.sum(one_hot * widths[None, :], axis=1), 1)
    place = jnp.arange(segments.shape[0], dtype=jnp.int32) - start_token
    row_place = (place // width_token).astype(f32)
    col_place = (place % width_token).astype(f32)
    freqs = 10000.0 ** (-jnp.arange(QUARTER, dtype=f32) / QUARTER)
    angle_row = row_place[:, None] * freqs[None, :]
    angle_col = col_place[:, None] * freqs[None, :]
    cos_row, sin_row, cos_col, sin_col = (
        jnp.cos(angle_row),
        jnp.sin(angle_row),
        jnp.cos(angle_col),
        jnp.sin(angle_col),
    )
    cos = jnp.concatenate([cos_row, cos_row, cos_col, cos_col], axis=1)
    sin = jnp.concatenate([-sin_row, sin_row, -sin_col, sin_col], axis=1)
    return jnp.tile(cos, (1, HEADS)), jnp.tile(sin, (1, HEADS))


def part(index):
    return slice(index * WIDTH, (index + 1) * WIDTH)


def rotate(values, cos, sin):
    lane = lax.broadcasted_iota(jnp.int32, (1, WIDTH), 1)
    leading = lane % (2 * QUARTER) < QUARTER
    partner = jnp.where(
        leading,
        pltpu.roll(values, WIDTH - QUARTER, 1),
        pltpu.roll(values, QUARTER, 1),
    )
    return values * cos + partner * sin


def take(start, size):
    return pl.ds(pl.multiple_of(start, 128 if size % 128 == 0 else 16), size)


def first_part(rows):
    return -(-rows // 32) * 16


def placed(refs, rows):
    first = first_part(rows)
    each = len(refs) // HALVES
    for other in range(HALVES):
        here = refs[each * other : each * other + each]
        for j in range(3):
            yield j, other, 0, rows, here[j]
        if each == COLUMNS:
            yield 3, other, 0, rows, here[3]
        else:
            yield 3, other, 0, first, here[3]
            yield 3, other, first, rows - first, here[4]


def piece_copies(where, count, sources, target, rows, sem):
    place, column, side = where
    copies = []
    for j, other, start, size, ref in placed(sources, rows):
        for by in range(1, count):
            owner = (place + (count - by)) % count
            to = target(column ^ j, side ^ other, owner, start, size)
            copies.append(pltpu.make_async_copy(ref.at[by - 1], to, sem(column ^ j, side ^ other, owner)))
    return copies


def wait_for(ref, sem):
    pltpu.make_async_copy(ref, ref, sem).wait()


def first_kernel(
    count, where_ref, x_ref, mod_ref, cos_ref, sin_ref, joint_ref, project_ref, *refs
):
    sources, refs = refs[:-9], refs[-9:]
    turned_ref, query_ref, keys_ref, values_ref, weight_ref, weight, first_ref, total, sems = refs
    where = where_ref[0], where_ref[1], where_ref[2]
    rows_in = joint_ref.shape[0]
    half = rows_in // HALVES

    def target(column, side, place, start, size):
        return weight.at[column, take(place * rows_in + side * half + start, size)]

    copies = piece_copies(where, count, sources, target, half, lambda c, s, z: sems.at[c])
    for c in range(COLUMNS):
        shard = project_ref if c == 3 else joint_ref.at[:, pl.ds(c * WIDTH, WIDTH)]
        copies.append(pltpu.make_async_copy(shard, weight.at[c, take(where[0] * rows_in, rows_in)], sems.at[c]))
    for copy in copies:
        copy.start()
    tokens = x_ref.shape[0]
    for i in range(tokens // CHUNK):
        rows = slice(i * CHUNK, (i + 1) * CHUNK)
        normed, _ = normalize(x_ref[rows, :].astype(f32))
        first_ref[rows, :] = (
            normed * (1.0 + mod_ref[i : i + 1, part(1)]) + mod_ref[i : i + 1, part(0)]
        ).astype(bf16)
    turned_ref[...] = first_ref[...].T
    writes = [
        pltpu.make_async_copy(weight.at[c], weight_ref.at[c], sems.at[c]) for c in range(COLUMNS)
    ]
    wait_for(weight.at[3], sems.at[3])
    writes[3].start()
    for c, out in enumerate((query_ref, keys_ref, values_ref)):
        wait_for(weight.at[c], sems.at[c])
        writes[c].start()
        if c == 2:
            out[...] = matmul(first_ref[...], weight[c]).astype(bf16)
        else:
            total[...] = matmul(first_ref[...], weight[c])

            @pl.loop(0, tokens // CHUNK)
            def _(i):
                rows = pl.ds(pl.multiple_of(i * CHUNK, CHUNK), CHUNK)
                out[rows, :] = rotate(total[rows, :], cos_ref[rows, :], sin_ref[rows, :]).astype(bf16)

    for write in writes:
        write.wait()


def window(head):
    start = head * HEAD_DIM // LANES * LANES
    stop = -(-(head + 1) * HEAD_DIM // LANES) * LANES
    lane = lax.broadcasted_iota(jnp.int32, (1, stop - start), 1) + start
    inside = (lane >= head * HEAD_DIM) & (lane < (head + 1) * HEAD_DIM)
    return slice(start, stop), inside


def soft_scores(left, right, allowed, axis):
    scores = times_transposed(left, right) * HEAD_DIM ** (-0.5)
    scores = jnp.where(allowed, scores, masked_score)
    exponent = jnp.exp(scores - jnp.max(scores, axis=axis, keepdims=True))
    return exponent * (1.0 / jnp.sum(exponent, axis=axis, keepdims=True))


def attend_kernel(
    query_ref, keys_ref, values_ref, column_ids, row_ids, x_ref, mod_ref,
    weight, turned_ref, branch_ref, middle_ref, second_ref, mixed,
):
    allowed = column_ids[...] == row_ids[...]
    for head in range(HEADS):
        lanes, inside = window(head)
        query = jnp.where(inside, query_ref[:, lanes], jnp.zeros((), bf16))
        probs = soft_scores(query, keys_ref[:, lanes], allowed, 1).astype(bf16)
        mixed[:, lanes] = jnp.where(inside, matmul(probs, values_ref[:, lanes]), mixed[:, lanes])
    attended = mixed[...].astype(bf16)
    turned_ref[...] = attended.T
    branch_ref[...] = matmul(attended, weight[0])
    for i in range(BLOCK // CHUNK):
        rows = slice(i * CHUNK, (i + 1) * CHUNK)
        mod = mod_ref.at[0]
        middle = x_ref[rows, :].astype(f32) + mod[i : i + 1, part(0)] * branch_ref[rows, :]
        middle_ref[rows, :] = middle
        normed, _ = normalize(middle)
        second_ref[rows, :] = (
            normed * (1.0 + mod[i : i + 1, part(2)]) + mod[i : i + 1, part(1)]
        ).astype(bf16)


def tile_copies(r, where, count, tile, pair, downs):
    place, mine, side = where
    t, j = tile
    column = mine ^ j
    rows, width = r["gate"].shape[0], r["hidden_w"].shape[1]
    sem = r["pair_sems"].at[t]
    copies = [
        pltpu.make_async_copy(
            r[name].at[:, take(column * width, width)], r["pair_w"].at[t, which, take(place * rows, rows)], sem
        )
        for which, name in enumerate(("gate", "up"))
    ]
    first = first_part(rows)
    for other in range(HALVES):
        for by in range(1, count):
            owner = (place + (count - by)) % count
            if j < 3:
                spans = [(pair[other][0].at[by - 1], 0, rows)]
            else:
                spans = [(pair[other][0].at[by - 1], 0, first), (pair[other][1].at[by - 1], first, rows - first)]
            for ref, start, size in spans:
                to = r["pair_w"].at[t, side ^ other, take(owner * rows + start, size)]
                copies.append(pltpu.make_async_copy(ref, to, sem))
    for copy in copies:
        copy.start()

    sem = r["down_sems"].at[t]
    target = r["down_w"].at[t]
    piece = width // PIECES

    @pl.when(column == place)
    def _():
        pltpu.make_async_copy(r["down"], target, sem).start()

    @pl.when(column != place)
    def _():
        by = jnp.maximum((place + count - column) % count, 1)
        for i, other, start, size, ref in placed(downs, piece):
            to = target.at[take(((mine ^ i) * HALVES + (side ^ other)) * piece + start, size)]
            pltpu.make_async_copy(ref.at[by - 1], to, sem).start()


def ffn_kernel(count, js, names, *refs):
    r = dict(zip(names, refs, strict=True))
    r["hidden_w"] = r["hidden"]
    first, last = js[0] == 0, js[-1] == COLUMNS - 1
    step = pl.program_id(0)
    tile = r["hidden"].shape[1]
    tokens = r["second"].shape[0]
    second, feed_back = r["second"], r["feed_back"]
    feed, second_back = r["feed"], r["second_back"]

    @pl.when(step == 0)
    def _():
        where = r["where"][0], r["where"][1], r["where"][2]
        for t, j in enumerate(js):
            pair = [
                [r[f"pair{j}_{other}_{i}"] for i in range(1 if j < 3 else 2)]
                for other in range(HALVES)
            ]
            tile_copies(r, where, count, (t, j), pair, [r[name] for name in names if name[:4] == "down" and name[5:].isdigit()])
        if first:
            r["turned"][...] = second[...].T
            for i in range(tokens // CHUNK):
                rows = slice(i * CHUNK, (i + 1) * CHUNK)
                upstream = r["cot"][rows, :].astype(f32) * r["factor"][0]
                feed_back[rows, :] = (upstream * r["mod"][i : i + 1, part(3)]).astype(bf16)

    pair_w, down_w = r["pair_w"].at[step], r["down_w"].at[step]
    wait_for(pair_w, r["pair_sems"].at[step])
    wait_for(down_w, r["down_sems"].at[step])
    sub = 256
    for n in range(tile // sub):
        lanes = slice(n * sub, (n + 1) * sub)
        gate = matmul(second[...], pair_w[0, :, lanes])
        upval = matmul(second[...], pair_w[1, :, lanes])
        hidden_back = times_transposed(feed_back[...], down_w[lanes, :])
        sigmoid = jax.nn.sigmoid(gate)
        silu = gate * sigmoid
        r["hidden"][:, lanes] = (silu * upval).astype(bf16)
        r["pair_back"][0, 1, :, lanes] = (hidden_back * silu).astype(bf16)
        r["pair_back"][0, 0, :, lanes] = (
            hidden_back * upval * (sigmoid * (1.0 + gate * (1.0 - sigmoid)))
        ).astype(bf16)

    r["hidden_turned"][0] = r["hidden"][...].T
    feed_part = matmul(r["hidden"][...], down_w[...])
    back_part = times_transposed(r["pair_back"][0, 0], pair_w[0]) + times_transposed(
        r["pair_back"][0, 1], pair_w[1]
    )

    @pl.when(step == 0)
    def _():
        feed[...] = feed_part if first else r["feed_in"][...] + feed_part
        second_back[...] = back_part if first else r["back_in"][...] + back_part

    @pl.when(step > 0)
    def _():
        feed[...] += feed_part
        second_back[...] += back_part

    if not last:
        return

    @pl.when(step == len(js) - 1)
    def _():
        for i in range(tokens // CHUNK):
            rows = slice(i * CHUNK, (i + 1) * CHUNK)
            gate_one = r["mod"][i : i + 1, part(0)]
            scale_two = r["mod"][i : i + 1, part(2)]
            gate_two = r["mod"][i : i + 1, part(3)]
            middle = r["middle"][rows, :]
            r["output"][rows, :] = (middle + gate_two * feed[rows, :]).astype(bf16)
            upstream = r["cot"][rows, :].astype(f32) * r["factor"][0]
            normed, inverse = normalize(middle)
            back = second_back[rows, :]
            middle_back = upstream + normalize_back(normed, inverse, back * (1.0 + scale_two))
            r["middle_back"][rows, :] = middle_back
            r["branch_back"][rows, :] = (middle_back * gate_one).astype(bf16)
            for where, values in enumerate(
                (middle_back * r["branch"][rows, :], back, back * normed, upstream * feed[rows, :])
            ):
                r["sums"][i : i + 1, part(where)] = jnp.sum(values, axis=0, keepdims=True)


ORDER = (1, 3, 2, 0)
SEND_X, KEEP_X, SEND_Y, KEEP_Y = (1, 3), (2, 0), (3, 2), (1, 0)
CUT = (SEND_X, KEEP_X, SEND_Y, KEEP_Y)


def put_grad(grad, other_ref, out_refs):
    step = pl.program_id(0)
    if other_ref is None:
        out_refs[0][0] = grad.astype(bf16)
        return
    total = (grad + other_ref[0].astype(f32)).astype(bf16)
    first = first_part(total.shape[1])
    for at, j in enumerate(ORDER):

        @pl.when(step == at)
        def _():
            for columns, ref in zip(CUT, out_refs, strict=True):
                if j in columns:
                    ref[0] = total[:, :first] if columns in (SEND_X, KEEP_X) else total[:, first:]


def cut_specs(count, rows, breadth):
    first = first_part(rows)
    shapes, specs = [], []
    for columns in CUT:
        size = first if columns in (SEND_X, KEEP_X) else rows - first
        shapes.append(struct((2, count, size, breadth), bf16))
        second = ORDER.index(columns[1])
        specs.append(
            pl.BlockSpec(
                (1, count, size, breadth),
                lambda s, where, second=second: (jnp.where(s >= second, 1, 0), 0, 0, 0),
            )
        )
    return tuple(shapes), tuple(specs)


def split_refs(mine, refs):
    return (refs[0], refs[1:]) if mine else (None, refs)


def pair_grad_kernel(mine, count, where_ref, turned_ref, own_ref, near_ref, far_ref, *refs):
    other_ref, out_refs = split_refs(mine, refs)
    for at, j in enumerate(ORDER):

        @pl.when(pl.program_id(0) == at)
        def _():
            back = {0: own_ref, 3: far_ref}.get(j, near_ref)
            grad = matmul(turned_ref[...], back[0, 0])
            put_grad(grad.reshape(count, grad.shape[0] // count, grad.shape[1]), other_ref, out_refs)


def down_grad_kernel(mine, where_ref, *refs):
    hiddens, feed_back_ref, out_ref = refs[:3], refs[3], refs[-1]
    other_ref = refs[4] if mine else None
    side = where_ref[2] if mine else where_ref[2] ^ 1
    count, _, rows, _ = out_ref.shape
    tiles = [(hidden, t) for hidden in hiddens for t in range(hidden.shape[0])]
    for j, (hidden, t) in enumerate(tiles):
        pieces = [hidden[t, take(((where_ref[1] ^ c) * HALVES + side) * rows, rows), :] for c in ORDER]
        grad = matmul(jnp.concatenate(pieces, axis=0), feed_back_ref[...]).reshape(COLUMNS, rows, WIDTH)
        owner = where_ref[1] ^ j
        if mine:
            grad = grad + other_ref[owner].astype(f32)
        out_ref[owner] = grad.astype(bf16)


def attn_grad_kernel(
    mine, where_ref, first_ref, attended_ref, joint_back_ref, branch_back_ref, *refs
):
    other_ref, out_refs = split_refs(mine, refs)
    column = where_ref[1] ^ where_ref[3 + pl.program_id(0)]
    side = where_ref[2] if mine else where_ref[2] ^ 1
    _, count, _, _ = out_refs[0].shape
    rows = WIDTH // count // HALVES

    def put(turned, right):
        taken = [turned[take((z * HALVES + side) * rows, rows), :] for z in range(count)]
        grad = matmul(jnp.concatenate(taken, axis=0), right[...])
        put_grad(grad.reshape(count, rows, WIDTH), other_ref, out_refs)

    @pl.when(column < 3)
    def _():
        put(first_ref, joint_back_ref)

    @pl.when(column == 3)
    def _():
        put(attended_ref, branch_back_ref)


def place_pair_kernel(where_ref, *refs):
    sources, outs = refs[:-2], refs[-2:]
    rows, tile = sources[0].shape
    for way in range(HALVES):

        @pl.when(where_ref[2] == way)
        def _():
            for j, other, start, size, ref in placed(sources, rows):
                lanes = take((where_ref[1] ^ j) * tile, tile)
                outs[way ^ other][start : start + size, lanes] = ref[...].astype(f32)


def place_down_kernel(rows, offset, where_ref, *refs):
    sources, out = refs[:-1], refs[-1]
    for j, other, start, size, ref in placed(sources, rows):
        piece = (where_ref[1] ^ j) * HALVES + (where_ref[2] ^ other)
        out[take(piece * rows + start, size), :] = ref[offset : offset + size, :].astype(f32)


def place_attn_kernel(rows, where_ref, *refs):
    sources, joint_ref, project_ref = refs[:-2], refs[-2], refs[-1]
    for column in range(COLUMNS):

        @pl.when(where_ref[1] == column)
        def _():
            for j, other, start, size, ref in placed(sources, rows):
                to = take((where_ref[2] ^ other) * rows + start, size)
                if column ^ j == 3:
                    project_ref[to, :] = ref[:size, :].astype(f32)
                else:
                    joint_ref[to, part(column ^ j)] = ref[:size, :].astype(f32)


def attend_back_kernel(
    query_ref, keys_ref, values_ref, branch_back_ref, column_ids, row_ids, cos_ref,
    sin_ref, weight, joint_back_ref, mixed_back, query_back, keys_back, values_back,
):
    mixed_back[...] = times_transposed(branch_back_ref[...], weight[0]).astype(bf16)
    allowed = column_ids[...] == row_ids[...]
    scaling = HEAD_DIM ** (-0.5)
    for head in range(HEADS):
        lanes, inside = window(head)
        zero = jnp.zeros((), bf16)
        query = jnp.where(inside, query_ref[:, lanes], zero)
        back = jnp.where(inside, mixed_back[:, lanes], zero)
        soft = soft_scores(keys_ref[:, lanes], query, allowed, 0)
        probs_back = times_transposed(values_ref[:, lanes], back)
        scores_back = (
            soft * (probs_back - jnp.sum(soft * probs_back, axis=0, keepdims=True))
        ).astype(bf16)
        query_back[:, lanes] = jnp.where(
            inside, contract_rows(scores_back, keys_ref[:, lanes]) * scaling, query_back[:, lanes]
        )
        keys_back[:, lanes] = jnp.where(
            inside, matmul(scores_back, query) * scaling, keys_back[:, lanes]
        )
        values_back[:, lanes] = jnp.where(
            inside, matmul(soft.astype(bf16), back), values_back[:, lanes]
        )

    @pl.loop(0, BLOCK // CHUNK)
    def _(i):
        rows = pl.ds(pl.multiple_of(i * CHUNK, CHUNK), CHUNK)
        cos, sin = cos_ref[rows, :], sin_ref[rows, :]
        joint_back_ref[rows, part(0)] = rotate(query_back[rows, :], cos, -sin).astype(bf16)
        joint_back_ref[rows, part(1)] = rotate(keys_back[rows, :], cos, -sin).astype(bf16)
        joint_back_ref[rows, part(2)] = values_back[rows, :].astype(bf16)


def first_back_kernel(
    joint_back_ref, x_ref, middle_back_ref, mod_ref, weight, grad_ref, sums_ref, first_back
):
    step = pl.program_id(0)
    product = times_transposed(joint_back_ref[...], weight[0])

    @pl.when(step == 0)
    def _():
        first_back[...] = product

    @pl.when(step > 0)
    def _():
        first_back[...] += product

    @pl.when(step == pl.num_programs(0) - 1)
    def _():
        finish_first_back(x_ref, middle_back_ref, mod_ref, grad_ref, sums_ref, first_back)


def finish_first_back(x_ref, middle_back_ref, mod_ref, grad_ref, sums_ref, first_back):
    for i in range(x_ref.shape[0] // CHUNK):
        rows = slice(i * CHUNK, (i + 1) * CHUNK)
        normed, inverse = normalize(x_ref[rows, :].astype(f32))
        back = first_back[rows, :]
        grad_ref[rows, :] = middle_back_ref[rows, :] + normalize_back(
            normed, inverse, back * (1.0 + mod_ref[i : i + 1, part(1)])
        )
        sums_ref[i : i + 1, part(0)] = jnp.sum(back, axis=0, keepdims=True)
        sums_ref[i : i + 1, part(1)] = jnp.sum(back * normed, axis=0, keepdims=True)


SMEM = pl.BlockSpec(memory_space=pltpu.SMEM)
VMEM = pl.BlockSpec(memory_space=pltpu.VMEM)
ANY = pl.BlockSpec(memory_space=pl.ANY)


def struct(shape, dtype):
    return jax.ShapeDtypeStruct(shape, dtype)


def params(mega=56):
    return pltpu.CompilerParams(vmem_limit_bytes=mega * MEGA)


def cost(microseconds):
    return pl.CostEstimate(flops=int(microseconds * 1e9), bytes_accessed=1000, transcendentals=0)


def by_block(*shape):
    return pl.BlockSpec(shape, lambda b: (b,) + (0,) * (len(shape) - 1))


def whole(*shape):
    return pl.BlockSpec(shape, lambda *_: (0,) * len(shape))


def first_call(where, x, mod, cos, sin, joint, project, arrived):
    tokens = x.shape[0]
    count = arrived[0].shape[0] + 1
    shape = struct((tokens, WIDTH), bf16)
    return pl.pallas_call(
        functools.partial(first_kernel, count),
        out_shape=(struct((WIDTH, tokens), bf16),)
        + (shape,) * 3
        + (struct((COLUMNS, WIDTH, WIDTH), bf16),),
        in_specs=[SMEM, VMEM, VMEM, VMEM, VMEM] + [ANY] * (2 + len(arrived)),
        out_specs=(VMEM,) * 4 + (ANY,),
        scratch_shapes=[
            pltpu.VMEM((COLUMNS, WIDTH, WIDTH), bf16),
            pltpu.VMEM((tokens, WIDTH), bf16),
            pltpu.VMEM((tokens, WIDTH), f32),
            pltpu.SemaphoreType.DMA((COLUMNS,)),
        ],
        compiler_params=params(),
        cost_estimate=cost(20),
    )(where, x, mod, cos, sin, joint, project, *arrived)


def attend_call(query, keys, values, ids, x, mod, weight):
    tokens = x.shape[0]
    return pl.pallas_call(
        attend_kernel,
        grid=(tokens // BLOCK,),
        out_shape=(
            struct((WIDTH, tokens), bf16),
            struct((tokens, WIDTH), f32),
            struct((tokens, WIDTH), f32),
            struct((tokens, WIDTH), bf16),
        ),
        in_specs=[by_block(BLOCK, WIDTH)] * 3
        + [by_block(BLOCK, 1), pl.BlockSpec((1, BLOCK), lambda b: (0, b)), by_block(BLOCK, WIDTH)]
        + [by_block(1, BLOCK // CHUNK, 4 * WIDTH), pl.BlockSpec((1, WIDTH, WIDTH), lambda b: (3, 0, 0))],
        out_specs=(pl.BlockSpec((WIDTH, BLOCK), lambda b: (0, b)),) + (by_block(BLOCK, WIDTH),) * 3,
        scratch_shapes=[pltpu.VMEM((BLOCK, WIDTH), f32)],
        compiler_params=params(),
        cost_estimate=cost(2),
    )(
        query, keys, values, ids[:, None], ids[None, :], x,
        mod.reshape(tokens // BLOCK, BLOCK // CHUNK, 4 * WIDTH), weight,
    )


def ffn_call(js, where, given, shards, pairs, downs):
    second = given["second"]
    tokens = second.shape[0]
    ff = shards["gate"].shape[1]
    tile = ff // COLUMNS
    count = ff // shards["down"].shape[0]
    chunks = tokens // CHUNK
    first, last = js[0] == 0, js[-1] == COLUMNS - 1
    full = whole(tokens, WIDTH)
    wide = struct((tokens, WIDTH), f32)
    narrow = struct((tokens, WIDTH), bf16)
    inputs = [("where", where, SMEM), ("second", second, full)]
    if first or last:
        inputs += [
            ("factor", given["factor"], SMEM),
            ("cot", given["cot"], full),
            ("mod", given["mod"], whole(chunks, 4 * WIDTH)),
        ]
    if not first:
        inputs += [
            ("feed_back", given["feed_back"], full),
            ("feed_in", given["feed"], full),
            ("back_in", given["second_back"], full),
        ]
    if last:
        inputs += [("middle", given["middle"], full), ("branch", given["branch"], full)]
    inputs += [(name, shards[name], ANY) for name in ("gate", "up", "down")]
    for j in js:
        for other in range(HALVES):
            inputs += [(f"pair{j}_{other}_{i}", a, ANY) for i, a in enumerate(pairs[other][j])]
    inputs += [(f"down_{i}", a, ANY) for i, a in enumerate(downs)]
    outputs = [
        (
            "hidden_turned",
            struct((len(js), tile, tokens), bf16),
            pl.BlockSpec((1, tile, tokens), lambda t: (t, 0, 0)),
        ),
        (
            "pair_back",
            struct((len(js), HALVES, tokens, tile), bf16),
            pl.BlockSpec((1, HALVES, tokens, tile), lambda t: (t, 0, 0, 0)),
        ),
    ]
    if first:
        outputs += [
            ("turned", struct((WIDTH, tokens), bf16), whole(WIDTH, tokens)),
            ("feed_back", narrow, full),
        ]
    sums = ("feed", "second_back")
    scratch = [
        ("pair_w", pltpu.VMEM((len(js), HALVES, WIDTH, tile), bf16)),
        ("down_w", pltpu.VMEM((len(js), ff // count, WIDTH), bf16)),
        ("hidden", pltpu.VMEM((tokens, tile), bf16)),
        ("pair_sems", pltpu.SemaphoreType.DMA((len(js),))),
        ("down_sems", pltpu.SemaphoreType.DMA((len(js),))),
    ]
    if last:
        outputs += [
            ("output", narrow, full),
            ("middle_back", wide, full),
            ("branch_back", narrow, full),
            ("sums", struct((chunks, 4 * WIDTH), f32), whole(chunks, 4 * WIDTH)),
        ]
        scratch += [(name, pltpu.VMEM((tokens, WIDTH), f32)) for name in sums]
    else:
        outputs += [(name, wide, full) for name in sums]
    names = [each[0] for each in inputs + outputs + scratch]
    found = pl.pallas_call(
        functools.partial(ffn_kernel, count, js, names),
        grid=(len(js),),
        out_shape=tuple(shape for _, shape, _ in outputs),
        in_specs=[spec for _, _, spec in inputs],
        out_specs=tuple(spec for _, _, spec in outputs),
        scratch_shapes=[shape for _, shape in scratch],
        compiler_params=params(),
        cost_estimate=cost(2 if first else 12 * len(js)),
    )(*[array for _, array, _ in inputs])
    return {name: array for (name, _, _), array in zip(outputs, found, strict=True)}


def by_column(call, count, rows, breadth, in_specs, where, arrays, other):
    shapes, specs = cut_specs(count, rows, breadth)
    block = pl.BlockSpec((1, count, rows, breadth), lambda s, where: (s, 0, 0, 0))
    if other is None:
        shapes, specs = (struct((COLUMNS, count, rows, breadth), bf16),), (block,)
    else:
        in_specs, arrays = in_specs + [block], arrays + (other,)
    found = pl.pallas_call(
        call,
        out_shape=shapes,
        grid_spec=pltpu.PrefetchScalarGridSpec(
            num_scalar_prefetch=1, grid=(COLUMNS,), in_specs=in_specs, out_specs=specs
        ),
        compiler_params=params(),
        cost_estimate=cost(3),
    )(where, *arrays)
    return found[0] if other is None else found


def pair_grad_call(count, where, turned, backs, other=None):
    tokens, tile = backs[0].shape[2:]
    mine = other is not None

    def spec(tile_of):
        return pl.BlockSpec(
            (1, 1, tokens, tile),
            lambda s, where: (tile_of(where[3 + s]), where[2] if mine else where[2] ^ 1, 0, 0),
        )

    return by_column(
        functools.partial(pair_grad_kernel, mine, count),
        count, WIDTH // count, tile,
        [whole(WIDTH, tokens), spec(lambda j: 0), spec(lambda j: jnp.clip(j - 1, 0, 1)), spec(lambda j: 0)],
        where, (turned,) + tuple(backs), other,
    )


def attn_grad_call(count, where, first, attended, joint_back, branch_back, other=None):
    tokens = first.shape[1]
    return by_column(
        functools.partial(attn_grad_kernel, other is not None),
        count, WIDTH // count // HALVES, WIDTH,
        [
            whole(WIDTH, tokens),
            whole(WIDTH, tokens),
            pl.BlockSpec((tokens, WIDTH), lambda s, where: (0, jnp.minimum(where[1] ^ where[3 + s], 2))),
            whole(tokens, WIDTH),
        ],
        where, (first, attended, joint_back, branch_back), other,
    )


def down_grad_call(count, where, hiddens, feed_back, other=None):
    ff = sum(h.shape[0] * h.shape[1] for h in hiddens)
    out = struct((count, COLUMNS, ff // count // PIECES, WIDTH), bf16)
    arrays = tuple(hiddens) + (feed_back,) + (() if other is None else (other,))
    return pl.pallas_call(
        functools.partial(down_grad_kernel, other is not None),
        out_shape=out,
        in_specs=[SMEM] + [VMEM] * len(arrays),
        out_specs=VMEM,
        compiler_params=params(),
        cost_estimate=cost(3),
    )(where, *arrays)


def place_call(kernel, where, arrays, outs):
    return pl.pallas_call(
        kernel,
        out_shape=outs,
        in_specs=[SMEM] + [VMEM] * len(arrays),
        out_specs=jax.tree.map(lambda _: VMEM, outs),
        compiler_params=params(),
        cost_estimate=cost(4),
    )(where, *arrays)


def attend_back_call(query, keys, values, branch_back, ids, cos, sin, weight):
    tokens = query.shape[0]
    block = by_block(BLOCK, WIDTH)
    return pl.pallas_call(
        attend_back_kernel,
        grid=(tokens // BLOCK,),
        out_shape=struct((tokens, 3 * WIDTH), bf16),
        in_specs=[block, block, block, block]
        + [by_block(BLOCK, 1), pl.BlockSpec((1, BLOCK), lambda b: (0, b)), block, block]
        + [pl.BlockSpec((1, WIDTH, WIDTH), lambda b: (3, 0, 0))],
        out_specs=by_block(BLOCK, 3 * WIDTH),
        scratch_shapes=[
            pltpu.VMEM((BLOCK, WIDTH), bf16),
            pltpu.VMEM((BLOCK, WIDTH), f32),
            pltpu.VMEM((BLOCK, WIDTH), f32),
            pltpu.VMEM((BLOCK, WIDTH), f32),
        ],
        compiler_params=params(),
        cost_estimate=cost(8),
    )(query, keys, values, branch_back, ids[:, None], ids[None, :], cos, sin, weight)


def first_back_call(joint_back, x, middle_back, mod, weight):
    tokens = x.shape[0]
    chunks = tokens // CHUNK
    full = whole(tokens, WIDTH)
    return pl.pallas_call(
        first_back_kernel,
        grid=(3,),
        out_shape=(struct((tokens, WIDTH), f32), struct((chunks, 2 * WIDTH), f32)),
        in_specs=[
            pl.BlockSpec((tokens, WIDTH), lambda c: (0, c)),
            full,
            full,
            whole(chunks, 2 * WIDTH),
            pl.BlockSpec((1, WIDTH, WIDTH), lambda c: (c, 0, 0)),
        ],
        out_specs=(full, whole(chunks, 2 * WIDTH)),
        scratch_shapes=[pltpu.VMEM((tokens, WIDTH), f32)],
        compiler_params=params(),
        cost_estimate=cost(2),
    )(joint_back, x, middle_back, mod, weight)


def shifts(count, by):
    return [(i, (i + by) % count) for i in range(count)]


def pick(array, index):
    return lax.dynamic_index_in_dim(array, index, 0, keepdims=False)


def across(bit):
    return [(i, i ^ bit) for i in range(PIECES)]


def swap(array, bit):
    return lax.ppermute(array, "bucket", across(bit))


def after(arrays, *others):
    return lax.optimization_barrier((arrays, others))[0]


def add(left, right):
    return (left.astype(f32) + right.astype(f32)).astype(bf16)


def over_z(piece):
    count = lax.axis_size("fsdp")
    return [lax.ppermute(piece, "fsdp", shifts(count, by)) for by in range(1, count)]


def gather_z(piece, *others):
    count = lax.axis_size("fsdp")
    place = lax.axis_index("fsdp")
    full = after(lax.all_gather(piece, "fsdp", axis=0, tiled=False), *others)
    return jnp.stack([pick(full, (place + count - by) % count) for by in range(1, count)])


def cross(by_x, by_y, first):
    if first is not None:
        by_x, by_y = by_x[..., :first, :], by_y[..., first:, :]
    return swap(by_x, 4), swap(by_y, 2)


def both(here):
    return here + tuple(None if array is None else swap(array, 1) for array in here)


def direct(piece):
    return piece, swap(piece, 2), swap(piece, 4), swap(piece, 6)


def spread_whole(pieces):
    first = first_part(pieces.shape[1])

    def of(side):
        own, by_x, by_y, far = (pieces[c * HALVES + side] for c in range(COLUMNS))
        return own, by_x, by_y, far[:first], far[first:]

    return of(0) + of(1)


def halve_once(cut):
    send_x, (a2, a0), send_y, (b1, b0) = cut
    from_x, from_y = swap(send_x, 2), swap(send_y, 4)
    return add(a0, from_x[0]), add(a2, from_x[1]), add(b0, from_y[1]), add(b1, from_y[0])


def halve_twice(once, *others):
    a0, a2, b0, b1 = once
    if others:
        a0, b0 = after((a0, b0), *others)
    return jnp.concatenate([add(a0, swap(a2, 4)), add(b0, swap(b1, 2))], axis=-2)


def send_z(parts):
    count = lax.axis_size("fsdp")
    place = lax.axis_index("fsdp")
    return [
        lax.ppermute(pick(parts, (place + by) % count), "fsdp", shifts(count, by))
        for by in range(1, count)
    ]


def total_z(parts, others):
    total = pick(parts, lax.axis_index("fsdp")).astype(f32)
    for array in others:
        total = total + array.astype(f32)
    return total.astype(bf16)


def sum_z(parts):
    return total_z(parts, send_z(parts))


def cut_down(part, first):
    cut = []
    for columns in CUT:
        both_columns = jnp.stack([part[ORDER.index(j)] for j in columns])
        cut.append(both_columns[:, :first] if columns in (SEND_X, KEEP_X) else both_columns[:, first:])
    return cut


def uncut(cut):
    def of(j, pair):
        columns = next(c for c in pair if j in c)
        return cut[CUT.index(columns)][columns.index(j)]

    return jnp.stack(
        [jnp.concatenate([of(j, (SEND_X, KEEP_X)), of(j, (SEND_Y, KEEP_Y))], axis=1) for j in ORDER]
    )


def sum_whole(mine, theirs):
    parts = jnp.stack([mine, theirs], axis=1)
    parts = jnp.stack([parts[ORDER.index(c)] for c in range(COLUMNS)])
    rows, breadth = mine.shape[2:]
    parts = lax.psum(parts, "bucket").transpose(2, 0, 1, 3, 4)
    return spread_whole(sum_z(parts).reshape(PIECES, rows, breadth))


def arrived_whole(pieces):
    count = lax.axis_size("fsdp")
    place = lax.axis_index("fsdp")
    first = first_part(pieces.shape[1])
    full = lax.all_gather(pieces, "fsdp", axis=0, tiled=False)
    full = jnp.stack([pick(full, (place + count - by) % count) for by in range(1, count)])

    def of(side):
        own, by_x, by_y, far = (full[:, c * HALVES + side] for c in range(COLUMNS))
        return own, by_x, by_y, far[:, :first], far[:, first:]

    return of(0) + of(1)


def to_group(rows, count, place):
    relative = jnp.stack(
        [pick(rows, place)]
        + [
            lax.ppermute(pick(rows, (place + by) % count), "fsdp", shifts(count, by))
            for by in range(1, count)
        ]
    )
    return jnp.stack([pick(relative, (place - j) % count) for j in range(count)])


def on_device(
    inputs,
    condition,
    segment_ids,
    grid_widths,
    bucket_counts,
    modulate_weight,
    joint_weight,
    project_weight,
    gate_weight,
    up_weight,
    down_weight,
    cotangent,
):
    fsdp_count = lax.axis_size("fsdp")
    place = lax.axis_index("fsdp")
    bucket = lax.axis_index("bucket")
    height = joint_weight.shape[0]
    half = height // HALVES
    ff = gate_weight.shape[1]
    tile = ff // COLUMNS
    down_rows = down_weight.shape[0] // PIECES
    slots = condition.shape[0]

    cond_float = condition.astype(f32)
    lifted = jax.nn.silu(cond_float).astype(bf16)
    lifted_rows = to_group(
        lifted.reshape(slots, fsdp_count, height).transpose(1, 0, 2), fsdp_count, place
    ).reshape(fsdp_count * slots, height)
    one_hot = (
        segment_ids[::CHUNK, None] == jnp.arange(slots, dtype=jnp.int32)[None, :]
    ).astype(f32)

    def modulation_parts(weight, rows):
        parts = matmul(rows, weight).reshape(fsdp_count, slots, weight.shape[1])
        return [pick(parts, place)] + [
            lax.ppermute(pick(parts, (place + by) % fsdp_count), "fsdp", shifts(fsdp_count, by))
            for by in range(1, fsdp_count)
        ]

    def modulation(parts):
        return jnp.dot(
            one_hot,
            sum(parts[1:], parts[0]),
            precision=lax.Precision.HIGHEST,
            preferred_element_type=f32,
        )

    first_rows = modulation_parts(modulate_weight[:, : 2 * WIDTH], lifted_rows)
    mod_one = modulation(first_rows)
    fast = lax.axis_size("bucket") == PIECES
    if fast:
        column, side = bucket // HALVES, bucket % HALVES
        where = jnp.stack([place, column, side] + [jnp.int32(j) for j in ORDER])
        attn_piece = jnp.where(
            column == 3,
            lax.dynamic_slice(project_weight, (side * half, 0), (half, WIDTH)),
            lax.dynamic_slice(joint_weight, (side * half, column * WIDTH), (half, WIDTH)),
        )
        ffn_piece = jnp.where(
            side == 0,
            lax.dynamic_slice(gate_weight, (0, column * tile), (height, tile)),
            lax.dynamic_slice(up_weight, (0, column * tile), (height, tile)),
        )
        down_piece = lax.dynamic_slice_in_dim(down_weight, bucket * down_rows, down_rows, 0)
        attn_z = gather_z(attn_piece, first_rows)
        down_k = over_z(after(down_piece, attn_z))
        attn_x, attn_y = swap(attn_z, 2), swap(attn_z, 4)
        attn_x, attn_y, down_k = after((attn_x, attn_y, down_k))
        attn_far = cross(attn_x, attn_y, first_part(half))
        pair_z = gather_z(after(ffn_piece, down_k))
        down_z = jnp.stack(down_k)
        attn_arrived = both((attn_z, attn_x, attn_y) + attn_far)
        inputs, down_z = after((inputs, down_z), attn_far)
        down_x, down_y = swap(down_z, 2), swap(down_z, 4)
        inputs = after(inputs, down_z)
    else:
        where = jnp.stack([place, 0 * place, 0 * place] + [jnp.int32(j) for j in ORDER])
        attn_arrived = arrived_whole(
            jnp.concatenate([joint_weight, project_weight], axis=1)
            .reshape(HALVES, half, COLUMNS, WIDTH)
            .transpose(2, 0, 1, 3)
            .reshape(PIECES, half, WIDTH)
        )
        pairs = arrived_whole(
            jnp.stack([gate_weight, up_weight])
            .reshape(HALVES, height, COLUMNS, tile)
            .transpose(2, 0, 1, 3)
            .reshape(PIECES, height, tile)
        )
        downs = arrived_whole(down_weight.reshape(PIECES, down_rows, WIDTH))

    if fast:
        lifted_rows = after(lifted_rows, down_k)
    late_rows = modulation_parts(modulate_weight[:, 2 * WIDTH :], lifted_rows)
    counts = bucket_counts.astype(f32)
    mine = jnp.sum(jnp.where(jnp.arange(counts.shape[0], dtype=jnp.int32) == bucket, counts, 0.0))
    factor = (mine * counts.shape[0] / jnp.sum(counts)).reshape(1)
    cos, sin = rope_tables(segment_ids, grid_widths)

    first, query, keys, values, weight = first_call(
        where, inputs, mod_one, cos, sin, joint_weight, project_weight, attn_arrived
    )
    if fast:
        late_rows = [late_rows[0], *after(late_rows[1:], query)]
        down_x, down_y = after((down_x, down_y), query)
        down_far = cross(down_x, down_y, first_part(down_rows))
        downs = (down_z, down_x, down_y) + down_far
        pair_z = after(pair_z, query)
        pair_x, pair_y = swap(pair_z, 2), swap(pair_z, 4)
    mod = modulation(late_rows)
    attended, branch, middle, second = attend_call(
        query, keys, values, segment_ids, inputs, mod, weight
    )
    shards = dict(gate=gate_weight, up=up_weight, down=down_weight)
    given = dict(
        second=second, factor=factor, cot=cotangent, mod=mod, middle=middle, branch=branch
    )
    if fast:
        downs = both(after(downs, second))
        pairs = (pair_z, pair_x, pair_y, None, None, swap(pair_z, 1), None, None, None, None)
    pairs = [
        [[group] for group in pairs[5 * k : 5 * k + 3]] + [list(pairs[5 * k + 3 : 5 * k + 5])]
        for k in range(HALVES)
    ]
    found = ffn_call((0,), where, given, shards, pairs, downs)
    turned, feed_back = found["turned"], found["feed_back"]
    steps = [found]
    if fast:
        pair_x, pair_y = after((pair_x, pair_y), feed_back)
        far = cross(pair_x, pair_y, first_part(height))
        pairs[1][1:3] = [swap(pair_x, 1)], [swap(pair_y, 1)]
    for js in ((1, 2), (3,)):
        given.update(feed_back=feed_back, feed=found["feed"], second_back=found["second_back"])
        if fast and js == (3,):
            far = after(far, found["feed"])
            pairs[0][3], pairs[1][3] = list(far), [swap(array, 1) for array in far]
        found = ffn_call(js, where, given, shards, pairs, downs)
        steps.append(found)
    output, middle_back, branch_back = found["output"], found["middle_back"], found["branch_back"]
    late_sums = found["sums"]

    def by_slot(chunk_sums):
        return lax.dot_general(
            one_hot,
            chunk_sums,
            (((0,), (0,)), ((), ())),
            precision=lax.Precision.HIGHEST,
            preferred_element_type=f32,
        ).astype(bf16)

    late = lax.all_gather(
        jnp.concatenate([by_slot(late_sums), lifted], axis=1), ("bucket", "fsdp"), axis=0, tiled=True
    )

    count = fsdp_count
    hiddens = [step["hidden_turned"] for step in steps]
    backs = [step["pair_back"] for step in steps]
    pair_theirs = pair_grad_call(count, where, turned, backs)
    if fast:
        pair_other = swap(pair_theirs, 1)
        feed_back = after(feed_back, pair_theirs)
    else:
        pair_other = jnp.zeros_like(pair_theirs)
    down_theirs = down_grad_call(count, where, hiddens, feed_back)
    if fast:
        pair_other, down_theirs = after((pair_other, down_theirs))
        down_other = swap(down_theirs, 1)
    else:
        down_other = jnp.zeros_like(down_theirs)
    pair_cut = pair_grad_call(count, where, turned, backs, pair_other)
    if fast:
        feed_back = after(feed_back, pair_cut)
    down_mine = down_grad_call(count, where, hiddens, feed_back, down_other)
    if fast:
        down_mine, late = after((down_mine, late))
        down_part = lax.psum_scatter(down_mine, "fsdp", scatter_dimension=0, tiled=False)
        branch_back = after(branch_back, down_mine)
    joint_back = attend_back_call(
        query, keys, values, branch_back, segment_ids, cos, sin, weight
    )
    attn_theirs = attn_grad_call(count, where, first, attended, joint_back, branch_back)
    if fast:
        send_x, keep_x, send_y, keep_y = pair_cut
        keep_x, keep_y, attn_theirs = after((keep_x, keep_y, attn_theirs))
        pair_once = halve_once((send_x, keep_x, send_y, keep_y))
        pair_once, attn_theirs, middle_back = after((pair_once, attn_theirs, middle_back))
        attn_other = swap(attn_theirs, 1)
    grad_inputs, early_sums = first_back_call(joint_back, inputs, middle_back, mod_one, weight)
    if fast:
        a0, a2, b0, b1 = pair_once
        a0, b0, grad_inputs = after((a0, b0, grad_inputs))
        pair_parts, branch_back = after((halve_twice((a0, a2, b0, b1)), branch_back))
        pair_z = send_z(pair_parts)
        attn_cut = attn_grad_call(
            count, where, first, attended, joint_back, branch_back, attn_other
        )
        attn_cut, down_part = after((attn_cut, down_part))
        down_cut = cut_down(down_part, first_part(down_rows))
        cut = [
            jnp.concatenate([attn.reshape(2, -1, WIDTH), down], axis=1)
            for attn, down in zip(attn_cut, down_cut, strict=True)
        ]
        once, pair_z = after((halve_once(cut), pair_z))
        pair_sum = total_z(pair_parts, pair_z)
        pair_x, pair_y = swap(pair_sum, 2), swap(pair_sum, 4)
        a0, a2, b0, b1 = once
        ahead, behind = add(a0, swap(a2, 4)), add(b0, swap(b1, 2))
        at, other_at = (part.shape[1] * part.shape[2] for part in (attn_cut[0], attn_cut[2]))
        attn_parts = jnp.concatenate(
            [half.reshape(count, -1, WIDTH) for half in (ahead[:at], behind[:other_at])], axis=1
        )
        down_total = jnp.concatenate([ahead[at:], behind[other_at:]], axis=0)
        attn_parts, down_total, pair_x, pair_y = after((attn_parts, down_total, pair_x, pair_y))
        attn_z = send_z(attn_parts)
        pair_sums = (pair_sum, pair_x, pair_y) + cross(pair_x, pair_y, first_part(height))
        attn_z, pair_sums = after((attn_z, both(pair_sums)))
        attn_sum = total_z(attn_parts, attn_z)
    else:
        down_sums = sum_whole(down_mine.swapaxes(0, 1), down_theirs.swapaxes(0, 1))
        pair_sums = sum_whole(uncut(pair_cut), pair_theirs)
        attn_cut = attn_grad_call(
            count, where, first, attended, joint_back, branch_back, jnp.zeros_like(attn_theirs)
        )
        attn_sums = sum_whole(uncut(attn_cut), attn_theirs)
    early = lax.all_gather(by_slot(early_sums), ("bucket", "fsdp"), axis=0, tiled=True)
    if fast:
        early, attn_sum = after((early, attn_sum))
        both_sums = direct(jnp.concatenate([attn_sum, down_total], axis=0))
    all_back = jnp.concatenate([early, late[:, : 4 * WIDTH]], axis=1)
    all_lifted = lax.dynamic_slice_in_dim(late, 4 * WIDTH + place * height, height, 1)
    modulate_gradient = contract_rows(all_lifted, all_back)
    group_back = lax.dynamic_slice_in_dim(
        all_back, bucket * fsdp_count * slots, fsdp_count * slots, 0
    )
    slope_rows = times_transposed(group_back, modulate_weight)
    pair_grad = place_call(
        place_pair_kernel, where, pair_sums, (struct(gate_weight.shape, f32),) * 2
    )
    if fast:
        both_sums, pair_grad, modulate_gradient, slope_rows = after(
            (both_sums, pair_grad, modulate_gradient, slope_rows)
        )
        attn_sums = down_sums = both(both_sums)
    condition_slope = (
        to_group(slope_rows.reshape(fsdp_count, slots, height), fsdp_count, place)
        .transpose(1, 0, 2)
        .reshape(slots, WIDTH)
    )
    grad_condition = condition_slope * silu_slope(cond_float)
    down_grad = place_call(functools.partial(place_down_kernel, down_rows, half if fast else 0), where, down_sums, struct(down_weight.shape, f32))
    attn_grad = place_call(
        functools.partial(place_attn_kernel, half),
        where,
        attn_sums,
        (struct(joint_weight.shape, f32), struct(project_weight.shape, f32)),
    )

    return (
        output,
        grad_inputs,
        grad_condition,
        modulate_gradient,
        *attn_grad,
        *pair_grad,
        down_grad,
    )


def solution(mesh):
    spread = P(("bucket", "fsdp"), None)
    rows = P("fsdp", None)
    in_specs = (
        spread, spread, P(("bucket", "fsdp")), P(("bucket", "fsdp")), P(),
        rows, rows, rows, rows, rows, rows, spread,
    )
    out_specs = (spread, spread, spread, rows, rows, rows, rows, rows, rows)
    return jax.shard_map(
        on_device, mesh=mesh, in_specs=in_specs, out_specs=out_specs, check_vma=False
    )
```

```python
import functools

import jax
import jax.numpy as jnp
from jax import lax
from jax.experimental import pallas as pl
from jax.experimental.pallas import tpu as pltpu
from jax.sharding import PartitionSpec as P

HEADS = 16
HEAD_DIM = 72
WIDTH = HEADS * HEAD_DIM
QUARTER = HEAD_DIM // 4
BLOCK = 256
CHUNK = 64
COLUMNS = 4
HALVES = 2
PIECES = COLUMNS * HALVES
LANES = 128

epsilon = 1e-06
masked_score = -1e30
f32 = jnp.float32
bf16 = jnp.bfloat16
MEGA = 2**20


def normalize(values):
    average = jnp.mean(values, axis=-1, keepdims=True)
    centered = values - average
    inverse = lax.rsqrt(jnp.mean(centered * centered, axis=-1, keepdims=True) + epsilon)
    return (centered * inverse, inverse)


def normalize_back(normed, inverse, upstream):
    return inverse * (
        upstream
        - jnp.mean(upstream, axis=-1, keepdims=True)
        - normed * jnp.mean(upstream * normed, axis=-1, keepdims=True)
    )


def matmul(left, right):
    return jnp.dot(left, right, preferred_element_type=f32)


def contract_rows(left, right):
    return lax.dot_general(left, right, (((0,), (0,)), ((), ())), preferred_element_type=f32)


def times_transposed(left, right):
    return lax.dot_general(left, right, (((1,), (1,)), ((), ())), preferred_element_type=f32)


def silu_slope(values):
    sigmoid = jax.nn.sigmoid(values)
    return sigmoid * (1.0 + values * (1.0 - sigmoid))


def rope_tables(segments, widths):
    slots = widths.shape[0]
    one_hot = (segments[:, None] == jnp.arange(slots, dtype=jnp.int32)[None, :]).astype(jnp.int32)
    counts = jnp.sum(one_hot, axis=0)
    starts = jnp.cumsum(counts) - counts
    start_token = jnp.sum(one_hot * starts[None, :], axis=1)
    width_token = jnp.maximum(jnp.sum(one_hot * widths[None, :], axis=1), 1)
    place = jnp.arange(segments.shape[0], dtype=jnp.int32) - start_token
    row_place = (place // width_token).astype(f32)
    col_place = (place % width_token).astype(f32)
    freqs = 10000.0 ** (-jnp.arange(QUARTER, dtype=f32) / QUARTER)
    angle_row = row_place[:, None] * freqs[None, :]
    angle_col = col_place[:, None] * freqs[None, :]
    cos_row, sin_row, cos_col, sin_col = (
        jnp.cos(angle_row),
        jnp.sin(angle_row),
        jnp.cos(angle_col),
        jnp.sin(angle_col),
    )
    cos = jnp.concatenate([cos_row, cos_row, cos_col, cos_col], axis=1)
    sin = jnp.concatenate([-sin_row, sin_row, -sin_col, sin_col], axis=1)
    return jnp.tile(cos, (1, HEADS)), jnp.tile(sin, (1, HEADS))


def part(index):
    return slice(index * WIDTH, (index + 1) * WIDTH)


def rotate(values, cos, sin):
    lane = lax.broadcasted_iota(jnp.int32, (1, WIDTH), 1)
    leading = lane % (2 * QUARTER) < QUARTER
    partner = jnp.where(
        leading,
        pltpu.roll(values, WIDTH - QUARTER, 1),
        pltpu.roll(values, QUARTER, 1),
    )
    return values * cos + partner * sin


def take(start, size):
    return pl.ds(pl.multiple_of(start, 128 if size % 128 == 0 else 16), size)


def first_part(rows):
    return -(-rows // 32) * 16


def placed(refs, rows):
    first = first_part(rows)
    each = len(refs) // HALVES
    for other in range(HALVES):
        here = refs[each * other : each * other + each]
        for j in range(3):
            yield j, other, 0, rows, here[j]
        if each == COLUMNS:
            yield 3, other, 0, rows, here[3]
        else:
            yield 3, other, 0, first, here[3]
            yield 3, other, first, rows - first, here[4]


def piece_copies(where, count, sources, target, rows, sem):
    place, column, side = where
    copies = []
    for j, other, start, size, ref in placed(sources, rows):
        for by in range(1, count):
            owner = (place + (count - by)) % count
            to = target(column ^ j, side ^ other, owner, start, size)
            copies.append(pltpu.make_async_copy(ref.at[by - 1], to, sem(column ^ j, side ^ other, owner)))
    return copies


def wait_for(ref, sem):
    pltpu.make_async_copy(ref, ref, sem).wait()


def first_kernel(
    count, where_ref, x_ref, mod_ref, cos_ref, sin_ref, joint_ref, project_ref, *refs
):
    sources, refs = refs[:-9], refs[-9:]
    turned_ref, query_ref, keys_ref, values_ref, weight_ref, weight, first_ref, total, sems = refs
    where = where_ref[0], where_ref[1], where_ref[2]
    rows_in = joint_ref.shape[0]
    half = rows_in // HALVES

    def target(column, side, place, start, size):
        return weight.at[column, take(place * rows_in + side * half + start, size)]

    copies = piece_copies(where, count, sources, target, half, lambda c, s, z: sems.at[c])
    for c in range(COLUMNS):
        shard = project_ref if c == 3 else joint_ref.at[:, pl.ds(c * WIDTH, WIDTH)]
        copies.append(pltpu.make_async_copy(shard, weight.at[c, take(where[0] * rows_in, rows_in)], sems.at[c]))
    for copy in copies:
        copy.start()
    tokens = x_ref.shape[0]
    for i in range(tokens // CHUNK):
        rows = slice(i * CHUNK, (i + 1) * CHUNK)
        normed, _ = normalize(x_ref[rows, :].astype(f32))
        first_ref[rows, :] = (
            normed * (1.0 + mod_ref[i : i + 1, part(1)]) + mod_ref[i : i + 1, part(0)]
        ).astype(bf16)
    turned_ref[...] = first_ref[...].T
    writes = [
        pltpu.make_async_copy(weight.at[c], weight_ref.at[c], sems.at[c]) for c in range(COLUMNS)
    ]
    wait_for(weight.at[3], sems.at[3])
    writes[3].start()
    for c, out in enumerate((query_ref, keys_ref, values_ref)):
        wait_for(weight.at[c], sems.at[c])
        writes[c].start()
        if c == 2:
            out[...] = matmul(first_ref[...], weight[c]).astype(bf16)
        else:
            total[...] = matmul(first_ref[...], weight[c])

            @pl.loop(0, tokens // CHUNK)
            def _(i):
                rows = pl.ds(pl.multiple_of(i * CHUNK, CHUNK), CHUNK)
                out[rows, :] = rotate(total[rows, :], cos_ref[rows, :], sin_ref[rows, :]).astype(bf16)

    for write in writes:
        write.wait()


def window(head):
    start = head * HEAD_DIM // LANES * LANES
    stop = -(-(head + 1) * HEAD_DIM // LANES) * LANES
    lane = lax.broadcasted_iota(jnp.int32, (1, stop - start), 1) + start
    inside = (lane >= head * HEAD_DIM) & (lane < (head + 1) * HEAD_DIM)
    return slice(start, stop), inside


def soft_scores(left, right, allowed, axis):
    scores = times_transposed(left, right) * HEAD_DIM ** (-0.5)
    scores = jnp.where(allowed, scores, masked_score)
    exponent = jnp.exp(scores - jnp.max(scores, axis=axis, keepdims=True))
    return exponent * (1.0 / jnp.sum(exponent, axis=axis, keepdims=True))


def attend_kernel(
    query_ref, keys_ref, values_ref, column_ids, row_ids, x_ref, mod_ref,
    weight, turned_ref, branch_ref, middle_ref, second_ref, mixed,
):
    allowed = column_ids[...] == row_ids[...]
    for head in range(HEADS):
        lanes, inside = window(head)
        query = jnp.where(inside, query_ref[:, lanes], jnp.zeros((), bf16))
        probs = soft_scores(query, keys_ref[:, lanes], allowed, 1).astype(bf16)
        mixed[:, lanes] = jnp.where(inside, matmul(probs, values_ref[:, lanes]), mixed[:, lanes])
    attended = mixed[...].astype(bf16)
    turned_ref[...] = attended.T
    branch_ref[...] = matmul(attended, weight[0])
    for i in range(BLOCK // CHUNK):
        rows = slice(i * CHUNK, (i + 1) * CHUNK)
        mod = mod_ref.at[0]
        middle = x_ref[rows, :].astype(f32) + mod[i : i + 1, part(0)] * branch_ref[rows, :]
        middle_ref[rows, :] = middle
        normed, _ = normalize(middle)
        second_ref[rows, :] = (
            normed * (1.0 + mod[i : i + 1, part(2)]) + mod[i : i + 1, part(1)]
        ).astype(bf16)


def tile_copies(r, where, count, tile, pair, downs):
    place, mine, side = where
    t, j = tile
    column = mine ^ j
    rows, width = r["gate"].shape[0], r["hidden_w"].shape[1]
    sem = r["pair_sems"].at[t]
    copies = [
        pltpu.make_async_copy(
            r[name].at[:, take(column * width, width)], r["pair_w"].at[t, which, take(place * rows, rows)], sem
        )
        for which, name in enumerate(("gate", "up"))
    ]
    first = first_part(rows)
    for other in range(HALVES):
        for by in range(1, count):
            owner = (place + (count - by)) % count
            if j < 3:
                spans = [(pair[other][0].at[by - 1], 0, rows)]
            else:
                spans = [(pair[other][0].at[by - 1], 0, first), (pair[other][1].at[by - 1], first, rows - first)]
            for ref, start, size in spans:
                to = r["pair_w"].at[t, side ^ other, take(owner * rows + start, size)]
                copies.append(pltpu.make_async_copy(ref, to, sem))
    for copy in copies:
        copy.start()

    sem = r["down_sems"].at[t]
    target = r["down_w"].at[t]
    piece = width // PIECES

    @pl.when(column == place)
    def _():
        pltpu.make_async_copy(r["down"], target, sem).start()

    @pl.when(column != place)
    def _():
        by = jnp.maximum((place + count - column) % count, 1)
        for i, other, start, size, ref in placed(downs, piece):
            to = target.at[take(((mine ^ i) * HALVES + (side ^ other)) * piece + start, size)]
            pltpu.make_async_copy(ref.at[by - 1], to, sem).start()


def ffn_kernel(count, js, names, *refs):
    r = dict(zip(names, refs, strict=True))
    r["hidden_w"] = r["hidden"]
    first, last = js[0] == 0, js[-1] == COLUMNS - 1
    step = pl.program_id(0)
    tile = r["hidden"].shape[1]
    tokens = r["second"].shape[0]
    second, feed_back = r["second"], r["feed_back"]
    feed, second_back = r["feed"], r["second_back"]

    @pl.when(step == 0)
    def _():
        where = r["where"][0], r["where"][1], r["where"][2]
        for t, j in enumerate(js):
            pair = [
                [r[f"pair{j}_{other}_{i}"] for i in range(1 if j < 3 else 2)]
                for other in range(HALVES)
            ]
            tile_copies(r, where, count, (t, j), pair, [r[name] for name in names if name[:4] == "down" and name[5:].isdigit()])
        if first:
            r["turned"][...] = second[...].T
            for i in range(tokens // CHUNK):
                rows = slice(i * CHUNK, (i + 1) * CHUNK)
                upstream = r["cot"][rows, :].astype(f32) * r["factor"][0]
                feed_back[rows, :] = (upstream * r["mod"][i : i + 1, part(3)]).astype(bf16)

    pair_w, down_w = r["pair_w"].at[step], r["down_w"].at[step]
    wait_for(pair_w, r["pair_sems"].at[step])
    wait_for(down_w, r["down_sems"].at[step])
    sub = 256
    for n in range(tile // sub):
        lanes = slice(n * sub, (n + 1) * sub)
        gate = matmul(second[...], pair_w[0, :, lanes])
        upval = matmul(second[...], pair_w[1, :, lanes])
        hidden_back = times_transposed(feed_back[...], down_w[lanes, :])
        sigmoid = jax.nn.sigmoid(gate)
        silu = gate * sigmoid
        r["hidden"][:, lanes] = (silu * upval).astype(bf16)
        r["pair_back"][0, 1, :, lanes] = (hidden_back * silu).astype(bf16)
        r["pair_back"][0, 0, :, lanes] = (
            hidden_back * upval * (sigmoid * (1.0 + gate * (1.0 - sigmoid)))
        ).astype(bf16)

    r["hidden_turned"][0] = r["hidden"][...].T
    feed_part = matmul(r["hidden"][...], down_w[...])
    back_part = times_transposed(r["pair_back"][0, 0], pair_w[0]) + times_transposed(
        r["pair_back"][0, 1], pair_w[1]
    )

    @pl.when(step == 0)
    def _():
        feed[...] = feed_part if first else r["feed_in"][...] + feed_part
        second_back[...] = back_part if first else r["back_in"][...] + back_part

    @pl.when(step > 0)
    def _():
        feed[...] += feed_part
        second_back[...] += back_part

    if not last:
        return

    @pl.when(step == len(js) - 1)
    def _():
        for i in range(tokens // CHUNK):
            rows = slice(i * CHUNK, (i + 1) * CHUNK)
            gate_one = r["mod"][i : i + 1, part(0)]
            scale_two = r["mod"][i : i + 1, part(2)]
            gate_two = r["mod"][i : i + 1, part(3)]
            middle = r["middle"][rows, :]
            r["output"][rows, :] = (middle + gate_two * feed[rows, :]).astype(bf16)
            upstream = r["cot"][rows, :].astype(f32) * r["factor"][0]
            normed, inverse = normalize(middle)
            back = second_back[rows, :]
            middle_back = upstream + normalize_back(normed, inverse, back * (1.0 + scale_two))
            r["middle_back"][rows, :] = middle_back
            r["branch_back"][rows, :] = (middle_back * gate_one).astype(bf16)
            for where, values in enumerate(
                (middle_back * r["branch"][rows, :], back, back * normed, upstream * feed[rows, :])
            ):
                r["sums"][i : i + 1, part(where)] = jnp.sum(values, axis=0, keepdims=True)


ORDER = (1, 3, 2, 0)
SEND_X, KEEP_X, SEND_Y, KEEP_Y = (1, 3), (2, 0), (3, 2), (1, 0)
CUT = (SEND_X, KEEP_X, SEND_Y, KEEP_Y)


def put_grad(grad, other_ref, out_refs):
    step = pl.program_id(0)
    if other_ref is None:
        out_refs[0][0] = grad.astype(bf16)
        return
    total = (grad + other_ref[0].astype(f32)).astype(bf16)
    first = first_part(total.shape[1])
    for at, j in enumerate(ORDER):

        @pl.when(step == at)
        def _():
            for columns, ref in zip(CUT, out_refs, strict=True):
                if j in columns:
                    ref[0] = total[:, :first] if columns in (SEND_X, KEEP_X) else total[:, first:]


def cut_specs(count, rows, breadth):
    first = first_part(rows)
    shapes, specs = [], []
    for columns in CUT:
        size = first if columns in (SEND_X, KEEP_X) else rows - first
        shapes.append(struct((2, count, size, breadth), bf16))
        second = ORDER.index(columns[1])
        specs.append(
            pl.BlockSpec(
                (1, count, size, breadth),
                lambda s, where, second=second: (jnp.where(s >= second, 1, 0), 0, 0, 0),
            )
        )
    return tuple(shapes), tuple(specs)


def split_refs(mine, refs):
    return (refs[0], refs[1:]) if mine else (None, refs)


def pair_grad_kernel(mine, count, where_ref, turned_ref, own_ref, near_ref, far_ref, *refs):
    other_ref, out_refs = split_refs(mine, refs)
    for at, j in enumerate(ORDER):

        @pl.when(pl.program_id(0) == at)
        def _():
            back = {0: own_ref, 3: far_ref}.get(j, near_ref)
            grad = matmul(turned_ref[...], back[0, 0])
            put_grad(grad.reshape(count, grad.shape[0] // count, grad.shape[1]), other_ref, out_refs)


def down_grad_kernel(mine, where_ref, *refs):
    hiddens, feed_back_ref, out_ref = refs[:3], refs[3], refs[-1]
    other_ref = refs[4] if mine else None
    side = where_ref[2] if mine else where_ref[2] ^ 1
    count, _, rows, _ = out_ref.shape
    tiles = [(hidden, t) for hidden in hiddens for t in range(hidden.shape[0])]
    for j, (hidden, t) in enumerate(tiles):
        pieces = [hidden[t, take(((where_ref[1] ^ c) * HALVES + side) * rows, rows), :] for c in ORDER]
        grad = matmul(jnp.concatenate(pieces, axis=0), feed_back_ref[...]).reshape(COLUMNS, rows, WIDTH)
        owner = where_ref[1] ^ j
        if mine:
            grad = grad + other_ref[owner].astype(f32)
        out_ref[owner] = grad.astype(bf16)


def attn_grad_kernel(
    mine, where_ref, first_ref, attended_ref, joint_back_ref, branch_back_ref, *refs
):
    other_ref, out_refs = split_refs(mine, refs)
    column = where_ref[1] ^ where_ref[3 + pl.program_id(0)]
    side = where_ref[2] if mine else where_ref[2] ^ 1
    _, count, _, _ = out_refs[0].shape
    rows = WIDTH // count // HALVES

    def put(turned, right):
        taken = [turned[take((z * HALVES + side) * rows, rows), :] for z in range(count)]
        grad = matmul(jnp.concatenate(taken, axis=0), right[...])
        put_grad(grad.reshape(count, rows, WIDTH), other_ref, out_refs)

    @pl.when(column < 3)
    def _():
        put(first_ref, joint_back_ref)

    @pl.when(column == 3)
    def _():
        put(attended_ref, branch_back_ref)


def place_pair_kernel(where_ref, *refs):
    sources, outs = refs[:-2], refs[-2:]
    rows, tile = sources[0].shape
    for way in range(HALVES):

        @pl.when(where_ref[2] == way)
        def _():
            for j, other, start, size, ref in placed(sources, rows):
                lanes = take((where_ref[1] ^ j) * tile, tile)
                outs[way ^ other][start : start + size, lanes] = ref[...].astype(f32)


def place_down_kernel(rows, offset, where_ref, *refs):
    sources, out = refs[:-1], refs[-1]
    for j, other, start, size, ref in placed(sources, rows):
        piece = (where_ref[1] ^ j) * HALVES + (where_ref[2] ^ other)
        out[take(piece * rows + start, size), :] = ref[offset : offset + size, :].astype(f32)


def place_attn_kernel(rows, where_ref, *refs):
    sources, joint_ref, project_ref = refs[:-2], refs[-2], refs[-1]
    for column in range(COLUMNS):

        @pl.when(where_ref[1] == column)
        def _():
            for j, other, start, size, ref in placed(sources, rows):
                to = take((where_ref[2] ^ other) * rows + start, size)
                if column ^ j == 3:
                    project_ref[to, :] = ref[:size, :].astype(f32)
                else:
                    joint_ref[to, part(column ^ j)] = ref[:size, :].astype(f32)


def attend_back_kernel(
    query_ref, keys_ref, values_ref, branch_back_ref, column_ids, row_ids, cos_ref,
    sin_ref, weight, joint_back_ref, mixed_back, query_back, keys_back, values_back,
):
    mixed_back[...] = times_transposed(branch_back_ref[...], weight[0]).astype(bf16)
    allowed = column_ids[...] == row_ids[...]
    scaling = HEAD_DIM ** (-0.5)
    for head in range(HEADS):
        lanes, inside = window(head)
        zero = jnp.zeros((), bf16)
        query = jnp.where(inside, query_ref[:, lanes], zero)
        back = jnp.where(inside, mixed_back[:, lanes], zero)
        soft = soft_scores(keys_ref[:, lanes], query, allowed, 0)
        probs_back = times_transposed(values_ref[:, lanes], back)
        scores_back = (
            soft * (probs_back - jnp.sum(soft * probs_back, axis=0, keepdims=True))
        ).astype(bf16)
        query_back[:, lanes] = jnp.where(
            inside, contract_rows(scores_back, keys_ref[:, lanes]) * scaling, query_back[:, lanes]
        )
        keys_back[:, lanes] = jnp.where(
            inside, matmul(scores_back, query) * scaling, keys_back[:, lanes]
        )
        values_back[:, lanes] = jnp.where(
            inside, matmul(soft.astype(bf16), back), values_back[:, lanes]
        )

    @pl.loop(0, BLOCK // CHUNK)
    def _(i):
        rows = pl.ds(pl.multiple_of(i * CHUNK, CHUNK), CHUNK)
        cos, sin = cos_ref[rows, :], sin_ref[rows, :]
        joint_back_ref[rows, part(0)] = rotate(query_back[rows, :], cos, -sin).astype(bf16)
        joint_back_ref[rows, part(1)] = rotate(keys_back[rows, :], cos, -sin).astype(bf16)
        joint_back_ref[rows, part(2)] = values_back[rows, :].astype(bf16)


def first_back_kernel(
    joint_back_ref, x_ref, middle_back_ref, mod_ref, weight, grad_ref, sums_ref, first_back
):
    step = pl.program_id(0)
    product = times_transposed(joint_back_ref[...], weight[0])

    @pl.when(step == 0)
    def _():
        first_back[...] = product

    @pl.when(step > 0)
    def _():
        first_back[...] += product

    @pl.when(step == pl.num_programs(0) - 1)
    def _():
        finish_first_back(x_ref, middle_back_ref, mod_ref, grad_ref, sums_ref, first_back)


def finish_first_back(x_ref, middle_back_ref, mod_ref, grad_ref, sums_ref, first_back):
    for i in range(x_ref.shape[0] // CHUNK):
        rows = slice(i * CHUNK, (i + 1) * CHUNK)
        normed, inverse = normalize(x_ref[rows, :].astype(f32))
        back = first_back[rows, :]
        grad_ref[rows, :] = middle_back_ref[rows, :] + normalize_back(
            normed, inverse, back * (1.0 + mod_ref[i : i + 1, part(1)])
        )
        sums_ref[i : i + 1, part(0)] = jnp.sum(back, axis=0, keepdims=True)
        sums_ref[i : i + 1, part(1)] = jnp.sum(back * normed, axis=0, keepdims=True)


SMEM = pl.BlockSpec(memory_space=pltpu.SMEM)
VMEM = pl.BlockSpec(memory_space=pltpu.VMEM)
ANY = pl.BlockSpec(memory_space=pl.ANY)


def struct(shape, dtype):
    return jax.ShapeDtypeStruct(shape, dtype)


def params(mega=56):
    return pltpu.CompilerParams(vmem_limit_bytes=mega * MEGA)


def cost(microseconds):
    return pl.CostEstimate(flops=int(microseconds * 1e9), bytes_accessed=1000, transcendentals=0)


def by_block(*shape):
    return pl.BlockSpec(shape, lambda b: (b,) + (0,) * (len(shape) - 1))


def whole(*shape):
    return pl.BlockSpec(shape, lambda *_: (0,) * len(shape))


def first_call(where, x, mod, cos, sin, joint, project, arrived):
    tokens = x.shape[0]
    count = arrived[0].shape[0] + 1
    shape = struct((tokens, WIDTH), bf16)
    return pl.pallas_call(
        functools.partial(first_kernel, count),
        out_shape=(struct((WIDTH, tokens), bf16),)
        + (shape,) * 3
        + (struct((COLUMNS, WIDTH, WIDTH), bf16),),
        in_specs=[SMEM, VMEM, VMEM, VMEM, VMEM] + [ANY] * (2 + len(arrived)),
        out_specs=(VMEM,) * 4 + (ANY,),
        scratch_shapes=[
            pltpu.VMEM((COLUMNS, WIDTH, WIDTH), bf16),
            pltpu.VMEM((tokens, WIDTH), bf16),
            pltpu.VMEM((tokens, WIDTH), f32),
            pltpu.SemaphoreType.DMA((COLUMNS,)),
        ],
        compiler_params=params(),
        cost_estimate=cost(5),
    )(where, x, mod, cos, sin, joint, project, *arrived)


def attend_call(query, keys, values, ids, x, mod, weight):
    tokens = x.shape[0]
    return pl.pallas_call(
        attend_kernel,
        grid=(tokens // BLOCK,),
        out_shape=(
            struct((WIDTH, tokens), bf16),
            struct((tokens, WIDTH), f32),
            struct((tokens, WIDTH), f32),
            struct((tokens, WIDTH), bf16),
        ),
        in_specs=[by_block(BLOCK, WIDTH)] * 3
        + [by_block(BLOCK, 1), pl.BlockSpec((1, BLOCK), lambda b: (0, b)), by_block(BLOCK, WIDTH)]
        + [by_block(1, BLOCK // CHUNK, 4 * WIDTH), pl.BlockSpec((1, WIDTH, WIDTH), lambda b: (3, 0, 0))],
        out_specs=(pl.BlockSpec((WIDTH, BLOCK), lambda b: (0, b)),) + (by_block(BLOCK, WIDTH),) * 3,
        scratch_shapes=[pltpu.VMEM((BLOCK, WIDTH), f32)],
        compiler_params=params(),
        cost_estimate=cost(2),
    )(
        query, keys, values, ids[:, None], ids[None, :], x,
        mod.reshape(tokens // BLOCK, BLOCK // CHUNK, 4 * WIDTH), weight,
    )


def ffn_call(js, where, given, shards, pairs, downs):
    second = given["second"]
    tokens = second.shape[0]
    ff = shards["gate"].shape[1]
    tile = ff // COLUMNS
    count = ff // shards["down"].shape[0]
    chunks = tokens // CHUNK
    first, last = js[0] == 0, js[-1] == COLUMNS - 1
    full = whole(tokens, WIDTH)
    wide = struct((tokens, WIDTH), f32)
    narrow = struct((tokens, WIDTH), bf16)
    inputs = [("where", where, SMEM), ("second", second, full)]
    if first or last:
        inputs += [
            ("factor", given["factor"], SMEM),
            ("cot", given["cot"], full),
            ("mod", given["mod"], whole(chunks, 4 * WIDTH)),
        ]
    if not first:
        inputs += [
            ("feed_back", given["feed_back"], full),
            ("feed_in", given["feed"], full),
            ("back_in", given["second_back"], full),
        ]
    if last:
        inputs += [("middle", given["middle"], full), ("branch", given["branch"], full)]
    inputs += [(name, shards[name], ANY) for name in ("gate", "up", "down")]
    for j in js:
        for other in range(HALVES):
            inputs += [(f"pair{j}_{other}_{i}", a, ANY) for i, a in enumerate(pairs[other][j])]
    inputs += [(f"down_{i}", a, ANY) for i, a in enumerate(downs)]
    outputs = [
        (
            "hidden_turned",
            struct((len(js), tile, tokens), bf16),
            pl.BlockSpec((1, tile, tokens), lambda t: (t, 0, 0)),
        ),
        (
            "pair_back",
            struct((len(js), HALVES, tokens, tile), bf16),
            pl.BlockSpec((1, HALVES, tokens, tile), lambda t: (t, 0, 0, 0)),
        ),
    ]
    if first:
        outputs += [
            ("turned", struct((WIDTH, tokens), bf16), whole(WIDTH, tokens)),
            ("feed_back", narrow, full),
        ]
    sums = ("feed", "second_back")
    scratch = [
        ("pair_w", pltpu.VMEM((len(js), HALVES, WIDTH, tile), bf16)),
        ("down_w", pltpu.VMEM((len(js), ff // count, WIDTH), bf16)),
        ("hidden", pltpu.VMEM((tokens, tile), bf16)),
        ("pair_sems", pltpu.SemaphoreType.DMA((len(js),))),
        ("down_sems", pltpu.SemaphoreType.DMA((len(js),))),
    ]
    if last:
        outputs += [
            ("output", narrow, full),
            ("middle_back", wide, full),
            ("branch_back", narrow, full),
            ("sums", struct((chunks, 4 * WIDTH), f32), whole(chunks, 4 * WIDTH)),
        ]
        scratch += [(name, pltpu.VMEM((tokens, WIDTH), f32)) for name in sums]
    else:
        outputs += [(name, wide, full) for name in sums]
    names = [each[0] for each in inputs + outputs + scratch]
    found = pl.pallas_call(
        functools.partial(ffn_kernel, count, js, names),
        grid=(len(js),),
        out_shape=tuple(shape for _, shape, _ in outputs),
        in_specs=[spec for _, _, spec in inputs],
        out_specs=tuple(spec for _, _, spec in outputs),
        scratch_shapes=[shape for _, shape in scratch],
        compiler_params=params(),
        cost_estimate=cost(2 if first else 12 * len(js)),
    )(*[array for _, array, _ in inputs])
    return {name: array for (name, _, _), array in zip(outputs, found, strict=True)}


def by_column(call, count, rows, breadth, in_specs, where, arrays, other):
    shapes, specs = cut_specs(count, rows, breadth)
    block = pl.BlockSpec((1, count, rows, breadth), lambda s, where: (s, 0, 0, 0))
    if other is None:
        shapes, specs = (struct((COLUMNS, count, rows, breadth), bf16),), (block,)
    else:
        in_specs, arrays = in_specs + [block], arrays + (other,)
    found = pl.pallas_call(
        call,
        out_shape=shapes,
        grid_spec=pltpu.PrefetchScalarGridSpec(
            num_scalar_prefetch=1, grid=(COLUMNS,), in_specs=in_specs, out_specs=specs
        ),
        compiler_params=params(),
        cost_estimate=cost(3),
    )(where, *arrays)
    return found[0] if other is None else found


def pair_grad_call(count, where, turned, backs, other=None):
    tokens, tile = backs[0].shape[2:]
    mine = other is not None

    def spec(tile_of):
        return pl.BlockSpec(
            (1, 1, tokens, tile),
            lambda s, where: (tile_of(where[3 + s]), where[2] if mine else where[2] ^ 1, 0, 0),
        )

    return by_column(
        functools.partial(pair_grad_kernel, mine, count),
        count, WIDTH // count, tile,
        [whole(WIDTH, tokens), spec(lambda j: 0), spec(lambda j: jnp.clip(j - 1, 0, 1)), spec(lambda j: 0)],
        where, (turned,) + tuple(backs), other,
    )


def attn_grad_call(count, where, first, attended, joint_back, branch_back, other=None):
    tokens = first.shape[1]
    return by_column(
        functools.partial(attn_grad_kernel, other is not None),
        count, WIDTH // count // HALVES, WIDTH,
        [
            whole(WIDTH, tokens),
            whole(WIDTH, tokens),
            pl.BlockSpec((tokens, WIDTH), lambda s, where: (0, jnp.minimum(where[1] ^ where[3 + s], 2))),
            whole(tokens, WIDTH),
        ],
        where, (first, attended, joint_back, branch_back), other,
    )


def down_grad_call(count, where, hiddens, feed_back, other=None):
    ff = sum(h.shape[0] * h.shape[1] for h in hiddens)
    out = struct((count, COLUMNS, ff // count // PIECES, WIDTH), bf16)
    arrays = tuple(hiddens) + (feed_back,) + (() if other is None else (other,))
    return pl.pallas_call(
        functools.partial(down_grad_kernel, other is not None),
        out_shape=out,
        in_specs=[SMEM] + [VMEM] * len(arrays),
        out_specs=VMEM,
        compiler_params=params(),
        cost_estimate=cost(3),
    )(where, *arrays)


def place_call(kernel, where, arrays, outs):
    return pl.pallas_call(
        kernel,
        out_shape=outs,
        in_specs=[SMEM] + [VMEM] * len(arrays),
        out_specs=jax.tree.map(lambda _: VMEM, outs),
        compiler_params=params(),
        cost_estimate=cost(4),
    )(where, *arrays)


def attend_back_call(query, keys, values, branch_back, ids, cos, sin, weight):
    tokens = query.shape[0]
    block = by_block(BLOCK, WIDTH)
    return pl.pallas_call(
        attend_back_kernel,
        grid=(tokens // BLOCK,),
        out_shape=struct((tokens, 3 * WIDTH), bf16),
        in_specs=[block, block, block, block]
        + [by_block(BLOCK, 1), pl.BlockSpec((1, BLOCK), lambda b: (0, b)), block, block]
        + [pl.BlockSpec((1, WIDTH, WIDTH), lambda b: (3, 0, 0))],
        out_specs=by_block(BLOCK, 3 * WIDTH),
        scratch_shapes=[
            pltpu.VMEM((BLOCK, WIDTH), bf16),
            pltpu.VMEM((BLOCK, WIDTH), f32),
            pltpu.VMEM((BLOCK, WIDTH), f32),
            pltpu.VMEM((BLOCK, WIDTH), f32),
        ],
        compiler_params=params(),
        cost_estimate=cost(8),
    )(query, keys, values, branch_back, ids[:, None], ids[None, :], cos, sin, weight)


def first_back_call(joint_back, x, middle_back, mod, weight):
    tokens = x.shape[0]
    chunks = tokens // CHUNK
    full = whole(tokens, WIDTH)
    return pl.pallas_call(
        first_back_kernel,
        grid=(3,),
        out_shape=(struct((tokens, WIDTH), f32), struct((chunks, 2 * WIDTH), f32)),
        in_specs=[
            pl.BlockSpec((tokens, WIDTH), lambda c: (0, c)),
            full,
            full,
            whole(chunks, 2 * WIDTH),
            pl.BlockSpec((1, WIDTH, WIDTH), lambda c: (c, 0, 0)),
        ],
        out_specs=(full, whole(chunks, 2 * WIDTH)),
        scratch_shapes=[pltpu.VMEM((tokens, WIDTH), f32)],
        compiler_params=params(),
        cost_estimate=cost(2),
    )(joint_back, x, middle_back, mod, weight)


def shifts(count, by):
    return [(i, (i + by) % count) for i in range(count)]


def pick(array, index):
    return lax.dynamic_index_in_dim(array, index, 0, keepdims=False)


def across(bit):
    return [(i, i ^ bit) for i in range(PIECES)]


def swap(array, bit):
    return lax.ppermute(array, "bucket", across(bit))


def after(arrays, *others):
    return lax.optimization_barrier((arrays, others))[0]


def add(left, right):
    return (left.astype(f32) + right.astype(f32)).astype(bf16)


def over_z(piece):
    count = lax.axis_size("fsdp")
    return [lax.ppermute(piece, "fsdp", shifts(count, by)) for by in range(1, count)]


def gather_z(piece, *others):
    count = lax.axis_size("fsdp")
    place = lax.axis_index("fsdp")
    full = after(lax.all_gather(piece, "fsdp", axis=0, tiled=False), *others)
    return jnp.stack([pick(full, (place + count - by) % count) for by in range(1, count)])


def cross(by_x, by_y, first):
    if first is not None:
        by_x, by_y = by_x[..., :first, :], by_y[..., first:, :]
    return swap(by_x, 4), swap(by_y, 2)


def both(here):
    return here + tuple(None if array is None else swap(array, 1) for array in here)


def direct(piece):
    return piece, swap(piece, 2), swap(piece, 4), swap(piece, 6)


def spread_whole(pieces):
    first = first_part(pieces.shape[1])

    def of(side):
        own, by_x, by_y, far = (pieces[c * HALVES + side] for c in range(COLUMNS))
        return own, by_x, by_y, far[:first], far[first:]

    return of(0) + of(1)


def halve_once(cut):
    send_x, (a2, a0), send_y, (b1, b0) = cut
    from_x, from_y = swap(send_x, 2), swap(send_y, 4)
    return add(a0, from_x[0]), add(a2, from_x[1]), add(b0, from_y[1]), add(b1, from_y[0])


def halve_twice(once, *others):
    a0, a2, b0, b1 = once
    if others:
        a0, b0 = after((a0, b0), *others)
    return jnp.concatenate([add(a0, swap(a2, 4)), add(b0, swap(b1, 2))], axis=-2)


def send_z(parts):
    count = lax.axis_size("fsdp")
    place = lax.axis_index("fsdp")
    return [
        lax.ppermute(pick(parts, (place + by) % count), "fsdp", shifts(count, by))
        for by in range(1, count)
    ]


def total_z(parts, others):
    total = pick(parts, lax.axis_index("fsdp")).astype(f32)
    for array in others:
        total = total + array.astype(f32)
    return total.astype(bf16)


def sum_z(parts):
    return total_z(parts, send_z(parts))


def cut_down(part, first):
    cut = []
    for columns in CUT:
        both_columns = jnp.stack([part[ORDER.index(j)] for j in columns])
        cut.append(both_columns[:, :first] if columns in (SEND_X, KEEP_X) else both_columns[:, first:])
    return cut


def uncut(cut):
    def of(j, pair):
        columns = next(c for c in pair if j in c)
        return cut[CUT.index(columns)][columns.index(j)]

    return jnp.stack(
        [jnp.concatenate([of(j, (SEND_X, KEEP_X)), of(j, (SEND_Y, KEEP_Y))], axis=1) for j in ORDER]
    )


def sum_whole(mine, theirs):
    parts = jnp.stack([mine, theirs], axis=1)
    parts = jnp.stack([parts[ORDER.index(c)] for c in range(COLUMNS)])
    rows, breadth = mine.shape[2:]
    parts = lax.psum(parts, "bucket").transpose(2, 0, 1, 3, 4)
    return spread_whole(sum_z(parts).reshape(PIECES, rows, breadth))


def arrived_whole(pieces):
    count = lax.axis_size("fsdp")
    place = lax.axis_index("fsdp")
    first = first_part(pieces.shape[1])
    full = lax.all_gather(pieces, "fsdp", axis=0, tiled=False)
    full = jnp.stack([pick(full, (place + count - by) % count) for by in range(1, count)])

    def of(side):
        own, by_x, by_y, far = (full[:, c * HALVES + side] for c in range(COLUMNS))
        return own, by_x, by_y, far[:, :first], far[:, first:]

    return of(0) + of(1)


def to_group(rows, count, place):
    relative = jnp.stack(
        [pick(rows, place)]
        + [
            lax.ppermute(pick(rows, (place + by) % count), "fsdp", shifts(count, by))
            for by in range(1, count)
        ]
    )
    return jnp.stack([pick(relative, (place - j) % count) for j in range(count)])


def on_device(
    inputs,
    condition,
    segment_ids,
    grid_widths,
    bucket_counts,
    modulate_weight,
    joint_weight,
    project_weight,
    gate_weight,
    up_weight,
    down_weight,
    cotangent,
):
    fsdp_count = lax.axis_size("fsdp")
    place = lax.axis_index("fsdp")
    bucket = lax.axis_index("bucket")
    height = joint_weight.shape[0]
    half = height // HALVES
    ff = gate_weight.shape[1]
    tile = ff // COLUMNS
    down_rows = down_weight.shape[0] // PIECES
    slots = condition.shape[0]

    cond_float = condition.astype(f32)
    lifted = jax.nn.silu(cond_float).astype(bf16)
    lifted_rows = to_group(
        lifted.reshape(slots, fsdp_count, height).transpose(1, 0, 2), fsdp_count, place
    ).reshape(fsdp_count * slots, height)
    one_hot = (
        segment_ids[::CHUNK, None] == jnp.arange(slots, dtype=jnp.int32)[None, :]
    ).astype(f32)

    def modulation_parts(weight, rows):
        parts = matmul(rows, weight).reshape(fsdp_count, slots, weight.shape[1])
        return [pick(parts, place)] + [
            lax.ppermute(pick(parts, (place + by) % fsdp_count), "fsdp", shifts(fsdp_count, by))
            for by in range(1, fsdp_count)
        ]

    def modulation(parts):
        return jnp.dot(
            one_hot,
            sum(parts[1:], parts[0]),
            precision=lax.Precision.HIGHEST,
            preferred_element_type=f32,
        )

    first_rows = modulation_parts(modulate_weight[:, : 2 * WIDTH], lifted_rows)
    mod_one = modulation(first_rows)
    fast = lax.axis_size("bucket") == PIECES
    if fast:
        column, side = bucket // HALVES, bucket % HALVES
        where = jnp.stack([place, column, side] + [jnp.int32(j) for j in ORDER])
        attn_piece = jnp.where(
            column == 3,
            lax.dynamic_slice(project_weight, (side * half, 0), (half, WIDTH)),
            lax.dynamic_slice(joint_weight, (side * half, column * WIDTH), (half, WIDTH)),
        )
        ffn_piece = jnp.where(
            side == 0,
            lax.dynamic_slice(gate_weight, (0, column * tile), (height, tile)),
            lax.dynamic_slice(up_weight, (0, column * tile), (height, tile)),
        )
        down_piece = lax.dynamic_slice_in_dim(down_weight, bucket * down_rows, down_rows, 0)
        attn_z = gather_z(attn_piece, first_rows)
        down_k = over_z(after(down_piece, attn_z))
        attn_x, attn_y = swap(attn_z, 2), swap(attn_z, 4)
        attn_x, attn_y, down_k = after((attn_x, attn_y, down_k))
        attn_far = cross(attn_x, attn_y, first_part(half))
        pair_z = gather_z(after(ffn_piece, down_k))
        down_z = jnp.stack(down_k)
        attn_arrived = both((attn_z, attn_x, attn_y) + attn_far)
        inputs, down_z = after((inputs, down_z), attn_far)
        down_x, down_y = swap(down_z, 2), swap(down_z, 4)
        inputs = after(inputs, down_z)
    else:
        where = jnp.stack([place, 0 * place, 0 * place] + [jnp.int32(j) for j in ORDER])
        attn_arrived = arrived_whole(
            jnp.concatenate([joint_weight, project_weight], axis=1)
            .reshape(HALVES, half, COLUMNS, WIDTH)
            .transpose(2, 0, 1, 3)
            .reshape(PIECES, half, WIDTH)
        )
        pairs = arrived_whole(
            jnp.stack([gate_weight, up_weight])
            .reshape(HALVES, height, COLUMNS, tile)
            .transpose(2, 0, 1, 3)
            .reshape(PIECES, height, tile)
        )
        downs = arrived_whole(down_weight.reshape(PIECES, down_rows, WIDTH))

    if fast:
        lifted_rows = after(lifted_rows, down_k)
    late_rows = modulation_parts(modulate_weight[:, 2 * WIDTH :], lifted_rows)
    counts = bucket_counts.astype(f32)
    mine = jnp.sum(jnp.where(jnp.arange(counts.shape[0], dtype=jnp.int32) == bucket, counts, 0.0))
    factor = (mine * counts.shape[0] / jnp.sum(counts)).reshape(1)
    cos, sin = rope_tables(segment_ids, grid_widths)

    first, query, keys, values, weight = first_call(
        where, inputs, mod_one, cos, sin, joint_weight, project_weight, attn_arrived
    )
    if fast:
        late_rows = [late_rows[0], *after(late_rows[1:], query)]
        down_x, down_y = after((down_x, down_y), query)
        down_far = cross(down_x, down_y, first_part(down_rows))
        downs = (down_z, down_x, down_y) + down_far
        pair_z = after(pair_z, query)
        pair_x, pair_y = swap(pair_z, 2), swap(pair_z, 4)
    mod = modulation(late_rows)
    attended, branch, middle, second = attend_call(
        query, keys, values, segment_ids, inputs, mod, weight
    )
    shards = dict(gate=gate_weight, up=up_weight, down=down_weight)
    given = dict(
        second=second, factor=factor, cot=cotangent, mod=mod, middle=middle, branch=branch
    )
    if fast:
        downs = both(after(downs, second))
        pairs = (pair_z, pair_x, pair_y, None, None, swap(pair_z, 1), None, None, None, None)
    pairs = [
        [[group] for group in pairs[5 * k : 5 * k + 3]] + [list(pairs[5 * k + 3 : 5 * k + 5])]
        for k in range(HALVES)
    ]
    found = ffn_call((0,), where, given, shards, pairs, downs)
    turned, feed_back = found["turned"], found["feed_back"]
    steps = [found]
    if fast:
        pair_x, pair_y = after((pair_x, pair_y), feed_back)
        far = cross(pair_x, pair_y, first_part(height))
        pairs[1][1:3] = [swap(pair_x, 1)], [swap(pair_y, 1)]
    for js in ((1, 2), (3,)):
        given.update(feed_back=feed_back, feed=found["feed"], second_back=found["second_back"])
        if fast and js == (3,):
            far = after(far, found["feed"])
            pairs[0][3], pairs[1][3] = list(far), [swap(array, 1) for array in far]
        found = ffn_call(js, where, given, shards, pairs, downs)
        steps.append(found)
    output, middle_back, branch_back = found["output"], found["middle_back"], found["branch_back"]
    late_sums = found["sums"]

    def by_slot(chunk_sums):
        return lax.dot_general(
            one_hot,
            chunk_sums,
            (((0,), (0,)), ((), ())),
            precision=lax.Precision.HIGHEST,
            preferred_element_type=f32,
        ).astype(bf16)

    def near_rows(rows):
        return jnp.concatenate([rows] + over_z(rows), axis=0)

    late_rows = jnp.concatenate([by_slot(late_sums), lifted], axis=1)
    late_k = over_z(late_rows)

    count = fsdp_count
    hiddens = [step["hidden_turned"] for step in steps]
    backs = [step["pair_back"] for step in steps]
    pair_theirs = pair_grad_call(count, where, turned, backs)
    late_k, pair_theirs = after((late_k, pair_theirs))
    near_late = jnp.concatenate([late_rows] + late_k, axis=0)
    late = lax.all_gather(near_late, "bucket", axis=0, tiled=True)
    if fast:
        pair_other = swap(pair_theirs, 1)
        feed_back = after(feed_back, pair_theirs)
    else:
        pair_other = jnp.zeros_like(pair_theirs)
    down_theirs = down_grad_call(count, where, hiddens, feed_back)
    if fast:
        pair_other, down_theirs = after((pair_other, down_theirs))
        down_other = swap(down_theirs, 1)
    else:
        down_other = jnp.zeros_like(down_theirs)
    pair_cut = pair_grad_call(count, where, turned, backs, pair_other)
    if fast:
        feed_back = after(feed_back, pair_cut)
    down_mine = down_grad_call(count, where, hiddens, feed_back, down_other)
    if fast:
        down_mine, late = after((down_mine, late))
        down_part = lax.psum_scatter(down_mine, "fsdp", scatter_dimension=0, tiled=False)
        branch_back = after(branch_back, down_mine)
    joint_back = attend_back_call(
        query, keys, values, branch_back, segment_ids, cos, sin, weight
    )
    attn_theirs = attn_grad_call(count, where, first, attended, joint_back, branch_back)
    if fast:
        send_x, keep_x, send_y, keep_y = pair_cut
        keep_x, keep_y, attn_theirs = after((keep_x, keep_y, attn_theirs))
        pair_once = halve_once((send_x, keep_x, send_y, keep_y))
        pair_once, attn_theirs, middle_back = after((pair_once, attn_theirs, middle_back))
        attn_other = swap(attn_theirs, 1)
    grad_inputs, early_sums = first_back_call(joint_back, inputs, middle_back, mod_one, weight)
    near_early = near_rows(by_slot(early_sums))
    if fast:
        a0, a2, b0, b1 = pair_once
        a0, b0, grad_inputs = after((a0, b0, grad_inputs))
        pair_parts, branch_back, near_early = after(
            (halve_twice((a0, a2, b0, b1)), branch_back, near_early)
        )
        pair_z = send_z(pair_parts)
    early = lax.all_gather(near_early, "bucket", axis=0, tiled=True)
    slope_rows = times_transposed(
        jnp.concatenate([near_early, near_late[:, : 4 * WIDTH]], axis=1), modulate_weight
    ).reshape(fsdp_count, slots, height)
    slopes = [slope_rows[0]] + [
        lax.ppermute(slope_rows[count - by], "fsdp", shifts(count, by)) for by in range(1, count)
    ]
    if fast:
        attn_cut = attn_grad_call(
            count, where, first, attended, joint_back, branch_back, attn_other
        )
        attn_cut, down_part, slopes = after((attn_cut, down_part, slopes))
        down_cut = cut_down(down_part, first_part(down_rows))
        cut = [
            jnp.concatenate([attn.reshape(2, -1, WIDTH), down], axis=1)
            for attn, down in zip(attn_cut, down_cut, strict=True)
        ]
        once, pair_z = after((halve_once(cut), pair_z))
        pair_sum = total_z(pair_parts, pair_z)
        pair_x, pair_y = swap(pair_sum, 2), swap(pair_sum, 4)
        a0, a2, b0, b1 = once
        ahead, behind = add(a0, swap(a2, 4)), add(b0, swap(b1, 2))
        at, other_at = (part.shape[1] * part.shape[2] for part in (attn_cut[0], attn_cut[2]))
        attn_parts = jnp.concatenate(
            [half.reshape(count, -1, WIDTH) for half in (ahead[:at], behind[:other_at])], axis=1
        )
        down_total = jnp.concatenate([ahead[at:], behind[other_at:]], axis=0)
        attn_parts, down_total, pair_x, pair_y = after((attn_parts, down_total, pair_x, pair_y))
        attn_z = send_z(attn_parts)
        pair_sums = (pair_sum, pair_x, pair_y) + cross(pair_x, pair_y, first_part(height))
        attn_z, pair_sums = after((attn_z, both(pair_sums)))
        attn_sum = total_z(attn_parts, attn_z)
    else:
        down_sums = sum_whole(down_mine.swapaxes(0, 1), down_theirs.swapaxes(0, 1))
        pair_sums = sum_whole(uncut(pair_cut), pair_theirs)
        attn_cut = attn_grad_call(
            count, where, first, attended, joint_back, branch_back, jnp.zeros_like(attn_theirs)
        )
        attn_sums = sum_whole(uncut(attn_cut), attn_theirs)
    if fast:
        early, attn_sum = after((early, attn_sum))
        both_sums = direct(jnp.concatenate([attn_sum, down_total], axis=0))
    all_back = jnp.concatenate([early, late[:, : 4 * WIDTH]], axis=1)
    all_lifted = lax.dynamic_slice_in_dim(late, 4 * WIDTH + place * height, height, 1)
    modulate_gradient = contract_rows(all_lifted, all_back)
    pair_grad = place_call(
        place_pair_kernel, where, pair_sums, (struct(gate_weight.shape, f32),) * 2
    )
    if fast:
        both_sums, pair_grad, modulate_gradient = after((both_sums, pair_grad, modulate_gradient))
        attn_sums = down_sums = both(both_sums)
    slopes = jnp.stack(slopes)
    condition_slope = (
        jnp.stack([pick(slopes, (place + count - j) % count) for j in range(count)])
        .transpose(1, 0, 2)
        .reshape(slots, WIDTH)
    )
    grad_condition = condition_slope * silu_slope(cond_float)
    down_grad = place_call(functools.partial(place_down_kernel, down_rows, half if fast else 0), where, down_sums, struct(down_weight.shape, f32))
    attn_grad = place_call(
        functools.partial(place_attn_kernel, half),
        where,
        attn_sums,
        (struct(joint_weight.shape, f32), struct(project_weight.shape, f32)),
    )

    return (
        output,
        grad_inputs,
        grad_condition,
        modulate_gradient,
        *attn_grad,
        *pair_grad,
        down_grad,
    )


def solution(mesh):
    spread = P(("bucket", "fsdp"), None)
    rows = P("fsdp", None)
    in_specs = (
        spread, spread, P(("bucket", "fsdp")), P(("bucket", "fsdp")), P(),
        rows, rows, rows, rows, rows, rows, spread,
    )
    out_specs = (spread, spread, spread, rows, rows, rows, rows, rows, rows)
    return jax.shard_map(
        on_device, mesh=mesh, in_specs=in_specs, out_specs=out_specs, check_vma=False
    )
```

```python
import functools

import jax
import jax.numpy as jnp
from jax import lax
from jax.experimental import pallas as pl
from jax.experimental.pallas import tpu as pltpu
from jax.sharding import PartitionSpec as P

HEADS = 16
HEAD_DIM = 72
WIDTH = HEADS * HEAD_DIM
QUARTER = HEAD_DIM // 4
BLOCK = 256
CHUNK = 64
COLUMNS = 4
HALVES = 2
PIECES = COLUMNS * HALVES
LANES = 128

epsilon = 1e-06
masked_score = -1e30
f32 = jnp.float32
bf16 = jnp.bfloat16
MEGA = 2**20


def normalize(values):
    average = jnp.mean(values, axis=-1, keepdims=True)
    centered = values - average
    inverse = lax.rsqrt(jnp.mean(centered * centered, axis=-1, keepdims=True) + epsilon)
    return (centered * inverse, inverse)


def normalize_back(normed, inverse, upstream):
    return inverse * (
        upstream
        - jnp.mean(upstream, axis=-1, keepdims=True)
        - normed * jnp.mean(upstream * normed, axis=-1, keepdims=True)
    )


def matmul(left, right):
    return jnp.dot(left, right, preferred_element_type=f32)


def contract_rows(left, right):
    return lax.dot_general(left, right, (((0,), (0,)), ((), ())), preferred_element_type=f32)


def times_transposed(left, right):
    return lax.dot_general(left, right, (((1,), (1,)), ((), ())), preferred_element_type=f32)


def silu_slope(values):
    sigmoid = jax.nn.sigmoid(values)
    return sigmoid * (1.0 + values * (1.0 - sigmoid))


def rope_tables(segments, widths):
    slots = widths.shape[0]
    one_hot = (segments[:, None] == jnp.arange(slots, dtype=jnp.int32)[None, :]).astype(jnp.int32)
    counts = jnp.sum(one_hot, axis=0)
    starts = jnp.cumsum(counts) - counts
    start_token = jnp.sum(one_hot * starts[None, :], axis=1)
    width_token = jnp.maximum(jnp.sum(one_hot * widths[None, :], axis=1), 1)
    place = jnp.arange(segments.shape[0], dtype=jnp.int32) - start_token
    row_place = (place // width_token).astype(f32)
    col_place = (place % width_token).astype(f32)
    freqs = 10000.0 ** (-jnp.arange(QUARTER, dtype=f32) / QUARTER)
    angle_row = row_place[:, None] * freqs[None, :]
    angle_col = col_place[:, None] * freqs[None, :]
    cos_row, sin_row, cos_col, sin_col = (
        jnp.cos(angle_row),
        jnp.sin(angle_row),
        jnp.cos(angle_col),
        jnp.sin(angle_col),
    )
    cos = jnp.concatenate([cos_row, cos_row, cos_col, cos_col], axis=1)
    sin = jnp.concatenate([-sin_row, sin_row, -sin_col, sin_col], axis=1)
    return jnp.tile(cos, (1, HEADS)), jnp.tile(sin, (1, HEADS))


def part(index):
    return slice(index * WIDTH, (index + 1) * WIDTH)


def rotate(values, cos, sin):
    lane = lax.broadcasted_iota(jnp.int32, (1, WIDTH), 1)
    leading = lane % (2 * QUARTER) < QUARTER
    partner = jnp.where(
        leading,
        pltpu.roll(values, WIDTH - QUARTER, 1),
        pltpu.roll(values, QUARTER, 1),
    )
    return values * cos + partner * sin


def take(start, size):
    return pl.ds(pl.multiple_of(start, 128 if size % 128 == 0 else 16), size)


def first_part(rows):
    return -(-rows // 32) * 16


def placed(refs, rows):
    first = first_part(rows)
    each = len(refs) // HALVES
    for other in range(HALVES):
        here = refs[each * other : each * other + each]
        for j in range(3):
            yield j, other, 0, rows, here[j]
        if each == COLUMNS:
            yield 3, other, 0, rows, here[3]
        else:
            yield 3, other, 0, first, here[3]
            yield 3, other, first, rows - first, here[4]


def piece_copies(where, count, sources, target, rows, sem):
    place, column, side = where
    copies = []
    for j, other, start, size, ref in placed(sources, rows):
        for by in range(1, count):
            owner = (place + (count - by)) % count
            to = target(column ^ j, side ^ other, owner, start, size)
            copies.append(pltpu.make_async_copy(ref.at[by - 1], to, sem(column ^ j, side ^ other, owner)))
    return copies


def wait_for(ref, sem):
    pltpu.make_async_copy(ref, ref, sem).wait()


def first_kernel(
    count, where_ref, x_ref, mod_ref, cos_ref, sin_ref, joint_ref, project_ref, *refs
):
    sources, refs = refs[:-9], refs[-9:]
    turned_ref, query_ref, keys_ref, values_ref, weight_ref, weight, first_ref, total, sems = refs
    where = where_ref[0], where_ref[1], where_ref[2]
    rows_in = joint_ref.shape[0]
    half = rows_in // HALVES

    def target(column, side, place, start, size):
        return weight.at[column, take(place * rows_in + side * half + start, size)]

    copies = piece_copies(where, count, sources, target, half, lambda c, s, z: sems.at[c])
    for c in range(COLUMNS):
        shard = project_ref if c == 3 else joint_ref.at[:, pl.ds(c * WIDTH, WIDTH)]
        copies.append(pltpu.make_async_copy(shard, weight.at[c, take(where[0] * rows_in, rows_in)], sems.at[c]))
    for copy in copies:
        copy.start()
    tokens = x_ref.shape[0]
    for i in range(tokens // CHUNK):
        rows = slice(i * CHUNK, (i + 1) * CHUNK)
        normed, _ = normalize(x_ref[rows, :].astype(f32))
        first_ref[rows, :] = (
            normed * (1.0 + mod_ref[i : i + 1, part(1)]) + mod_ref[i : i + 1, part(0)]
        ).astype(bf16)
    turned_ref[...] = first_ref[...].T
    writes = [
        pltpu.make_async_copy(weight.at[c], weight_ref.at[c], sems.at[c]) for c in range(COLUMNS)
    ]
    wait_for(weight.at[3], sems.at[3])
    writes[3].start()
    for c, out in enumerate((query_ref, keys_ref, values_ref)):
        wait_for(weight.at[c], sems.at[c])
        writes[c].start()
        if c == 2:
            out[...] = matmul(first_ref[...], weight[c]).astype(bf16)
        else:
            total[...] = matmul(first_ref[...], weight[c])

            @pl.loop(0, tokens // CHUNK)
            def _(i):
                rows = pl.ds(pl.multiple_of(i * CHUNK, CHUNK), CHUNK)
                out[rows, :] = rotate(total[rows, :], cos_ref[rows, :], sin_ref[rows, :]).astype(bf16)

    for write in writes:
        write.wait()


def window(head):
    start = head * HEAD_DIM // LANES * LANES
    stop = -(-(head + 1) * HEAD_DIM // LANES) * LANES
    lane = lax.broadcasted_iota(jnp.int32, (1, stop - start), 1) + start
    inside = (lane >= head * HEAD_DIM) & (lane < (head + 1) * HEAD_DIM)
    return slice(start, stop), inside


def soft_scores(left, right, allowed, axis):
    scores = times_transposed(left, right) * HEAD_DIM ** (-0.5)
    scores = jnp.where(allowed, scores, masked_score)
    exponent = jnp.exp(scores - jnp.max(scores, axis=axis, keepdims=True))
    return exponent * (1.0 / jnp.sum(exponent, axis=axis, keepdims=True))


def attend_kernel(
    query_ref, keys_ref, values_ref, column_ids, row_ids, x_ref, mod_ref,
    weight, turned_ref, branch_ref, middle_ref, second_ref, mixed,
):
    allowed = column_ids[...] == row_ids[...]
    for head in range(HEADS):
        lanes, inside = window(head)
        query = jnp.where(inside, query_ref[:, lanes], jnp.zeros((), bf16))
        probs = soft_scores(query, keys_ref[:, lanes], allowed, 1).astype(bf16)
        mixed[:, lanes] = jnp.where(inside, matmul(probs, values_ref[:, lanes]), mixed[:, lanes])
    attended = mixed[...].astype(bf16)
    turned_ref[...] = attended.T
    branch_ref[...] = matmul(attended, weight[0])
    for i in range(BLOCK // CHUNK):
        rows = slice(i * CHUNK, (i + 1) * CHUNK)
        mod = mod_ref.at[0]
        middle = x_ref[rows, :].astype(f32) + mod[i : i + 1, part(0)] * branch_ref[rows, :]
        middle_ref[rows, :] = middle
        normed, _ = normalize(middle)
        second_ref[rows, :] = (
            normed * (1.0 + mod[i : i + 1, part(2)]) + mod[i : i + 1, part(1)]
        ).astype(bf16)


def tile_copies(r, where, count, tile, pair, downs):
    place, mine, side = where
    t, j = tile
    column = mine ^ j
    rows, width = r["gate"].shape[0], r["hidden_w"].shape[1]
    sem = r["pair_sems"].at[t]
    copies = [
        pltpu.make_async_copy(
            r[name].at[:, take(column * width, width)], r["pair_w"].at[t, which, take(place * rows, rows)], sem
        )
        for which, name in enumerate(("gate", "up"))
    ]
    first = first_part(rows)
    for other in range(HALVES):
        for by in range(1, count):
            owner = (place + (count - by)) % count
            if j < 3:
                spans = [(pair[other][0].at[by - 1], 0, rows)]
            else:
                spans = [(pair[other][0].at[by - 1], 0, first), (pair[other][1].at[by - 1], first, rows - first)]
            for ref, start, size in spans:
                to = r["pair_w"].at[t, side ^ other, take(owner * rows + start, size)]
                copies.append(pltpu.make_async_copy(ref, to, sem))
    for copy in copies:
        copy.start()

    sem = r["down_sems"].at[t]
    target = r["down_w"].at[t]
    piece = width // PIECES

    @pl.when(column == place)
    def _():
        pltpu.make_async_copy(r["down"], target, sem).start()

    @pl.when(column != place)
    def _():
        by = jnp.maximum((place + count - column) % count, 1)
        for i, other, start, size, ref in placed(downs, piece):
            to = target.at[take(((mine ^ i) * HALVES + (side ^ other)) * piece + start, size)]
            pltpu.make_async_copy(ref.at[by - 1], to, sem).start()


def ffn_kernel(count, js, names, *refs):
    r = dict(zip(names, refs, strict=True))
    r["hidden_w"] = r["hidden"]
    first, last = js[0] == 0, js[-1] == COLUMNS - 1
    step = pl.program_id(0)
    tile = r["hidden"].shape[1]
    tokens = r["second"].shape[0]
    second, feed_back = r["second"], r["feed_back"]
    feed, second_back = r["feed"], r["second_back"]

    @pl.when(step == 0)
    def _():
        where = r["where"][0], r["where"][1], r["where"][2]
        for t, j in enumerate(js):
            pair = [
                [r[f"pair{j}_{other}_{i}"] for i in range(1 if j < 3 else 2)]
                for other in range(HALVES)
            ]
            tile_copies(r, where, count, (t, j), pair, [r[name] for name in names if name[:4] == "down" and name[5:].isdigit()])
        if first:
            r["turned"][...] = second[...].T
            for i in range(tokens // CHUNK):
                rows = slice(i * CHUNK, (i + 1) * CHUNK)
                upstream = r["cot"][rows, :].astype(f32) * r["factor"][0]
                feed_back[rows, :] = (upstream * r["mod"][i : i + 1, part(3)]).astype(bf16)

    pair_w, down_w = r["pair_w"].at[step], r["down_w"].at[step]
    wait_for(pair_w, r["pair_sems"].at[step])
    wait_for(down_w, r["down_sems"].at[step])
    sub = 256
    for n in range(tile // sub):
        lanes = slice(n * sub, (n + 1) * sub)
        gate = matmul(second[...], pair_w[0, :, lanes])
        upval = matmul(second[...], pair_w[1, :, lanes])
        hidden_back = times_transposed(feed_back[...], down_w[lanes, :])
        sigmoid = jax.nn.sigmoid(gate)
        silu = gate * sigmoid
        r["hidden"][:, lanes] = (silu * upval).astype(bf16)
        r["pair_back"][0, 1, :, lanes] = (hidden_back * silu).astype(bf16)
        r["pair_back"][0, 0, :, lanes] = (
            hidden_back * upval * (sigmoid * (1.0 + gate * (1.0 - sigmoid)))
        ).astype(bf16)

    r["hidden_turned"][0] = r["hidden"][...].T
    feed_part = matmul(r["hidden"][...], down_w[...])
    back_part = times_transposed(r["pair_back"][0, 0], pair_w[0]) + times_transposed(
        r["pair_back"][0, 1], pair_w[1]
    )

    @pl.when(step == 0)
    def _():
        feed[...] = feed_part if first else r["feed_in"][...] + feed_part
        second_back[...] = back_part if first else r["back_in"][...] + back_part

    @pl.when(step > 0)
    def _():
        feed[...] += feed_part
        second_back[...] += back_part

    if not last:
        return

    @pl.when(step == len(js) - 1)
    def _():
        for i in range(tokens // CHUNK):
            rows = slice(i * CHUNK, (i + 1) * CHUNK)
            gate_one = r["mod"][i : i + 1, part(0)]
            scale_two = r["mod"][i : i + 1, part(2)]
            gate_two = r["mod"][i : i + 1, part(3)]
            middle = r["middle"][rows, :]
            r["output"][rows, :] = (middle + gate_two * feed[rows, :]).astype(bf16)
            upstream = r["cot"][rows, :].astype(f32) * r["factor"][0]
            normed, inverse = normalize(middle)
            back = second_back[rows, :]
            middle_back = upstream + normalize_back(normed, inverse, back * (1.0 + scale_two))
            r["middle_back"][rows, :] = middle_back
            r["branch_back"][rows, :] = (middle_back * gate_one).astype(bf16)
            for where, values in enumerate(
                (middle_back * r["branch"][rows, :], back, back * normed, upstream * feed[rows, :])
            ):
                r["sums"][i : i + 1, part(where)] = jnp.sum(values, axis=0, keepdims=True)


ORDER = (1, 3, 2, 0)
SEND_X, KEEP_X, SEND_Y, KEEP_Y = (1, 3), (2, 0), (3, 2), (1, 0)
CUT = (SEND_X, KEEP_X, SEND_Y, KEEP_Y)


def put_grad(grad, other_ref, out_refs):
    step = pl.program_id(0)
    if other_ref is None:
        out_refs[0][0] = grad.astype(bf16)
        return
    total = (grad + other_ref[0].astype(f32)).astype(bf16)
    first = first_part(total.shape[1])
    for at, j in enumerate(ORDER):

        @pl.when(step == at)
        def _():
            for columns, ref in zip(CUT, out_refs, strict=True):
                if j in columns:
                    ref[0] = total[:, :first] if columns in (SEND_X, KEEP_X) else total[:, first:]


def cut_specs(count, rows, breadth):
    first = first_part(rows)
    shapes, specs = [], []
    for columns in CUT:
        size = first if columns in (SEND_X, KEEP_X) else rows - first
        shapes.append(struct((2, count, size, breadth), bf16))
        second = ORDER.index(columns[1])
        specs.append(
            pl.BlockSpec(
                (1, count, size, breadth),
                lambda s, where, second=second: (jnp.where(s >= second, 1, 0), 0, 0, 0),
            )
        )
    return tuple(shapes), tuple(specs)


def split_refs(mine, refs):
    return (refs[0], refs[1:]) if mine else (None, refs)


def pair_grad_kernel(mine, count, where_ref, turned_ref, own_ref, near_ref, far_ref, *refs):
    other_ref, out_refs = split_refs(mine, refs)
    for at, j in enumerate(ORDER):

        @pl.when(pl.program_id(0) == at)
        def _():
            back = {0: own_ref, 3: far_ref}.get(j, near_ref)
            grad = matmul(turned_ref[...], back[0, 0])
            put_grad(grad.reshape(count, grad.shape[0] // count, grad.shape[1]), other_ref, out_refs)


def down_grad_kernel(mine, where_ref, *refs):
    hiddens, feed_back_ref, out_ref = refs[:3], refs[3], refs[-1]
    other_ref = refs[4] if mine else None
    side = where_ref[2] if mine else where_ref[2] ^ 1
    count, _, rows, _ = out_ref.shape
    tiles = [(hidden, t) for hidden in hiddens for t in range(hidden.shape[0])]
    for j, (hidden, t) in enumerate(tiles):
        pieces = [hidden[t, take(((where_ref[1] ^ c) * HALVES + side) * rows, rows), :] for c in ORDER]
        grad = matmul(jnp.concatenate(pieces, axis=0), feed_back_ref[...]).reshape(COLUMNS, rows, WIDTH)
        owner = where_ref[1] ^ j
        if mine:
            grad = grad + other_ref[owner].astype(f32)
        out_ref[owner] = grad.astype(bf16)


def attn_grad_kernel(
    mine, where_ref, first_ref, attended_ref, joint_back_ref, branch_back_ref, *refs
):
    other_ref, out_refs = split_refs(mine, refs)
    column = where_ref[1] ^ where_ref[3 + pl.program_id(0)]
    side = where_ref[2] if mine else where_ref[2] ^ 1
    _, count, _, _ = out_refs[0].shape
    rows = WIDTH // count // HALVES

    def put(turned, right):
        taken = [turned[take((z * HALVES + side) * rows, rows), :] for z in range(count)]
        grad = matmul(jnp.concatenate(taken, axis=0), right[...])
        put_grad(grad.reshape(count, rows, WIDTH), other_ref, out_refs)

    @pl.when(column < 3)
    def _():
        put(first_ref, joint_back_ref)

    @pl.when(column == 3)
    def _():
        put(attended_ref, branch_back_ref)


def place_pair_kernel(where_ref, *refs):
    sources, outs = refs[:-2], refs[-2:]
    rows, tile = sources[0].shape
    for way in range(HALVES):

        @pl.when(where_ref[2] == way)
        def _():
            for j, other, start, size, ref in placed(sources, rows):
                lanes = take((where_ref[1] ^ j) * tile, tile)
                outs[way ^ other][start : start + size, lanes] = ref[...].astype(f32)


def place_down_kernel(rows, offset, where_ref, *refs):
    sources, out = refs[:-1], refs[-1]
    for j, other, start, size, ref in placed(sources, rows):
        piece = (where_ref[1] ^ j) * HALVES + (where_ref[2] ^ other)
        out[take(piece * rows + start, size), :] = ref[offset : offset + size, :].astype(f32)


def place_attn_kernel(rows, where_ref, *refs):
    sources, joint_ref, project_ref = refs[:-2], refs[-2], refs[-1]
    for column in range(COLUMNS):

        @pl.when(where_ref[1] == column)
        def _():
            for j, other, start, size, ref in placed(sources, rows):
                to = take((where_ref[2] ^ other) * rows + start, size)
                if column ^ j == 3:
                    project_ref[to, :] = ref[:size, :].astype(f32)
                else:
                    joint_ref[to, part(column ^ j)] = ref[:size, :].astype(f32)


def attend_back_kernel(
    query_ref, keys_ref, values_ref, branch_back_ref, column_ids, row_ids, cos_ref,
    sin_ref, weight, joint_back_ref, mixed_back, query_back, keys_back, values_back,
):
    mixed_back[...] = times_transposed(branch_back_ref[...], weight[0]).astype(bf16)
    allowed = column_ids[...] == row_ids[...]
    scaling = HEAD_DIM ** (-0.5)
    for head in range(HEADS):
        lanes, inside = window(head)
        zero = jnp.zeros((), bf16)
        query = jnp.where(inside, query_ref[:, lanes], zero)
        back = jnp.where(inside, mixed_back[:, lanes], zero)
        soft = soft_scores(keys_ref[:, lanes], query, allowed, 0)
        probs_back = times_transposed(values_ref[:, lanes], back)
        scores_back = (
            soft * (probs_back - jnp.sum(soft * probs_back, axis=0, keepdims=True))
        ).astype(bf16)
        query_back[:, lanes] = jnp.where(
            inside, contract_rows(scores_back, keys_ref[:, lanes]) * scaling, query_back[:, lanes]
        )
        keys_back[:, lanes] = jnp.where(
            inside, matmul(scores_back, query) * scaling, keys_back[:, lanes]
        )
        values_back[:, lanes] = jnp.where(
            inside, matmul(soft.astype(bf16), back), values_back[:, lanes]
        )

    @pl.loop(0, BLOCK // CHUNK)
    def _(i):
        rows = pl.ds(pl.multiple_of(i * CHUNK, CHUNK), CHUNK)
        cos, sin = cos_ref[rows, :], sin_ref[rows, :]
        joint_back_ref[rows, part(0)] = rotate(query_back[rows, :], cos, -sin).astype(bf16)
        joint_back_ref[rows, part(1)] = rotate(keys_back[rows, :], cos, -sin).astype(bf16)
        joint_back_ref[rows, part(2)] = values_back[rows, :].astype(bf16)


def first_back_kernel(
    joint_back_ref, x_ref, middle_back_ref, mod_ref, weight, grad_ref, sums_ref, first_back
):
    step = pl.program_id(0)
    product = times_transposed(joint_back_ref[...], weight[0])

    @pl.when(step == 0)
    def _():
        first_back[...] = product

    @pl.when(step > 0)
    def _():
        first_back[...] += product

    @pl.when(step == pl.num_programs(0) - 1)
    def _():
        finish_first_back(x_ref, middle_back_ref, mod_ref, grad_ref, sums_ref, first_back)


def finish_first_back(x_ref, middle_back_ref, mod_ref, grad_ref, sums_ref, first_back):
    for i in range(x_ref.shape[0] // CHUNK):
        rows = slice(i * CHUNK, (i + 1) * CHUNK)
        normed, inverse = normalize(x_ref[rows, :].astype(f32))
        back = first_back[rows, :]
        grad_ref[rows, :] = middle_back_ref[rows, :] + normalize_back(
            normed, inverse, back * (1.0 + mod_ref[i : i + 1, part(1)])
        )
        sums_ref[i : i + 1, part(0)] = jnp.sum(back, axis=0, keepdims=True)
        sums_ref[i : i + 1, part(1)] = jnp.sum(back * normed, axis=0, keepdims=True)


SMEM = pl.BlockSpec(memory_space=pltpu.SMEM)
VMEM = pl.BlockSpec(memory_space=pltpu.VMEM)
ANY = pl.BlockSpec(memory_space=pl.ANY)


def struct(shape, dtype):
    return jax.ShapeDtypeStruct(shape, dtype)


def params(mega=56):
    return pltpu.CompilerParams(vmem_limit_bytes=mega * MEGA)


def cost(microseconds):
    return pl.CostEstimate(flops=int(microseconds * 1e9), bytes_accessed=1000, transcendentals=0)


def by_block(*shape):
    return pl.BlockSpec(shape, lambda b: (b,) + (0,) * (len(shape) - 1))


def whole(*shape):
    return pl.BlockSpec(shape, lambda *_: (0,) * len(shape))


def first_call(where, x, mod, cos, sin, joint, project, arrived):
    tokens = x.shape[0]
    count = arrived[0].shape[0] + 1
    shape = struct((tokens, WIDTH), bf16)
    return pl.pallas_call(
        functools.partial(first_kernel, count),
        out_shape=(struct((WIDTH, tokens), bf16),)
        + (shape,) * 3
        + (struct((COLUMNS, WIDTH, WIDTH), bf16),),
        in_specs=[SMEM, VMEM, VMEM, VMEM, VMEM] + [ANY] * (2 + len(arrived)),
        out_specs=(VMEM,) * 4 + (ANY,),
        scratch_shapes=[
            pltpu.VMEM((COLUMNS, WIDTH, WIDTH), bf16),
            pltpu.VMEM((tokens, WIDTH), bf16),
            pltpu.VMEM((tokens, WIDTH), f32),
            pltpu.SemaphoreType.DMA((COLUMNS,)),
        ],
        compiler_params=params(),
        cost_estimate=cost(20),
    )(where, x, mod, cos, sin, joint, project, *arrived)


def attend_call(query, keys, values, ids, x, mod, weight):
    tokens = x.shape[0]
    return pl.pallas_call(
        attend_kernel,
        grid=(tokens // BLOCK,),
        out_shape=(
            struct((WIDTH, tokens), bf16),
            struct((tokens, WIDTH), f32),
            struct((tokens, WIDTH), f32),
            struct((tokens, WIDTH), bf16),
        ),
        in_specs=[by_block(BLOCK, WIDTH)] * 3
        + [by_block(BLOCK, 1), pl.BlockSpec((1, BLOCK), lambda b: (0, b)), by_block(BLOCK, WIDTH)]
        + [by_block(1, BLOCK // CHUNK, 4 * WIDTH), pl.BlockSpec((1, WIDTH, WIDTH), lambda b: (3, 0, 0))],
        out_specs=(pl.BlockSpec((WIDTH, BLOCK), lambda b: (0, b)),) + (by_block(BLOCK, WIDTH),) * 3,
        scratch_shapes=[pltpu.VMEM((BLOCK, WIDTH), f32)],
        compiler_params=params(),
        cost_estimate=cost(2),
    )(
        query, keys, values, ids[:, None], ids[None, :], x,
        mod.reshape(tokens // BLOCK, BLOCK // CHUNK, 4 * WIDTH), weight,
    )


def ffn_call(js, where, given, shards, pairs, downs):
    second = given["second"]
    tokens = second.shape[0]
    ff = shards["gate"].shape[1]
    tile = ff // COLUMNS
    count = ff // shards["down"].shape[0]
    chunks = tokens // CHUNK
    first, last = js[0] == 0, js[-1] == COLUMNS - 1
    full = whole(tokens, WIDTH)
    wide = struct((tokens, WIDTH), f32)
    narrow = struct((tokens, WIDTH), bf16)
    inputs = [("where", where, SMEM), ("second", second, full)]
    if first or last:
        inputs += [
            ("factor", given["factor"], SMEM),
            ("cot", given["cot"], full),
            ("mod", given["mod"], whole(chunks, 4 * WIDTH)),
        ]
    if not first:
        inputs += [
            ("feed_back", given["feed_back"], full),
            ("feed_in", given["feed"], full),
            ("back_in", given["second_back"], full),
        ]
    if last:
        inputs += [("middle", given["middle"], full), ("branch", given["branch"], full)]
    inputs += [(name, shards[name], ANY) for name in ("gate", "up", "down")]
    for j in js:
        for other in range(HALVES):
            inputs += [(f"pair{j}_{other}_{i}", a, ANY) for i, a in enumerate(pairs[other][j])]
    inputs += [(f"down_{i}", a, ANY) for i, a in enumerate(downs)]
    outputs = [
        (
            "hidden_turned",
            struct((len(js), tile, tokens), bf16),
            pl.BlockSpec((1, tile, tokens), lambda t: (t, 0, 0)),
        ),
        (
            "pair_back",
            struct((len(js), HALVES, tokens, tile), bf16),
            pl.BlockSpec((1, HALVES, tokens, tile), lambda t: (t, 0, 0, 0)),
        ),
    ]
    if first:
        outputs += [
            ("turned", struct((WIDTH, tokens), bf16), whole(WIDTH, tokens)),
            ("feed_back", narrow, full),
        ]
    sums = ("feed", "second_back")
    scratch = [
        ("pair_w", pltpu.VMEM((len(js), HALVES, WIDTH, tile), bf16)),
        ("down_w", pltpu.VMEM((len(js), ff // count, WIDTH), bf16)),
        ("hidden", pltpu.VMEM((tokens, tile), bf16)),
        ("pair_sems", pltpu.SemaphoreType.DMA((len(js),))),
        ("down_sems", pltpu.SemaphoreType.DMA((len(js),))),
    ]
    if last:
        outputs += [
            ("output", narrow, full),
            ("middle_back", wide, full),
            ("branch_back", narrow, full),
            ("sums", struct((chunks, 4 * WIDTH), f32), whole(chunks, 4 * WIDTH)),
        ]
        scratch += [(name, pltpu.VMEM((tokens, WIDTH), f32)) for name in sums]
    else:
        outputs += [(name, wide, full) for name in sums]
    names = [each[0] for each in inputs + outputs + scratch]
    found = pl.pallas_call(
        functools.partial(ffn_kernel, count, js, names),
        grid=(len(js),),
        out_shape=tuple(shape for _, shape, _ in outputs),
        in_specs=[spec for _, _, spec in inputs],
        out_specs=tuple(spec for _, _, spec in outputs),
        scratch_shapes=[shape for _, shape in scratch],
        compiler_params=params(),
        cost_estimate=cost(2 if first else 12 * len(js)),
    )(*[array for _, array, _ in inputs])
    return {name: array for (name, _, _), array in zip(outputs, found, strict=True)}


def by_column(call, count, rows, breadth, in_specs, where, arrays, other):
    shapes, specs = cut_specs(count, rows, breadth)
    block = pl.BlockSpec((1, count, rows, breadth), lambda s, where: (s, 0, 0, 0))
    if other is None:
        shapes, specs = (struct((COLUMNS, count, rows, breadth), bf16),), (block,)
    else:
        in_specs, arrays = in_specs + [block], arrays + (other,)
    found = pl.pallas_call(
        call,
        out_shape=shapes,
        grid_spec=pltpu.PrefetchScalarGridSpec(
            num_scalar_prefetch=1, grid=(COLUMNS,), in_specs=in_specs, out_specs=specs
        ),
        compiler_params=params(),
        cost_estimate=cost(3),
    )(where, *arrays)
    return found[0] if other is None else found


def pair_grad_call(count, where, turned, backs, other=None):
    tokens, tile = backs[0].shape[2:]
    mine = other is not None

    def spec(tile_of):
        return pl.BlockSpec(
            (1, 1, tokens, tile),
            lambda s, where: (tile_of(where[3 + s]), where[2] if mine else where[2] ^ 1, 0, 0),
        )

    return by_column(
        functools.partial(pair_grad_kernel, mine, count),
        count, WIDTH // count, tile,
        [whole(WIDTH, tokens), spec(lambda j: 0), spec(lambda j: jnp.clip(j - 1, 0, 1)), spec(lambda j: 0)],
        where, (turned,) + tuple(backs), other,
    )


def attn_grad_call(count, where, first, attended, joint_back, branch_back, other=None):
    tokens = first.shape[1]
    return by_column(
        functools.partial(attn_grad_kernel, other is not None),
        count, WIDTH // count // HALVES, WIDTH,
        [
            whole(WIDTH, tokens),
            whole(WIDTH, tokens),
            pl.BlockSpec((tokens, WIDTH), lambda s, where: (0, jnp.minimum(where[1] ^ where[3 + s], 2))),
            whole(tokens, WIDTH),
        ],
        where, (first, attended, joint_back, branch_back), other,
    )


def down_grad_call(count, where, hiddens, feed_back, other=None):
    ff = sum(h.shape[0] * h.shape[1] for h in hiddens)
    out = struct((count, COLUMNS, ff // count // PIECES, WIDTH), bf16)
    arrays = tuple(hiddens) + (feed_back,) + (() if other is None else (other,))
    return pl.pallas_call(
        functools.partial(down_grad_kernel, other is not None),
        out_shape=out,
        in_specs=[SMEM] + [VMEM] * len(arrays),
        out_specs=VMEM,
        compiler_params=params(),
        cost_estimate=cost(3),
    )(where, *arrays)


def place_call(kernel, where, arrays, outs):
    return pl.pallas_call(
        kernel,
        out_shape=outs,
        in_specs=[SMEM] + [VMEM] * len(arrays),
        out_specs=jax.tree.map(lambda _: VMEM, outs),
        compiler_params=params(),
        cost_estimate=cost(4),
    )(where, *arrays)


def attend_back_call(query, keys, values, branch_back, ids, cos, sin, weight):
    tokens = query.shape[0]
    block = by_block(BLOCK, WIDTH)
    return pl.pallas_call(
        attend_back_kernel,
        grid=(tokens // BLOCK,),
        out_shape=struct((tokens, 3 * WIDTH), bf16),
        in_specs=[block, block, block, block]
        + [by_block(BLOCK, 1), pl.BlockSpec((1, BLOCK), lambda b: (0, b)), block, block]
        + [pl.BlockSpec((1, WIDTH, WIDTH), lambda b: (3, 0, 0))],
        out_specs=by_block(BLOCK, 3 * WIDTH),
        scratch_shapes=[
            pltpu.VMEM((BLOCK, WIDTH), bf16),
            pltpu.VMEM((BLOCK, WIDTH), f32),
            pltpu.VMEM((BLOCK, WIDTH), f32),
            pltpu.VMEM((BLOCK, WIDTH), f32),
        ],
        compiler_params=params(),
        cost_estimate=cost(8),
    )(query, keys, values, branch_back, ids[:, None], ids[None, :], cos, sin, weight)


def first_back_call(joint_back, x, middle_back, mod, weight):
    tokens = x.shape[0]
    chunks = tokens // CHUNK
    full = whole(tokens, WIDTH)
    return pl.pallas_call(
        first_back_kernel,
        grid=(3,),
        out_shape=(struct((tokens, WIDTH), f32), struct((chunks, 2 * WIDTH), f32)),
        in_specs=[
            pl.BlockSpec((tokens, WIDTH), lambda c: (0, c)),
            full,
            full,
            whole(chunks, 2 * WIDTH),
            pl.BlockSpec((1, WIDTH, WIDTH), lambda c: (c, 0, 0)),
        ],
        out_specs=(full, whole(chunks, 2 * WIDTH)),
        scratch_shapes=[pltpu.VMEM((tokens, WIDTH), f32)],
        compiler_params=params(),
        cost_estimate=cost(2),
    )(joint_back, x, middle_back, mod, weight)


def shifts(count, by):
    return [(i, (i + by) % count) for i in range(count)]


def pick(array, index):
    return lax.dynamic_index_in_dim(array, index, 0, keepdims=False)


def across(bit):
    return [(i, i ^ bit) for i in range(PIECES)]


def swap(array, bit):
    return lax.ppermute(array, "bucket", across(bit))


def after(arrays, *others):
    return lax.optimization_barrier((arrays, others))[0]


def add(left, right):
    return (left.astype(f32) + right.astype(f32)).astype(bf16)


def over_z(piece):
    count = lax.axis_size("fsdp")
    return [lax.ppermute(piece, "fsdp", shifts(count, by)) for by in range(1, count)]


def gather_z(piece, *others):
    count = lax.axis_size("fsdp")
    place = lax.axis_index("fsdp")
    full = after(lax.all_gather(piece, "fsdp", axis=0, tiled=False), *others)
    return jnp.stack([pick(full, (place + count - by) % count) for by in range(1, count)])


def cross(by_x, by_y, first):
    if first is not None:
        by_x, by_y = by_x[..., :first, :], by_y[..., first:, :]
    return swap(by_x, 4), swap(by_y, 2)


def both(here):
    return here + tuple(None if array is None else swap(array, 1) for array in here)


def direct(piece):
    return piece, swap(piece, 2), swap(piece, 4), swap(piece, 6)


def spread_whole(pieces):
    first = first_part(pieces.shape[1])

    def of(side):
        own, by_x, by_y, far = (pieces[c * HALVES + side] for c in range(COLUMNS))
        return own, by_x, by_y, far[:first], far[first:]

    return of(0) + of(1)


def halve_once(cut):
    send_x, (a2, a0), send_y, (b1, b0) = cut
    from_x, from_y = swap(send_x, 2), swap(send_y, 4)
    return add(a0, from_x[0]), add(a2, from_x[1]), add(b0, from_y[1]), add(b1, from_y[0])


def halve_twice(once, *others):
    a0, a2, b0, b1 = once
    if others:
        a0, b0 = after((a0, b0), *others)
    return jnp.concatenate([add(a0, swap(a2, 4)), add(b0, swap(b1, 2))], axis=-2)


def send_z(parts):
    count = lax.axis_size("fsdp")
    place = lax.axis_index("fsdp")
    return [
        lax.ppermute(pick(parts, (place + by) % count), "fsdp", shifts(count, by))
        for by in range(1, count)
    ]


def total_z(parts, others):
    total = pick(parts, lax.axis_index("fsdp")).astype(f32)
    for array in others:
        total = total + array.astype(f32)
    return total.astype(bf16)


def sum_z(parts):
    return total_z(parts, send_z(parts))


def cut_down(part, first):
    cut = []
    for columns in CUT:
        both_columns = jnp.stack([part[ORDER.index(j)] for j in columns])
        cut.append(both_columns[:, :first] if columns in (SEND_X, KEEP_X) else both_columns[:, first:])
    return cut


def uncut(cut):
    def of(j, pair):
        columns = next(c for c in pair if j in c)
        return cut[CUT.index(columns)][columns.index(j)]

    return jnp.stack(
        [jnp.concatenate([of(j, (SEND_X, KEEP_X)), of(j, (SEND_Y, KEEP_Y))], axis=1) for j in ORDER]
    )


def sum_whole(mine, theirs):
    parts = jnp.stack([mine, theirs], axis=1)
    parts = jnp.stack([parts[ORDER.index(c)] for c in range(COLUMNS)])
    rows, breadth = mine.shape[2:]
    parts = lax.psum(parts, "bucket").transpose(2, 0, 1, 3, 4)
    return spread_whole(sum_z(parts).reshape(PIECES, rows, breadth))


def arrived_whole(pieces):
    count = lax.axis_size("fsdp")
    place = lax.axis_index("fsdp")
    first = first_part(pieces.shape[1])
    full = lax.all_gather(pieces, "fsdp", axis=0, tiled=False)
    full = jnp.stack([pick(full, (place + count - by) % count) for by in range(1, count)])

    def of(side):
        own, by_x, by_y, far = (full[:, c * HALVES + side] for c in range(COLUMNS))
        return own, by_x, by_y, far[:, :first], far[:, first:]

    return of(0) + of(1)


def to_group(rows, count, place):
    relative = jnp.stack(
        [pick(rows, place)]
        + [
            lax.ppermute(pick(rows, (place + by) % count), "fsdp", shifts(count, by))
            for by in range(1, count)
        ]
    )
    return jnp.stack([pick(relative, (place - j) % count) for j in range(count)])


def on_device(
    inputs,
    condition,
    segment_ids,
    grid_widths,
    bucket_counts,
    modulate_weight,
    joint_weight,
    project_weight,
    gate_weight,
    up_weight,
    down_weight,
    cotangent,
):
    fsdp_count = lax.axis_size("fsdp")
    place = lax.axis_index("fsdp")
    bucket = lax.axis_index("bucket")
    height = joint_weight.shape[0]
    half = height // HALVES
    ff = gate_weight.shape[1]
    tile = ff // COLUMNS
    down_rows = down_weight.shape[0] // PIECES
    slots = condition.shape[0]

    cond_float = condition.astype(f32)
    lifted = jax.nn.silu(cond_float).astype(bf16)
    lifted_rows = to_group(
        lifted.reshape(slots, fsdp_count, height).transpose(1, 0, 2), fsdp_count, place
    ).reshape(fsdp_count * slots, height)
    one_hot = (
        segment_ids[::CHUNK, None] == jnp.arange(slots, dtype=jnp.int32)[None, :]
    ).astype(f32)

    def modulation_parts(weight, rows):
        parts = matmul(rows, weight).reshape(fsdp_count, slots, weight.shape[1])
        return [pick(parts, place)] + [
            lax.ppermute(pick(parts, (place + by) % fsdp_count), "fsdp", shifts(fsdp_count, by))
            for by in range(1, fsdp_count)
        ]

    def modulation(parts):
        return jnp.dot(
            one_hot,
            sum(parts[1:], parts[0]),
            precision=lax.Precision.HIGHEST,
            preferred_element_type=f32,
        )

    first_rows = modulation_parts(modulate_weight[:, : 2 * WIDTH], lifted_rows)
    mod_one = modulation(first_rows)
    fast = lax.axis_size("bucket") == PIECES
    if fast:
        column, side = bucket // HALVES, bucket % HALVES
        where = jnp.stack([place, column, side] + [jnp.int32(j) for j in ORDER])
        attn_piece = jnp.where(
            column == 3,
            lax.dynamic_slice(project_weight, (side * half, 0), (half, WIDTH)),
            lax.dynamic_slice(joint_weight, (side * half, column * WIDTH), (half, WIDTH)),
        )
        ffn_piece = jnp.where(
            side == 0,
            lax.dynamic_slice(gate_weight, (0, column * tile), (height, tile)),
            lax.dynamic_slice(up_weight, (0, column * tile), (height, tile)),
        )
        down_piece = lax.dynamic_slice_in_dim(down_weight, bucket * down_rows, down_rows, 0)
        attn_z = gather_z(attn_piece, first_rows)
        down_k = over_z(after(down_piece, attn_z))
        attn_x, attn_y = swap(attn_z, 2), swap(attn_z, 4)
        attn_x, attn_y, down_k = after((attn_x, attn_y, down_k))
        attn_far = cross(attn_x, attn_y, first_part(half))
        pair_z = gather_z(after(ffn_piece, down_k))
        down_z = jnp.stack(down_k)
        attn_arrived = both((attn_z, attn_x, attn_y) + attn_far)
        inputs, down_z = after((inputs, down_z), attn_far)
        down_x, down_y = swap(down_z, 2), swap(down_z, 4)
        inputs = after(inputs, down_z)
    else:
        where = jnp.stack([place, 0 * place, 0 * place] + [jnp.int32(j) for j in ORDER])
        attn_arrived = arrived_whole(
            jnp.concatenate([joint_weight, project_weight], axis=1)
            .reshape(HALVES, half, COLUMNS, WIDTH)
            .transpose(2, 0, 1, 3)
            .reshape(PIECES, half, WIDTH)
        )
        pairs = arrived_whole(
            jnp.stack([gate_weight, up_weight])
            .reshape(HALVES, height, COLUMNS, tile)
            .transpose(2, 0, 1, 3)
            .reshape(PIECES, height, tile)
        )
        downs = arrived_whole(down_weight.reshape(PIECES, down_rows, WIDTH))

    if fast:
        lifted_rows = after(lifted_rows, down_k)
    late_rows = modulation_parts(modulate_weight[:, 2 * WIDTH :], lifted_rows)
    counts = bucket_counts.astype(f32)
    mine = jnp.sum(jnp.where(jnp.arange(counts.shape[0], dtype=jnp.int32) == bucket, counts, 0.0))
    factor = (mine * counts.shape[0] / jnp.sum(counts)).reshape(1)
    cos, sin = rope_tables(segment_ids, grid_widths)

    first, query, keys, values, weight = first_call(
        where, inputs, mod_one, cos, sin, joint_weight, project_weight, attn_arrived
    )
    if fast:
        late_rows = [late_rows[0], *after(late_rows[1:], query)]
        down_x, down_y = after((down_x, down_y), query)
        down_far = cross(down_x, down_y, first_part(down_rows))
        downs = (down_z, down_x, down_y) + down_far
        pair_z = after(pair_z, query)
        pair_x, pair_y = swap(pair_z, 2), swap(pair_z, 4)
    mod = modulation(late_rows)
    attended, branch, middle, second = attend_call(
        query, keys, values, segment_ids, inputs, mod, weight
    )
    shards = dict(gate=gate_weight, up=up_weight, down=down_weight)
    given = dict(
        second=second, factor=factor, cot=cotangent, mod=mod, middle=middle, branch=branch
    )
    if fast:
        downs = both(after(downs, second))
        pairs = (pair_z, pair_x, pair_y, None, None, swap(pair_z, 1), None, None, None, None)
    pairs = [
        [[group] for group in pairs[5 * k : 5 * k + 3]] + [list(pairs[5 * k + 3 : 5 * k + 5])]
        for k in range(HALVES)
    ]
    found = ffn_call((0,), where, given, shards, pairs, downs)
    turned, feed_back = found["turned"], found["feed_back"]
    steps = [found]
    if fast:
        pair_x, pair_y = after((pair_x, pair_y), feed_back)
        far = cross(pair_x, pair_y, first_part(height))
        pairs[1][1:3] = [swap(pair_x, 1)], [swap(pair_y, 1)]
    for js in ((1, 2), (3,)):
        given.update(feed_back=feed_back, feed=found["feed"], second_back=found["second_back"])
        if fast and js == (3,):
            far = after(far, found["feed"])
            pairs[0][3], pairs[1][3] = list(far), [swap(array, 1) for array in far]
        found = ffn_call(js, where, given, shards, pairs, downs)
        steps.append(found)
    output, middle_back, branch_back = found["output"], found["middle_back"], found["branch_back"]
    late_sums = found["sums"]

    def by_slot(chunk_sums):
        return lax.dot_general(
            one_hot,
            chunk_sums,
            (((0,), (0,)), ((), ())),
            precision=lax.Precision.HIGHEST,
            preferred_element_type=f32,
        ).astype(bf16)

    def near_rows(rows):
        return jnp.concatenate([rows] + over_z(rows), axis=0)

    late_rows = jnp.concatenate([by_slot(late_sums), lifted], axis=1)
    late_k = over_z(late_rows)

    count = fsdp_count
    hiddens = [step["hidden_turned"] for step in steps]
    backs = [step["pair_back"] for step in steps]
    pair_theirs = pair_grad_call(count, where, turned, backs)
    late_k, pair_theirs = after((late_k, pair_theirs))
    near_late = jnp.concatenate([late_rows] + late_k, axis=0)
    late = lax.all_gather(near_late, "bucket", axis=0, tiled=True)
    if fast:
        pair_other = swap(pair_theirs, 1)
        feed_back = after(feed_back, pair_theirs)
    else:
        pair_other = jnp.zeros_like(pair_theirs)
    down_theirs = down_grad_call(count, where, hiddens, feed_back)
    if fast:
        pair_other, down_theirs = after((pair_other, down_theirs))
        down_other = swap(down_theirs, 1)
    else:
        down_other = jnp.zeros_like(down_theirs)
    pair_cut = pair_grad_call(count, where, turned, backs, pair_other)
    if fast:
        feed_back = after(feed_back, pair_cut)
    down_mine = down_grad_call(count, where, hiddens, feed_back, down_other)
    if fast:
        down_mine, late = after((down_mine, late))
        down_part = lax.psum_scatter(down_mine, "fsdp", scatter_dimension=0, tiled=False)
        branch_back = after(branch_back, down_mine)
    joint_back = attend_back_call(
        query, keys, values, branch_back, segment_ids, cos, sin, weight
    )
    attn_theirs = attn_grad_call(count, where, first, attended, joint_back, branch_back)
    if fast:
        send_x, keep_x, send_y, keep_y = pair_cut
        keep_x, keep_y, attn_theirs = after((keep_x, keep_y, attn_theirs))
        pair_once = halve_once((send_x, keep_x, send_y, keep_y))
        pair_once, attn_theirs, middle_back = after((pair_once, attn_theirs, middle_back))
        attn_other = swap(attn_theirs, 1)
    grad_inputs, early_sums = first_back_call(joint_back, inputs, middle_back, mod_one, weight)
    if fast:
        a0, a2, b0, b1 = pair_once
        a0, b0, grad_inputs = after((a0, b0, grad_inputs))
        pair_parts, branch_back = after((halve_twice((a0, a2, b0, b1)), branch_back))
        attn_cut = attn_grad_call(
            count, where, first, attended, joint_back, branch_back, attn_other
        )
        attn_cut, down_part, pair_parts, early_sums = after(
            (attn_cut, down_part, pair_parts, early_sums)
        )
        pair_sum = lax.psum_scatter(pair_parts, "fsdp", scatter_dimension=0, tiled=False)
    near_early = near_rows(by_slot(early_sums))
    early = lax.all_gather(near_early, "bucket", axis=0, tiled=True)
    slope_rows = times_transposed(
        jnp.concatenate([near_early, near_late[:, : 4 * WIDTH]], axis=1), modulate_weight
    ).reshape(fsdp_count, slots, height)
    slopes = [slope_rows[0]] + [
        lax.ppermute(slope_rows[count - by], "fsdp", shifts(count, by)) for by in range(1, count)
    ]
    if fast:
        down_cut = cut_down(down_part, first_part(down_rows))
        send_x, keep_x, send_y, keep_y = (
            jnp.concatenate([attn.reshape(2, -1, WIDTH), down], axis=1)
            for attn, down in zip(attn_cut, down_cut, strict=True)
        )
        keep_x, keep_y, slopes = after((keep_x, keep_y, slopes))
        (a0, a2, b0, b1), pair_sum = after((halve_once((send_x, keep_x, send_y, keep_y)), pair_sum))
        pair_x, pair_y = swap(pair_sum, 2), swap(pair_sum, 4)
        ahead, behind = add(a0, swap(a2, 4)), add(b0, swap(b1, 2))
        at, other_at = (part.shape[1] * part.shape[2] for part in (attn_cut[0], attn_cut[2]))
        attn_parts = jnp.concatenate(
            [half.reshape(count, -1, WIDTH) for half in (ahead[:at], behind[:other_at])], axis=1
        )
        down_total = jnp.concatenate([ahead[at:], behind[other_at:]], axis=0)
        attn_parts, down_total, pair_x, pair_y = after((attn_parts, down_total, pair_x, pair_y))
        attn_z = send_z(attn_parts)
        pair_sums = (pair_sum, pair_x, pair_y) + cross(pair_x, pair_y, first_part(height))
        attn_z, pair_sums = after((attn_z, both(pair_sums)))
        attn_sum = total_z(attn_parts, attn_z)
    else:
        down_sums = sum_whole(down_mine.swapaxes(0, 1), down_theirs.swapaxes(0, 1))
        pair_sums = sum_whole(uncut(pair_cut), pair_theirs)
        attn_cut = attn_grad_call(
            count, where, first, attended, joint_back, branch_back, jnp.zeros_like(attn_theirs)
        )
        attn_sums = sum_whole(uncut(attn_cut), attn_theirs)
    if fast:
        early, attn_sum = after((early, attn_sum))
        both_sums = direct(jnp.concatenate([attn_sum, down_total], axis=0))
    all_back = jnp.concatenate([early, late[:, : 4 * WIDTH]], axis=1)
    all_lifted = lax.dynamic_slice_in_dim(late, 4 * WIDTH + place * height, height, 1)
    modulate_gradient = contract_rows(all_lifted, all_back)
    pair_grad = place_call(
        place_pair_kernel, where, pair_sums, (struct(gate_weight.shape, f32),) * 2
    )
    if fast:
        both_sums, pair_grad, modulate_gradient = after((both_sums, pair_grad, modulate_gradient))
        attn_sums = down_sums = both(both_sums)
    slopes = jnp.stack(slopes)
    condition_slope = (
        jnp.stack([pick(slopes, (place + count - j) % count) for j in range(count)])
        .transpose(1, 0, 2)
        .reshape(slots, WIDTH)
    )
    grad_condition = condition_slope * silu_slope(cond_float)
    down_grad = place_call(functools.partial(place_down_kernel, down_rows, half if fast else 0), where, down_sums, struct(down_weight.shape, f32))
    attn_grad = place_call(
        functools.partial(place_attn_kernel, half),
        where,
        attn_sums,
        (struct(joint_weight.shape, f32), struct(project_weight.shape, f32)),
    )

    return (
        output,
        grad_inputs,
        grad_condition,
        modulate_gradient,
        *attn_grad,
        *pair_grad,
        down_grad,
    )


def solution(mesh):
    spread = P(("bucket", "fsdp"), None)
    rows = P("fsdp", None)
    in_specs = (
        spread, spread, P(("bucket", "fsdp")), P(("bucket", "fsdp")), P(),
        rows, rows, rows, rows, rows, rows, spread,
    )
    out_specs = (spread, spread, spread, rows, rows, rows, rows, rows, rows)
    return jax.shard_map(
        on_device, mesh=mesh, in_specs=in_specs, out_specs=out_specs, check_vma=False
    )
```

```python
import functools

import jax
import jax.numpy as jnp
from jax import lax
from jax.experimental import pallas as pl
from jax.experimental.pallas import tpu as pltpu
from jax.sharding import PartitionSpec as P

HEADS = 16
HEAD_DIM = 72
WIDTH = HEADS * HEAD_DIM
QUARTER = HEAD_DIM // 4
BLOCK = 256
CHUNK = 64
COLUMNS = 4
HALVES = 2
PIECES = COLUMNS * HALVES
LANES = 128

epsilon = 1e-06
masked_score = -1e30
f32 = jnp.float32
bf16 = jnp.bfloat16
MEGA = 2**20


def normalize(values):
    average = jnp.mean(values, axis=-1, keepdims=True)
    centered = values - average
    inverse = lax.rsqrt(jnp.mean(centered * centered, axis=-1, keepdims=True) + epsilon)
    return (centered * inverse, inverse)


def normalize_back(normed, inverse, upstream):
    return inverse * (
        upstream
        - jnp.mean(upstream, axis=-1, keepdims=True)
        - normed * jnp.mean(upstream * normed, axis=-1, keepdims=True)
    )


def matmul(left, right):
    return jnp.dot(left, right, preferred_element_type=f32)


def contract_rows(left, right):
    return lax.dot_general(left, right, (((0,), (0,)), ((), ())), preferred_element_type=f32)


def times_transposed(left, right):
    return lax.dot_general(left, right, (((1,), (1,)), ((), ())), preferred_element_type=f32)


def silu_slope(values):
    sigmoid = jax.nn.sigmoid(values)
    return sigmoid * (1.0 + values * (1.0 - sigmoid))


def rope_tables(segments, widths):
    slots = widths.shape[0]
    one_hot = (segments[:, None] == jnp.arange(slots, dtype=jnp.int32)[None, :]).astype(jnp.int32)
    counts = jnp.sum(one_hot, axis=0)
    starts = jnp.cumsum(counts) - counts
    start_token = jnp.sum(one_hot * starts[None, :], axis=1)
    width_token = jnp.maximum(jnp.sum(one_hot * widths[None, :], axis=1), 1)
    place = jnp.arange(segments.shape[0], dtype=jnp.int32) - start_token
    row_place = (place // width_token).astype(f32)
    col_place = (place % width_token).astype(f32)
    freqs = 10000.0 ** (-jnp.arange(QUARTER, dtype=f32) / QUARTER)
    angle_row = row_place[:, None] * freqs[None, :]
    angle_col = col_place[:, None] * freqs[None, :]
    cos_row, sin_row, cos_col, sin_col = (
        jnp.cos(angle_row),
        jnp.sin(angle_row),
        jnp.cos(angle_col),
        jnp.sin(angle_col),
    )
    cos = jnp.concatenate([cos_row, cos_row, cos_col, cos_col], axis=1)
    sin = jnp.concatenate([-sin_row, sin_row, -sin_col, sin_col], axis=1)
    return jnp.tile(cos, (1, HEADS)), jnp.tile(sin, (1, HEADS))


def part(index):
    return slice(index * WIDTH, (index + 1) * WIDTH)


def rotate(values, cos, sin):
    lane = lax.broadcasted_iota(jnp.int32, (1, WIDTH), 1)
    leading = lane % (2 * QUARTER) < QUARTER
    partner = jnp.where(
        leading,
        pltpu.roll(values, WIDTH - QUARTER, 1),
        pltpu.roll(values, QUARTER, 1),
    )
    return values * cos + partner * sin


def take(start, size):
    return pl.ds(pl.multiple_of(start, 128 if size % 128 == 0 else 16), size)


def first_part(rows):
    return -(-rows // 32) * 16


def placed(refs, rows):
    first = first_part(rows)
    each = len(refs) // HALVES
    for other in range(HALVES):
        here = refs[each * other : each * other + each]
        for j in range(3):
            yield j, other, 0, rows, here[j]
        if each == COLUMNS:
            yield 3, other, 0, rows, here[3]
        else:
            yield 3, other, 0, first, here[3]
            yield 3, other, first, rows - first, here[4]


def piece_copies(where, count, sources, target, rows, sem):
    place, column, side = where
    copies = []
    for j, other, start, size, ref in placed(sources, rows):
        for by in range(1, count):
            owner = (place + (count - by)) % count
            to = target(column ^ j, side ^ other, owner, start, size)
            copies.append(pltpu.make_async_copy(ref.at[by - 1], to, sem(column ^ j, side ^ other, owner)))
    return copies


def wait_for(ref, sem):
    pltpu.make_async_copy(ref, ref, sem).wait()


def first_kernel(
    count, where_ref, x_ref, mod_ref, cos_ref, sin_ref, joint_ref, project_ref, *refs
):
    sources, refs = refs[:-9], refs[-9:]
    turned_ref, query_ref, keys_ref, values_ref, weight_ref, weight, first_ref, total, sems = refs
    where = where_ref[0], where_ref[1], where_ref[2]
    rows_in = joint_ref.shape[0]
    half = rows_in // HALVES

    def target(column, side, place, start, size):
        return weight.at[column, take(place * rows_in + side * half + start, size)]

    copies = piece_copies(where, count, sources, target, half, lambda c, s, z: sems.at[c])
    for c in range(COLUMNS):
        shard = project_ref if c == 3 else joint_ref.at[:, pl.ds(c * WIDTH, WIDTH)]
        copies.append(pltpu.make_async_copy(shard, weight.at[c, take(where[0] * rows_in, rows_in)], sems.at[c]))
    for copy in copies:
        copy.start()
    tokens = x_ref.shape[0]
    for i in range(tokens // CHUNK):
        rows = slice(i * CHUNK, (i + 1) * CHUNK)
        normed, _ = normalize(x_ref[rows, :].astype(f32))
        first_ref[rows, :] = (
            normed * (1.0 + mod_ref[i : i + 1, part(1)]) + mod_ref[i : i + 1, part(0)]
        ).astype(bf16)
    turned_ref[...] = first_ref[...].T
    writes = [
        pltpu.make_async_copy(weight.at[c], weight_ref.at[c], sems.at[c]) for c in range(COLUMNS)
    ]
    wait_for(weight.at[3], sems.at[3])
    writes[3].start()
    for c, out in enumerate((query_ref, keys_ref, values_ref)):
        wait_for(weight.at[c], sems.at[c])
        writes[c].start()
        if c == 2:
            out[...] = matmul(first_ref[...], weight[c]).astype(bf16)
        else:
            total[...] = matmul(first_ref[...], weight[c])

            @pl.loop(0, tokens // CHUNK)
            def _(i):
                rows = pl.ds(pl.multiple_of(i * CHUNK, CHUNK), CHUNK)
                out[rows, :] = rotate(total[rows, :], cos_ref[rows, :], sin_ref[rows, :]).astype(bf16)

    for write in writes:
        write.wait()


def window(head):
    start = head * HEAD_DIM // LANES * LANES
    stop = -(-(head + 1) * HEAD_DIM // LANES) * LANES
    lane = lax.broadcasted_iota(jnp.int32, (1, stop - start), 1) + start
    inside = (lane >= head * HEAD_DIM) & (lane < (head + 1) * HEAD_DIM)
    return slice(start, stop), inside


def soft_scores(left, right, allowed, axis):
    scores = times_transposed(left, right) * HEAD_DIM ** (-0.5)
    scores = jnp.where(allowed, scores, masked_score)
    exponent = jnp.exp(scores - jnp.max(scores, axis=axis, keepdims=True))
    return exponent * (1.0 / jnp.sum(exponent, axis=axis, keepdims=True))


def attend_kernel(
    query_ref, keys_ref, values_ref, column_ids, row_ids, x_ref, mod_ref,
    weight, turned_ref, branch_ref, middle_ref, second_ref, mixed,
):
    allowed = column_ids[...] == row_ids[...]
    for head in range(HEADS):
        lanes, inside = window(head)
        query = jnp.where(inside, query_ref[:, lanes], jnp.zeros((), bf16))
        probs = soft_scores(query, keys_ref[:, lanes], allowed, 1).astype(bf16)
        mixed[:, lanes] = jnp.where(inside, matmul(probs, values_ref[:, lanes]), mixed[:, lanes])
    attended = mixed[...].astype(bf16)
    turned_ref[...] = attended.T
    branch_ref[...] = matmul(attended, weight[0])
    for i in range(BLOCK // CHUNK):
        rows = slice(i * CHUNK, (i + 1) * CHUNK)
        mod = mod_ref.at[0]
        middle = x_ref[rows, :].astype(f32) + mod[i : i + 1, part(0)] * branch_ref[rows, :]
        middle_ref[rows, :] = middle
        normed, _ = normalize(middle)
        second_ref[rows, :] = (
            normed * (1.0 + mod[i : i + 1, part(2)]) + mod[i : i + 1, part(1)]
        ).astype(bf16)


def tile_copies(r, where, count, tile, pair, downs):
    place, mine, side = where
    t, j = tile
    column = mine ^ j
    rows, width = r["gate"].shape[0], r["hidden_w"].shape[1]
    sem = r["pair_sems"].at[t]
    copies = [
        pltpu.make_async_copy(
            r[name].at[:, take(column * width, width)], r["pair_w"].at[t, which, take(place * rows, rows)], sem
        )
        for which, name in enumerate(("gate", "up"))
    ]
    first = first_part(rows)
    for other in range(HALVES):
        for by in range(1, count):
            owner = (place + (count - by)) % count
            if j < 3:
                spans = [(pair[other][0].at[by - 1], 0, rows)]
            else:
                spans = [(pair[other][0].at[by - 1], 0, first), (pair[other][1].at[by - 1], first, rows - first)]
            for ref, start, size in spans:
                to = r["pair_w"].at[t, side ^ other, take(owner * rows + start, size)]
                copies.append(pltpu.make_async_copy(ref, to, sem))
    for copy in copies:
        copy.start()

    sem = r["down_sems"].at[t]
    target = r["down_w"].at[t]
    piece = width // PIECES

    @pl.when(column == place)
    def _():
        pltpu.make_async_copy(r["down"], target, sem).start()

    @pl.when(column != place)
    def _():
        by = jnp.maximum((place + count - column) % count, 1)
        for i, other, start, size, ref in placed(downs, piece):
            to = target.at[take(((mine ^ i) * HALVES + (side ^ other)) * piece + start, size)]
            pltpu.make_async_copy(ref.at[by - 1], to, sem).start()


def ffn_kernel(count, js, names, *refs):
    r = dict(zip(names, refs, strict=True))
    r["hidden_w"] = r["hidden"]
    first, last = js[0] == 0, js[-1] == COLUMNS - 1
    step = pl.program_id(0)
    tile = r["hidden"].shape[1]
    tokens = r["second"].shape[0]
    second, feed_back = r["second"], r["feed_back"]
    feed, second_back = r["feed"], r["second_back"]

    @pl.when(step == 0)
    def _():
        where = r["where"][0], r["where"][1], r["where"][2]
        for t, j in enumerate(js):
            pair = [
                [r[f"pair{j}_{other}_{i}"] for i in range(1 if j < 3 else 2)]
                for other in range(HALVES)
            ]
            tile_copies(r, where, count, (t, j), pair, [r[name] for name in names if name[:4] == "down" and name[5:].isdigit()])
        if first:
            r["turned"][...] = second[...].T
            for i in range(tokens // CHUNK):
                rows = slice(i * CHUNK, (i + 1) * CHUNK)
                upstream = r["cot"][rows, :].astype(f32) * r["factor"][0]
                feed_back[rows, :] = (upstream * r["mod"][i : i + 1, part(3)]).astype(bf16)

    pair_w, down_w = r["pair_w"].at[step], r["down_w"].at[step]
    wait_for(pair_w, r["pair_sems"].at[step])
    wait_for(down_w, r["down_sems"].at[step])
    sub = 256
    for n in range(tile // sub):
        lanes = slice(n * sub, (n + 1) * sub)
        gate = matmul(second[...], pair_w[0, :, lanes])
        upval = matmul(second[...], pair_w[1, :, lanes])
        hidden_back = times_transposed(feed_back[...], down_w[lanes, :])
        sigmoid = jax.nn.sigmoid(gate)
        silu = gate * sigmoid
        r["hidden"][:, lanes] = (silu * upval).astype(bf16)
        r["pair_back"][0, 1, :, lanes] = (hidden_back * silu).astype(bf16)
        r["pair_back"][0, 0, :, lanes] = (
            hidden_back * upval * (sigmoid * (1.0 + gate * (1.0 - sigmoid)))
        ).astype(bf16)

    r["hidden_turned"][0] = r["hidden"][...].T
    feed_part = matmul(r["hidden"][...], down_w[...])
    back_part = times_transposed(r["pair_back"][0, 0], pair_w[0]) + times_transposed(
        r["pair_back"][0, 1], pair_w[1]
    )

    @pl.when(step == 0)
    def _():
        feed[...] = feed_part if first else r["feed_in"][...] + feed_part
        second_back[...] = back_part if first else r["back_in"][...] + back_part

    @pl.when(step > 0)
    def _():
        feed[...] += feed_part
        second_back[...] += back_part

    if not last:
        return

    @pl.when(step == len(js) - 1)
    def _():
        for i in range(tokens // CHUNK):
            rows = slice(i * CHUNK, (i + 1) * CHUNK)
            gate_one = r["mod"][i : i + 1, part(0)]
            scale_two = r["mod"][i : i + 1, part(2)]
            gate_two = r["mod"][i : i + 1, part(3)]
            middle = r["middle"][rows, :]
            r["output"][rows, :] = (middle + gate_two * feed[rows, :]).astype(bf16)
            upstream = r["cot"][rows, :].astype(f32) * r["factor"][0]
            normed, inverse = normalize(middle)
            back = second_back[rows, :]
            middle_back = upstream + normalize_back(normed, inverse, back * (1.0 + scale_two))
            r["middle_back"][rows, :] = middle_back
            r["branch_back"][rows, :] = (middle_back * gate_one).astype(bf16)
            for where, values in enumerate(
                (middle_back * r["branch"][rows, :], back, back * normed, upstream * feed[rows, :])
            ):
                r["sums"][i : i + 1, part(where)] = jnp.sum(values, axis=0, keepdims=True)


ORDER = (1, 3, 2, 0)
SEND_X, KEEP_X, SEND_Y, KEEP_Y = (1, 3), (2, 0), (3, 2), (1, 0)
CUT = (SEND_X, KEEP_X, SEND_Y, KEEP_Y)


def put_grad(grad, other_ref, out_refs):
    step = pl.program_id(0)
    if other_ref is None:
        out_refs[0][0] = grad.astype(bf16)
        return
    total = (grad + other_ref[0].astype(f32)).astype(bf16)
    first = first_part(total.shape[1])
    for at, j in enumerate(ORDER):

        @pl.when(step == at)
        def _():
            for columns, ref in zip(CUT, out_refs, strict=True):
                if j in columns:
                    ref[0] = total[:, :first] if columns in (SEND_X, KEEP_X) else total[:, first:]


def cut_specs(count, rows, breadth):
    first = first_part(rows)
    shapes, specs = [], []
    for columns in CUT:
        size = first if columns in (SEND_X, KEEP_X) else rows - first
        shapes.append(struct((2, count, size, breadth), bf16))
        second = ORDER.index(columns[1])
        specs.append(
            pl.BlockSpec(
                (1, count, size, breadth),
                lambda s, where, second=second: (jnp.where(s >= second, 1, 0), 0, 0, 0),
            )
        )
    return tuple(shapes), tuple(specs)


def split_refs(mine, refs):
    return (refs[0], refs[1:]) if mine else (None, refs)


def pair_grad_kernel(mine, count, where_ref, turned_ref, own_ref, near_ref, far_ref, *refs):
    other_ref, out_refs = split_refs(mine, refs)
    for at, j in enumerate(ORDER):

        @pl.when(pl.program_id(0) == at)
        def _():
            back = {0: own_ref, 3: far_ref}.get(j, near_ref)
            grad = matmul(turned_ref[...], back[0, 0])
            put_grad(grad.reshape(count, grad.shape[0] // count, grad.shape[1]), other_ref, out_refs)


def down_grad_kernel(mine, where_ref, *refs):
    hiddens, feed_back_ref, out_ref = refs[:3], refs[3], refs[-1]
    other_ref = refs[4] if mine else None
    side = where_ref[2] if mine else where_ref[2] ^ 1
    count, _, rows, _ = out_ref.shape
    tiles = [(hidden, t) for hidden in hiddens for t in range(hidden.shape[0])]
    for j, (hidden, t) in enumerate(tiles):
        pieces = [hidden[t, take(((where_ref[1] ^ c) * HALVES + side) * rows, rows), :] for c in ORDER]
        grad = matmul(jnp.concatenate(pieces, axis=0), feed_back_ref[...]).reshape(COLUMNS, rows, WIDTH)
        owner = where_ref[1] ^ j
        if mine:
            grad = grad + other_ref[owner].astype(f32)
        out_ref[owner] = grad.astype(bf16)


def attn_grad_kernel(
    mine, where_ref, first_ref, attended_ref, joint_back_ref, branch_back_ref, *refs
):
    other_ref, out_refs = split_refs(mine, refs)
    column = where_ref[1] ^ where_ref[3 + pl.program_id(0)]
    side = where_ref[2] if mine else where_ref[2] ^ 1
    _, count, _, _ = out_refs[0].shape
    rows = WIDTH // count // HALVES

    def put(turned, right):
        taken = [turned[take((z * HALVES + side) * rows, rows), :] for z in range(count)]
        grad = matmul(jnp.concatenate(taken, axis=0), right[...])
        put_grad(grad.reshape(count, rows, WIDTH), other_ref, out_refs)

    @pl.when(column < 3)
    def _():
        put(first_ref, joint_back_ref)

    @pl.when(column == 3)
    def _():
        put(attended_ref, branch_back_ref)


def place_pair_kernel(where_ref, *refs):
    sources, outs = refs[:-2], refs[-2:]
    rows, tile = sources[0].shape
    for way in range(HALVES):

        @pl.when(where_ref[2] == way)
        def _():
            for j, other, start, size, ref in placed(sources, rows):
                lanes = take((where_ref[1] ^ j) * tile, tile)
                outs[way ^ other][start : start + size, lanes] = ref[...].astype(f32)


def place_down_kernel(rows, offset, where_ref, *refs):
    sources, out = refs[:-1], refs[-1]
    for j, other, start, size, ref in placed(sources, rows):
        piece = (where_ref[1] ^ j) * HALVES + (where_ref[2] ^ other)
        out[take(piece * rows + start, size), :] = ref[offset : offset + size, :].astype(f32)


def place_attn_kernel(rows, where_ref, *refs):
    sources, joint_ref, project_ref = refs[:-2], refs[-2], refs[-1]
    for column in range(COLUMNS):

        @pl.when(where_ref[1] == column)
        def _():
            for j, other, start, size, ref in placed(sources, rows):
                to = take((where_ref[2] ^ other) * rows + start, size)
                if column ^ j == 3:
                    project_ref[to, :] = ref[:size, :].astype(f32)
                else:
                    joint_ref[to, part(column ^ j)] = ref[:size, :].astype(f32)


def attend_back_kernel(
    query_ref, keys_ref, values_ref, branch_back_ref, column_ids, row_ids, cos_ref,
    sin_ref, weight, joint_back_ref, mixed_back, query_back, keys_back, values_back,
):
    mixed_back[...] = times_transposed(branch_back_ref[...], weight[0]).astype(bf16)
    allowed = column_ids[...] == row_ids[...]
    scaling = HEAD_DIM ** (-0.5)
    for head in range(HEADS):
        lanes, inside = window(head)
        zero = jnp.zeros((), bf16)
        query = jnp.where(inside, query_ref[:, lanes], zero)
        back = jnp.where(inside, mixed_back[:, lanes], zero)
        soft = soft_scores(keys_ref[:, lanes], query, allowed, 0)
        probs_back = times_transposed(values_ref[:, lanes], back)
        scores_back = (
            soft * (probs_back - jnp.sum(soft * probs_back, axis=0, keepdims=True))
        ).astype(bf16)
        query_back[:, lanes] = jnp.where(
            inside, contract_rows(scores_back, keys_ref[:, lanes]) * scaling, query_back[:, lanes]
        )
        keys_back[:, lanes] = jnp.where(
            inside, matmul(scores_back, query) * scaling, keys_back[:, lanes]
        )
        values_back[:, lanes] = jnp.where(
            inside, matmul(soft.astype(bf16), back), values_back[:, lanes]
        )

    @pl.loop(0, BLOCK // CHUNK)
    def _(i):
        rows = pl.ds(pl.multiple_of(i * CHUNK, CHUNK), CHUNK)
        cos, sin = cos_ref[rows, :], sin_ref[rows, :]
        joint_back_ref[rows, part(0)] = rotate(query_back[rows, :], cos, -sin).astype(bf16)
        joint_back_ref[rows, part(1)] = rotate(keys_back[rows, :], cos, -sin).astype(bf16)
        joint_back_ref[rows, part(2)] = values_back[rows, :].astype(bf16)


def first_back_kernel(
    joint_back_ref, x_ref, middle_back_ref, mod_ref, weight, grad_ref, sums_ref, first_back
):
    step = pl.program_id(0)
    product = times_transposed(joint_back_ref[...], weight[0])

    @pl.when(step == 0)
    def _():
        first_back[...] = product

    @pl.when(step > 0)
    def _():
        first_back[...] += product

    @pl.when(step == pl.num_programs(0) - 1)
    def _():
        finish_first_back(x_ref, middle_back_ref, mod_ref, grad_ref, sums_ref, first_back)


def finish_first_back(x_ref, middle_back_ref, mod_ref, grad_ref, sums_ref, first_back):
    for i in range(x_ref.shape[0] // CHUNK):
        rows = slice(i * CHUNK, (i + 1) * CHUNK)
        normed, inverse = normalize(x_ref[rows, :].astype(f32))
        back = first_back[rows, :]
        grad_ref[rows, :] = middle_back_ref[rows, :] + normalize_back(
            normed, inverse, back * (1.0 + mod_ref[i : i + 1, part(1)])
        )
        sums_ref[i : i + 1, part(0)] = jnp.sum(back, axis=0, keepdims=True)
        sums_ref[i : i + 1, part(1)] = jnp.sum(back * normed, axis=0, keepdims=True)


SMEM = pl.BlockSpec(memory_space=pltpu.SMEM)
VMEM = pl.BlockSpec(memory_space=pltpu.VMEM)
ANY = pl.BlockSpec(memory_space=pl.ANY)


def struct(shape, dtype):
    return jax.ShapeDtypeStruct(shape, dtype)


def params(mega=56):
    return pltpu.CompilerParams(vmem_limit_bytes=mega * MEGA)


def cost(microseconds):
    return pl.CostEstimate(flops=int(microseconds * 1e9), bytes_accessed=1000, transcendentals=0)


def by_block(*shape):
    return pl.BlockSpec(shape, lambda b: (b,) + (0,) * (len(shape) - 1))


def whole(*shape):
    return pl.BlockSpec(shape, lambda *_: (0,) * len(shape))


def first_call(where, x, mod, cos, sin, joint, project, arrived):
    tokens = x.shape[0]
    count = arrived[0].shape[0] + 1
    shape = struct((tokens, WIDTH), bf16)
    return pl.pallas_call(
        functools.partial(first_kernel, count),
        out_shape=(struct((WIDTH, tokens), bf16),)
        + (shape,) * 3
        + (struct((COLUMNS, WIDTH, WIDTH), bf16),),
        in_specs=[SMEM, VMEM, VMEM, VMEM, VMEM] + [ANY] * (2 + len(arrived)),
        out_specs=(VMEM,) * 4 + (ANY,),
        scratch_shapes=[
            pltpu.VMEM((COLUMNS, WIDTH, WIDTH), bf16),
            pltpu.VMEM((tokens, WIDTH), bf16),
            pltpu.VMEM((tokens, WIDTH), f32),
            pltpu.SemaphoreType.DMA((COLUMNS,)),
        ],
        compiler_params=params(),
        cost_estimate=cost(20),
    )(where, x, mod, cos, sin, joint, project, *arrived)


def attend_call(query, keys, values, ids, x, mod, weight):
    tokens = x.shape[0]
    return pl.pallas_call(
        attend_kernel,
        grid=(tokens // BLOCK,),
        out_shape=(
            struct((WIDTH, tokens), bf16),
            struct((tokens, WIDTH), f32),
            struct((tokens, WIDTH), f32),
            struct((tokens, WIDTH), bf16),
        ),
        in_specs=[by_block(BLOCK, WIDTH)] * 3
        + [by_block(BLOCK, 1), pl.BlockSpec((1, BLOCK), lambda b: (0, b)), by_block(BLOCK, WIDTH)]
        + [by_block(1, BLOCK // CHUNK, 4 * WIDTH), pl.BlockSpec((1, WIDTH, WIDTH), lambda b: (3, 0, 0))],
        out_specs=(pl.BlockSpec((WIDTH, BLOCK), lambda b: (0, b)),) + (by_block(BLOCK, WIDTH),) * 3,
        scratch_shapes=[pltpu.VMEM((BLOCK, WIDTH), f32)],
        compiler_params=params(),
        cost_estimate=cost(2),
    )(
        query, keys, values, ids[:, None], ids[None, :], x,
        mod.reshape(tokens // BLOCK, BLOCK // CHUNK, 4 * WIDTH), weight,
    )


def ffn_call(js, where, given, shards, pairs, downs):
    second = given["second"]
    tokens = second.shape[0]
    ff = shards["gate"].shape[1]
    tile = ff // COLUMNS
    count = ff // shards["down"].shape[0]
    chunks = tokens // CHUNK
    first, last = js[0] == 0, js[-1] == COLUMNS - 1
    full = whole(tokens, WIDTH)
    wide = struct((tokens, WIDTH), f32)
    narrow = struct((tokens, WIDTH), bf16)
    inputs = [("where", where, SMEM), ("second", second, full)]
    if first or last:
        inputs += [
            ("factor", given["factor"], SMEM),
            ("cot", given["cot"], full),
            ("mod", given["mod"], whole(chunks, 4 * WIDTH)),
        ]
    if not first:
        inputs += [
            ("feed_back", given["feed_back"], full),
            ("feed_in", given["feed"], full),
            ("back_in", given["second_back"], full),
        ]
    if last:
        inputs += [("middle", given["middle"], full), ("branch", given["branch"], full)]
    inputs += [(name, shards[name], ANY) for name in ("gate", "up", "down")]
    for j in js:
        for other in range(HALVES):
            inputs += [(f"pair{j}_{other}_{i}", a, ANY) for i, a in enumerate(pairs[other][j])]
    inputs += [(f"down_{i}", a, ANY) for i, a in enumerate(downs)]
    outputs = [
        (
            "hidden_turned",
            struct((len(js), tile, tokens), bf16),
            pl.BlockSpec((1, tile, tokens), lambda t: (t, 0, 0)),
        ),
        (
            "pair_back",
            struct((len(js), HALVES, tokens, tile), bf16),
            pl.BlockSpec((1, HALVES, tokens, tile), lambda t: (t, 0, 0, 0)),
        ),
    ]
    if first:
        outputs += [
            ("turned", struct((WIDTH, tokens), bf16), whole(WIDTH, tokens)),
            ("feed_back", narrow, full),
        ]
    sums = ("feed", "second_back")
    scratch = [
        ("pair_w", pltpu.VMEM((len(js), HALVES, WIDTH, tile), bf16)),
        ("down_w", pltpu.VMEM((len(js), ff // count, WIDTH), bf16)),
        ("hidden", pltpu.VMEM((tokens, tile), bf16)),
        ("pair_sems", pltpu.SemaphoreType.DMA((len(js),))),
        ("down_sems", pltpu.SemaphoreType.DMA((len(js),))),
    ]
    if last:
        outputs += [
            ("output", narrow, full),
            ("middle_back", wide, full),
            ("branch_back", narrow, full),
            ("sums", struct((chunks, 4 * WIDTH), f32), whole(chunks, 4 * WIDTH)),
        ]
        scratch += [(name, pltpu.VMEM((tokens, WIDTH), f32)) for name in sums]
    else:
        outputs += [(name, wide, full) for name in sums]
    names = [each[0] for each in inputs + outputs + scratch]
    found = pl.pallas_call(
        functools.partial(ffn_kernel, count, js, names),
        grid=(len(js),),
        out_shape=tuple(shape for _, shape, _ in outputs),
        in_specs=[spec for _, _, spec in inputs],
        out_specs=tuple(spec for _, _, spec in outputs),
        scratch_shapes=[shape for _, shape in scratch],
        compiler_params=params(),
        cost_estimate=cost(2 if first else 12 * len(js)),
    )(*[array for _, array, _ in inputs])
    return {name: array for (name, _, _), array in zip(outputs, found, strict=True)}


def by_column(call, count, rows, breadth, in_specs, where, arrays, other):
    shapes, specs = cut_specs(count, rows, breadth)
    block = pl.BlockSpec((1, count, rows, breadth), lambda s, where: (s, 0, 0, 0))
    if other is None:
        shapes, specs = (struct((COLUMNS, count, rows, breadth), bf16),), (block,)
    else:
        in_specs, arrays = in_specs + [block], arrays + (other,)
    found = pl.pallas_call(
        call,
        out_shape=shapes,
        grid_spec=pltpu.PrefetchScalarGridSpec(
            num_scalar_prefetch=1, grid=(COLUMNS,), in_specs=in_specs, out_specs=specs
        ),
        compiler_params=params(),
        cost_estimate=cost(3),
    )(where, *arrays)
    return found[0] if other is None else found


def pair_grad_call(count, where, turned, backs, other=None):
    tokens, tile = backs[0].shape[2:]
    mine = other is not None

    def spec(tile_of):
        return pl.BlockSpec(
            (1, 1, tokens, tile),
            lambda s, where: (tile_of(where[3 + s]), where[2] if mine else where[2] ^ 1, 0, 0),
        )

    return by_column(
        functools.partial(pair_grad_kernel, mine, count),
        count, WIDTH // count, tile,
        [whole(WIDTH, tokens), spec(lambda j: 0), spec(lambda j: jnp.clip(j - 1, 0, 1)), spec(lambda j: 0)],
        where, (turned,) + tuple(backs), other,
    )


def attn_grad_call(count, where, first, attended, joint_back, branch_back, other=None):
    tokens = first.shape[1]
    return by_column(
        functools.partial(attn_grad_kernel, other is not None),
        count, WIDTH // count // HALVES, WIDTH,
        [
            whole(WIDTH, tokens),
            whole(WIDTH, tokens),
            pl.BlockSpec((tokens, WIDTH), lambda s, where: (0, jnp.minimum(where[1] ^ where[3 + s], 2))),
            whole(tokens, WIDTH),
        ],
        where, (first, attended, joint_back, branch_back), other,
    )


def down_grad_call(count, where, hiddens, feed_back, other=None):
    ff = sum(h.shape[0] * h.shape[1] for h in hiddens)
    out = struct((count, COLUMNS, ff // count // PIECES, WIDTH), bf16)
    arrays = tuple(hiddens) + (feed_back,) + (() if other is None else (other,))
    return pl.pallas_call(
        functools.partial(down_grad_kernel, other is not None),
        out_shape=out,
        in_specs=[SMEM] + [VMEM] * len(arrays),
        out_specs=VMEM,
        compiler_params=params(),
        cost_estimate=cost(3),
    )(where, *arrays)


def place_call(kernel, where, arrays, outs):
    return pl.pallas_call(
        kernel,
        out_shape=outs,
        in_specs=[SMEM] + [VMEM] * len(arrays),
        out_specs=jax.tree.map(lambda _: VMEM, outs),
        compiler_params=params(),
        cost_estimate=cost(4),
    )(where, *arrays)


def attend_back_call(query, keys, values, branch_back, ids, cos, sin, weight):
    tokens = query.shape[0]
    block = by_block(BLOCK, WIDTH)
    return pl.pallas_call(
        attend_back_kernel,
        grid=(tokens // BLOCK,),
        out_shape=struct((tokens, 3 * WIDTH), bf16),
        in_specs=[block, block, block, block]
        + [by_block(BLOCK, 1), pl.BlockSpec((1, BLOCK), lambda b: (0, b)), block, block]
        + [pl.BlockSpec((1, WIDTH, WIDTH), lambda b: (3, 0, 0))],
        out_specs=by_block(BLOCK, 3 * WIDTH),
        scratch_shapes=[
            pltpu.VMEM((BLOCK, WIDTH), bf16),
            pltpu.VMEM((BLOCK, WIDTH), f32),
            pltpu.VMEM((BLOCK, WIDTH), f32),
            pltpu.VMEM((BLOCK, WIDTH), f32),
        ],
        compiler_params=params(),
        cost_estimate=cost(8),
    )(query, keys, values, branch_back, ids[:, None], ids[None, :], cos, sin, weight)


def first_back_call(joint_back, x, middle_back, mod, weight):
    tokens = x.shape[0]
    chunks = tokens // CHUNK
    full = whole(tokens, WIDTH)
    return pl.pallas_call(
        first_back_kernel,
        grid=(3,),
        out_shape=(struct((tokens, WIDTH), f32), struct((chunks, 2 * WIDTH), f32)),
        in_specs=[
            pl.BlockSpec((tokens, WIDTH), lambda c: (0, c)),
            full,
            full,
            whole(chunks, 2 * WIDTH),
            pl.BlockSpec((1, WIDTH, WIDTH), lambda c: (c, 0, 0)),
        ],
        out_specs=(full, whole(chunks, 2 * WIDTH)),
        scratch_shapes=[pltpu.VMEM((tokens, WIDTH), f32)],
        compiler_params=params(),
        cost_estimate=cost(2),
    )(joint_back, x, middle_back, mod, weight)


def shifts(count, by):
    return [(i, (i + by) % count) for i in range(count)]


def pick(array, index):
    return lax.dynamic_index_in_dim(array, index, 0, keepdims=False)


def across(bit):
    return [(i, i ^ bit) for i in range(PIECES)]


def swap(array, bit):
    return lax.ppermute(array, "bucket", across(bit))


def after(arrays, *others):
    return lax.optimization_barrier((arrays, others))[0]


def add(left, right):
    return (left.astype(f32) + right.astype(f32)).astype(bf16)


def over_z(piece):
    count = lax.axis_size("fsdp")
    return [lax.ppermute(piece, "fsdp", shifts(count, by)) for by in range(1, count)]


def gather_z(piece, *others):
    count = lax.axis_size("fsdp")
    place = lax.axis_index("fsdp")
    full = after(lax.all_gather(piece, "fsdp", axis=0, tiled=False), *others)
    return jnp.stack([pick(full, (place + count - by) % count) for by in range(1, count)])


def cross(by_x, by_y, first):
    if first is not None:
        by_x, by_y = by_x[..., :first, :], by_y[..., first:, :]
    return swap(by_x, 4), swap(by_y, 2)


def both(here):
    return here + tuple(None if array is None else swap(array, 1) for array in here)


def direct(piece):
    return piece, swap(piece, 2), swap(piece, 4), swap(piece, 6)


def spread_whole(pieces):
    first = first_part(pieces.shape[1])

    def of(side):
        own, by_x, by_y, far = (pieces[c * HALVES + side] for c in range(COLUMNS))
        return own, by_x, by_y, far[:first], far[first:]

    return of(0) + of(1)


def halve_once(cut):
    send_x, (a2, a0), send_y, (b1, b0) = cut
    from_x, from_y = swap(send_x, 2), swap(send_y, 4)
    return add(a0, from_x[0]), add(a2, from_x[1]), add(b0, from_y[1]), add(b1, from_y[0])


def halve_twice(once, *others):
    a0, a2, b0, b1 = once
    if others:
        a0, b0 = after((a0, b0), *others)
    return jnp.concatenate([add(a0, swap(a2, 4)), add(b0, swap(b1, 2))], axis=-2)


def send_z(parts):
    count = lax.axis_size("fsdp")
    place = lax.axis_index("fsdp")
    return [
        lax.ppermute(pick(parts, (place + by) % count), "fsdp", shifts(count, by))
        for by in range(1, count)
    ]


def total_z(parts, others):
    total = pick(parts, lax.axis_index("fsdp")).astype(f32)
    for array in others:
        total = total + array.astype(f32)
    return total.astype(bf16)


def sum_z(parts):
    return total_z(parts, send_z(parts))


def cut_down(part, first):
    cut = []
    for columns in CUT:
        both_columns = jnp.stack([part[ORDER.index(j)] for j in columns])
        cut.append(both_columns[:, :first] if columns in (SEND_X, KEEP_X) else both_columns[:, first:])
    return cut


def uncut(cut):
    def of(j, pair):
        columns = next(c for c in pair if j in c)
        return cut[CUT.index(columns)][columns.index(j)]

    return jnp.stack(
        [jnp.concatenate([of(j, (SEND_X, KEEP_X)), of(j, (SEND_Y, KEEP_Y))], axis=1) for j in ORDER]
    )


def sum_whole(mine, theirs):
    parts = jnp.stack([mine, theirs], axis=1)
    parts = jnp.stack([parts[ORDER.index(c)] for c in range(COLUMNS)])
    rows, breadth = mine.shape[2:]
    parts = lax.psum(parts, "bucket").transpose(2, 0, 1, 3, 4)
    return spread_whole(sum_z(parts).reshape(PIECES, rows, breadth))


def arrived_whole(pieces):
    count = lax.axis_size("fsdp")
    place = lax.axis_index("fsdp")
    first = first_part(pieces.shape[1])
    full = lax.all_gather(pieces, "fsdp", axis=0, tiled=False)
    full = jnp.stack([pick(full, (place + count - by) % count) for by in range(1, count)])

    def of(side):
        own, by_x, by_y, far = (full[:, c * HALVES + side] for c in range(COLUMNS))
        return own, by_x, by_y, far[:, :first], far[:, first:]

    return of(0) + of(1)


def to_group(rows, count, place):
    relative = jnp.stack(
        [pick(rows, place)]
        + [
            lax.ppermute(pick(rows, (place + by) % count), "fsdp", shifts(count, by))
            for by in range(1, count)
        ]
    )
    return jnp.stack([pick(relative, (place - j) % count) for j in range(count)])


def on_device(
    inputs,
    condition,
    segment_ids,
    grid_widths,
    bucket_counts,
    modulate_weight,
    joint_weight,
    project_weight,
    gate_weight,
    up_weight,
    down_weight,
    cotangent,
):
    fsdp_count = lax.axis_size("fsdp")
    place = lax.axis_index("fsdp")
    bucket = lax.axis_index("bucket")
    height = joint_weight.shape[0]
    half = height // HALVES
    ff = gate_weight.shape[1]
    tile = ff // COLUMNS
    down_rows = down_weight.shape[0] // PIECES
    slots = condition.shape[0]

    cond_float = condition.astype(f32)
    lifted = jax.nn.silu(cond_float).astype(bf16)
    lifted_rows = to_group(
        lifted.reshape(slots, fsdp_count, height).transpose(1, 0, 2), fsdp_count, place
    ).reshape(fsdp_count * slots, height)
    one_hot = (
        segment_ids[::CHUNK, None] == jnp.arange(slots, dtype=jnp.int32)[None, :]
    ).astype(f32)

    def modulation_parts(weight, rows):
        parts = matmul(rows, weight).reshape(fsdp_count, slots, weight.shape[1])
        return [pick(parts, place)] + [
            lax.ppermute(pick(parts, (place + by) % fsdp_count), "fsdp", shifts(fsdp_count, by))
            for by in range(1, fsdp_count)
        ]

    def modulation(parts):
        return jnp.dot(
            one_hot,
            sum(parts[1:], parts[0]),
            precision=lax.Precision.HIGHEST,
            preferred_element_type=f32,
        )

    first_rows = modulation_parts(modulate_weight[:, : 2 * WIDTH], lifted_rows)
    mod_one = modulation(first_rows)
    fast = lax.axis_size("bucket") == PIECES
    if fast:
        column, side = bucket // HALVES, bucket % HALVES
        where = jnp.stack([place, column, side] + [jnp.int32(j) for j in ORDER])
        attn_piece = jnp.where(
            column == 3,
            lax.dynamic_slice(project_weight, (side * half, 0), (half, WIDTH)),
            lax.dynamic_slice(joint_weight, (side * half, column * WIDTH), (half, WIDTH)),
        )
        ffn_piece = jnp.where(
            side == 0,
            lax.dynamic_slice(gate_weight, (0, column * tile), (height, tile)),
            lax.dynamic_slice(up_weight, (0, column * tile), (height, tile)),
        )
        down_piece = lax.dynamic_slice_in_dim(down_weight, bucket * down_rows, down_rows, 0)
        attn_z = gather_z(attn_piece, first_rows)
        down_k = over_z(after(down_piece, attn_z))
        attn_x, attn_y = swap(attn_z, 2), swap(attn_z, 4)
        attn_x, attn_y, down_k = after((attn_x, attn_y, down_k))
        attn_far = cross(attn_x, attn_y, first_part(half))
        pair_z = gather_z(after(ffn_piece, down_k))
        down_z = jnp.stack(down_k)
        attn_arrived = both((attn_z, attn_x, attn_y) + attn_far)
        inputs, down_z = after((inputs, down_z), attn_far)
        down_x, down_y = swap(down_z, 2), swap(down_z, 4)
        inputs = after(inputs, down_z)
    else:
        where = jnp.stack([place, 0 * place, 0 * place] + [jnp.int32(j) for j in ORDER])
        attn_arrived = arrived_whole(
            jnp.concatenate([joint_weight, project_weight], axis=1)
            .reshape(HALVES, half, COLUMNS, WIDTH)
            .transpose(2, 0, 1, 3)
            .reshape(PIECES, half, WIDTH)
        )
        pairs = arrived_whole(
            jnp.stack([gate_weight, up_weight])
            .reshape(HALVES, height, COLUMNS, tile)
            .transpose(2, 0, 1, 3)
            .reshape(PIECES, height, tile)
        )
        downs = arrived_whole(down_weight.reshape(PIECES, down_rows, WIDTH))

    if fast:
        lifted_rows = after(lifted_rows, down_k)
    late_rows = modulation_parts(modulate_weight[:, 2 * WIDTH :], lifted_rows)
    counts = bucket_counts.astype(f32)
    mine = jnp.sum(jnp.where(jnp.arange(counts.shape[0], dtype=jnp.int32) == bucket, counts, 0.0))
    factor = (mine * counts.shape[0] / jnp.sum(counts)).reshape(1)
    cos, sin = rope_tables(segment_ids, grid_widths)

    first, query, keys, values, weight = first_call(
        where, inputs, mod_one, cos, sin, joint_weight, project_weight, attn_arrived
    )
    if fast:
        late_rows = [late_rows[0], *after(late_rows[1:], query)]
        down_x, down_y = after((down_x, down_y), query)
        down_far = cross(down_x, down_y, first_part(down_rows))
        downs = (down_z, down_x, down_y) + down_far
        pair_z = after(pair_z, query)
        pair_x, pair_y = swap(pair_z, 2), swap(pair_z, 4)
    mod = modulation(late_rows)
    attended, branch, middle, second = attend_call(
        query, keys, values, segment_ids, inputs, mod, weight
    )
    shards = dict(gate=gate_weight, up=up_weight, down=down_weight)
    given = dict(
        second=second, factor=factor, cot=cotangent, mod=mod, middle=middle, branch=branch
    )
    if fast:
        downs = both(after(downs, second))
        pairs = (pair_z, pair_x, pair_y, None, None, swap(pair_z, 1), None, None, None, None)
    pairs = [
        [[group] for group in pairs[5 * k : 5 * k + 3]] + [list(pairs[5 * k + 3 : 5 * k + 5])]
        for k in range(HALVES)
    ]
    found = ffn_call((0,), where, given, shards, pairs, downs)
    turned, feed_back = found["turned"], found["feed_back"]
    steps = [found]
    if fast:
        pair_x, pair_y = after((pair_x, pair_y), feed_back)
        far = cross(pair_x, pair_y, first_part(height))
        pairs[1][1:3] = [swap(pair_x, 1)], [swap(pair_y, 1)]
    for js in ((1, 2), (3,)):
        given.update(feed_back=feed_back, feed=found["feed"], second_back=found["second_back"])
        if fast and js == (3,):
            far = after(far, found["feed"])
            pairs[0][3], pairs[1][3] = list(far), [swap(array, 1) for array in far]
        found = ffn_call(js, where, given, shards, pairs, downs)
        steps.append(found)
    output, middle_back, branch_back = found["output"], found["middle_back"], found["branch_back"]
    late_sums = found["sums"]

    def by_slot(chunk_sums):
        return lax.dot_general(
            one_hot,
            chunk_sums,
            (((0,), (0,)), ((), ())),
            precision=lax.Precision.HIGHEST,
            preferred_element_type=f32,
        ).astype(bf16)

    def near_rows(rows):
        return jnp.concatenate([rows] + over_z(rows), axis=0)

    late_rows = jnp.concatenate([by_slot(late_sums), lifted], axis=1)
    late_k = over_z(late_rows)

    count = fsdp_count
    hiddens = [step["hidden_turned"] for step in steps]
    backs = [step["pair_back"] for step in steps]
    pair_theirs = pair_grad_call(count, where, turned, backs)
    late_k, pair_theirs = after((late_k, pair_theirs))
    near_late = jnp.concatenate([late_rows] + late_k, axis=0)
    late = lax.all_gather(near_late, "bucket", axis=0, tiled=True)
    if fast:
        pair_other = swap(pair_theirs, 1)
        feed_back = after(feed_back, pair_theirs)
    else:
        pair_other = jnp.zeros_like(pair_theirs)
    down_theirs = down_grad_call(count, where, hiddens, feed_back)
    if fast:
        pair_other, down_theirs = after((pair_other, down_theirs))
        down_other = swap(down_theirs, 1)
    else:
        down_other = jnp.zeros_like(down_theirs)
    pair_cut = pair_grad_call(count, where, turned, backs, pair_other)
    if fast:
        feed_back = after(feed_back, pair_cut)
    down_mine = down_grad_call(count, where, hiddens, feed_back, down_other)
    if fast:
        down_mine, late = after((down_mine, late))
        down_part = lax.psum_scatter(down_mine, "fsdp", scatter_dimension=0, tiled=False)
        branch_back = after(branch_back, down_mine)
    joint_back = attend_back_call(
        query, keys, values, branch_back, segment_ids, cos, sin, weight
    )
    attn_theirs = attn_grad_call(count, where, first, attended, joint_back, branch_back)
    if fast:
        send_x, keep_x, send_y, keep_y = pair_cut
        keep_x, keep_y, attn_theirs = after((keep_x, keep_y, attn_theirs))
        pair_once = halve_once((send_x, keep_x, send_y, keep_y))
        pair_once, attn_theirs, middle_back = after((pair_once, attn_theirs, middle_back))
        attn_other = swap(attn_theirs, 1)
    grad_inputs, early_sums = first_back_call(joint_back, inputs, middle_back, mod_one, weight)
    if fast:
        a0, a2, b0, b1 = pair_once
        branch_back, grad_inputs = after((branch_back, grad_inputs))
        attn_cut = attn_grad_call(
            count, where, first, attended, joint_back, branch_back, attn_other
        )
        a0, b0, attn_cut = after((a0, b0, attn_cut))
        pair_parts = halve_twice((a0, a2, b0, b1))
        attn_cut, down_part, pair_parts, early_sums = after(
            (attn_cut, down_part, pair_parts, early_sums)
        )
        pair_sum = lax.psum_scatter(pair_parts, "fsdp", scatter_dimension=0, tiled=False)
    near_early = near_rows(by_slot(early_sums))
    early = lax.all_gather(near_early, "bucket", axis=0, tiled=True)
    slope_rows = times_transposed(
        jnp.concatenate([near_early, near_late[:, : 4 * WIDTH]], axis=1), modulate_weight
    ).reshape(fsdp_count, slots, height)
    slopes = [slope_rows[0]] + [
        lax.ppermute(slope_rows[count - by], "fsdp", shifts(count, by)) for by in range(1, count)
    ]
    if fast:
        down_cut = cut_down(down_part, first_part(down_rows))
        send_x, keep_x, send_y, keep_y = (
            jnp.concatenate([attn.reshape(2, -1, WIDTH), down], axis=1)
            for attn, down in zip(attn_cut, down_cut, strict=True)
        )
        keep_x, keep_y, slopes = after((keep_x, keep_y, slopes))
        (a0, a2, b0, b1), pair_sum = after((halve_once((send_x, keep_x, send_y, keep_y)), pair_sum))
        pair_x, pair_y = swap(pair_sum, 2), swap(pair_sum, 4)
        ahead, behind = add(a0, swap(a2, 4)), add(b0, swap(b1, 2))
        at, other_at = (part.shape[1] * part.shape[2] for part in (attn_cut[0], attn_cut[2]))
        attn_parts = jnp.concatenate(
            [half.reshape(count, -1, WIDTH) for half in (ahead[:at], behind[:other_at])], axis=1
        )
        down_total = jnp.concatenate([ahead[at:], behind[other_at:]], axis=0)
        attn_parts, down_total = after((attn_parts, down_total))
        attn_z = send_z(attn_parts)
        pair_x, pair_y, attn_z[1] = after((pair_x, pair_y, attn_z[1]))
        pair_sums = (pair_sum, pair_x, pair_y) + cross(pair_x, pair_y, first_part(height))
        attn_z, pair_sums = after((attn_z, both(pair_sums)))
        attn_sum = total_z(attn_parts, attn_z)
    else:
        down_sums = sum_whole(down_mine.swapaxes(0, 1), down_theirs.swapaxes(0, 1))
        pair_sums = sum_whole(uncut(pair_cut), pair_theirs)
        attn_cut = attn_grad_call(
            count, where, first, attended, joint_back, branch_back, jnp.zeros_like(attn_theirs)
        )
        attn_sums = sum_whole(uncut(attn_cut), attn_theirs)
    if fast:
        early, attn_sum = after((early, attn_sum))
        both_sums = direct(jnp.concatenate([attn_sum, down_total], axis=0))
    all_back = jnp.concatenate([early, late[:, : 4 * WIDTH]], axis=1)
    all_lifted = lax.dynamic_slice_in_dim(late, 4 * WIDTH + place * height, height, 1)
    modulate_gradient = contract_rows(all_lifted, all_back)
    pair_grad = place_call(
        place_pair_kernel, where, pair_sums, (struct(gate_weight.shape, f32),) * 2
    )
    if fast:
        both_sums, pair_grad, modulate_gradient = after((both_sums, pair_grad, modulate_gradient))
        attn_sums = down_sums = both(both_sums)
    slopes = jnp.stack(slopes)
    condition_slope = (
        jnp.stack([pick(slopes, (place + count - j) % count) for j in range(count)])
        .transpose(1, 0, 2)
        .reshape(slots, WIDTH)
    )
    grad_condition = condition_slope * silu_slope(cond_float)
    down_grad = place_call(functools.partial(place_down_kernel, down_rows, half if fast else 0), where, down_sums, struct(down_weight.shape, f32))
    attn_grad = place_call(
        functools.partial(place_attn_kernel, half),
        where,
        attn_sums,
        (struct(joint_weight.shape, f32), struct(project_weight.shape, f32)),
    )

    return (
        output,
        grad_inputs,
        grad_condition,
        modulate_gradient,
        *attn_grad,
        *pair_grad,
        down_grad,
    )


def solution(mesh):
    spread = P(("bucket", "fsdp"), None)
    rows = P("fsdp", None)
    in_specs = (
        spread, spread, P(("bucket", "fsdp")), P(("bucket", "fsdp")), P(),
        rows, rows, rows, rows, rows, rows, spread,
    )
    out_specs = (spread, spread, spread, rows, rows, rows, rows, rows, rows)
    return jax.shard_map(
        on_device, mesh=mesh, in_specs=in_specs, out_specs=out_specs, check_vma=False
    )
```

```python
import functools

import jax
import jax.numpy as jnp
from jax import lax
from jax.experimental import pallas as pl
from jax.experimental.pallas import tpu as pltpu
from jax.sharding import PartitionSpec as P

HEADS = 16
HEAD_DIM = 72
WIDTH = HEADS * HEAD_DIM
QUARTER = HEAD_DIM // 4
BLOCK = 256
CHUNK = 64
COLUMNS = 4
HALVES = 2
PIECES = COLUMNS * HALVES
LANES = 128

epsilon = 1e-06
masked_score = -1e30
f32 = jnp.float32
bf16 = jnp.bfloat16
MEGA = 2**20


def normalize(values):
    average = jnp.mean(values, axis=-1, keepdims=True)
    centered = values - average
    inverse = lax.rsqrt(jnp.mean(centered * centered, axis=-1, keepdims=True) + epsilon)
    return (centered * inverse, inverse)


def normalize_back(normed, inverse, upstream):
    return inverse * (
        upstream
        - jnp.mean(upstream, axis=-1, keepdims=True)
        - normed * jnp.mean(upstream * normed, axis=-1, keepdims=True)
    )


def matmul(left, right):
    return jnp.dot(left, right, preferred_element_type=f32)


def contract_rows(left, right):
    return lax.dot_general(left, right, (((0,), (0,)), ((), ())), preferred_element_type=f32)


def times_transposed(left, right):
    return lax.dot_general(left, right, (((1,), (1,)), ((), ())), preferred_element_type=f32)


def silu_slope(values):
    sigmoid = jax.nn.sigmoid(values)
    return sigmoid * (1.0 + values * (1.0 - sigmoid))


def rope_tables(segments, widths):
    slots = widths.shape[0]
    one_hot = (segments[:, None] == jnp.arange(slots, dtype=jnp.int32)[None, :]).astype(jnp.int32)
    counts = jnp.sum(one_hot, axis=0)
    starts = jnp.cumsum(counts) - counts
    start_token = jnp.sum(one_hot * starts[None, :], axis=1)
    width_token = jnp.maximum(jnp.sum(one_hot * widths[None, :], axis=1), 1)
    place = jnp.arange(segments.shape[0], dtype=jnp.int32) - start_token
    row_place = (place // width_token).astype(f32)
    col_place = (place % width_token).astype(f32)
    freqs = 10000.0 ** (-jnp.arange(QUARTER, dtype=f32) / QUARTER)
    angle_row = row_place[:, None] * freqs[None, :]
    angle_col = col_place[:, None] * freqs[None, :]
    cos_row, sin_row, cos_col, sin_col = (
        jnp.cos(angle_row),
        jnp.sin(angle_row),
        jnp.cos(angle_col),
        jnp.sin(angle_col),
    )
    cos = jnp.concatenate([cos_row, cos_row, cos_col, cos_col], axis=1)
    sin = jnp.concatenate([-sin_row, sin_row, -sin_col, sin_col], axis=1)
    return jnp.tile(cos, (1, HEADS)), jnp.tile(sin, (1, HEADS))


def part(index):
    return slice(index * WIDTH, (index + 1) * WIDTH)


def rotate(values, cos, sin):
    lane = lax.broadcasted_iota(jnp.int32, (1, WIDTH), 1)
    leading = lane % (2 * QUARTER) < QUARTER
    partner = jnp.where(
        leading,
        pltpu.roll(values, WIDTH - QUARTER, 1),
        pltpu.roll(values, QUARTER, 1),
    )
    return values * cos + partner * sin


def take(start, size):
    return pl.ds(pl.multiple_of(start, 128 if size % 128 == 0 else 16), size)


def first_part(rows):
    return -(-rows // 32) * 16


def placed(refs, rows):
    first = first_part(rows)
    each = len(refs) // HALVES
    for other in range(HALVES):
        here = refs[each * other : each * other + each]
        for j in range(3):
            yield j, other, 0, rows, here[j]
        if each == COLUMNS:
            yield 3, other, 0, rows, here[3]
        else:
            yield 3, other, 0, first, here[3]
            yield 3, other, first, rows - first, here[4]


def piece_copies(where, count, sources, target, rows, sem):
    place, column, side = where
    copies = []
    for j, other, start, size, ref in placed(sources, rows):
        for by in range(1, count):
            owner = (place + (count - by)) % count
            to = target(column ^ j, side ^ other, owner, start, size)
            copies.append(pltpu.make_async_copy(ref.at[by - 1], to, sem(column ^ j, side ^ other, owner)))
    return copies


def wait_for(ref, sem):
    pltpu.make_async_copy(ref, ref, sem).wait()


def first_kernel(
    count, where_ref, x_ref, mod_ref, cos_ref, sin_ref, joint_ref, project_ref, *refs
):
    sources, refs = refs[:-9], refs[-9:]
    turned_ref, query_ref, keys_ref, values_ref, weight_ref, weight, first_ref, total, sems = refs
    where = where_ref[0], where_ref[1], where_ref[2]
    rows_in = joint_ref.shape[0]
    half = rows_in // HALVES

    def target(column, side, place, start, size):
        return weight.at[column, take(place * rows_in + side * half + start, size)]

    copies = piece_copies(where, count, sources, target, half, lambda c, s, z: sems.at[c])
    for c in range(COLUMNS):
        shard = project_ref if c == 3 else joint_ref.at[:, pl.ds(c * WIDTH, WIDTH)]
        copies.append(pltpu.make_async_copy(shard, weight.at[c, take(where[0] * rows_in, rows_in)], sems.at[c]))
    for copy in copies:
        copy.start()
    tokens = x_ref.shape[0]
    for i in range(tokens // CHUNK):
        rows = slice(i * CHUNK, (i + 1) * CHUNK)
        normed, _ = normalize(x_ref[rows, :].astype(f32))
        first_ref[rows, :] = (
            normed * (1.0 + mod_ref[i : i + 1, part(1)]) + mod_ref[i : i + 1, part(0)]
        ).astype(bf16)
    turned_ref[...] = first_ref[...].T
    writes = [
        pltpu.make_async_copy(weight.at[c], weight_ref.at[c], sems.at[c]) for c in range(COLUMNS)
    ]
    wait_for(weight.at[3], sems.at[3])
    writes[3].start()
    for c, out in enumerate((query_ref, keys_ref, values_ref)):
        wait_for(weight.at[c], sems.at[c])
        writes[c].start()
        if c == 2:
            out[...] = matmul(first_ref[...], weight[c]).astype(bf16)
        else:
            total[...] = matmul(first_ref[...], weight[c])

            @pl.loop(0, tokens // CHUNK)
            def _(i):
                rows = pl.ds(pl.multiple_of(i * CHUNK, CHUNK), CHUNK)
                out[rows, :] = rotate(total[rows, :], cos_ref[rows, :], sin_ref[rows, :]).astype(bf16)

    for write in writes:
        write.wait()


def window(head):
    start = head * HEAD_DIM // LANES * LANES
    stop = -(-(head + 1) * HEAD_DIM // LANES) * LANES
    lane = lax.broadcasted_iota(jnp.int32, (1, stop - start), 1) + start
    inside = (lane >= head * HEAD_DIM) & (lane < (head + 1) * HEAD_DIM)
    return slice(start, stop), inside


def soft_scores(left, right, allowed, axis):
    scores = times_transposed(left, right) * HEAD_DIM ** (-0.5)
    scores = jnp.where(allowed, scores, masked_score)
    exponent = jnp.exp(scores - jnp.max(scores, axis=axis, keepdims=True))
    return exponent * (1.0 / jnp.sum(exponent, axis=axis, keepdims=True))


def attend_kernel(
    query_ref, keys_ref, values_ref, column_ids, row_ids, x_ref, mod_ref,
    weight, turned_ref, branch_ref, middle_ref, second_ref, mixed,
):
    allowed = column_ids[...] == row_ids[...]
    for head in range(HEADS):
        lanes, inside = window(head)
        query = jnp.where(inside, query_ref[:, lanes], jnp.zeros((), bf16))
        probs = soft_scores(query, keys_ref[:, lanes], allowed, 1).astype(bf16)
        mixed[:, lanes] = jnp.where(inside, matmul(probs, values_ref[:, lanes]), mixed[:, lanes])
    attended = mixed[...].astype(bf16)
    turned_ref[...] = attended.T
    branch_ref[...] = matmul(attended, weight[0])
    for i in range(BLOCK // CHUNK):
        rows = slice(i * CHUNK, (i + 1) * CHUNK)
        mod = mod_ref.at[0]
        middle = x_ref[rows, :].astype(f32) + mod[i : i + 1, part(0)] * branch_ref[rows, :]
        middle_ref[rows, :] = middle
        normed, _ = normalize(middle)
        second_ref[rows, :] = (
            normed * (1.0 + mod[i : i + 1, part(2)]) + mod[i : i + 1, part(1)]
        ).astype(bf16)


def tile_copies(r, where, count, tile, pair, downs):
    place, mine, side = where
    t, j = tile
    column = mine ^ j
    rows, width = r["gate"].shape[0], r["hidden_w"].shape[1]
    sem = r["pair_sems"].at[t]
    copies = [
        pltpu.make_async_copy(
            r[name].at[:, take(column * width, width)], r["pair_w"].at[t, which, take(place * rows, rows)], sem
        )
        for which, name in enumerate(("gate", "up"))
    ]
    first = first_part(rows)
    for other in range(HALVES):
        for by in range(1, count):
            owner = (place + (count - by)) % count
            if j < 3:
                spans = [(pair[other][0].at[by - 1], 0, rows)]
            else:
                spans = [(pair[other][0].at[by - 1], 0, first), (pair[other][1].at[by - 1], first, rows - first)]
            for ref, start, size in spans:
                to = r["pair_w"].at[t, side ^ other, take(owner * rows + start, size)]
                copies.append(pltpu.make_async_copy(ref, to, sem))
    for copy in copies:
        copy.start()

    sem = r["down_sems"].at[t]
    target = r["down_w"].at[t]
    piece = width // PIECES

    @pl.when(column == place)
    def _():
        pltpu.make_async_copy(r["down"], target, sem).start()

    @pl.when(column != place)
    def _():
        by = jnp.maximum((place + count - column) % count, 1)
        for i, other, start, size, ref in placed(downs, piece):
            to = target.at[take(((mine ^ i) * HALVES + (side ^ other)) * piece + start, size)]
            pltpu.make_async_copy(ref.at[by - 1], to, sem).start()


def ffn_kernel(count, js, names, *refs):
    r = dict(zip(names, refs, strict=True))
    r["hidden_w"] = r["hidden"]
    first, last = js[0] == 0, js[-1] == COLUMNS - 1
    step = pl.program_id(0)
    tile = r["hidden"].shape[1]
    tokens = r["second"].shape[0]
    second, feed_back = r["second"], r["feed_back"]
    feed, second_back = r["feed"], r["second_back"]

    @pl.when(step == 0)
    def _():
        where = r["where"][0], r["where"][1], r["where"][2]
        for t, j in enumerate(js):
            pair = [
                [r[f"pair{j}_{other}_{i}"] for i in range(1 if j < 3 else 2)]
                for other in range(HALVES)
            ]
            tile_copies(r, where, count, (t, j), pair, [r[name] for name in names if name[:4] == "down" and name[5:].isdigit()])
        if first:
            r["turned"][...] = second[...].T
            for i in range(tokens // CHUNK):
                rows = slice(i * CHUNK, (i + 1) * CHUNK)
                upstream = r["cot"][rows, :].astype(f32) * r["factor"][0]
                feed_back[rows, :] = (upstream * r["mod"][i : i + 1, part(3)]).astype(bf16)

    pair_w, down_w = r["pair_w"].at[step], r["down_w"].at[step]
    wait_for(pair_w, r["pair_sems"].at[step])
    wait_for(down_w, r["down_sems"].at[step])
    sub = 256
    for n in range(tile // sub):
        lanes = slice(n * sub, (n + 1) * sub)
        gate = matmul(second[...], pair_w[0, :, lanes])
        upval = matmul(second[...], pair_w[1, :, lanes])
        hidden_back = times_transposed(feed_back[...], down_w[lanes, :])
        sigmoid = jax.nn.sigmoid(gate)
        silu = gate * sigmoid
        r["hidden"][:, lanes] = (silu * upval).astype(bf16)
        r["pair_back"][0, 1, :, lanes] = (hidden_back * silu).astype(bf16)
        r["pair_back"][0, 0, :, lanes] = (
            hidden_back * upval * (sigmoid * (1.0 + gate * (1.0 - sigmoid)))
        ).astype(bf16)

    r["hidden_turned"][0] = r["hidden"][...].T
    feed_part = matmul(r["hidden"][...], down_w[...])
    back_part = times_transposed(r["pair_back"][0, 0], pair_w[0]) + times_transposed(
        r["pair_back"][0, 1], pair_w[1]
    )

    @pl.when(step == 0)
    def _():
        feed[...] = feed_part if first else r["feed_in"][...] + feed_part
        second_back[...] = back_part if first else r["back_in"][...] + back_part

    @pl.when(step > 0)
    def _():
        feed[...] += feed_part
        second_back[...] += back_part

    if not last:
        return

    @pl.when(step == len(js) - 1)
    def _():
        for i in range(tokens // CHUNK):
            rows = slice(i * CHUNK, (i + 1) * CHUNK)
            gate_one = r["mod"][i : i + 1, part(0)]
            scale_two = r["mod"][i : i + 1, part(2)]
            gate_two = r["mod"][i : i + 1, part(3)]
            middle = r["middle"][rows, :]
            r["output"][rows, :] = (middle + gate_two * feed[rows, :]).astype(bf16)
            upstream = r["cot"][rows, :].astype(f32) * r["factor"][0]
            normed, inverse = normalize(middle)
            back = second_back[rows, :]
            middle_back = upstream + normalize_back(normed, inverse, back * (1.0 + scale_two))
            r["middle_back"][rows, :] = middle_back
            r["branch_back"][rows, :] = (middle_back * gate_one).astype(bf16)
            for where, values in enumerate(
                (middle_back * r["branch"][rows, :], back, back * normed, upstream * feed[rows, :])
            ):
                r["sums"][i : i + 1, part(where)] = jnp.sum(values, axis=0, keepdims=True)


ORDER = (1, 3, 2, 0)
SEND_X, KEEP_X, SEND_Y, KEEP_Y = (1, 3), (2, 0), (3, 2), (1, 0)
CUT = (SEND_X, KEEP_X, SEND_Y, KEEP_Y)


def put_grad(grad, other_ref, out_refs):
    step = pl.program_id(0)
    if other_ref is None:
        out_refs[0][0] = grad.astype(bf16)
        return
    total = (grad + other_ref[0].astype(f32)).astype(bf16)
    first = first_part(total.shape[1])
    for at, j in enumerate(ORDER):

        @pl.when(step == at)
        def _():
            for columns, ref in zip(CUT, out_refs, strict=True):
                if j in columns:
                    ref[0] = total[:, :first] if columns in (SEND_X, KEEP_X) else total[:, first:]


def cut_specs(count, rows, breadth):
    first = first_part(rows)
    shapes, specs = [], []
    for columns in CUT:
        size = first if columns in (SEND_X, KEEP_X) else rows - first
        shapes.append(struct((2, count, size, breadth), bf16))
        second = ORDER.index(columns[1])
        specs.append(
            pl.BlockSpec(
                (1, count, size, breadth),
                lambda s, where, second=second: (jnp.where(s >= second, 1, 0), 0, 0, 0),
            )
        )
    return tuple(shapes), tuple(specs)


def split_refs(mine, refs):
    return (refs[0], refs[1:]) if mine else (None, refs)


def pair_grad_kernel(mine, count, where_ref, turned_ref, own_ref, near_ref, far_ref, *refs):
    other_ref, out_refs = split_refs(mine, refs)
    for at, j in enumerate(ORDER):

        @pl.when(pl.program_id(0) == at)
        def _():
            back = {0: own_ref, 3: far_ref}.get(j, near_ref)
            grad = matmul(turned_ref[...], back[0, 0])
            put_grad(grad.reshape(count, grad.shape[0] // count, grad.shape[1]), other_ref, out_refs)


def down_grad_kernel(mine, where_ref, *refs):
    hiddens, feed_back_ref, out_ref = refs[:3], refs[3], refs[-1]
    other_ref = refs[4] if mine else None
    side = where_ref[2] if mine else where_ref[2] ^ 1
    count, _, rows, _ = out_ref.shape
    tiles = [(hidden, t) for hidden in hiddens for t in range(hidden.shape[0])]
    for j, (hidden, t) in enumerate(tiles):
        pieces = [hidden[t, take(((where_ref[1] ^ c) * HALVES + side) * rows, rows), :] for c in ORDER]
        grad = matmul(jnp.concatenate(pieces, axis=0), feed_back_ref[...]).reshape(COLUMNS, rows, WIDTH)
        owner = where_ref[1] ^ j
        if mine:
            grad = grad + other_ref[owner].astype(f32)
        out_ref[owner] = grad.astype(bf16)


def attn_grad_kernel(
    mine, where_ref, first_ref, attended_ref, joint_back_ref, branch_back_ref, *refs
):
    other_ref, out_refs = split_refs(mine, refs)
    column = where_ref[1] ^ where_ref[3 + pl.program_id(0)]
    side = where_ref[2] if mine else where_ref[2] ^ 1
    _, count, _, _ = out_refs[0].shape
    rows = WIDTH // count // HALVES

    def put(turned, right):
        taken = [turned[take((z * HALVES + side) * rows, rows), :] for z in range(count)]
        grad = matmul(jnp.concatenate(taken, axis=0), right[...])
        put_grad(grad.reshape(count, rows, WIDTH), other_ref, out_refs)

    @pl.when(column < 3)
    def _():
        put(first_ref, joint_back_ref)

    @pl.when(column == 3)
    def _():
        put(attended_ref, branch_back_ref)


def place_pair_kernel(where_ref, *refs):
    sources, outs = refs[:-2], refs[-2:]
    rows, tile = sources[0].shape
    for way in range(HALVES):

        @pl.when(where_ref[2] == way)
        def _():
            for j, other, start, size, ref in placed(sources, rows):
                lanes = take((where_ref[1] ^ j) * tile, tile)
                outs[way ^ other][start : start + size, lanes] = ref[...].astype(f32)


def place_down_kernel(rows, offset, where_ref, *refs):
    sources, out = refs[:-1], refs[-1]
    for j, other, start, size, ref in placed(sources, rows):
        piece = (where_ref[1] ^ j) * HALVES + (where_ref[2] ^ other)
        at = offset if ref.shape[0] > rows else 0
        out[take(piece * rows + start, size), :] = ref[at : at + size, :].astype(f32)


def place_attn_kernel(rows, where_ref, *refs):
    sources, joint_ref, project_ref = refs[:-2], refs[-2], refs[-1]
    for column in range(COLUMNS):

        @pl.when(where_ref[1] == column)
        def _():
            for j, other, start, size, ref in placed(sources, rows):
                to = take((where_ref[2] ^ other) * rows + start, size)
                if column ^ j == 3:
                    project_ref[to, :] = ref[:size, :].astype(f32)
                else:
                    joint_ref[to, part(column ^ j)] = ref[:size, :].astype(f32)


def place_both_kernel(attn_rows, down_rows, where_ref, *refs):
    sources, outs = refs[:-3], refs[-3:]
    each = len(sources) // HALVES
    sides = [sources[each * k : each * k + each] for k in range(HALVES)]
    place_attn_kernel(
        attn_rows, where_ref, *[ref for side in sides for ref in side[:4]], outs[0], outs[1]
    )
    downs = [ref for side in sides for ref in side[:3] + side[4:]]
    place_down_kernel(down_rows, attn_rows, where_ref, *downs, outs[2])


def attend_back_kernel(
    query_ref, keys_ref, values_ref, branch_back_ref, column_ids, row_ids, cos_ref,
    sin_ref, weight, joint_back_ref, mixed_back, query_back, keys_back, values_back,
):
    mixed_back[...] = times_transposed(branch_back_ref[...], weight[0]).astype(bf16)
    allowed = column_ids[...] == row_ids[...]
    scaling = HEAD_DIM ** (-0.5)
    for head in range(HEADS):
        lanes, inside = window(head)
        zero = jnp.zeros((), bf16)
        query = jnp.where(inside, query_ref[:, lanes], zero)
        back = jnp.where(inside, mixed_back[:, lanes], zero)
        soft = soft_scores(keys_ref[:, lanes], query, allowed, 0)
        probs_back = times_transposed(values_ref[:, lanes], back)
        scores_back = (
            soft * (probs_back - jnp.sum(soft * probs_back, axis=0, keepdims=True))
        ).astype(bf16)
        query_back[:, lanes] = jnp.where(
            inside, contract_rows(scores_back, keys_ref[:, lanes]) * scaling, query_back[:, lanes]
        )
        keys_back[:, lanes] = jnp.where(
            inside, matmul(scores_back, query) * scaling, keys_back[:, lanes]
        )
        values_back[:, lanes] = jnp.where(
            inside, matmul(soft.astype(bf16), back), values_back[:, lanes]
        )

    @pl.loop(0, BLOCK // CHUNK)
    def _(i):
        rows = pl.ds(pl.multiple_of(i * CHUNK, CHUNK), CHUNK)
        cos, sin = cos_ref[rows, :], sin_ref[rows, :]
        joint_back_ref[rows, part(0)] = rotate(query_back[rows, :], cos, -sin).astype(bf16)
        joint_back_ref[rows, part(1)] = rotate(keys_back[rows, :], cos, -sin).astype(bf16)
        joint_back_ref[rows, part(2)] = values_back[rows, :].astype(bf16)


def first_back_kernel(
    joint_back_ref, x_ref, middle_back_ref, mod_ref, weight, grad_ref, sums_ref, first_back
):
    step = pl.program_id(0)
    product = times_transposed(joint_back_ref[...], weight[0])

    @pl.when(step == 0)
    def _():
        first_back[...] = product

    @pl.when(step > 0)
    def _():
        first_back[...] += product

    @pl.when(step == pl.num_programs(0) - 1)
    def _():
        finish_first_back(x_ref, middle_back_ref, mod_ref, grad_ref, sums_ref, first_back)


def finish_first_back(x_ref, middle_back_ref, mod_ref, grad_ref, sums_ref, first_back):
    for i in range(x_ref.shape[0] // CHUNK):
        rows = slice(i * CHUNK, (i + 1) * CHUNK)
        normed, inverse = normalize(x_ref[rows, :].astype(f32))
        back = first_back[rows, :]
        grad_ref[rows, :] = middle_back_ref[rows, :] + normalize_back(
            normed, inverse, back * (1.0 + mod_ref[i : i + 1, part(1)])
        )
        sums_ref[i : i + 1, part(0)] = jnp.sum(back, axis=0, keepdims=True)
        sums_ref[i : i + 1, part(1)] = jnp.sum(back * normed, axis=0, keepdims=True)


SMEM = pl.BlockSpec(memory_space=pltpu.SMEM)
VMEM = pl.BlockSpec(memory_space=pltpu.VMEM)
ANY = pl.BlockSpec(memory_space=pl.ANY)


def struct(shape, dtype):
    return jax.ShapeDtypeStruct(shape, dtype)


def params(mega=56):
    return pltpu.CompilerParams(vmem_limit_bytes=mega * MEGA)


def cost(microseconds):
    return pl.CostEstimate(flops=int(microseconds * 1e9), bytes_accessed=1000, transcendentals=0)


def by_block(*shape):
    return pl.BlockSpec(shape, lambda b: (b,) + (0,) * (len(shape) - 1))


def whole(*shape):
    return pl.BlockSpec(shape, lambda *_: (0,) * len(shape))


def first_call(where, x, mod, cos, sin, joint, project, arrived):
    tokens = x.shape[0]
    count = arrived[0].shape[0] + 1
    shape = struct((tokens, WIDTH), bf16)
    return pl.pallas_call(
        functools.partial(first_kernel, count),
        out_shape=(struct((WIDTH, tokens), bf16),)
        + (shape,) * 3
        + (struct((COLUMNS, WIDTH, WIDTH), bf16),),
        in_specs=[SMEM, VMEM, VMEM, VMEM, VMEM] + [ANY] * (2 + len(arrived)),
        out_specs=(VMEM,) * 4 + (ANY,),
        scratch_shapes=[
            pltpu.VMEM((COLUMNS, WIDTH, WIDTH), bf16),
            pltpu.VMEM((tokens, WIDTH), bf16),
            pltpu.VMEM((tokens, WIDTH), f32),
            pltpu.SemaphoreType.DMA((COLUMNS,)),
        ],
        compiler_params=params(),
        cost_estimate=cost(20),
    )(where, x, mod, cos, sin, joint, project, *arrived)


def attend_call(query, keys, values, ids, x, mod, weight):
    tokens = x.shape[0]
    return pl.pallas_call(
        attend_kernel,
        grid=(tokens // BLOCK,),
        out_shape=(
            struct((WIDTH, tokens), bf16),
            struct((tokens, WIDTH), f32),
            struct((tokens, WIDTH), f32),
            struct((tokens, WIDTH), bf16),
        ),
        in_specs=[by_block(BLOCK, WIDTH)] * 3
        + [by_block(BLOCK, 1), pl.BlockSpec((1, BLOCK), lambda b: (0, b)), by_block(BLOCK, WIDTH)]
        + [by_block(1, BLOCK // CHUNK, 4 * WIDTH), pl.BlockSpec((1, WIDTH, WIDTH), lambda b: (3, 0, 0))],
        out_specs=(pl.BlockSpec((WIDTH, BLOCK), lambda b: (0, b)),) + (by_block(BLOCK, WIDTH),) * 3,
        scratch_shapes=[pltpu.VMEM((BLOCK, WIDTH), f32)],
        compiler_params=params(),
        cost_estimate=cost(2),
    )(
        query, keys, values, ids[:, None], ids[None, :], x,
        mod.reshape(tokens // BLOCK, BLOCK // CHUNK, 4 * WIDTH), weight,
    )


def ffn_call(js, where, given, shards, pairs, downs):
    second = given["second"]
    tokens = second.shape[0]
    ff = shards["gate"].shape[1]
    tile = ff // COLUMNS
    count = ff // shards["down"].shape[0]
    chunks = tokens // CHUNK
    first, last = js[0] == 0, js[-1] == COLUMNS - 1
    full = whole(tokens, WIDTH)
    wide = struct((tokens, WIDTH), f32)
    narrow = struct((tokens, WIDTH), bf16)
    inputs = [("where", where, SMEM), ("second", second, full)]
    if first or last:
        inputs += [
            ("factor", given["factor"], SMEM),
            ("cot", given["cot"], full),
            ("mod", given["mod"], whole(chunks, 4 * WIDTH)),
        ]
    if not first:
        inputs += [
            ("feed_back", given["feed_back"], full),
            ("feed_in", given["feed"], full),
            ("back_in", given["second_back"], full),
        ]
    if last:
        inputs += [("middle", given["middle"], full), ("branch", given["branch"], full)]
    inputs += [(name, shards[name], ANY) for name in ("gate", "up", "down")]
    for j in js:
        for other in range(HALVES):
            inputs += [(f"pair{j}_{other}_{i}", a, ANY) for i, a in enumerate(pairs[other][j])]
    inputs += [(f"down_{i}", a, ANY) for i, a in enumerate(downs)]
    outputs = [
        (
            "hidden_turned",
            struct((len(js), tile, tokens), bf16),
            pl.BlockSpec((1, tile, tokens), lambda t: (t, 0, 0)),
        ),
        (
            "pair_back",
            struct((len(js), HALVES, tokens, tile), bf16),
            pl.BlockSpec((1, HALVES, tokens, tile), lambda t: (t, 0, 0, 0)),
        ),
    ]
    if first:
        outputs += [
            ("turned", struct((WIDTH, tokens), bf16), whole(WIDTH, tokens)),
            ("feed_back", narrow, full),
        ]
    sums = ("feed", "second_back")
    scratch = [
        ("pair_w", pltpu.VMEM((len(js), HALVES, WIDTH, tile), bf16)),
        ("down_w", pltpu.VMEM((len(js), ff // count, WIDTH), bf16)),
        ("hidden", pltpu.VMEM((tokens, tile), bf16)),
        ("pair_sems", pltpu.SemaphoreType.DMA((len(js),))),
        ("down_sems", pltpu.SemaphoreType.DMA((len(js),))),
    ]
    if last:
        outputs += [
            ("output", narrow, full),
            ("middle_back", wide, full),
            ("branch_back", narrow, full),
            ("sums", struct((chunks, 4 * WIDTH), f32), whole(chunks, 4 * WIDTH)),
        ]
        scratch += [(name, pltpu.VMEM((tokens, WIDTH), f32)) for name in sums]
    else:
        outputs += [(name, wide, full) for name in sums]
    names = [each[0] for each in inputs + outputs + scratch]
    found = pl.pallas_call(
        functools.partial(ffn_kernel, count, js, names),
        grid=(len(js),),
        out_shape=tuple(shape for _, shape, _ in outputs),
        in_specs=[spec for _, _, spec in inputs],
        out_specs=tuple(spec for _, _, spec in outputs),
        scratch_shapes=[shape for _, shape in scratch],
        compiler_params=params(),
        cost_estimate=cost(2 if first else 12 * len(js)),
    )(*[array for _, array, _ in inputs])
    return {name: array for (name, _, _), array in zip(outputs, found, strict=True)}


def by_column(call, count, rows, breadth, in_specs, where, arrays, other):
    shapes, specs = cut_specs(count, rows, breadth)
    block = pl.BlockSpec((1, count, rows, breadth), lambda s, where: (s, 0, 0, 0))
    if other is None:
        shapes, specs = (struct((COLUMNS, count, rows, breadth), bf16),), (block,)
    else:
        in_specs, arrays = in_specs + [block], arrays + (other,)
    found = pl.pallas_call(
        call,
        out_shape=shapes,
        grid_spec=pltpu.PrefetchScalarGridSpec(
            num_scalar_prefetch=1, grid=(COLUMNS,), in_specs=in_specs, out_specs=specs
        ),
        compiler_params=params(),
        cost_estimate=cost(3),
    )(where, *arrays)
    return found[0] if other is None else found


def pair_grad_call(count, where, turned, backs, other=None):
    tokens, tile = backs[0].shape[2:]
    mine = other is not None

    def spec(tile_of):
        return pl.BlockSpec(
            (1, 1, tokens, tile),
            lambda s, where: (tile_of(where[3 + s]), where[2] if mine else where[2] ^ 1, 0, 0),
        )

    return by_column(
        functools.partial(pair_grad_kernel, mine, count),
        count, WIDTH // count, tile,
        [whole(WIDTH, tokens), spec(lambda j: 0), spec(lambda j: jnp.clip(j - 1, 0, 1)), spec(lambda j: 0)],
        where, (turned,) + tuple(backs), other,
    )


def attn_grad_call(count, where, first, attended, joint_back, branch_back, other=None):
    tokens = first.shape[1]
    return by_column(
        functools.partial(attn_grad_kernel, other is not None),
        count, WIDTH // count // HALVES, WIDTH,
        [
            whole(WIDTH, tokens),
            whole(WIDTH, tokens),
            pl.BlockSpec((tokens, WIDTH), lambda s, where: (0, jnp.minimum(where[1] ^ where[3 + s], 2))),
            whole(tokens, WIDTH),
        ],
        where, (first, attended, joint_back, branch_back), other,
    )


def down_grad_call(count, where, hiddens, feed_back, other=None):
    ff = sum(h.shape[0] * h.shape[1] for h in hiddens)
    out = struct((count, COLUMNS, ff // count // PIECES, WIDTH), bf16)
    arrays = tuple(hiddens) + (feed_back,) + (() if other is None else (other,))
    return pl.pallas_call(
        functools.partial(down_grad_kernel, other is not None),
        out_shape=out,
        in_specs=[SMEM] + [VMEM] * len(arrays),
        out_specs=VMEM,
        compiler_params=params(),
        cost_estimate=cost(3),
    )(where, *arrays)


def place_call(kernel, where, arrays, outs):
    return pl.pallas_call(
        kernel,
        out_shape=outs,
        in_specs=[SMEM] + [VMEM] * len(arrays),
        out_specs=jax.tree.map(lambda _: VMEM, outs),
        compiler_params=params(),
        cost_estimate=cost(4),
    )(where, *arrays)


def attend_back_call(query, keys, values, branch_back, ids, cos, sin, weight):
    tokens = query.shape[0]
    block = by_block(BLOCK, WIDTH)
    return pl.pallas_call(
        attend_back_kernel,
        grid=(tokens // BLOCK,),
        out_shape=struct((tokens, 3 * WIDTH), bf16),
        in_specs=[block, block, block, block]
        + [by_block(BLOCK, 1), pl.BlockSpec((1, BLOCK), lambda b: (0, b)), block, block]
        + [pl.BlockSpec((1, WIDTH, WIDTH), lambda b: (3, 0, 0))],
        out_specs=by_block(BLOCK, 3 * WIDTH),
        scratch_shapes=[
            pltpu.VMEM((BLOCK, WIDTH), bf16),
            pltpu.VMEM((BLOCK, WIDTH), f32),
            pltpu.VMEM((BLOCK, WIDTH), f32),
            pltpu.VMEM((BLOCK, WIDTH), f32),
        ],
        compiler_params=params(),
        cost_estimate=cost(8),
    )(query, keys, values, branch_back, ids[:, None], ids[None, :], cos, sin, weight)


def first_back_call(joint_back, x, middle_back, mod, weight):
    tokens = x.shape[0]
    chunks = tokens // CHUNK
    full = whole(tokens, WIDTH)
    return pl.pallas_call(
        first_back_kernel,
        grid=(3,),
        out_shape=(struct((tokens, WIDTH), f32), struct((chunks, 2 * WIDTH), f32)),
        in_specs=[
            pl.BlockSpec((tokens, WIDTH), lambda c: (0, c)),
            full,
            full,
            whole(chunks, 2 * WIDTH),
            pl.BlockSpec((1, WIDTH, WIDTH), lambda c: (c, 0, 0)),
        ],
        out_specs=(full, whole(chunks, 2 * WIDTH)),
        scratch_shapes=[pltpu.VMEM((tokens, WIDTH), f32)],
        compiler_params=params(),
        cost_estimate=cost(2),
    )(joint_back, x, middle_back, mod, weight)


def shifts(count, by):
    return [(i, (i + by) % count) for i in range(count)]


def pick(array, index):
    return lax.dynamic_index_in_dim(array, index, 0, keepdims=False)


def across(bit):
    return [(i, i ^ bit) for i in range(PIECES)]


def swap(array, bit):
    return lax.ppermute(array, "bucket", across(bit))


def after(arrays, *others):
    return lax.optimization_barrier((arrays, others))[0]


def add(left, right):
    return (left.astype(f32) + right.astype(f32)).astype(bf16)


def over_z(piece):
    count = lax.axis_size("fsdp")
    return [lax.ppermute(piece, "fsdp", shifts(count, by)) for by in range(1, count)]


def gather_z(piece, *others):
    count = lax.axis_size("fsdp")
    place = lax.axis_index("fsdp")
    full = after(lax.all_gather(piece, "fsdp", axis=0, tiled=False), *others)
    return jnp.stack([pick(full, (place + count - by) % count) for by in range(1, count)])


def cross(by_x, by_y, first):
    if first is not None:
        by_x, by_y = by_x[..., :first, :], by_y[..., first:, :]
    return swap(by_x, 4), swap(by_y, 2)


def both(here):
    return here + tuple(None if array is None else swap(array, 1) for array in here)


def direct(piece):
    return piece, swap(piece, 2), swap(piece, 4), swap(piece, 6)


def spread_whole(pieces):
    first = first_part(pieces.shape[1])

    def of(side):
        own, by_x, by_y, far = (pieces[c * HALVES + side] for c in range(COLUMNS))
        return own, by_x, by_y, far[:first], far[first:]

    return of(0) + of(1)


def halve_once(cut):
    send_x, (a2, a0), send_y, (b1, b0) = cut
    from_x, from_y = swap(send_x, 2), swap(send_y, 4)
    return add(a0, from_x[0]), add(a2, from_x[1]), add(b0, from_y[1]), add(b1, from_y[0])


def halve_twice(once, *others):
    a0, a2, b0, b1 = once
    if others:
        a0, b0 = after((a0, b0), *others)
    return jnp.concatenate([add(a0, swap(a2, 4)), add(b0, swap(b1, 2))], axis=-2)


def send_z(parts):
    count = lax.axis_size("fsdp")
    place = lax.axis_index("fsdp")
    return [
        lax.ppermute(pick(parts, (place + by) % count), "fsdp", shifts(count, by))
        for by in range(1, count)
    ]


def total_z(parts, others):
    total = pick(parts, lax.axis_index("fsdp")).astype(f32)
    for array in others:
        total = total + array.astype(f32)
    return total.astype(bf16)


def sum_z(parts):
    return total_z(parts, send_z(parts))


def cut_down(part, first):
    cut = []
    for columns in CUT:
        both_columns = jnp.stack([part[ORDER.index(j)] for j in columns])
        cut.append(both_columns[:, :first] if columns in (SEND_X, KEEP_X) else both_columns[:, first:])
    return cut


def uncut(cut):
    def of(j, pair):
        columns = next(c for c in pair if j in c)
        return cut[CUT.index(columns)][columns.index(j)]

    return jnp.stack(
        [jnp.concatenate([of(j, (SEND_X, KEEP_X)), of(j, (SEND_Y, KEEP_Y))], axis=1) for j in ORDER]
    )


def sum_whole(mine, theirs):
    parts = jnp.stack([mine, theirs], axis=1)
    parts = jnp.stack([parts[ORDER.index(c)] for c in range(COLUMNS)])
    rows, breadth = mine.shape[2:]
    parts = lax.psum(parts, "bucket").transpose(2, 0, 1, 3, 4)
    return spread_whole(sum_z(parts).reshape(PIECES, rows, breadth))


def arrived_whole(pieces):
    count = lax.axis_size("fsdp")
    place = lax.axis_index("fsdp")
    first = first_part(pieces.shape[1])
    full = lax.all_gather(pieces, "fsdp", axis=0, tiled=False)
    full = jnp.stack([pick(full, (place + count - by) % count) for by in range(1, count)])

    def of(side):
        own, by_x, by_y, far = (full[:, c * HALVES + side] for c in range(COLUMNS))
        return own, by_x, by_y, far[:, :first], far[:, first:]

    return of(0) + of(1)


def to_group(rows, count, place):
    relative = jnp.stack(
        [pick(rows, place)]
        + [
            lax.ppermute(pick(rows, (place + by) % count), "fsdp", shifts(count, by))
            for by in range(1, count)
        ]
    )
    return jnp.stack([pick(relative, (place - j) % count) for j in range(count)])


def on_device(
    inputs,
    condition,
    segment_ids,
    grid_widths,
    bucket_counts,
    modulate_weight,
    joint_weight,
    project_weight,
    gate_weight,
    up_weight,
    down_weight,
    cotangent,
):
    fsdp_count = lax.axis_size("fsdp")
    place = lax.axis_index("fsdp")
    bucket = lax.axis_index("bucket")
    height = joint_weight.shape[0]
    half = height // HALVES
    ff = gate_weight.shape[1]
    tile = ff // COLUMNS
    down_rows = down_weight.shape[0] // PIECES
    slots = condition.shape[0]

    cond_float = condition.astype(f32)
    lifted = jax.nn.silu(cond_float).astype(bf16)
    lifted_rows = to_group(
        lifted.reshape(slots, fsdp_count, height).transpose(1, 0, 2), fsdp_count, place
    ).reshape(fsdp_count * slots, height)
    one_hot = (
        segment_ids[::CHUNK, None] == jnp.arange(slots, dtype=jnp.int32)[None, :]
    ).astype(f32)

    def modulation_parts(weight, rows):
        parts = matmul(rows, weight).reshape(fsdp_count, slots, weight.shape[1])
        return [pick(parts, place)] + [
            lax.ppermute(pick(parts, (place + by) % fsdp_count), "fsdp", shifts(fsdp_count, by))
            for by in range(1, fsdp_count)
        ]

    def modulation(parts):
        return jnp.dot(
            one_hot,
            sum(parts[1:], parts[0]),
            precision=lax.Precision.HIGHEST,
            preferred_element_type=f32,
        )

    first_rows = modulation_parts(modulate_weight[:, : 2 * WIDTH], lifted_rows)
    mod_one = modulation(first_rows)
    fast = lax.axis_size("bucket") == PIECES
    if fast:
        column, side = bucket // HALVES, bucket % HALVES
        where = jnp.stack([place, column, side] + [jnp.int32(j) for j in ORDER])
        attn_piece = jnp.where(
            column == 3,
            lax.dynamic_slice(project_weight, (side * half, 0), (half, WIDTH)),
            lax.dynamic_slice(joint_weight, (side * half, column * WIDTH), (half, WIDTH)),
        )
        ffn_piece = jnp.where(
            side == 0,
            lax.dynamic_slice(gate_weight, (0, column * tile), (height, tile)),
            lax.dynamic_slice(up_weight, (0, column * tile), (height, tile)),
        )
        down_piece = lax.dynamic_slice_in_dim(down_weight, bucket * down_rows, down_rows, 0)
        attn_z = gather_z(attn_piece, first_rows)
        down_k = over_z(after(down_piece, attn_z))
        attn_x, attn_y = swap(attn_z, 2), swap(attn_z, 4)
        attn_x, attn_y, down_k = after((attn_x, attn_y, down_k))
        attn_far = cross(attn_x, attn_y, first_part(half))
        pair_z = gather_z(after(ffn_piece, down_k))
        down_z = jnp.stack(down_k)
        attn_arrived = both((attn_z, attn_x, attn_y) + attn_far)
        inputs, down_z = after((inputs, down_z), attn_far)
        down_x, down_y = swap(down_z, 2), swap(down_z, 4)
        inputs = after(inputs, down_z)
    else:
        where = jnp.stack([place, 0 * place, 0 * place] + [jnp.int32(j) for j in ORDER])
        attn_arrived = arrived_whole(
            jnp.concatenate([joint_weight, project_weight], axis=1)
            .reshape(HALVES, half, COLUMNS, WIDTH)
            .transpose(2, 0, 1, 3)
            .reshape(PIECES, half, WIDTH)
        )
        pairs = arrived_whole(
            jnp.stack([gate_weight, up_weight])
            .reshape(HALVES, height, COLUMNS, tile)
            .transpose(2, 0, 1, 3)
            .reshape(PIECES, height, tile)
        )
        downs = arrived_whole(down_weight.reshape(PIECES, down_rows, WIDTH))

    if fast:
        lifted_rows = after(lifted_rows, down_k)
    late_rows = modulation_parts(modulate_weight[:, 2 * WIDTH :], lifted_rows)
    counts = bucket_counts.astype(f32)
    mine = jnp.sum(jnp.where(jnp.arange(counts.shape[0], dtype=jnp.int32) == bucket, counts, 0.0))
    factor = (mine * counts.shape[0] / jnp.sum(counts)).reshape(1)
    cos, sin = rope_tables(segment_ids, grid_widths)

    first, query, keys, values, weight = first_call(
        where, inputs, mod_one, cos, sin, joint_weight, project_weight, attn_arrived
    )
    if fast:
        late_rows = [late_rows[0], *after(late_rows[1:], query)]
        down_x, down_y = after((down_x, down_y), query)
        down_far = cross(down_x, down_y, first_part(down_rows))
        downs = (down_z, down_x, down_y) + down_far
        pair_z = after(pair_z, query)
        pair_x, pair_y = swap(pair_z, 2), swap(pair_z, 4)
    mod = modulation(late_rows)
    attended, branch, middle, second = attend_call(
        query, keys, values, segment_ids, inputs, mod, weight
    )
    shards = dict(gate=gate_weight, up=up_weight, down=down_weight)
    given = dict(
        second=second, factor=factor, cot=cotangent, mod=mod, middle=middle, branch=branch
    )
    if fast:
        downs = both(after(downs, second))
        pairs = (pair_z, pair_x, pair_y, None, None, swap(pair_z, 1), None, None, None, None)
    pairs = [
        [[group] for group in pairs[5 * k : 5 * k + 3]] + [list(pairs[5 * k + 3 : 5 * k + 5])]
        for k in range(HALVES)
    ]
    found = ffn_call((0,), where, given, shards, pairs, downs)
    turned, feed_back = found["turned"], found["feed_back"]
    steps = [found]
    if fast:
        pair_x, pair_y = after((pair_x, pair_y), feed_back)
        far = cross(pair_x, pair_y, first_part(height))
        pairs[1][1:3] = [swap(pair_x, 1)], [swap(pair_y, 1)]
    for js in ((1, 2), (3,)):
        given.update(feed_back=feed_back, feed=found["feed"], second_back=found["second_back"])
        if fast and js == (3,):
            far = after(far, found["feed"])
            pairs[0][3], pairs[1][3] = list(far), [swap(array, 1) for array in far]
        found = ffn_call(js, where, given, shards, pairs, downs)
        steps.append(found)
    output, middle_back, branch_back = found["output"], found["middle_back"], found["branch_back"]
    late_sums = found["sums"]

    def by_slot(chunk_sums):
        return lax.dot_general(
            one_hot,
            chunk_sums,
            (((0,), (0,)), ((), ())),
            precision=lax.Precision.HIGHEST,
            preferred_element_type=f32,
        ).astype(bf16)

    def near_rows(rows):
        return jnp.concatenate([rows] + over_z(rows), axis=0)

    late_rows = jnp.concatenate([by_slot(late_sums), lifted], axis=1)
    late_k = over_z(late_rows)

    count = fsdp_count
    hiddens = [step["hidden_turned"] for step in steps]
    backs = [step["pair_back"] for step in steps]
    pair_theirs = pair_grad_call(count, where, turned, backs)
    late_k, pair_theirs = after((late_k, pair_theirs))
    near_late = jnp.concatenate([late_rows] + late_k, axis=0)
    late = lax.all_gather(near_late, "bucket", axis=0, tiled=True)
    if fast:
        pair_other = swap(pair_theirs, 1)
        feed_back = after(feed_back, pair_theirs)
    else:
        pair_other = jnp.zeros_like(pair_theirs)
    down_theirs = down_grad_call(count, where, hiddens, feed_back)
    if fast:
        pair_other, down_theirs = after((pair_other, down_theirs))
        down_other = swap(down_theirs, 1)
    else:
        down_other = jnp.zeros_like(down_theirs)
    pair_cut = pair_grad_call(count, where, turned, backs, pair_other)
    if fast:
        feed_back = after(feed_back, pair_cut)
    down_mine = down_grad_call(count, where, hiddens, feed_back, down_other)
    if fast:
        down_mine, late = after((down_mine, late))
        down_part = lax.psum_scatter(down_mine, "fsdp", scatter_dimension=0, tiled=False)
        branch_back = after(branch_back, down_mine)
    joint_back = attend_back_call(
        query, keys, values, branch_back, segment_ids, cos, sin, weight
    )
    attn_theirs = attn_grad_call(count, where, first, attended, joint_back, branch_back)
    if fast:
        send_x, keep_x, send_y, keep_y = pair_cut
        keep_x, keep_y, attn_theirs = after((keep_x, keep_y, attn_theirs))
        pair_once = halve_once((send_x, keep_x, send_y, keep_y))
        pair_once, attn_theirs, middle_back = after((pair_once, attn_theirs, middle_back))
        attn_other = swap(attn_theirs, 1)
    grad_inputs, early_sums = first_back_call(joint_back, inputs, middle_back, mod_one, weight)
    if fast:
        a0, a2, b0, b1 = pair_once
        branch_back, grad_inputs = after((branch_back, grad_inputs))
        attn_cut = attn_grad_call(
            count, where, first, attended, joint_back, branch_back, attn_other
        )
        a0, b0, attn_cut = after((a0, b0, attn_cut))
        pair_parts = halve_twice((a0, a2, b0, b1))
        attn_cut, down_part, pair_parts, early_sums = after(
            (attn_cut, down_part, pair_parts, early_sums)
        )
        pair_sum = lax.psum_scatter(pair_parts, "fsdp", scatter_dimension=0, tiled=False)
    near_early = near_rows(by_slot(early_sums))
    early = lax.all_gather(near_early, "bucket", axis=0, tiled=True)
    slope_rows = times_transposed(
        jnp.concatenate([near_early, near_late[:, : 4 * WIDTH]], axis=1), modulate_weight
    ).reshape(fsdp_count, slots, height)
    slopes = [slope_rows[0]] + [
        lax.ppermute(slope_rows[count - by], "fsdp", shifts(count, by)) for by in range(1, count)
    ]
    if fast:
        down_cut = cut_down(down_part, first_part(down_rows))
        send_x, keep_x, send_y, keep_y = (
            jnp.concatenate([attn.reshape(2, -1, WIDTH), down], axis=1)
            for attn, down in zip(attn_cut, down_cut, strict=True)
        )
        keep_x, keep_y, slopes = after((keep_x, keep_y, slopes))
        (a0, a2, b0, b1), pair_sum = after((halve_once((send_x, keep_x, send_y, keep_y)), pair_sum))
        pair_x, pair_y = swap(pair_sum, 2), swap(pair_sum, 4)
        ahead, behind = add(a0, swap(a2, 4)), add(b0, swap(b1, 2))
        at, other_at = (part.shape[1] * part.shape[2] for part in (attn_cut[0], attn_cut[2]))
        attn_parts = jnp.concatenate(
            [half.reshape(count, -1, WIDTH) for half in (ahead[:at], behind[:other_at])], axis=1
        )
        down_total = jnp.concatenate([ahead[at:], behind[other_at:]], axis=0)
        attn_parts, down_total = after((attn_parts, down_total))
        attn_z = send_z(attn_parts)
        pair_x, pair_y, attn_z[1] = after((pair_x, pair_y, attn_z[1]))
        pair_sums = (pair_sum, pair_x, pair_y) + cross(pair_x, pair_y, first_part(height))
        attn_z, pair_sums = after((attn_z, both(pair_sums)))
        attn_sum = total_z(attn_parts, attn_z)
    else:
        down_sums = sum_whole(down_mine.swapaxes(0, 1), down_theirs.swapaxes(0, 1))
        pair_sums = sum_whole(uncut(pair_cut), pair_theirs)
        attn_cut = attn_grad_call(
            count, where, first, attended, joint_back, branch_back, jnp.zeros_like(attn_theirs)
        )
        attn_sums = sum_whole(uncut(attn_cut), attn_theirs)
    if fast:
        early, attn_sum = after((early, attn_sum))
        both_sum = jnp.concatenate([attn_sum, down_total], axis=0)
        both_x, both_y = swap(both_sum, 2), swap(both_sum, 4)
    all_back = jnp.concatenate([early, late[:, : 4 * WIDTH]], axis=1)
    all_lifted = lax.dynamic_slice_in_dim(late, 4 * WIDTH + place * height, height, 1)
    modulate_gradient = contract_rows(all_lifted, all_back)
    pair_grad = place_call(
        place_pair_kernel, where, pair_sums, (struct(gate_weight.shape, f32),) * 2
    )
    if fast:
        both_x, both_y, pair_grad, modulate_gradient = after(
            (both_x, both_y, pair_grad, modulate_gradient)
        )
        both_sums = both((both_sum, both_x, both_y) + cross(both_x, both_y, half))
    slopes = jnp.stack(slopes)
    condition_slope = (
        jnp.stack([pick(slopes, (place + count - j) % count) for j in range(count)])
        .transpose(1, 0, 2)
        .reshape(slots, WIDTH)
    )
    grad_condition = condition_slope * silu_slope(cond_float)
    attn_shapes = (struct(joint_weight.shape, f32), struct(project_weight.shape, f32))
    down_shape = struct(down_weight.shape, f32)
    if fast:
        *attn_grad, down_grad = place_call(
            functools.partial(place_both_kernel, half, down_rows),
            where,
            both_sums,
            attn_shapes + (down_shape,),
        )
    else:
        down_grad = place_call(
            functools.partial(place_down_kernel, down_rows, 0), where, down_sums, down_shape
        )
        attn_grad = place_call(
            functools.partial(place_attn_kernel, half), where, attn_sums, attn_shapes
        )
    return (
        output,
        grad_inputs,
        grad_condition,
        modulate_gradient,
        *attn_grad,
        *pair_grad,
        down_grad,
    )


def solution(mesh):
    spread = P(("bucket", "fsdp"), None)
    rows = P("fsdp", None)
    in_specs = (
        spread, spread, P(("bucket", "fsdp")), P(("bucket", "fsdp")), P(),
        rows, rows, rows, rows, rows, rows, spread,
    )
    out_specs = (spread, spread, spread, rows, rows, rows, rows, rows, rows)
    return jax.shard_map(
        on_device, mesh=mesh, in_specs=in_specs, out_specs=out_specs, check_vma=False
    )
```

```python
import functools

import jax
import jax.numpy as jnp
from jax import lax
from jax.experimental import pallas as pl
from jax.experimental.pallas import tpu as pltpu
from jax.sharding import PartitionSpec as P

HEADS = 16
HEAD_DIM = 72
WIDTH = HEADS * HEAD_DIM
QUARTER = HEAD_DIM // 4
BLOCK = 256
CHUNK = 64
COLUMNS = 4
HALVES = 2
PIECES = COLUMNS * HALVES
LANES = 128

epsilon = 1e-06
masked_score = -1e30
f32 = jnp.float32
bf16 = jnp.bfloat16
MEGA = 2**20


def normalize(values):
    average = jnp.mean(values, axis=-1, keepdims=True)
    centered = values - average
    inverse = lax.rsqrt(jnp.mean(centered * centered, axis=-1, keepdims=True) + epsilon)
    return (centered * inverse, inverse)


def normalize_back(normed, inverse, upstream):
    return inverse * (
        upstream
        - jnp.mean(upstream, axis=-1, keepdims=True)
        - normed * jnp.mean(upstream * normed, axis=-1, keepdims=True)
    )


def matmul(left, right):
    return jnp.dot(left, right, preferred_element_type=f32)


def contract_rows(left, right):
    return lax.dot_general(left, right, (((0,), (0,)), ((), ())), preferred_element_type=f32)


def times_transposed(left, right):
    return lax.dot_general(left, right, (((1,), (1,)), ((), ())), preferred_element_type=f32)


def silu_slope(values):
    sigmoid = jax.nn.sigmoid(values)
    return sigmoid * (1.0 + values * (1.0 - sigmoid))


def rope_tables(segments, widths):
    slots = widths.shape[0]
    one_hot = (segments[:, None] == jnp.arange(slots, dtype=jnp.int32)[None, :]).astype(jnp.int32)
    counts = jnp.sum(one_hot, axis=0)
    starts = jnp.cumsum(counts) - counts
    start_token = jnp.sum(one_hot * starts[None, :], axis=1)
    width_token = jnp.maximum(jnp.sum(one_hot * widths[None, :], axis=1), 1)
    place = jnp.arange(segments.shape[0], dtype=jnp.int32) - start_token
    row_place = (place // width_token).astype(f32)
    col_place = (place % width_token).astype(f32)
    freqs = 10000.0 ** (-jnp.arange(QUARTER, dtype=f32) / QUARTER)
    angle_row = row_place[:, None] * freqs[None, :]
    angle_col = col_place[:, None] * freqs[None, :]
    cos_row, sin_row, cos_col, sin_col = (
        jnp.cos(angle_row),
        jnp.sin(angle_row),
        jnp.cos(angle_col),
        jnp.sin(angle_col),
    )
    cos = jnp.concatenate([cos_row, cos_row, cos_col, cos_col], axis=1)
    sin = jnp.concatenate([-sin_row, sin_row, -sin_col, sin_col], axis=1)
    return jnp.tile(cos, (1, HEADS)), jnp.tile(sin, (1, HEADS))


def part(index):
    return slice(index * WIDTH, (index + 1) * WIDTH)


def rotate(values, cos, sin):
    lane = lax.broadcasted_iota(jnp.int32, (1, WIDTH), 1)
    leading = lane % (2 * QUARTER) < QUARTER
    partner = jnp.where(
        leading,
        pltpu.roll(values, WIDTH - QUARTER, 1),
        pltpu.roll(values, QUARTER, 1),
    )
    return values * cos + partner * sin


def take(start, size):
    return pl.ds(pl.multiple_of(start, 128 if size % 128 == 0 else 16), size)


def first_part(rows):
    return -(-rows // 32) * 16


def placed(refs, rows):
    first = first_part(rows)
    each = len(refs) // HALVES
    for other in range(HALVES):
        here = refs[each * other : each * other + each]
        for j in range(3):
            yield j, other, 0, rows, here[j]
        if each == COLUMNS:
            yield 3, other, 0, rows, here[3]
        else:
            yield 3, other, 0, first, here[3]
            yield 3, other, first, rows - first, here[4]


def piece_copies(where, count, sources, target, rows, sem):
    place, column, side = where
    copies = []
    for j, other, start, size, ref in placed(sources, rows):
        for by in range(1, count):
            owner = (place + (count - by)) % count
            to = target(column ^ j, side ^ other, owner, start, size)
            copies.append(pltpu.make_async_copy(ref.at[by - 1], to, sem(column ^ j, side ^ other, owner)))
    return copies


def wait_for(ref, sem):
    pltpu.make_async_copy(ref, ref, sem).wait()


def first_kernel(
    count, where_ref, x_ref, mod_ref, cos_ref, sin_ref, joint_ref, project_ref, *refs
):
    sources, refs = refs[:-9], refs[-9:]
    turned_ref, query_ref, keys_ref, values_ref, weight_ref, weight, first_ref, total, sems = refs
    where = where_ref[0], where_ref[1], where_ref[2]
    rows_in = joint_ref.shape[0]
    half = rows_in // HALVES

    def target(column, side, place, start, size):
        return weight.at[column, take(place * rows_in + side * half + start, size)]

    copies = piece_copies(where, count, sources, target, half, lambda c, s, z: sems.at[c])
    for c in range(COLUMNS):
        shard = project_ref if c == 3 else joint_ref.at[:, pl.ds(c * WIDTH, WIDTH)]
        copies.append(pltpu.make_async_copy(shard, weight.at[c, take(where[0] * rows_in, rows_in)], sems.at[c]))
    for copy in copies:
        copy.start()
    tokens = x_ref.shape[0]
    for i in range(tokens // CHUNK):
        rows = slice(i * CHUNK, (i + 1) * CHUNK)
        normed, _ = normalize(x_ref[rows, :].astype(f32))
        first_ref[rows, :] = (
            normed * (1.0 + mod_ref[i : i + 1, part(1)]) + mod_ref[i : i + 1, part(0)]
        ).astype(bf16)
    turned_ref[...] = first_ref[...].T
    writes = [
        pltpu.make_async_copy(weight.at[c], weight_ref.at[c], sems.at[c]) for c in range(COLUMNS)
    ]
    wait_for(weight.at[3], sems.at[3])
    writes[3].start()
    for c, out in enumerate((query_ref, keys_ref, values_ref)):
        wait_for(weight.at[c], sems.at[c])
        writes[c].start()
        if c == 2:
            out[...] = matmul(first_ref[...], weight[c]).astype(bf16)
        else:
            total[...] = matmul(first_ref[...], weight[c])

            @pl.loop(0, tokens // CHUNK)
            def _(i):
                rows = pl.ds(pl.multiple_of(i * CHUNK, CHUNK), CHUNK)
                out[rows, :] = rotate(total[rows, :], cos_ref[rows, :], sin_ref[rows, :]).astype(bf16)

    for write in writes:
        write.wait()


def window(head):
    start = head * HEAD_DIM // LANES * LANES
    stop = -(-(head + 1) * HEAD_DIM // LANES) * LANES
    lane = lax.broadcasted_iota(jnp.int32, (1, stop - start), 1) + start
    inside = (lane >= head * HEAD_DIM) & (lane < (head + 1) * HEAD_DIM)
    return slice(start, stop), inside


def soft_scores(left, right, allowed, axis):
    scores = times_transposed(left, right) * HEAD_DIM ** (-0.5)
    scores = jnp.where(allowed, scores, masked_score)
    exponent = jnp.exp(scores - jnp.max(scores, axis=axis, keepdims=True))
    return exponent * (1.0 / jnp.sum(exponent, axis=axis, keepdims=True))


def attend_kernel(
    query_ref, keys_ref, values_ref, column_ids, row_ids, x_ref, mod_ref,
    weight, turned_ref, branch_ref, middle_ref, second_ref, mixed,
):
    allowed = column_ids[...] == row_ids[...]
    for head in range(HEADS):
        lanes, inside = window(head)
        query = jnp.where(inside, query_ref[:, lanes], jnp.zeros((), bf16))
        probs = soft_scores(query, keys_ref[:, lanes], allowed, 1).astype(bf16)
        mixed[:, lanes] = jnp.where(inside, matmul(probs, values_ref[:, lanes]), mixed[:, lanes])
    attended = mixed[...].astype(bf16)
    turned_ref[...] = attended.T
    branch_ref[...] = matmul(attended, weight[0])
    for i in range(BLOCK // CHUNK):
        rows = slice(i * CHUNK, (i + 1) * CHUNK)
        mod = mod_ref.at[0]
        middle = x_ref[rows, :].astype(f32) + mod[i : i + 1, part(0)] * branch_ref[rows, :]
        middle_ref[rows, :] = middle
        normed, _ = normalize(middle)
        second_ref[rows, :] = (
            normed * (1.0 + mod[i : i + 1, part(2)]) + mod[i : i + 1, part(1)]
        ).astype(bf16)


def tile_copies(r, where, count, tile, pair, downs):
    place, mine, side = where
    t, j = tile
    column = mine ^ j
    rows, width = r["gate"].shape[0], r["hidden_w"].shape[1]
    sem = r["pair_sems"].at[t]
    copies = [
        pltpu.make_async_copy(
            r[name].at[:, take(column * width, width)], r["pair_w"].at[t, which, take(place * rows, rows)], sem
        )
        for which, name in enumerate(("gate", "up"))
    ]
    first = first_part(rows)
    for other in range(HALVES):
        for by in range(1, count):
            owner = (place + (count - by)) % count
            if j < 3:
                spans = [(pair[other][0].at[by - 1], 0, rows)]
            else:
                spans = [(pair[other][0].at[by - 1], 0, first), (pair[other][1].at[by - 1], first, rows - first)]
            for ref, start, size in spans:
                to = r["pair_w"].at[t, side ^ other, take(owner * rows + start, size)]
                copies.append(pltpu.make_async_copy(ref, to, sem))
    for copy in copies:
        copy.start()

    sem = r["down_sems"].at[t]
    target = r["down_w"].at[t]
    piece = width // PIECES

    @pl.when(column == place)
    def _():
        pltpu.make_async_copy(r["down"], target, sem).start()

    @pl.when(column != place)
    def _():
        by = jnp.maximum((place + count - column) % count, 1)
        for i, other, start, size, ref in placed(downs, piece):
            to = target.at[take(((mine ^ i) * HALVES + (side ^ other)) * piece + start, size)]
            pltpu.make_async_copy(ref.at[by - 1], to, sem).start()


def ffn_kernel(count, js, names, *refs):
    r = dict(zip(names, refs, strict=True))
    r["hidden_w"] = r["hidden"]
    first, last = js[0] == 0, js[-1] == COLUMNS - 1
    step = pl.program_id(0)
    tile = r["hidden"].shape[1]
    tokens = r["second"].shape[0]
    second, feed_back = r["second"], r["feed_back"]
    feed, second_back = r["feed"], r["second_back"]

    @pl.when(step == 0)
    def _():
        where = r["where"][0], r["where"][1], r["where"][2]
        for t, j in enumerate(js):
            pair = [
                [r[f"pair{j}_{other}_{i}"] for i in range(1 if j < 3 else 2)]
                for other in range(HALVES)
            ]
            tile_copies(r, where, count, (t, j), pair, [r[name] for name in names if name[:4] == "down" and name[5:].isdigit()])
        if first:
            r["turned"][...] = second[...].T
            for i in range(tokens // CHUNK):
                rows = slice(i * CHUNK, (i + 1) * CHUNK)
                upstream = r["cot"][rows, :].astype(f32) * r["factor"][0]
                feed_back[rows, :] = (upstream * r["mod"][i : i + 1, part(3)]).astype(bf16)

    pair_w, down_w = r["pair_w"].at[step], r["down_w"].at[step]
    wait_for(pair_w, r["pair_sems"].at[step])
    wait_for(down_w, r["down_sems"].at[step])
    sub = tile
    for n in range(tile // sub):
        lanes = slice(n * sub, (n + 1) * sub)
        gate = matmul(second[...], pair_w[0, :, lanes])
        upval = matmul(second[...], pair_w[1, :, lanes])
        hidden_back = times_transposed(feed_back[...], down_w[lanes, :])
        sigmoid = jax.nn.sigmoid(gate)
        silu = gate * sigmoid
        r["hidden"][:, lanes] = (silu * upval).astype(bf16)
        r["pair_back"][0, 1, :, lanes] = (hidden_back * silu).astype(bf16)
        r["pair_back"][0, 0, :, lanes] = (
            hidden_back * upval * (sigmoid * (1.0 + gate * (1.0 - sigmoid)))
        ).astype(bf16)

    r["hidden_turned"][0] = r["hidden"][...].T
    feed_part = matmul(r["hidden"][...], down_w[...])
    back_part = times_transposed(r["pair_back"][0, 0], pair_w[0]) + times_transposed(
        r["pair_back"][0, 1], pair_w[1]
    )

    @pl.when(step == 0)
    def _():
        feed[...] = feed_part if first else r["feed_in"][...] + feed_part
        second_back[...] = back_part if first else r["back_in"][...] + back_part

    @pl.when(step > 0)
    def _():
        feed[...] += feed_part
        second_back[...] += back_part

    if not last:
        return

    @pl.when(step == len(js) - 1)
    def _():
        for i in range(tokens // CHUNK):
            rows = slice(i * CHUNK, (i + 1) * CHUNK)
            gate_one = r["mod"][i : i + 1, part(0)]
            scale_two = r["mod"][i : i + 1, part(2)]
            gate_two = r["mod"][i : i + 1, part(3)]
            middle = r["middle"][rows, :]
            r["output"][rows, :] = (middle + gate_two * feed[rows, :]).astype(bf16)
            upstream = r["cot"][rows, :].astype(f32) * r["factor"][0]
            normed, inverse = normalize(middle)
            back = second_back[rows, :]
            middle_back = upstream + normalize_back(normed, inverse, back * (1.0 + scale_two))
            r["middle_back"][rows, :] = middle_back
            r["branch_back"][rows, :] = (middle_back * gate_one).astype(bf16)
            for where, values in enumerate(
                (middle_back * r["branch"][rows, :], back, back * normed, upstream * feed[rows, :])
            ):
                r["sums"][i : i + 1, part(where)] = jnp.sum(values, axis=0, keepdims=True)


ORDER = (1, 3, 2, 0)
SEND_X, KEEP_X, SEND_Y, KEEP_Y = (1, 3), (2, 0), (3, 2), (1, 0)
CUT = (SEND_X, KEEP_X, SEND_Y, KEEP_Y)


def put_grad(grad, other_ref, out_refs):
    step = pl.program_id(0)
    if other_ref is None:
        out_refs[0][0] = grad.astype(bf16)
        return
    total = (grad + other_ref[0].astype(f32)).astype(bf16)
    first = first_part(total.shape[1])
    for at, j in enumerate(ORDER):

        @pl.when(step == at)
        def _():
            for columns, ref in zip(CUT, out_refs, strict=True):
                if j in columns:
                    ref[0] = total[:, :first] if columns in (SEND_X, KEEP_X) else total[:, first:]


def cut_specs(count, rows, breadth):
    first = first_part(rows)
    shapes, specs = [], []
    for columns in CUT:
        size = first if columns in (SEND_X, KEEP_X) else rows - first
        shapes.append(struct((2, count, size, breadth), bf16))
        second = ORDER.index(columns[1])
        specs.append(
            pl.BlockSpec(
                (1, count, size, breadth),
                lambda s, where, second=second: (jnp.where(s >= second, 1, 0), 0, 0, 0),
            )
        )
    return tuple(shapes), tuple(specs)


def split_refs(mine, refs):
    return (refs[0], refs[1:]) if mine else (None, refs)


def pair_grad_kernel(mine, count, where_ref, turned_ref, own_ref, near_ref, far_ref, *refs):
    other_ref, out_refs = split_refs(mine, refs)
    for at, j in enumerate(ORDER):

        @pl.when(pl.program_id(0) == at)
        def _():
            back = {0: own_ref, 3: far_ref}.get(j, near_ref)
            grad = matmul(turned_ref[...], back[0, 0])
            put_grad(grad.reshape(count, grad.shape[0] // count, grad.shape[1]), other_ref, out_refs)


def down_grad_kernel(mine, where_ref, *refs):
    hiddens, feed_back_ref, out_ref = refs[:3], refs[3], refs[-1]
    other_ref = refs[4] if mine else None
    side = where_ref[2] if mine else where_ref[2] ^ 1
    count, _, rows, _ = out_ref.shape
    tiles = [(hidden, t) for hidden in hiddens for t in range(hidden.shape[0])]
    for j, (hidden, t) in enumerate(tiles):
        pieces = [hidden[t, take(((where_ref[1] ^ c) * HALVES + side) * rows, rows), :] for c in ORDER]
        grad = matmul(jnp.concatenate(pieces, axis=0), feed_back_ref[...]).reshape(COLUMNS, rows, WIDTH)
        owner = where_ref[1] ^ j
        if mine:
            grad = grad + other_ref[owner].astype(f32)
        out_ref[owner] = grad.astype(bf16)


def attn_grad_kernel(
    mine, where_ref, first_ref, attended_ref, joint_back_ref, branch_back_ref, *refs
):
    other_ref, out_refs = split_refs(mine, refs)
    column = where_ref[1] ^ where_ref[3 + pl.program_id(0)]
    side = where_ref[2] if mine else where_ref[2] ^ 1
    _, count, _, _ = out_refs[0].shape
    rows = WIDTH // count // HALVES

    def put(turned, right):
        taken = [turned[take((z * HALVES + side) * rows, rows), :] for z in range(count)]
        grad = matmul(jnp.concatenate(taken, axis=0), right[...])
        put_grad(grad.reshape(count, rows, WIDTH), other_ref, out_refs)

    @pl.when(column < 3)
    def _():
        put(first_ref, joint_back_ref)

    @pl.when(column == 3)
    def _():
        put(attended_ref, branch_back_ref)


def place_pair_kernel(where_ref, *refs):
    sources, outs = refs[:-2], refs[-2:]
    rows, tile = sources[0].shape
    for way in range(HALVES):

        @pl.when(where_ref[2] == way)
        def _():
            for j, other, start, size, ref in placed(sources, rows):
                lanes = take((where_ref[1] ^ j) * tile, tile)
                outs[way ^ other][start : start + size, lanes] = ref[...].astype(f32)


def place_down_kernel(rows, offset, where_ref, *refs):
    sources, out = refs[:-1], refs[-1]
    for j, other, start, size, ref in placed(sources, rows):
        piece = (where_ref[1] ^ j) * HALVES + (where_ref[2] ^ other)
        at = offset if ref.shape[0] > rows else 0
        out[take(piece * rows + start, size), :] = ref[at : at + size, :].astype(f32)


def place_attn_kernel(rows, where_ref, *refs):
    sources, joint_ref, project_ref = refs[:-2], refs[-2], refs[-1]
    for column in range(COLUMNS):

        @pl.when(where_ref[1] == column)
        def _():
            for j, other, start, size, ref in placed(sources, rows):
                to = take((where_ref[2] ^ other) * rows + start, size)
                if column ^ j == 3:
                    project_ref[to, :] = ref[:size, :].astype(f32)
                else:
                    joint_ref[to, part(column ^ j)] = ref[:size, :].astype(f32)


def place_both_kernel(attn_rows, down_rows, where_ref, *refs):
    sources, outs = refs[:-3], refs[-3:]
    each = len(sources) // HALVES
    sides = [sources[each * k : each * k + each] for k in range(HALVES)]
    place_attn_kernel(
        attn_rows, where_ref, *[ref for side in sides for ref in side[:4]], outs[0], outs[1]
    )
    downs = [ref for side in sides for ref in side[:3] + side[4:]]
    place_down_kernel(down_rows, attn_rows, where_ref, *downs, outs[2])


def attend_back_kernel(
    query_ref, keys_ref, values_ref, branch_back_ref, column_ids, row_ids, cos_ref,
    sin_ref, weight, joint_back_ref, mixed_back, query_back, keys_back, values_back,
):
    mixed_back[...] = times_transposed(branch_back_ref[...], weight[0]).astype(bf16)
    allowed = column_ids[...] == row_ids[...]
    scaling = HEAD_DIM ** (-0.5)
    for head in range(HEADS):
        lanes, inside = window(head)
        zero = jnp.zeros((), bf16)
        query = jnp.where(inside, query_ref[:, lanes], zero)
        back = jnp.where(inside, mixed_back[:, lanes], zero)
        soft = soft_scores(keys_ref[:, lanes], query, allowed, 0)
        probs_back = times_transposed(values_ref[:, lanes], back)
        scores_back = (
            soft * (probs_back - jnp.sum(soft * probs_back, axis=0, keepdims=True))
        ).astype(bf16)
        query_back[:, lanes] = jnp.where(
            inside, contract_rows(scores_back, keys_ref[:, lanes]) * scaling, query_back[:, lanes]
        )
        keys_back[:, lanes] = jnp.where(
            inside, matmul(scores_back, query) * scaling, keys_back[:, lanes]
        )
        values_back[:, lanes] = jnp.where(
            inside, matmul(soft.astype(bf16), back), values_back[:, lanes]
        )

    @pl.loop(0, BLOCK // CHUNK)
    def _(i):
        rows = pl.ds(pl.multiple_of(i * CHUNK, CHUNK), CHUNK)
        cos, sin = cos_ref[rows, :], sin_ref[rows, :]
        joint_back_ref[rows, part(0)] = rotate(query_back[rows, :], cos, -sin).astype(bf16)
        joint_back_ref[rows, part(1)] = rotate(keys_back[rows, :], cos, -sin).astype(bf16)
        joint_back_ref[rows, part(2)] = values_back[rows, :].astype(bf16)


def first_back_kernel(
    joint_back_ref, x_ref, middle_back_ref, mod_ref, weight, grad_ref, sums_ref, first_back
):
    step = pl.program_id(0)
    product = times_transposed(joint_back_ref[...], weight[0])

    @pl.when(step == 0)
    def _():
        first_back[...] = product

    @pl.when(step > 0)
    def _():
        first_back[...] += product

    @pl.when(step == pl.num_programs(0) - 1)
    def _():
        finish_first_back(x_ref, middle_back_ref, mod_ref, grad_ref, sums_ref, first_back)


def finish_first_back(x_ref, middle_back_ref, mod_ref, grad_ref, sums_ref, first_back):
    for i in range(x_ref.shape[0] // CHUNK):
        rows = slice(i * CHUNK, (i + 1) * CHUNK)
        normed, inverse = normalize(x_ref[rows, :].astype(f32))
        back = first_back[rows, :]
        grad_ref[rows, :] = middle_back_ref[rows, :] + normalize_back(
            normed, inverse, back * (1.0 + mod_ref[i : i + 1, part(1)])
        )
        sums_ref[i : i + 1, part(0)] = jnp.sum(back, axis=0, keepdims=True)
        sums_ref[i : i + 1, part(1)] = jnp.sum(back * normed, axis=0, keepdims=True)


SMEM = pl.BlockSpec(memory_space=pltpu.SMEM)
VMEM = pl.BlockSpec(memory_space=pltpu.VMEM)
ANY = pl.BlockSpec(memory_space=pl.ANY)


def struct(shape, dtype):
    return jax.ShapeDtypeStruct(shape, dtype)


def params(mega=56):
    return pltpu.CompilerParams(vmem_limit_bytes=mega * MEGA)


def cost(microseconds):
    return pl.CostEstimate(flops=int(microseconds * 1e9), bytes_accessed=1000, transcendentals=0)


def by_block(*shape):
    return pl.BlockSpec(shape, lambda b: (b,) + (0,) * (len(shape) - 1))


def whole(*shape):
    return pl.BlockSpec(shape, lambda *_: (0,) * len(shape))


def first_call(where, x, mod, cos, sin, joint, project, arrived):
    tokens = x.shape[0]
    count = arrived[0].shape[0] + 1
    shape = struct((tokens, WIDTH), bf16)
    return pl.pallas_call(
        functools.partial(first_kernel, count),
        out_shape=(struct((WIDTH, tokens), bf16),)
        + (shape,) * 3
        + (struct((COLUMNS, WIDTH, WIDTH), bf16),),
        in_specs=[SMEM, VMEM, VMEM, VMEM, VMEM] + [ANY] * (2 + len(arrived)),
        out_specs=(VMEM,) * 4 + (ANY,),
        scratch_shapes=[
            pltpu.VMEM((COLUMNS, WIDTH, WIDTH), bf16),
            pltpu.VMEM((tokens, WIDTH), bf16),
            pltpu.VMEM((tokens, WIDTH), f32),
            pltpu.SemaphoreType.DMA((COLUMNS,)),
        ],
        compiler_params=params(),
        cost_estimate=cost(20),
    )(where, x, mod, cos, sin, joint, project, *arrived)


def attend_call(query, keys, values, ids, x, mod, weight):
    tokens = x.shape[0]
    return pl.pallas_call(
        attend_kernel,
        grid=(tokens // BLOCK,),
        out_shape=(
            struct((WIDTH, tokens), bf16),
            struct((tokens, WIDTH), f32),
            struct((tokens, WIDTH), f32),
            struct((tokens, WIDTH), bf16),
        ),
        in_specs=[by_block(BLOCK, WIDTH)] * 3
        + [by_block(BLOCK, 1), pl.BlockSpec((1, BLOCK), lambda b: (0, b)), by_block(BLOCK, WIDTH)]
        + [by_block(1, BLOCK // CHUNK, 4 * WIDTH), pl.BlockSpec((1, WIDTH, WIDTH), lambda b: (3, 0, 0))],
        out_specs=(pl.BlockSpec((WIDTH, BLOCK), lambda b: (0, b)),) + (by_block(BLOCK, WIDTH),) * 3,
        scratch_shapes=[pltpu.VMEM((BLOCK, WIDTH), f32)],
        compiler_params=params(),
        cost_estimate=cost(2),
    )(
        query, keys, values, ids[:, None], ids[None, :], x,
        mod.reshape(tokens // BLOCK, BLOCK // CHUNK, 4 * WIDTH), weight,
    )


def ffn_call(js, where, given, shards, pairs, downs):
    second = given["second"]
    tokens = second.shape[0]
    ff = shards["gate"].shape[1]
    tile = ff // COLUMNS
    count = ff // shards["down"].shape[0]
    chunks = tokens // CHUNK
    first, last = js[0] == 0, js[-1] == COLUMNS - 1
    full = whole(tokens, WIDTH)
    wide = struct((tokens, WIDTH), f32)
    narrow = struct((tokens, WIDTH), bf16)
    inputs = [("where", where, SMEM), ("second", second, full)]
    if first or last:
        inputs += [
            ("factor", given["factor"], SMEM),
            ("cot", given["cot"], full),
            ("mod", given["mod"], whole(chunks, 4 * WIDTH)),
        ]
    if not first:
        inputs += [
            ("feed_back", given["feed_back"], full),
            ("feed_in", given["feed"], full),
            ("back_in", given["second_back"], full),
        ]
    if last:
        inputs += [("middle", given["middle"], full), ("branch", given["branch"], full)]
    inputs += [(name, shards[name], ANY) for name in ("gate", "up", "down")]
    for j in js:
        for other in range(HALVES):
            inputs += [(f"pair{j}_{other}_{i}", a, ANY) for i, a in enumerate(pairs[other][j])]
    inputs += [(f"down_{i}", a, ANY) for i, a in enumerate(downs)]
    outputs = [
        (
            "hidden_turned",
            struct((len(js), tile, tokens), bf16),
            pl.BlockSpec((1, tile, tokens), lambda t: (t, 0, 0)),
        ),
        (
            "pair_back",
            struct((len(js), HALVES, tokens, tile), bf16),
            pl.BlockSpec((1, HALVES, tokens, tile), lambda t: (t, 0, 0, 0)),
        ),
    ]
    if first:
        outputs += [
            ("turned", struct((WIDTH, tokens), bf16), whole(WIDTH, tokens)),
            ("feed_back", narrow, full),
        ]
    sums = ("feed", "second_back")
    scratch = [
        ("pair_w", pltpu.VMEM((len(js), HALVES, WIDTH, tile), bf16)),
        ("down_w", pltpu.VMEM((len(js), ff // count, WIDTH), bf16)),
        ("hidden", pltpu.VMEM((tokens, tile), bf16)),
        ("pair_sems", pltpu.SemaphoreType.DMA((len(js),))),
        ("down_sems", pltpu.SemaphoreType.DMA((len(js),))),
    ]
    if last:
        outputs += [
            ("output", narrow, full),
            ("middle_back", wide, full),
            ("branch_back", narrow, full),
            ("sums", struct((chunks, 4 * WIDTH), f32), whole(chunks, 4 * WIDTH)),
        ]
        scratch += [(name, pltpu.VMEM((tokens, WIDTH), f32)) for name in sums]
    else:
        outputs += [(name, wide, full) for name in sums]
    names = [each[0] for each in inputs + outputs + scratch]
    found = pl.pallas_call(
        functools.partial(ffn_kernel, count, js, names),
        grid=(len(js),),
        out_shape=tuple(shape for _, shape, _ in outputs),
        in_specs=[spec for _, _, spec in inputs],
        out_specs=tuple(spec for _, _, spec in outputs),
        scratch_shapes=[shape for _, shape in scratch],
        compiler_params=params(),
        cost_estimate=cost(2 if first else 12 * len(js)),
    )(*[array for _, array, _ in inputs])
    return {name: array for (name, _, _), array in zip(outputs, found, strict=True)}


def by_column(call, count, rows, breadth, in_specs, where, arrays, other):
    shapes, specs = cut_specs(count, rows, breadth)
    block = pl.BlockSpec((1, count, rows, breadth), lambda s, where: (s, 0, 0, 0))
    if other is None:
        shapes, specs = (struct((COLUMNS, count, rows, breadth), bf16),), (block,)
    else:
        in_specs, arrays = in_specs + [block], arrays + (other,)
    found = pl.pallas_call(
        call,
        out_shape=shapes,
        grid_spec=pltpu.PrefetchScalarGridSpec(
            num_scalar_prefetch=1, grid=(COLUMNS,), in_specs=in_specs, out_specs=specs
        ),
        compiler_params=params(),
        cost_estimate=cost(3),
    )(where, *arrays)
    return found[0] if other is None else found


def pair_grad_call(count, where, turned, backs, other=None):
    tokens, tile = backs[0].shape[2:]
    mine = other is not None

    def spec(tile_of):
        return pl.BlockSpec(
            (1, 1, tokens, tile),
            lambda s, where: (tile_of(where[3 + s]), where[2] if mine else where[2] ^ 1, 0, 0),
        )

    return by_column(
        functools.partial(pair_grad_kernel, mine, count),
        count, WIDTH // count, tile,
        [whole(WIDTH, tokens), spec(lambda j: 0), spec(lambda j: jnp.clip(j - 1, 0, 1)), spec(lambda j: 0)],
        where, (turned,) + tuple(backs), other,
    )


def attn_grad_call(count, where, first, attended, joint_back, branch_back, other=None):
    tokens = first.shape[1]
    return by_column(
        functools.partial(attn_grad_kernel, other is not None),
        count, WIDTH // count // HALVES, WIDTH,
        [
            whole(WIDTH, tokens),
            whole(WIDTH, tokens),
            pl.BlockSpec((tokens, WIDTH), lambda s, where: (0, jnp.minimum(where[1] ^ where[3 + s], 2))),
            whole(tokens, WIDTH),
        ],
        where, (first, attended, joint_back, branch_back), other,
    )


def down_grad_call(count, where, hiddens, feed_back, other=None):
    ff = sum(h.shape[0] * h.shape[1] for h in hiddens)
    out = struct((count, COLUMNS, ff // count // PIECES, WIDTH), bf16)
    arrays = tuple(hiddens) + (feed_back,) + (() if other is None else (other,))
    return pl.pallas_call(
        functools.partial(down_grad_kernel, other is not None),
        out_shape=out,
        in_specs=[SMEM] + [VMEM] * len(arrays),
        out_specs=VMEM,
        compiler_params=params(),
        cost_estimate=cost(3),
    )(where, *arrays)


def place_call(kernel, where, arrays, outs):
    return pl.pallas_call(
        kernel,
        out_shape=outs,
        in_specs=[SMEM] + [VMEM] * len(arrays),
        out_specs=jax.tree.map(lambda _: VMEM, outs),
        compiler_params=params(),
        cost_estimate=cost(4),
    )(where, *arrays)


def attend_back_call(query, keys, values, branch_back, ids, cos, sin, weight):
    tokens = query.shape[0]
    block = by_block(BLOCK, WIDTH)
    return pl.pallas_call(
        attend_back_kernel,
        grid=(tokens // BLOCK,),
        out_shape=struct((tokens, 3 * WIDTH), bf16),
        in_specs=[block, block, block, block]
        + [by_block(BLOCK, 1), pl.BlockSpec((1, BLOCK), lambda b: (0, b)), block, block]
        + [pl.BlockSpec((1, WIDTH, WIDTH), lambda b: (3, 0, 0))],
        out_specs=by_block(BLOCK, 3 * WIDTH),
        scratch_shapes=[
            pltpu.VMEM((BLOCK, WIDTH), bf16),
            pltpu.VMEM((BLOCK, WIDTH), f32),
            pltpu.VMEM((BLOCK, WIDTH), f32),
            pltpu.VMEM((BLOCK, WIDTH), f32),
        ],
        compiler_params=params(),
        cost_estimate=cost(8),
    )(query, keys, values, branch_back, ids[:, None], ids[None, :], cos, sin, weight)


def first_back_call(joint_back, x, middle_back, mod, weight):
    tokens = x.shape[0]
    chunks = tokens // CHUNK
    full = whole(tokens, WIDTH)
    return pl.pallas_call(
        first_back_kernel,
        grid=(3,),
        out_shape=(struct((tokens, WIDTH), f32), struct((chunks, 2 * WIDTH), f32)),
        in_specs=[
            pl.BlockSpec((tokens, WIDTH), lambda c: (0, c)),
            full,
            full,
            whole(chunks, 2 * WIDTH),
            pl.BlockSpec((1, WIDTH, WIDTH), lambda c: (c, 0, 0)),
        ],
        out_specs=(full, whole(chunks, 2 * WIDTH)),
        scratch_shapes=[pltpu.VMEM((tokens, WIDTH), f32)],
        compiler_params=params(),
        cost_estimate=cost(2),
    )(joint_back, x, middle_back, mod, weight)


def shifts(count, by):
    return [(i, (i + by) % count) for i in range(count)]


def pick(array, index):
    return lax.dynamic_index_in_dim(array, index, 0, keepdims=False)


def across(bit):
    return [(i, i ^ bit) for i in range(PIECES)]


def swap(array, bit):
    return lax.ppermute(array, "bucket", across(bit))


def after(arrays, *others):
    return lax.optimization_barrier((arrays, others))[0]


def add(left, right):
    return (left.astype(f32) + right.astype(f32)).astype(bf16)


def over_z(piece):
    count = lax.axis_size("fsdp")
    return [lax.ppermute(piece, "fsdp", shifts(count, by)) for by in range(1, count)]


def gather_z(piece, *others):
    count = lax.axis_size("fsdp")
    place = lax.axis_index("fsdp")
    full = after(lax.all_gather(piece, "fsdp", axis=0, tiled=False), *others)
    return jnp.stack([pick(full, (place + count - by) % count) for by in range(1, count)])


def cross(by_x, by_y, first):
    if first is not None:
        by_x, by_y = by_x[..., :first, :], by_y[..., first:, :]
    return swap(by_x, 4), swap(by_y, 2)


def both(here):
    return here + tuple(None if array is None else swap(array, 1) for array in here)


def direct(piece):
    return piece, swap(piece, 2), swap(piece, 4), swap(piece, 6)


def spread_whole(pieces):
    first = first_part(pieces.shape[1])

    def of(side):
        own, by_x, by_y, far = (pieces[c * HALVES + side] for c in range(COLUMNS))
        return own, by_x, by_y, far[:first], far[first:]

    return of(0) + of(1)


def halve_once(cut):
    send_x, (a2, a0), send_y, (b1, b0) = cut
    from_x, from_y = swap(send_x, 2), swap(send_y, 4)
    return add(a0, from_x[0]), add(a2, from_x[1]), add(b0, from_y[1]), add(b1, from_y[0])


def halve_twice(once, *others):
    a0, a2, b0, b1 = once
    if others:
        a0, b0 = after((a0, b0), *others)
    return jnp.concatenate([add(a0, swap(a2, 4)), add(b0, swap(b1, 2))], axis=-2)


def send_z(parts):
    count = lax.axis_size("fsdp")
    place = lax.axis_index("fsdp")
    return [
        lax.ppermute(pick(parts, (place + by) % count), "fsdp", shifts(count, by))
        for by in range(1, count)
    ]


def total_z(parts, others):
    total = pick(parts, lax.axis_index("fsdp")).astype(f32)
    for array in others:
        total = total + array.astype(f32)
    return total.astype(bf16)


def sum_z(parts):
    return total_z(parts, send_z(parts))


def cut_down(part, first):
    cut = []
    for columns in CUT:
        both_columns = jnp.stack([part[ORDER.index(j)] for j in columns])
        cut.append(both_columns[:, :first] if columns in (SEND_X, KEEP_X) else both_columns[:, first:])
    return cut


def uncut(cut):
    def of(j, pair):
        columns = next(c for c in pair if j in c)
        return cut[CUT.index(columns)][columns.index(j)]

    return jnp.stack(
        [jnp.concatenate([of(j, (SEND_X, KEEP_X)), of(j, (SEND_Y, KEEP_Y))], axis=1) for j in ORDER]
    )


def sum_whole(mine, theirs):
    parts = jnp.stack([mine, theirs], axis=1)
    parts = jnp.stack([parts[ORDER.index(c)] for c in range(COLUMNS)])
    rows, breadth = mine.shape[2:]
    parts = lax.psum(parts, "bucket").transpose(2, 0, 1, 3, 4)
    return spread_whole(sum_z(parts).reshape(PIECES, rows, breadth))


def arrived_whole(pieces):
    count = lax.axis_size("fsdp")
    place = lax.axis_index("fsdp")
    first = first_part(pieces.shape[1])
    full = lax.all_gather(pieces, "fsdp", axis=0, tiled=False)
    full = jnp.stack([pick(full, (place + count - by) % count) for by in range(1, count)])

    def of(side):
        own, by_x, by_y, far = (full[:, c * HALVES + side] for c in range(COLUMNS))
        return own, by_x, by_y, far[:, :first], far[:, first:]

    return of(0) + of(1)


def to_group(rows, count, place):
    relative = jnp.stack(
        [pick(rows, place)]
        + [
            lax.ppermute(pick(rows, (place + by) % count), "fsdp", shifts(count, by))
            for by in range(1, count)
        ]
    )
    return jnp.stack([pick(relative, (place - j) % count) for j in range(count)])


def on_device(
    inputs,
    condition,
    segment_ids,
    grid_widths,
    bucket_counts,
    modulate_weight,
    joint_weight,
    project_weight,
    gate_weight,
    up_weight,
    down_weight,
    cotangent,
):
    fsdp_count = lax.axis_size("fsdp")
    place = lax.axis_index("fsdp")
    bucket = lax.axis_index("bucket")
    height = joint_weight.shape[0]
    half = height // HALVES
    ff = gate_weight.shape[1]
    tile = ff // COLUMNS
    down_rows = down_weight.shape[0] // PIECES
    slots = condition.shape[0]

    cond_float = condition.astype(f32)
    lifted = jax.nn.silu(cond_float).astype(bf16)
    lifted_rows = to_group(
        lifted.reshape(slots, fsdp_count, height).transpose(1, 0, 2), fsdp_count, place
    ).reshape(fsdp_count * slots, height)
    one_hot = (
        segment_ids[::CHUNK, None] == jnp.arange(slots, dtype=jnp.int32)[None, :]
    ).astype(f32)

    def modulation_parts(weight, rows):
        parts = matmul(rows, weight).reshape(fsdp_count, slots, weight.shape[1])
        return [pick(parts, place)] + [
            lax.ppermute(pick(parts, (place + by) % fsdp_count), "fsdp", shifts(fsdp_count, by))
            for by in range(1, fsdp_count)
        ]

    def modulation(parts):
        return jnp.dot(
            one_hot,
            sum(parts[1:], parts[0]),
            precision=lax.Precision.HIGHEST,
            preferred_element_type=f32,
        )

    first_rows = modulation_parts(modulate_weight[:, : 2 * WIDTH], lifted_rows)
    mod_one = modulation(first_rows)
    fast = lax.axis_size("bucket") == PIECES
    if fast:
        column, side = bucket // HALVES, bucket % HALVES
        where = jnp.stack([place, column, side] + [jnp.int32(j) for j in ORDER])
        attn_piece = jnp.where(
            column == 3,
            lax.dynamic_slice(project_weight, (side * half, 0), (half, WIDTH)),
            lax.dynamic_slice(joint_weight, (side * half, column * WIDTH), (half, WIDTH)),
        )
        ffn_piece = jnp.where(
            side == 0,
            lax.dynamic_slice(gate_weight, (0, column * tile), (height, tile)),
            lax.dynamic_slice(up_weight, (0, column * tile), (height, tile)),
        )
        down_piece = lax.dynamic_slice_in_dim(down_weight, bucket * down_rows, down_rows, 0)
        attn_z = gather_z(attn_piece, first_rows)
        down_k = over_z(after(down_piece, attn_z))
        attn_x, attn_y = swap(attn_z, 2), swap(attn_z, 4)
        attn_x, attn_y, down_k = after((attn_x, attn_y, down_k))
        attn_far = cross(attn_x, attn_y, first_part(half))
        pair_z = gather_z(after(ffn_piece, down_k))
        down_z = jnp.stack(down_k)
        attn_arrived = both((attn_z, attn_x, attn_y) + attn_far)
        inputs, down_z = after((inputs, down_z), attn_far)
        down_x, down_y = swap(down_z, 2), swap(down_z, 4)
        inputs = after(inputs, down_z)
    else:
        where = jnp.stack([place, 0 * place, 0 * place] + [jnp.int32(j) for j in ORDER])
        attn_arrived = arrived_whole(
            jnp.concatenate([joint_weight, project_weight], axis=1)
            .reshape(HALVES, half, COLUMNS, WIDTH)
            .transpose(2, 0, 1, 3)
            .reshape(PIECES, half, WIDTH)
        )
        pairs = arrived_whole(
            jnp.stack([gate_weight, up_weight])
            .reshape(HALVES, height, COLUMNS, tile)
            .transpose(2, 0, 1, 3)
            .reshape(PIECES, height, tile)
        )
        downs = arrived_whole(down_weight.reshape(PIECES, down_rows, WIDTH))

    if fast:
        lifted_rows = after(lifted_rows, down_k)
    late_rows = modulation_parts(modulate_weight[:, 2 * WIDTH :], lifted_rows)
    counts = bucket_counts.astype(f32)
    mine = jnp.sum(jnp.where(jnp.arange(counts.shape[0], dtype=jnp.int32) == bucket, counts, 0.0))
    factor = (mine * counts.shape[0] / jnp.sum(counts)).reshape(1)
    cos, sin = rope_tables(segment_ids, grid_widths)

    first, query, keys, values, weight = first_call(
        where, inputs, mod_one, cos, sin, joint_weight, project_weight, attn_arrived
    )
    if fast:
        late_rows = [late_rows[0], *after(late_rows[1:], query)]
        down_x, down_y = after((down_x, down_y), query)
        down_far = cross(down_x, down_y, first_part(down_rows))
        downs = (down_z, down_x, down_y) + down_far
        pair_z = after(pair_z, query)
        pair_x, pair_y = swap(pair_z, 2), swap(pair_z, 4)
    mod = modulation(late_rows)
    attended, branch, middle, second = attend_call(
        query, keys, values, segment_ids, inputs, mod, weight
    )
    shards = dict(gate=gate_weight, up=up_weight, down=down_weight)
    given = dict(
        second=second, factor=factor, cot=cotangent, mod=mod, middle=middle, branch=branch
    )
    if fast:
        downs = both(after(downs, second))
        pairs = (pair_z, pair_x, pair_y, None, None, swap(pair_z, 1), None, None, None, None)
    pairs = [
        [[group] for group in pairs[5 * k : 5 * k + 3]] + [list(pairs[5 * k + 3 : 5 * k + 5])]
        for k in range(HALVES)
    ]
    found = ffn_call((0,), where, given, shards, pairs, downs)
    turned, feed_back = found["turned"], found["feed_back"]
    steps = [found]
    if fast:
        pair_x, pair_y = after((pair_x, pair_y), feed_back)
        far = cross(pair_x, pair_y, first_part(height))
        pairs[1][1:3] = [swap(pair_x, 1)], [swap(pair_y, 1)]
    for js in ((1, 2), (3,)):
        given.update(feed_back=feed_back, feed=found["feed"], second_back=found["second_back"])
        if fast and js == (3,):
            far = after(far, found["feed"])
            pairs[0][3], pairs[1][3] = list(far), [swap(array, 1) for array in far]
        found = ffn_call(js, where, given, shards, pairs, downs)
        steps.append(found)
    output, middle_back, branch_back = found["output"], found["middle_back"], found["branch_back"]
    late_sums = found["sums"]

    def by_slot(chunk_sums):
        return lax.dot_general(
            one_hot,
            chunk_sums,
            (((0,), (0,)), ((), ())),
            precision=lax.Precision.HIGHEST,
            preferred_element_type=f32,
        ).astype(bf16)

    def near_rows(rows):
        return jnp.concatenate([rows] + over_z(rows), axis=0)

    late_rows = jnp.concatenate([by_slot(late_sums), lifted], axis=1)
    late_k = over_z(late_rows)

    count = fsdp_count
    hiddens = [step["hidden_turned"] for step in steps]
    backs = [step["pair_back"] for step in steps]
    pair_theirs = pair_grad_call(count, where, turned, backs)
    late_k, pair_theirs = after((late_k, pair_theirs))
    near_late = jnp.concatenate([late_rows] + late_k, axis=0)
    late = lax.all_gather(near_late, "bucket", axis=0, tiled=True)
    if fast:
        pair_other = swap(pair_theirs, 1)
        feed_back = after(feed_back, pair_theirs)
    else:
        pair_other = jnp.zeros_like(pair_theirs)
    down_theirs = down_grad_call(count, where, hiddens, feed_back)
    if fast:
        pair_other, down_theirs = after((pair_other, down_theirs))
        down_other = swap(down_theirs, 1)
    else:
        down_other = jnp.zeros_like(down_theirs)
    pair_cut = pair_grad_call(count, where, turned, backs, pair_other)
    if fast:
        feed_back = after(feed_back, pair_cut)
    down_mine = down_grad_call(count, where, hiddens, feed_back, down_other)
    if fast:
        down_mine, late = after((down_mine, late))
        down_part = lax.psum_scatter(down_mine, "fsdp", scatter_dimension=0, tiled=False)
        branch_back = after(branch_back, down_mine)
    joint_back = attend_back_call(
        query, keys, values, branch_back, segment_ids, cos, sin, weight
    )
    attn_theirs = attn_grad_call(count, where, first, attended, joint_back, branch_back)
    if fast:
        send_x, keep_x, send_y, keep_y = pair_cut
        keep_x, keep_y, attn_theirs = after((keep_x, keep_y, attn_theirs))
        pair_once = halve_once((send_x, keep_x, send_y, keep_y))
        pair_once, attn_theirs, middle_back = after((pair_once, attn_theirs, middle_back))
        attn_other = swap(attn_theirs, 1)
    grad_inputs, early_sums = first_back_call(joint_back, inputs, middle_back, mod_one, weight)
    if fast:
        a0, a2, b0, b1 = pair_once
        branch_back, grad_inputs = after((branch_back, grad_inputs))
        attn_cut = attn_grad_call(
            count, where, first, attended, joint_back, branch_back, attn_other
        )
        a0, b0, attn_cut = after((a0, b0, attn_cut))
        pair_parts = halve_twice((a0, a2, b0, b1))
        attn_cut, down_part, pair_parts, early_sums = after(
            (attn_cut, down_part, pair_parts, early_sums)
        )
        pair_sum = lax.psum_scatter(pair_parts, "fsdp", scatter_dimension=0, tiled=False)
    near_early = near_rows(by_slot(early_sums))
    early = lax.all_gather(near_early, "bucket", axis=0, tiled=True)
    slope_rows = times_transposed(
        jnp.concatenate([near_early, near_late[:, : 4 * WIDTH]], axis=1), modulate_weight
    ).reshape(fsdp_count, slots, height)
    slopes = [slope_rows[0]] + [
        lax.ppermute(slope_rows[count - by], "fsdp", shifts(count, by)) for by in range(1, count)
    ]
    if fast:
        down_cut = cut_down(down_part, first_part(down_rows))
        send_x, keep_x, send_y, keep_y = (
            jnp.concatenate([attn.reshape(2, -1, WIDTH), down], axis=1)
            for attn, down in zip(attn_cut, down_cut, strict=True)
        )
        keep_x, keep_y, slopes = after((keep_x, keep_y, slopes))
        (a0, a2, b0, b1), pair_sum = after((halve_once((send_x, keep_x, send_y, keep_y)), pair_sum))
        pair_x, pair_y = swap(pair_sum, 2), swap(pair_sum, 4)
        ahead, behind = add(a0, swap(a2, 4)), add(b0, swap(b1, 2))
        at, other_at = (part.shape[1] * part.shape[2] for part in (attn_cut[0], attn_cut[2]))
        attn_parts = jnp.concatenate(
            [half.reshape(count, -1, WIDTH) for half in (ahead[:at], behind[:other_at])], axis=1
        )
        down_total = jnp.concatenate([ahead[at:], behind[other_at:]], axis=0)
        attn_parts, down_total = after((attn_parts, down_total))
        attn_z = send_z(attn_parts)
        pair_x, pair_y, attn_z[1] = after((pair_x, pair_y, attn_z[1]))
        pair_sums = (pair_sum, pair_x, pair_y) + cross(pair_x, pair_y, first_part(height))
        attn_z, pair_sums = after((attn_z, both(pair_sums)))
        attn_sum = total_z(attn_parts, attn_z)
    else:
        down_sums = sum_whole(down_mine.swapaxes(0, 1), down_theirs.swapaxes(0, 1))
        pair_sums = sum_whole(uncut(pair_cut), pair_theirs)
        attn_cut = attn_grad_call(
            count, where, first, attended, joint_back, branch_back, jnp.zeros_like(attn_theirs)
        )
        attn_sums = sum_whole(uncut(attn_cut), attn_theirs)
    if fast:
        early, attn_sum = after((early, attn_sum))
        both_sum = jnp.concatenate([attn_sum, down_total], axis=0)
        both_x, both_y = swap(both_sum, 2), swap(both_sum, 4)
    all_back = jnp.concatenate([early, late[:, : 4 * WIDTH]], axis=1)
    all_lifted = lax.dynamic_slice_in_dim(late, 4 * WIDTH + place * height, height, 1)
    modulate_gradient = contract_rows(all_lifted, all_back)
    pair_grad = place_call(
        place_pair_kernel, where, pair_sums, (struct(gate_weight.shape, f32),) * 2
    )
    if fast:
        both_x, both_y, pair_grad, modulate_gradient = after(
            (both_x, both_y, pair_grad, modulate_gradient)
        )
        both_sums = both((both_sum, both_x, both_y) + cross(both_x, both_y, half))
    slopes = jnp.stack(slopes)
    condition_slope = (
        jnp.stack([pick(slopes, (place + count - j) % count) for j in range(count)])
        .transpose(1, 0, 2)
        .reshape(slots, WIDTH)
    )
    grad_condition = condition_slope * silu_slope(cond_float)
    attn_shapes = (struct(joint_weight.shape, f32), struct(project_weight.shape, f32))
    down_shape = struct(down_weight.shape, f32)
    if fast:
        *attn_grad, down_grad = place_call(
            functools.partial(place_both_kernel, half, down_rows),
            where,
            both_sums,
            attn_shapes + (down_shape,),
        )
    else:
        down_grad = place_call(
            functools.partial(place_down_kernel, down_rows, 0), where, down_sums, down_shape
        )
        attn_grad = place_call(
            functools.partial(place_attn_kernel, half), where, attn_sums, attn_shapes
        )
    return (
        output,
        grad_inputs,
        grad_condition,
        modulate_gradient,
        *attn_grad,
        *pair_grad,
        down_grad,
    )


def solution(mesh):
    spread = P(("bucket", "fsdp"), None)
    rows = P("fsdp", None)
    in_specs = (
        spread, spread, P(("bucket", "fsdp")), P(("bucket", "fsdp")), P(),
        rows, rows, rows, rows, rows, rows, spread,
    )
    out_specs = (spread, spread, spread, rows, rows, rows, rows, rows, rows)
    return jax.shard_map(
        on_device, mesh=mesh, in_specs=in_specs, out_specs=out_specs, check_vma=False
    )
```
